256 devices in a mesh: gx: 8 (over y, x_hi), yz: 32 (over x_lo, z, core).
Axes of the slice: x: 4 (x_hi: 2, x_lo: 2; x = x_hi * 2 + x_lo), y: 4, z: 8, core: 2. Of those that a mesh axis runs over, the one named last changes fastest.
Arguments:
- features: bfloat16 [16, 32, 128, 1152], P('gx', 'yz'), may hold values from -6 to 6
- positions: float32 [16, 32, 3, 128], P('gx', 'yz'), may hold values from 0 to 1
- edge_dst: int32 [3, 16, 32, 128], P(None, 'gx', 'yz'), may hold values from 0 to 1535, as said below
- edge_shift: int32 [3, 16, 32, 128], P(None, 'gx', 'yz'), may hold values from -1 to 1
- radial_weights: float32 [8, 896], replicated, may hold values from -2 to 2
- readout_weights: float32 [8, 256], replicated, may hold values from -0.1875 to 0.1875
- w_scalar: bfloat16 [128, 128], replicated, may hold values from -0.5 to 0.5
- w_gate: bfloat16 [128, 128], replicated, may hold values from -0.5 to 0.5
- w_vector: bfloat16 [128, 128], replicated, may hold values from -0.5 to 0.5
- w_tensor: bfloat16 [128, 128], replicated, may hold values from -0.5 to 0.5
Outputs:
- mixed_features: bfloat16 [16, 32, 128, 1152], P('gx', 'yz')
- forces: float32 [16, 32, 3, 128], P('gx', 'yz')
The draws below stay inside these ranges and needn't reach their ends.
Inputs may be any that keep to these rules, and one draw needn't show every extreme that they name: `edge_dst`: each index names a slot of a pillar in the local layout of (4) x (3) pillars of 128 slots (ghost pillars around the device's own, pillar after pillar, then slot); its pillar is the edge's own pillar or one of the eight around it.
All inputs are finite; a program needn't handle non-finite values.
Results may differ from the reference program's by a relative error of at most 0.005.
Values may be sent and summed in bfloat16 or wider, within the bound.
A program may use at most 64 MiB of HBM per device.

```python
import math
import jax
import jax.numpy as jnp
from jax import lax

C = 128
NB = 8
SLOTS = 128
K = 3
CX = 2
CY = 1
GX_PILLARS = 16
GY_PILLARS = 32


def draw_edge_dst(key, part):
    key = jax.random.fold_in(key, 11)
    key_x, key_y, key_s = jax.random.split(key, 3)
    edge_shape = (K, GX_PILLARS, GY_PILLARS, SLOTS)
    step_x = jax.random.randint(key_x, edge_shape, -1, 2)
    step_y = jax.random.randint(key_y, edge_shape, -1, 2)
    slot_pick = jax.random.randint(key_s, edge_shape, 0, SLOTS)
    local_x = (jnp.arange(GX_PILLARS) % CX)[None, :, None, None]
    local_y = (jnp.arange(GY_PILLARS) % CY)[None, None, :, None]
    slot_ids = jnp.arange(SLOTS)[None, None, None, :]
    edge_ids = jnp.arange(K)[:, None, None, None]
    upper = (edge_ids == 0) & (slot_ids == SLOTS - 1)
    lower = (edge_ids == K - 1) & (slot_ids == 0)
    step_x = jnp.where(upper, 1, jnp.where(lower, -1, step_x))
    step_y = jnp.where(upper, 1, jnp.where(lower, -1, step_y))
    slot_pick = jnp.where(upper, SLOTS - 1, jnp.where(lower, 0, slot_pick))
    ext_x = local_x + 1 + step_x
    ext_y = local_y + 1 + step_y
    return ((ext_x * (CY + 2) + ext_y) * SLOTS + slot_pick).astype(jnp.int32)


def with_ends(result, stream_key, smallest, largest):
    longest = result.shape.index(max(result.shape))
    spots = []
    for shift in (0, 1):
        where = [jax.random.randint(jax.random.fold_in(stream_key, axis), (), 0, length) for axis, length in enumerate(result.shape)]
        where[longest] = (where[longest] + shift) % result.shape[longest]
        spots.append(tuple(where))
    return result.at[spots[0]].set(smallest).at[spots[1]].set(largest)


def block_scale(rng, shape, cuts, low, largest):
    loudness, own = 1.0, jax.random.fold_in(rng, 6)
    for position, blocks in cuts:
        heights = jnp.exp(jax.random.uniform(jax.random.fold_in(own, position), (blocks,), jnp.float32, low / len(cuts), largest / len(cuts)))
        loudness = loudness * jnp.repeat(heights, shape[position] // blocks).reshape([-1 if axis == position else 1 for axis in range(len(shape))])
    return loudness


def noise(key, dims, spread, most, shards=(), dtype=jnp.bfloat16):
    array = jax.random.normal(key, dims, jnp.float32) * spread
    if len(shards) > 0:
        array = block_scale(key, dims, shards, -0.22, 0.18) * array
    return jnp.clip(array, min=-most, max=most).astype(dtype)


def setup_inputs(seed: int = 0) -> dict:
    arg_keys = jax.random.split(jax.random.key(seed), 11)
    return {
        "features": noise(arg_keys[0], (GX_PILLARS, GY_PILLARS, SLOTS, 9 * C), 1.0, 6.0, ((0, 8), (1, 32))),
        "positions": jnp.clip(1.0 * jax.random.uniform(arg_keys[1], (GX_PILLARS, GY_PILLARS, 3, SLOTS), jnp.float32) ** block_scale(arg_keys[1], (GX_PILLARS, GY_PILLARS, 3, SLOTS), ((0, 8), (1, 32)), -0.2, 0.2), 0.0, 1.0),
        "edge_dst": draw_edge_dst(jax.random.fold_in(arg_keys[10], 71), 0),
        "edge_shift": with_ends(jax.random.randint(arg_keys[3], (K, GX_PILLARS, GY_PILLARS, SLOTS), -1, 2), jax.random.fold_in(arg_keys[3], 1), -1, 1).astype(jnp.int32),
        "radial_weights": noise(arg_keys[4], (NB, 7 * C), NB ** -0.5, 2.0, (), jnp.float32),
        "readout_weights": noise(arg_keys[5], (NB, 2 * C), (NB * C) ** -0.5, 0.1875, (), jnp.float32),
        "w_scalar": noise(arg_keys[6], (C, C), C ** -0.5, 0.5),
        "w_gate": noise(arg_keys[7], (C, C), C ** -0.5, 0.5),
        "w_vector": noise(arg_keys[8], (C, C), C ** -0.5, 0.5),
        "w_tensor": noise(arg_keys[9], (C, C), C ** -0.5, 0.5),
    }


SOFTENING = 0.25
SPACING = 0.6
ROOT_THREE = math.sqrt(3.0)

def geometry(displace, nbasis):
    softened = jnp.sqrt(lax.optimization_barrier(jnp.sum(displace * displace, axis=0)) + SOFTENING)
    direction = displace / softened
    centers = 0.5 + SPACING * jnp.arange(nbasis).astype(jnp.float32)
    radial_basis = jnp.exp(-jnp.square((softened[:, None] - centers[None, :]) / SPACING))
    unit_x, unit_y, unit_z = (direction[0], direction[1], direction[2])
    length_sq = unit_x * unit_x + unit_y * unit_y + unit_z * unit_z
    harmonics = jnp.stack([ROOT_THREE * unit_x * unit_y, ROOT_THREE * unit_y * unit_z, 0.5 * (3.0 * unit_z * unit_z - length_sq), ROOT_THREE * unit_x * unit_z, 0.5 * ROOT_THREE * (unit_x * unit_x - unit_y * unit_y)])
    return (direction, radial_basis, harmonics)

def messages(gathered, displace, radial_weights, channels):
    atom_count = gathered.shape[0]
    direction, radial_basis, harmonics = geometry(displace, radial_weights.shape[0])
    radial = jnp.dot(radial_basis, radial_weights, precision=lax.Precision.HIGHEST, preferred_element_type=jnp.float32).reshape(atom_count, 7, channels)
    scalars = gathered[:, :channels].astype(jnp.float32)
    vectors = gathered[:, channels:4 * channels].astype(jnp.float32).reshape(atom_count, 3, channels)
    tensors = gathered[:, 4 * channels:9 * channels].astype(jnp.float32).reshape(atom_count, 5, channels)
    dir_cols = direction.T[:, :, None]
    harm_cols = harmonics.T[:, :, None]
    msg_scalar = radial[:, 0] * scalars + radial[:, 1] * lax.optimization_barrier(jnp.sum(dir_cols * vectors, axis=1)) + radial[:, 2] * lax.optimization_barrier(jnp.sum(harm_cols * tensors, axis=1))
    msg_vector = radial[:, 3:4] * scalars[:, None] * dir_cols + radial[:, 4:5] * vectors
    msg_tensor = radial[:, 5:6] * scalars[:, None] * harm_cols + radial[:, 6:7] * tensors
    return jnp.concatenate([msg_scalar, msg_vector.reshape(atom_count, 3 * channels), msg_tensor.reshape(atom_count, 5 * channels)], axis=1)

def update(own_rows, summed, w_scalar, w_gate, w_vector, w_tensor, channels):
    atom_count = own_rows.shape[0]
    rounded = summed.astype(jnp.bfloat16)
    scalar_part = rounded[:, :channels]
    scalar_pre = jnp.dot(scalar_part, w_scalar, preferred_element_type=jnp.float32)
    gating = jax.nn.sigmoid(jnp.dot(scalar_part, w_gate, preferred_element_type=jnp.float32))
    vec_mix = jnp.dot(rounded[:, channels:4 * channels].reshape(atom_count * 3, channels), w_vector, preferred_element_type=jnp.float32).reshape(atom_count, 3, channels)
    ten_mix = jnp.dot(rounded[:, 4 * channels:].reshape(atom_count * 5, channels), w_tensor, preferred_element_type=jnp.float32).reshape(atom_count, 5, channels)
    residual_in = own_rows.astype(jnp.float32)
    new_scalar = residual_in[:, :channels] + jax.nn.silu(scalar_pre)
    new_vector = residual_in[:, channels:4 * channels].reshape(atom_count, 3, channels) + gating[:, None] * vec_mix
    new_tensor = residual_in[:, 4 * channels:].reshape(atom_count, 5, channels) + gating[:, None] * ten_mix
    return jnp.concatenate([new_scalar, new_vector.reshape(atom_count, 3 * channels), new_tensor.reshape(atom_count, 5 * channels)], axis=1).astype(jnp.bfloat16)

def pair_energy(displace, own_rows, far_rows, readout_weights, channels):
    atom_count = own_rows.shape[0]
    direction, radial_basis, harmonics = geometry(displace, readout_weights.shape[0])
    readout = jnp.dot(radial_basis, readout_weights, precision=lax.Precision.HIGHEST, preferred_element_type=jnp.float32).reshape(atom_count, 2, channels)
    dir_cols = direction.T[:, :, None]
    own_scalar = own_rows[:, :channels].astype(jnp.float32)
    far_scalar = far_rows[:, :channels].astype(jnp.float32)
    own_along = lax.optimization_barrier(jnp.sum(dir_cols * own_rows[:, channels:4 * channels].astype(jnp.float32).reshape(atom_count, 3, channels), axis=1))
    far_along = lax.optimization_barrier(jnp.sum(dir_cols * far_rows[:, channels:4 * channels].astype(jnp.float32).reshape(atom_count, 3, channels), axis=1))
    return jnp.sum(readout[:, 0] * own_scalar * far_scalar + readout[:, 1] * own_along * far_along)

def pair_force(displace, own_rows, far_rows, readout_weights, channels):
    return jax.grad(lambda moved: pair_energy(moved, own_rows, far_rows, readout_weights, channels))(displace)

def reference(features, positions, edge_dst, edge_shift, radial_weights, readout_weights, w_scalar, w_gate, w_vector, w_tensor):
    grid_x, grid_y, slot_count, columns = features.shape
    channels = columns // 9
    neighbours = edge_dst.shape[0]
    pillar_atoms = grid_y * slot_count
    flat_features = features.reshape(grid_x * pillar_atoms, columns)
    flat_positions = jnp.transpose(positions, (2, 0, 1, 3)).reshape(3, grid_x * pillar_atoms)
    ext_cols = (CY + 2) * slot_count
    column_ids = jnp.arange(grid_y).astype(jnp.int32)
    slot_ids = jnp.arange(slot_count).astype(jnp.int32)
    row_ids = jnp.arange(grid_x).astype(jnp.int32)

    def locate(pillar_row):
        edge_index = lax.dynamic_index_in_dim(edge_dst, pillar_row, 1, keepdims=False)
        image = lax.dynamic_index_in_dim(edge_shift, pillar_row, 1, keepdims=False).astype(jnp.float32)
        step_x = edge_index // ext_cols - 1 - pillar_row % CX
        step_y = edge_index // slot_count % (CY + 2) - 1 - (column_ids % CY)[None, :, None]
        far_x = (pillar_row + step_x) % grid_x
        far_y = (column_ids[None, :, None] + step_y) % grid_y
        far_index = ((far_x * grid_y + far_y) * slot_count + edge_index % slot_count).reshape(neighbours, pillar_atoms)
        near_index = ((pillar_row * grid_y + column_ids[:, None]) * slot_count + slot_ids[None, :]).reshape(pillar_atoms)
        own_places = flat_positions[:, near_index]
        displaced = []
        for neighbour in range(neighbours):
            offset = jnp.stack([step_x[neighbour].reshape(pillar_atoms).astype(jnp.float32), step_y[neighbour].reshape(pillar_atoms).astype(jnp.float32), image[neighbour].reshape(pillar_atoms)])
            displaced.append(flat_positions[:, far_index[neighbour]] - own_places + offset)
        return (far_index, near_index, displaced)

    def layer_row(pillar_row):
        far_index, near_index, displaced = locate(pillar_row)
        summed = jnp.zeros((pillar_atoms, columns), jnp.float32)
        for neighbour in range(neighbours):
            summed = summed + messages(flat_features[far_index[neighbour]], displaced[neighbour], radial_weights, channels)
        return update(flat_features[near_index], summed / neighbours, w_scalar, w_gate, w_vector, w_tensor, channels)
    mixed = lax.map(layer_row, row_ids).reshape(grid_x * pillar_atoms, columns)

    def force_row(force_sum, pillar_row):
        far_index, near_index, displaced = locate(pillar_row)
        own_rows = mixed[near_index]
        own_force = jnp.zeros((3, pillar_atoms), jnp.float32)
        for neighbour in range(neighbours):
            pair_grad = pair_force(displaced[neighbour], own_rows, mixed[far_index[neighbour]], readout_weights, channels)
            own_force = own_force + pair_grad
            force_sum = force_sum.at[:, far_index[neighbour]].add(-pair_grad)
        force_sum = force_sum.at[:, near_index].add(own_force)
        return (force_sum, None)
    forces = lax.scan(force_row, jnp.zeros((3, grid_x * pillar_atoms), jnp.float32), row_ids)[0]
    forces = jnp.transpose(forces.reshape(3, grid_x, grid_y, slot_count), (1, 2, 0, 3))
    return (mixed.reshape(grid_x, grid_y, slot_count, columns), forces)
```

```python
import math

import jax
import jax.numpy as jnp
from jax import lax
from jax.experimental import pallas as pl
from jax.experimental.pallas import tpu as pltpu
from jax.sharding import PartitionSpec as P

MESH = pl.DeviceIdType.MESH
F32 = jnp.float32
BF16 = jnp.bfloat16
SOFTENING = 0.25
SPACING = 0.6
ROOT_THREE = math.sqrt(3.0)
C = 128
S = 128
NB = 8
NE = 3
NP = 2
BLOCKS = 9
READ_BLOCKS = 4
KP = NE * NP
ROWS = NE * S
NEAR = 9 * S
STEP = 16
GROUPS = ((0, 4), (4, 7), (7, 9))
GROUPS2 = ((0, 2), (2, 4))
DIRECTIONS = tuple((dx, dy) for dx in (-1, 0, 1) for dy in (-1, 0, 1) if (dx, dy) != (0, 0))


def split(x):
    high = x.astype(BF16).astype(F32)
    return high, x - high


def dot(a, b, contract=(1, 0)):
    dims = (((contract[0],), (contract[1],)), ((), ()))
    return lax.dot_general(a, b, dims, preferred_element_type=F32)


PLACE = {0: 0, -1: 1, 1: 2}


def near_slot(p, j):
    return (j // 2, j % 2) if j < 6 else (j - 6, 3 - p)


def near_pillar(p, j):
    y, slot = near_slot(p, j)
    return (1, 2, 3, 0)[slot], (1, 0, 2)[y]


def block(bufs, c, *at):
    for buf in bufs:
        if c < buf.shape[2]:
            return buf.at[(*at, c)]
        c -= buf.shape[2]


class Halo:
    COUNT = 10

    def __init__(self, bufs, send, recv, device, low_wrap, high_wrap):
        self.copies = {}
        self.low_wrap, self.high_wrap = low_wrap, high_wrap
        own, ghosts = pl.ds(0, 2), pl.ds(2, 2)
        for g, buf in enumerate(bufs):
            spans = {
                "x0": (buf.at[0, 0], buf.at[0, 2], (-1, 0)),
                "x1": (buf.at[0, 1], buf.at[0, 3], (1, 0)),
            }
            for sign, step, to in (("m", -1, 2), ("p", 1, 1)):
                spans |= {
                    "y" + sign: (buf.at[0, own], buf.at[to, own], (0, step)),
                    "c" + sign: (buf.at[0, ghosts], buf.at[to, ghosts], (0, step)),
                    "w0" + sign: (buf.at[0, 0], buf.at[to, 2], (-1, step)),
                    "w1" + sign: (buf.at[0, 1], buf.at[to, 3], (1, step)),
                }
            for n, (name, (src, dst, step)) in enumerate(spans.items()):
                self.copies[name, g] = pltpu.make_async_remote_copy(
                    src_ref=src,
                    dst_ref=dst,
                    send_sem=send.at[g, n],
                    recv_sem=recv.at[g, n],
                    device_id=device(*step),
                    device_id_type=MESH,
                )

    def start(self, g, *names):
        for name in names:
            self.copies[name, g].start()

    def arrived(self, g, *names):
        for name in names:
            self.copies[name, g].wait_recv()

    def sends(self, sign, plain, wrap):
        wraps = self.low_wrap if sign == "m" else self.high_wrap
        if wrap is not None:
            pl.when(wraps)(wrap)
        if plain is not None:
            pl.when(jnp.logical_not(wraps))(plain)

    def own(self, g):
        self.start(g, "x0", "x1", "ym", "yp")
        for sign in "mp":
            self.sends(sign, None, lambda: self.start(g, "w0" + sign, "w1" + sign))

    def near(self, g):
        self.arrived(g, "ym", "yp")

    def corners(self, g):
        self.arrived(g, "x0", "x1")
        for sign in "mp":
            self.sends(sign, lambda: self.start(g, "c" + sign), None)

    def rest(self, g):
        for sign, wraps in (("m", self.high_wrap), ("p", self.low_wrap)):
            pl.when(wraps)(lambda: self.arrived(g, "w0" + sign, "w1" + sign))
            pl.when(jnp.logical_not(wraps))(lambda: self.arrived(g, "c" + sign))

    def sent(self, groups):
        def done(*names):
            for g in groups:
                for name in names:
                    self.copies[name, g].wait_send()

        done("x0", "x1", "ym", "yp")
        for sign in "mp":
            self.sends(sign, lambda: done("c" + sign), lambda: done("w0" + sign, "w1" + sign))


def kernel(
    gx_size,
    yz_size,
    feat,
    *refs,
):
    small_in, refs = refs[:9], refs[9:]
    mixed, forces, *refs = refs
    small, refs = refs[:9], refs[9:]
    run(gx_size, yz_size, feat, small_in, small, mixed, forces, *refs)


def run(
    gx_size,
    yz_size,
    feat,
    small_in,
    small,
    mixed,
    forces,
    ext0,
    ext1,
    ext2,
    mix0,
    mix1,
    posx,
    oh,
    coef,
    qcoef,
    wide,
    zf,
    pj,
    geo,
    edges,
    acc,
    gsc,
    mix_out,
    xq,
    grad,
    extf,
    frecv,
    small_sem,
    load_sem,
    out_sem,
    pos_send,
    pos_recv,
    f1_send,
    f1_recv,
    f2_send,
    f2_recv,
    fo_send,
    fo_recv,
):
    ext, ext2 = (ext0, ext1, ext2), (mix0, mix1)
    gx = lax.axis_index("gx")
    yz = lax.axis_index("yz")

    half = yz_size // 2
    low_wrap = lax.rem(yz, half) == 0
    high_wrap = lax.rem(yz, half) == half - 1

    def device(dx, dy):
        return (lax.rem(gx + dx + gx_size, gx_size), lax.rem(yz + dy + yz_size, yz_size))

    small_loads = [
        pltpu.make_async_copy(small_in[i], small[i], small_sem.at[i]) for i in range(len(small))
    ]
    for load in small_loads:
        load.start()
    pos, dst, shift, wr, wq, w_scalar, w_gate, w_vector, w_tensor = small
    loads = []
    for c in range(BLOCKS):
        load = pltpu.make_async_copy(
            feat.at[:, 0, :, pl.ds(c * C, C)], block(ext, c, 0, pl.ds(0, 2)), load_sem.at[c]
        )
        load.start()
        loads.append(load)

    barrier = pltpu.get_barrier_semaphore()
    for step in DIRECTIONS:
        pl.semaphore_signal(barrier, inc=1, device_id=device(*step), device_id_type=MESH)

    for load in small_loads:
        load.wait()
    for p in range(NP):
        posx[0, p] = jnp.zeros((8, S), F32)
        for m in range(3):
            posx[0, p, pl.ds(m, 1), :] = pos[p, m]
    pl.semaphore_wait(barrier, len(DIRECTIONS))

    pos_copies = []
    for n, (dx, dy) in enumerate(DIRECTIONS):
        if dx == 0:
            here, there = pl.ds(0, 2), pl.ds(0, 2)
        elif dx == 1:
            here, there = pl.ds(1, 1), pl.ds(3, 1)
        else:
            here, there = pl.ds(0, 1), pl.ds(2, 1)
        copy = pltpu.make_async_remote_copy(
            src_ref=posx.at[0, here],
            dst_ref=posx.at[PLACE[-dy], there],
            send_sem=pos_send.at[n],
            recv_sem=pos_recv.at[n],
            device_id=device(dx, dy),
            device_id_type=MESH,
        )
        copy.start()
        pos_copies.append(copy)

    halo = Halo(ext, f1_send, f1_recv, device, low_wrap, high_wrap)
    for g, (lo, hi) in enumerate(GROUPS):
        for c in range(lo, hi):
            loads[c].wait()
        halo.own(g)

    lane = lax.broadcasted_iota(jnp.int32, (S, S), 1).astype(F32)
    edges[...] = jnp.zeros_like(edges)
    for k in range(NE):
        for p in range(NP):
            row = dst[k, p].astype(F32)
            edges[0, pl.ds(k * NP + p, 1), :] = row
            edges[1, pl.ds(k * NP + p, 1), :] = shift[k, p].astype(F32)
            column = jnp.transpose(jnp.broadcast_to(row, (S, S))) - lane
            for j in range(9):
                x, y = near_pillar(p, j)
                hit = column == float((3 * x + y) * S)
                oh[p, pl.ds(k * S, S), pl.ds(j * S, S)] = jnp.where(hit, 1.0, 0.0).astype(BF16)

    wide[...] = jnp.zeros_like(wide)
    w_r, rest_r = split(wr[...])
    w_q, rest_q = split(wq[...])
    zeros_r = jnp.zeros_like(w_r)
    zeros_q = jnp.zeros_like(w_q)
    n_r, n_q = 7 * C, 2 * C
    wide[pl.ds(0, 32), pl.ds(0, n_r)] = jnp.concatenate([w_r, rest_r, w_r, zeros_r], 0).astype(BF16)
    wide[pl.ds(0, 32), pl.ds(n_r, n_q)] = jnp.concatenate([w_q, rest_q, w_q, zeros_q], 0).astype(BF16)
    wide[pl.ds(32, 32), pl.ds(n_r + n_q, n_q)] = jnp.concatenate([w_q, rest_q, w_q, zeros_q], 0).astype(BF16)
    copy_row = lax.broadcasted_iota(jnp.int32, (8, 8 * C), 0)
    copy_col = lax.broadcasted_iota(jnp.int32, (8, 8 * C), 1)
    copies = jnp.where((copy_col >= copy_row * C) & (copy_col < (copy_row + 1) * C), 1.0, 0.0)
    wide[pl.ds(64, 16), pl.ds(n_r + 2 * n_q, 8 * C)] = jnp.concatenate([copies, copies], 0).astype(BF16)

    for copy in pos_copies:
        copy.wait_recv()
    for p in range(NP):
        places = jnp.concatenate([posx[near_slot(p, j)] for j in range(9)], axis=1)
        first, rest = split(places)
        second, third = split(rest)
        parts = jnp.concatenate([first, second, third, jnp.zeros_like(first)], 0).astype(BF16)
        found = dot(parts, oh[p], (1, 1))
        far = (found[0:8] + found[8:16]) + found[16:24]
        for k in range(NE):
            pj[k * NP + p] = far[:, k * S : (k + 1) * S] - posx[0, p]

    place = edges[0]
    own_p = lax.rem(lax.broadcasted_iota(jnp.int32, (8, S), 0), NP).astype(F32)
    one = jnp.ones_like(place)
    nil = jnp.zeros_like(place)

    def at_least(x, bound):
        return jnp.where(x >= float(bound), one, nil)

    ext_x = at_least(place, 3 * S) + at_least(place, 6 * S) + at_least(place, 9 * S)
    left = place - ext_x * float(3 * S)
    ext_y = at_least(left, S) + at_least(left, 2 * S)
    disp_x = pj[:, 0, :] + (ext_x - 1.0 - own_p)
    disp_y = pj[:, 1, :] + (ext_y - 1.0)
    disp_z = pj[:, 2, :] + edges[1]
    rho = jnp.sqrt(disp_x * disp_x + disp_y * disp_y + disp_z * disp_z + SOFTENING)
    inverse = 1.0 / rho
    u_x, u_y, u_z = disp_x * inverse, disp_y * inverse, disp_z * inverse
    geo[0] = u_x
    geo[1] = u_y
    geo[2] = u_z
    geo[3] = inverse
    length_sq = u_x * u_x + u_y * u_y + u_z * u_z
    angular = (
        u_x,
        u_y,
        u_z,
        ROOT_THREE * u_x * u_y,
        ROOT_THREE * u_y * u_z,
        0.5 * (3.0 * u_z * u_z - length_sq),
        ROOT_THREE * u_x * u_z,
        0.5 * ROOT_THREE * (u_x * u_x - u_y * u_y),
    )
    zf[...] = jnp.zeros_like(zf)
    for b in range(NB):
        off = (rho - (0.5 + SPACING * b)) / SPACING
        basis = jnp.exp(-(off * off))
        slope = basis * off * (-2.0 / SPACING)
        high, low = split(basis)
        zf[b] = high
        zf[8 + b] = high
        zf[16 + b] = low
        high, low = split(slope)
        zf[32 + b] = high
        zf[40 + b] = high
        zf[48 + b] = low
        high, low = split(angular[b])
        zf[64 + b] = high
        zf[72 + b] = low

    halo.corners(0)
    for p in range(NP):
        for k in range(NE):
            rows = jnp.transpose(zf[:, k * NP + p, :]).astype(BF16)
            at = pl.ds(p * ROWS + k * S, S)
            for f in range(0, 19, 2):
                n = min(2, 19 - f)
                out = dot(rows, wide[:, pl.ds(f * C, n * C)])
                for i in range(n):
                    if f + i < 7:
                        coef[f + i, at, :] = out[:, i * C : (i + 1) * C]
                    elif f + i < 11:
                        qcoef[f + i - 7, at, :] = out[:, i * C : (i + 1) * C]
                    else:
                        coef[f + i - 4, at, :] = out[:, i * C : (i + 1) * C]

    def gather(bufs, lo, hi, beyond):
        for p in range(NP):
            for c in range(lo, hi, 2):
                n = min(2, hi - c)
                parts = [c + i for i in range(n)]
                if beyond:
                    rows = [block(bufs, i, pl.ds(0, 3), 3 - p)[...].reshape(3 * S, C) for i in parts]
                    out = dot(oh[p, :, pl.ds(6 * S, 3 * S)], jnp.concatenate(rows, axis=1))
                else:
                    rows = [block(bufs, i, pl.ds(0, 3), pl.ds(0, 2))[...].reshape(6 * S, C) for i in parts]
                    out = dot(oh[p, :, pl.ds(0, 6 * S)], jnp.concatenate(rows, axis=1))
                at = pl.ds(p * ROWS, ROWS)
                for i in range(n):
                    term = out[:, i * C : (i + 1) * C]
                    gsc[c + i, at, :] = gsc[c + i, at, :] + term if beyond else term

    def each_row(fn):
        for p in range(NP):

            def run(i, carry, p=p):
                r = pl.multiple_of(i * STEP, STEP)
                fn(p, r, [pl.ds(p * ROWS + k * S + r, STEP) for k in range(NE)], pl.ds(p * S + r, STEP))
                return carry

            lax.fori_loop(0, S // STEP, run, 0)

    def message_sv(p, r, at, to):
        total = [jnp.zeros((STEP, C), F32) for _ in range(BLOCKS)]
        for k in range(NE):
            e = at[k]
            s = gsc[0, e, :]
            v = [gsc[1 + m, e, :] for m in range(3)]
            u = [coef[7 + m, e, :] for m in range(3)]
            along = u[0] * v[0] + u[1] * v[1] + u[2] * v[2]
            total[0] = total[0] + coef[0, e, :] * s + coef[1, e, :] * along
            r3s = coef[3, e, :] * s
            r4 = coef[4, e, :]
            for m in range(3):
                total[1 + m] = total[1 + m] + r3s * u[m] + r4 * v[m]
            r5s = coef[5, e, :] * s
            for n in range(5):
                total[4 + n] = total[4 + n] + r5s * coef[10 + n, e, :]
        for b in range(BLOCKS):
            acc[b, to, :] = total[b]

    def message_t(lo, hi):
        def fn(p, r, at, to):
            total = [acc[b, to, :] for b in (0, *range(lo, hi))]
            for k in range(NE):
                e = at[k]
                along = None
                r6 = coef[6, e, :]
                for n in range(lo, hi):
                    t = gsc[n, e, :]
                    term = coef[6 + n, e, :] * t
                    along = term if along is None else along + term
                    total[1 + n - lo] = total[1 + n - lo] + r6 * t
                total[0] = total[0] + coef[2, e, :] * along
            for i, b in enumerate((0, *range(lo, hi))):
                acc[b, to, :] = total[i]

        return fn

    third = 1.0 / NE

    def mix(lo, hi, weight):
        for b in range(lo, hi):
            acc[b] = dot((acc[b] * third).astype(BF16), weight[...])

    halo.near(0)
    gather(ext, 0, 4, False)
    halo.near(1)
    gather(ext, 4, 7, False)
    halo.corners(1)
    halo.near(2)
    gather(ext, 7, 9, False)
    halo.rest(0)
    gather(ext, 0, 4, True)
    each_row(message_sv)
    mix(1, 4, w_vector)
    halo.corners(2)
    halo.rest(1)
    gather(ext, 4, 7, True)
    each_row(message_t(4, 7))
    mix(4, 7, w_tensor)
    halo.rest(2)
    gather(ext, 7, 9, True)
    each_row(message_t(7, 9))
    mix(7, 9, w_tensor)

    scalar = (acc[0] * third).astype(BF16)
    pre = dot(scalar, w_scalar[...])
    acc[0] = pre * jax.nn.sigmoid(pre)
    gsc[0, pl.ds(0, NP * S), :] = jax.nn.sigmoid(dot(scalar, w_gate[...]))

    def update_sv(p, r, at, to):
        gate = gsc[0, to, :]
        rows = pl.ds(r, STEP)
        for b in range(READ_BLOCKS):
            old = block(ext, b, 0, p)[rows, :].astype(F32)
            step = gate * acc[b, to, :] if b > 0 else acc[0, to, :]
            new = (old + step).astype(BF16)
            block(ext2, b, 0, p)[rows, :] = new
            mix_out[p, 0, rows, pl.ds(b * C, C)] = new

    each_row(update_sv)
    halo2 = Halo(ext2, f2_send, f2_recv, device, low_wrap, high_wrap)
    for g in range(len(GROUPS2)):
        halo2.own(g)

    def update_t(p, r, at, to):
        gate = gsc[0, to, :]
        rows = pl.ds(r, STEP)
        for b in range(READ_BLOCKS, BLOCKS):
            old = block(ext, b, 0, p)[rows, :].astype(F32)
            mix_out[p, 0, rows, pl.ds(b * C, C)] = (old + gate * acc[b, to, :]).astype(BF16)

    each_row(update_t)
    write = pltpu.make_async_copy(mix_out, mixed, out_sem)
    write.start()

    halo2.near(0)
    gather(ext2, 0, 2, False)
    halo2.corners(0)
    halo2.near(1)
    gather(ext2, 2, 4, False)
    halo2.corners(1)
    halo.sent(range(len(GROUPS)))
    halo2.rest(0)
    gather(ext2, 0, 2, True)
    halo2.rest(1)
    gather(ext2, 2, 4, True)

    def pair(p, r, at, to):
        rows = pl.ds(r, STEP)
        own = [block(ext2, b, 0, p)[rows, :].astype(F32) for b in range(READ_BLOCKS)]
        for k in range(NE):
            e = at[k]
            far = [gsc[b, e, :] for b in range(READ_BLOCKS)]
            u = [coef[7 + m, e, :] for m in range(3)]
            own_along = u[0] * own[1] + u[1] * own[2] + u[2] * own[3]
            far_along = u[0] * far[1] + u[1] * far[2] + u[2] * far[3]
            q1 = qcoef[1, e, :]
            own_q, far_q = q1 * own_along, q1 * far_along
            terms = [qcoef[2, e, :] * (own[0] * far[0]) + qcoef[3, e, :] * (own_along * far_along)]
            for m in range(3):
                terms.append(own[1 + m] * far_q + own_q * far[1 + m])
            at_col = (k * NP + p) * 2 * C
            for q in range(4):
                high, low = split(terms[q])
                xq[pl.ds(q * S + r, STEP), pl.ds(at_col, C)] = high.astype(BF16)
                xq[pl.ds(q * S + r, STEP), pl.ds(at_col + C, C)] = low.astype(BF16)

    each_row(pair)
    mask_row = lax.broadcasted_iota(jnp.int32, (16, KP * 2 * C), 0) * (2 * C)
    mask_col = lax.broadcasted_iota(jnp.int32, (16, KP * 2 * C), 1)
    mask = jnp.where((mask_col >= mask_row) & (mask_col < mask_row + 2 * C), 1.0, 0.0).astype(BF16)
    sums = dot(mask, xq[...], (1, 1))[0:8]
    t_rho, g_x, g_y, g_z = (sums[:, q * S : (q + 1) * S] for q in range(4))
    u_x, u_y, u_z = geo[0], geo[1], geo[2]
    inverse = geo[3]
    radial_part = t_rho - (u_x * g_x + u_y * g_y + u_z * g_z) * inverse
    grad[...] = jnp.zeros_like(grad)
    grad[0] = radial_part * u_x + g_x * inverse
    grad[1] = radial_part * u_y + g_y * inverse
    grad[2] = radial_part * u_z + g_z * inverse

    parts = []
    for p in range(NP):
        terms = jnp.concatenate([grad[:, k * NP + p, :] for k in range(NE)], axis=1)
        first, rest = split(terms)
        second, third_part = split(rest)
        parts.append(
            jnp.concatenate([first, second, third_part, jnp.zeros_like(first)], 0).astype(BF16)
        )

    def scatter(lo, hi):
        seen = {}
        for p in range(NP):
            out = dot(parts[p], oh[p, :, pl.ds(lo * S, (hi - lo) * S)])
            out = (out[0:8] + out[8:16]) + out[16:24]
            for j in range(lo, hi):
                term = out[:, (j - lo) * S : (j - lo + 1) * S]
                at = near_slot(p, j)
                seen[at] = seen[at] - term if at in seen else -term
        for at, value in seen.items():
            extf[at] = value

    scatter(2, 9)
    force_copies = []
    for n, (dx, dy) in enumerate(DIRECTIONS):
        if dx == 0:
            here, there = pl.ds(0, 2), pl.ds(0, 2)
        elif dx == 1:
            here, there = pl.ds(2, 1), pl.ds(0, 1)
        else:
            here, there = pl.ds(3, 1), pl.ds(1, 1)
        copy = pltpu.make_async_remote_copy(
            src_ref=extf.at[PLACE[dy], here],
            dst_ref=frecv.at[n, there],
            send_sem=fo_send.at[n],
            recv_sem=fo_recv.at[n],
            device_id=device(dx, dy),
            device_id_type=MESH,
        )
        copy.start()
        force_copies.append(copy)

    scatter(0, 2)
    total = []
    for p in range(NP):
        mine = extf[0, p]
        for k in range(NE):
            mine = mine + grad[:, k * NP + p, :]
        total.append(mine)
    for n, (dx, dy) in enumerate(DIRECTIONS):
        force_copies[n].wait_recv()
        for p in range(NP):
            if dx == 0 or (dx == 1) == (p == 0):
                total[p] = total[p] + frecv[n, p]
    for p in range(NP):
        for m in range(3):
            forces[p, m] = total[p][m : m + 1]

    for copy in (*pos_copies, *force_copies):
        copy.wait_send()
    halo2.sent(range(len(GROUPS2)))
    write.wait()


def solution(mesh):
    gx_size, yz_size = mesh.shape["gx"], mesh.shape["yz"]

    def body(features, positions, *rest):
        args = (features, jnp.transpose(positions, (0, 2, 1, 3)), *rest)
        vmem = pl.BlockSpec(memory_space=pltpu.VMEM)
        anywhere = pl.BlockSpec(memory_space=pl.ANY)
        dma = pltpu.SemaphoreType.DMA
        n_dir = len(DIRECTIONS)

        def run_all(*refs):
            kernel(gx_size, yz_size, *refs)

        small = [pltpu.VMEM(x.shape, x.dtype) for x in args[1:]]
        new_features, force = pl.pallas_call(
            run_all,
            out_shape=(
                jax.ShapeDtypeStruct((NP, 1, S, BLOCKS * C), BF16),
                jax.ShapeDtypeStruct((NP, 3, 1, S), F32),
            ),
            in_specs=[pl.BlockSpec(memory_space=pltpu.HBM)] * 10,
            out_specs=(anywhere, vmem),
            scratch_shapes=small
            + [
                *[pltpu.VMEM((3, 4, hi - lo, S, C), BF16) for lo, hi in GROUPS + GROUPS2],
                pltpu.VMEM((3, 4, 8, S), F32),
                pltpu.VMEM((NP, ROWS, NEAR), BF16),
                pltpu.VMEM((15, NP * ROWS, C), F32),
                pltpu.VMEM((4, NP * ROWS, C), F32),
                pltpu.VMEM((128, 19 * C), BF16),
                pltpu.VMEM((128, 8, S), F32),
                pltpu.VMEM((8, 8, S), F32),
                pltpu.VMEM((4, 8, S), F32),
                pltpu.VMEM((2, 8, S), F32),
                pltpu.VMEM((BLOCKS, NP * S, C), F32),
                pltpu.VMEM((BLOCKS, NP * ROWS, C), F32),
                pltpu.VMEM((NP, 1, S, BLOCKS * C), BF16),
                pltpu.VMEM((4 * S, KP * 2 * C), BF16),
                pltpu.VMEM((8, 8, S), F32),
                pltpu.VMEM((3, 4, 8, S), F32),
                pltpu.VMEM((n_dir, NP, 8, S), F32),
                dma((len(small),)),
                dma((BLOCKS,)),
                dma,
                dma((n_dir,)),
                dma((n_dir,)),
                dma((len(GROUPS), Halo.COUNT)),
                dma((len(GROUPS), Halo.COUNT)),
                dma((len(GROUPS2), Halo.COUNT)),
                dma((len(GROUPS2), Halo.COUNT)),
                dma((n_dir,)),
                dma((n_dir,)),
            ],
            compiler_params=pltpu.CompilerParams(
                collective_id=0, has_side_effects=True, vmem_limit_bytes=60 * 1024 * 1024
            ),
            cost_estimate=pl.CostEstimate(
                flops=4 * 10**9, bytes_accessed=2 * 10**6, transcendentals=10**5
            ),
        )(*args)
        return new_features, jnp.transpose(force, (0, 2, 1, 3))

    in_specs = (
        P("gx", "yz", None, None),
        P("gx", "yz", None, None),
        P(None, "gx", "yz", None),
        P(None, "gx", "yz", None),
        P(),
        P(),
        P(),
        P(),
        P(),
        P(),
    )
    out_specs = (P("gx", "yz", None, None), P("gx", "yz", None, None))
    return jax.shard_map(body, mesh=mesh, in_specs=in_specs, out_specs=out_specs, check_vma=False)
```

```python
import math

import jax
import jax.numpy as jnp
from jax import lax
from jax.experimental import pallas as pl
from jax.experimental.pallas import tpu as pltpu
from jax.sharding import PartitionSpec as P

MESH = pl.DeviceIdType.MESH
F32 = jnp.float32
BF16 = jnp.bfloat16
SOFTENING = 0.25
SPACING = 0.6
ROOT_THREE = math.sqrt(3.0)
C = 128
S = 128
NB = 8
NE = 3
NP = 2
BLOCKS = 9
READ_BLOCKS = 4
KP = NE * NP
ROWS = NE * S
NEAR = 9 * S
STEP = 16
GROUPS = ((0, 4), (4, 7), (7, 9))
GROUPS2 = ((0, 2), (2, 4))
DIRECTIONS = tuple((dx, dy) for dx in (-1, 0, 1) for dy in (-1, 0, 1) if (dx, dy) != (0, 0))


def split(x):
    high = x.astype(BF16).astype(F32)
    return high, x - high


def dot(a, b, contract=(1, 0)):
    dims = (((contract[0],), (contract[1],)), ((), ()))
    return lax.dot_general(a, b, dims, preferred_element_type=F32)


PLACE = {0: 0, -1: 1, 1: 2}


def near_slot(p, j):
    return (j // 2, j % 2) if j < 6 else (j - 6, 3 - p)


def near_pillar(p, j):
    y, slot = near_slot(p, j)
    return (1, 2, 3, 0)[slot], (1, 0, 2)[y]


def block(bufs, c, *at):
    for buf in bufs:
        if c < buf.shape[2]:
            return buf.at[(*at, c)]
        c -= buf.shape[2]


class Halo:
    COUNT = 10

    def __init__(self, bufs, send, recv, device, low_wrap, high_wrap):
        self.copies = {}
        self.low_wrap, self.high_wrap = low_wrap, high_wrap
        own, ghosts = pl.ds(0, 2), pl.ds(2, 2)
        for g, buf in enumerate(bufs):
            spans = {
                "x0": (buf.at[0, 0], buf.at[0, 2], (-1, 0)),
                "x1": (buf.at[0, 1], buf.at[0, 3], (1, 0)),
            }
            for sign, step, to in (("m", -1, 2), ("p", 1, 1)):
                spans |= {
                    "y" + sign: (buf.at[0, own], buf.at[to, own], (0, step)),
                    "c" + sign: (buf.at[0, ghosts], buf.at[to, ghosts], (0, step)),
                    "w0" + sign: (buf.at[0, 0], buf.at[to, 2], (-1, step)),
                    "w1" + sign: (buf.at[0, 1], buf.at[to, 3], (1, step)),
                }
            for n, (name, (src, dst, step)) in enumerate(spans.items()):
                self.copies[name, g] = pltpu.make_async_remote_copy(
                    src_ref=src,
                    dst_ref=dst,
                    send_sem=send.at[g, n],
                    recv_sem=recv.at[g, n],
                    device_id=device(*step),
                    device_id_type=MESH,
                )

    def start(self, g, *names):
        for name in names:
            self.copies[name, g].start()

    def arrived(self, g, *names):
        for name in names:
            self.copies[name, g].wait_recv()

    def sends(self, sign, plain, wrap):
        wraps = self.low_wrap if sign == "m" else self.high_wrap
        if wrap is not None:
            pl.when(wraps)(wrap)
        if plain is not None:
            pl.when(jnp.logical_not(wraps))(plain)

    def own(self, g):
        self.start(g, "x0", "x1", "ym", "yp")
        for sign in "mp":
            self.sends(sign, None, lambda: self.start(g, "w0" + sign, "w1" + sign))

    def near(self, g):
        self.arrived(g, "ym", "yp")

    def corners(self, g):
        self.arrived(g, "x0", "x1")
        for sign in "mp":
            self.sends(sign, lambda: self.start(g, "c" + sign), None)

    def rest(self, g):
        for sign, wraps in (("m", self.high_wrap), ("p", self.low_wrap)):
            pl.when(wraps)(lambda: self.arrived(g, "w0" + sign, "w1" + sign))
            pl.when(jnp.logical_not(wraps))(lambda: self.arrived(g, "c" + sign))

    def sent(self, groups):
        def done(*names):
            for g in groups:
                for name in names:
                    self.copies[name, g].wait_send()

        done("x0", "x1", "ym", "yp")
        for sign in "mp":
            self.sends(sign, lambda: done("c" + sign), lambda: done("w0" + sign, "w1" + sign))


def kernel(
    gx_size,
    yz_size,
    feat,
    *refs,
):
    small_in, refs = refs[:9], refs[9:]
    mixed, forces, *refs = refs
    small, refs = refs[:9], refs[9:]
    run(gx_size, yz_size, feat, small_in, small, mixed, forces, *refs)


def run(
    gx_size,
    yz_size,
    feat,
    small_in,
    small,
    mixed,
    forces,
    ext0,
    ext1,
    ext2,
    mix0,
    mix1,
    posx,
    oh,
    coef,
    qcoef,
    wide,
    w_turned,
    zf,
    ang,
    pj,
    geo,
    edges,
    acc,
    gate,
    gsc,
    raw,
    mix_out,
    side,
    sums,
    grad,
    extf,
    frecv,
    small_sem,
    load_sem,
    out_sem,
    pos_send,
    pos_recv,
    f1_send,
    f1_recv,
    f2_send,
    f2_recv,
    fo_send,
    fo_recv,
):
    ext, ext2 = (ext0, ext1, ext2), (mix0, mix1)
    gx = lax.axis_index("gx")
    yz = lax.axis_index("yz")

    half = yz_size // 2
    low_wrap = lax.rem(yz, half) == 0
    high_wrap = lax.rem(yz, half) == half - 1

    def device(dx, dy):
        return (lax.rem(gx + dx + gx_size, gx_size), lax.rem(yz + dy + yz_size, yz_size))

    small_loads = [
        pltpu.make_async_copy(small_in[i], small[i], small_sem.at[i]) for i in range(len(small))
    ]
    for load in small_loads:
        load.start()
    pos, dst, shift, wr, wq, w_scalar, w_gate, w_vector, w_tensor = small
    feat_load = pltpu.make_async_copy(feat, raw, load_sem)
    feat_load.start()

    barrier = pltpu.get_barrier_semaphore()
    for step in DIRECTIONS:
        pl.semaphore_signal(barrier, inc=1, device_id=device(*step), device_id_type=MESH)

    for load in small_loads:
        load.wait()
    for p in range(NP):
        posx[0, p] = jnp.zeros((8, S), F32)
        for m in range(3):
            posx[0, p, pl.ds(m, 1), :] = pos[p, m]

    def turn(g):
        for c in range(*GROUPS[g]):
            for p in range(NP):
                tile = raw[p, 0, :, pl.ds(c * C, C)].astype(F32)
                block(ext, c, 0, p)[...] = jnp.transpose(tile).astype(BF16)

    feat_load.wait()
    turn(0)
    pl.semaphore_wait(barrier, len(DIRECTIONS))

    pos_copies = []
    for n, (dx, dy) in enumerate(DIRECTIONS):
        if dx == 0:
            here, there = pl.ds(0, 2), pl.ds(0, 2)
        elif dx == 1:
            here, there = pl.ds(1, 1), pl.ds(3, 1)
        else:
            here, there = pl.ds(0, 1), pl.ds(2, 1)
        copy = pltpu.make_async_remote_copy(
            src_ref=posx.at[0, here],
            dst_ref=posx.at[PLACE[-dy], there],
            send_sem=pos_send.at[n],
            recv_sem=pos_recv.at[n],
            device_id=device(dx, dy),
            device_id_type=MESH,
        )
        copy.start()
        pos_copies.append(copy)

    halo = Halo(ext, f1_send, f1_recv, device, low_wrap, high_wrap)
    halo.own(0)
    for g in range(1, len(GROUPS)):
        turn(g)
        halo.own(g)

    atom = lax.broadcasted_iota(jnp.int32, (S, ROWS), 0).astype(F32)
    edges[...] = jnp.zeros_like(edges)
    for p in range(NP):
        rows = [dst[k, p].astype(F32) for k in range(NE)]
        for k in range(NE):
            edges[0, pl.ds(k * NP + p, 1), :] = rows[k]
            edges[1, pl.ds(k * NP + p, 1), :] = shift[k, p].astype(F32)
        place = jnp.concatenate(rows, axis=1) - atom
        for j in range(9):
            x, y = near_pillar(p, j)
            hit = place == float((3 * x + y) * S)
            oh[p, pl.ds(j * S, S), :] = jnp.where(hit, 1.0, 0.0).astype(BF16)

    for f in range(9):
        w = wr[:, pl.ds(f * C, C)] if f < 7 else wq[:, pl.ds((f - 7) * C, C)]
        high, low = split(w)
        rows = jnp.concatenate([high, low, high, jnp.zeros_like(w)], axis=0)
        wide[pl.ds(f * C, C), :] = jnp.transpose(rows).astype(BF16)
    for i, w in enumerate((w_scalar, w_gate, w_vector, w_tensor)):
        w_turned[pl.ds(i * C, C), :] = jnp.transpose(w[...].astype(F32)).astype(BF16)

    for copy in pos_copies:
        copy.wait_recv()
    for p in range(NP):
        places = jnp.concatenate([posx[near_slot(p, j)] for j in range(9)], axis=1)
        first, rest = split(places)
        second, third = split(rest)
        parts = jnp.concatenate([first, second, third, jnp.zeros_like(first)], 0).astype(BF16)
        found = dot(parts, oh[p])
        far = (found[0:8] + found[8:16]) + found[16:24]
        for k in range(NE):
            pj[k * NP + p] = far[:, k * S : (k + 1) * S] - posx[0, p]

    place = edges[0]
    pj[pl.ds(KP, 8 - KP)] = jnp.zeros((8 - KP, 8, S), F32)
    own_p = lax.rem(lax.broadcasted_iota(jnp.int32, (8, S), 0), NP).astype(F32)
    one = jnp.ones_like(place)
    nil = jnp.zeros_like(place)

    def at_least(x, bound):
        return jnp.where(x >= float(bound), one, nil)

    ext_x = at_least(place, 3 * S) + at_least(place, 6 * S) + at_least(place, 9 * S)
    left = place - ext_x * float(3 * S)
    ext_y = at_least(left, S) + at_least(left, 2 * S)
    disp_x = pj[:, 0, :] + (ext_x - 1.0 - own_p)
    disp_y = pj[:, 1, :] + (ext_y - 1.0)
    disp_z = pj[:, 2, :] + edges[1]
    rho = jnp.sqrt(disp_x * disp_x + disp_y * disp_y + disp_z * disp_z + SOFTENING)
    inverse = 1.0 / rho
    u_x, u_y, u_z = disp_x * inverse, disp_y * inverse, disp_z * inverse
    geo[...] = inverse
    length_sq = u_x * u_x + u_y * u_y + u_z * u_z
    angular = (
        u_x,
        u_y,
        u_z,
        ROOT_THREE * u_x * u_y,
        ROOT_THREE * u_y * u_z,
        0.5 * (3.0 * u_z * u_z - length_sq),
        ROOT_THREE * u_x * u_z,
        0.5 * ROOT_THREE * (u_x * u_x - u_y * u_y),
    )
    for f in range(8):
        ang[f] = angular[f]
    zf[...] = jnp.zeros_like(zf)
    for b in range(NB):
        off = (rho - (0.5 + SPACING * b)) / SPACING
        basis = jnp.exp(-(off * off))
        slope = basis * off * (-2.0 / SPACING)
        for i, value in enumerate((basis, slope)):
            high, low = split(value)
            zf[32 * i + b] = high
            zf[32 * i + 8 + b] = high
            zf[32 * i + 16 + b] = low

    def columns(p, k):
        return pl.ds((p * NE + k) * S, S)

    for p in range(NP):
        values = jnp.concatenate([zf[:, k * NP + p, :] for k in range(NE)], axis=1).astype(BF16)
        at = pl.ds(p * ROWS, ROWS)
        out = dot(wide[pl.ds(0, 7 * C), :], values[0:32])
        for f in range(7):
            coef[f, :, at] = out[f * C : (f + 1) * C]
        qcoef[0, :, at] = dot(wide[pl.ds(8 * C, C), :], values[0:32])
        out = dot(wide[pl.ds(7 * C, 2 * C), :], values[32:64])
        for f in range(2):
            qcoef[1 + f, :, at] = out[f * C : (f + 1) * C]

    def gather(bufs, g, lo, beyond):
        buf = bufs[g]
        n = buf.shape[2]
        for p in range(NP):
            around = range(6, 9) if beyond else range(6)
            tiles = [buf[near_slot(p, j)].reshape(n * C, S) for j in around]
            picks = oh[p, pl.ds(around[0] * S, len(around) * S), :]
            out = dot(jnp.concatenate(tiles, axis=1), picks)
            at = pl.ds(p * ROWS, ROWS)
            for i in range(n):
                term = out[i * C : (i + 1) * C]
                gsc[lo + i, :, at] = gsc[lo + i, :, at] + term if beyond else term

    def each_row(fn):
        for p in range(NP):

            def run(i, carry, p=p):
                fn(p, pl.ds(pl.multiple_of(i * STEP, STEP), STEP))
                return carry

            lax.fori_loop(0, C // STEP, run, 0)

    def angle(f, p, k):
        return ang[f, pl.ds(k * NP + p, 1), :]

    def own_columns(p):
        return pl.ds(p * S, S)

    def message_sv(p, r):
        total = [jnp.zeros((STEP, S), F32) for _ in range(BLOCKS)]
        for k in range(NE):
            e = columns(p, k)
            s = gsc[0, r, e]
            v = [gsc[1 + m, r, e] for m in range(3)]
            u = [angle(m, p, k) for m in range(3)]
            along = u[0] * v[0] + u[1] * v[1] + u[2] * v[2]
            total[0] = total[0] + coef[0, r, e] * s + coef[1, r, e] * along
            r3s = coef[3, r, e] * s
            r4 = coef[4, r, e]
            for m in range(3):
                total[1 + m] = total[1 + m] + r3s * u[m] + r4 * v[m]
            r5s = coef[5, r, e] * s
            for n in range(5):
                total[4 + n] = total[4 + n] + r5s * angle(3 + n, p, k)
        for b in range(BLOCKS):
            acc[b, r, own_columns(p)] = total[b]

    def message_t(lo, hi):
        def fn(p, r):
            at = own_columns(p)
            total = [acc[b, r, at] for b in (0, *range(lo, hi))]
            for k in range(NE):
                e = columns(p, k)
                along = None
                r6 = coef[6, r, e]
                for n in range(lo, hi):
                    t = gsc[n, r, e]
                    term = angle(n - 1, p, k) * t
                    along = term if along is None else along + term
                    total[1 + n - lo] = total[1 + n - lo] + r6 * t
                total[0] = total[0] + coef[2, r, e] * along
            for i, b in enumerate((0, *range(lo, hi))):
                acc[b, r, at] = total[i]

        return fn

    third = 1.0 / NE

    def mix(lo, hi, w):
        terms = jnp.concatenate([(acc[b] * third).astype(BF16) for b in range(lo, hi)], axis=1)
        out = dot(w_turned[pl.ds(w * C, C), :], terms)
        for b in range(lo, hi):
            acc[b] = out[:, (b - lo) * NP * S : (b - lo + 1) * NP * S]

    halo.near(0)
    gather(ext, 0, 0, False)
    halo.corners(0)
    halo.near(1)
    gather(ext, 1, 4, False)
    halo.near(2)
    gather(ext, 2, 7, False)
    halo.corners(1)
    halo.rest(0)
    gather(ext, 0, 0, True)
    each_row(message_sv)
    mix(1, 4, 2)
    halo.corners(2)
    halo.rest(1)
    gather(ext, 1, 4, True)
    each_row(message_t(4, 7))
    halo.rest(2)
    gather(ext, 2, 7, True)
    each_row(message_t(7, 9))

    out = dot(w_turned[pl.ds(0, 2 * C), :], (acc[0] * third).astype(BF16))
    pre = out[0:C]
    acc[0] = pre * jax.nn.sigmoid(pre)
    gate[...] = jax.nn.sigmoid(out[C : 2 * C])

    def update_sv(p, r):
        at = own_columns(p)
        g = gate[r, at]
        for b in range(READ_BLOCKS):
            old = block(ext, b, 0, p)[r, :].astype(F32)
            step = g * acc[b, r, at] if b > 0 else acc[0, r, at]
            block(ext2, b, 0, p)[r, :] = (old + step).astype(BF16)

    each_row(update_sv)
    halo2 = Halo(ext2, f2_send, f2_recv, device, low_wrap, high_wrap)
    for g in range(len(GROUPS2)):
        halo2.own(g)

    mix(4, 9, 3)
    for p in range(NP):
        for b in range(BLOCKS):
            if b < READ_BLOCKS:
                new = block(ext2, b, 0, p)[...].astype(F32)
            else:
                at = own_columns(p)
                new = block(ext, b, 0, p)[...].astype(F32) + gate[:, at] * acc[b, :, at]
            mix_out[p, 0, :, pl.ds(b * C, C)] = jnp.transpose(new).astype(BF16)
    write = pltpu.make_async_copy(mix_out, mixed, out_sem)
    write.start()

    def near_side(p, r):
        own = [block(ext2, b, 0, p)[r, :].astype(F32) for b in range(READ_BLOCKS)]
        for k in range(NE):
            e = columns(p, k)
            u = [angle(m, p, k) for m in range(3)]
            along = u[0] * own[1] + u[1] * own[2] + u[2] * own[3]
            q1 = qcoef[0, r, e]
            side[0, r, e] = qcoef[1, r, e] * own[0]
            side[1, r, e] = qcoef[2, r, e] * along
            side[2, r, e] = q1 * along
            for m in range(3):
                side[3 + m, r, e] = q1 * own[1 + m]

    halo2.near(0)
    gather(ext2, 0, 0, False)
    halo2.corners(0)
    each_row(near_side)
    halo2.near(1)
    gather(ext2, 1, 2, False)
    halo2.corners(1)
    halo.sent(range(len(GROUPS)))
    halo2.rest(0)
    gather(ext2, 0, 0, True)
    halo2.rest(1)
    gather(ext2, 1, 2, True)

    sums[...] = jnp.zeros_like(sums)
    for p in range(NP):

        def pair(i, carry, p=p):
            r = pl.ds(pl.multiple_of(i * STEP, STEP), STEP)
            carry = list(carry)
            for k in range(NE):
                e = columns(p, k)
                far = [gsc[b, r, e] for b in range(READ_BLOCKS)]
                u = [angle(m, p, k) for m in range(3)]
                along = u[0] * far[1] + u[1] * far[2] + u[2] * far[3]
                carry[4 * k] = carry[4 * k] + side[0, r, e] * far[0] + side[1, r, e] * along
                own_q = side[2, r, e]
                for m in range(3):
                    term = side[3 + m, r, e] * along + own_q * far[1 + m]
                    carry[4 * k + 1 + m] = carry[4 * k + 1 + m] + term
            return tuple(carry)

        zero = jnp.zeros((STEP, S), F32)
        totals = lax.fori_loop(0, C // STEP, pair, (zero,) * (4 * NE))
        for k in range(NE):
            for q in range(4):
                row = jnp.sum(totals[4 * k + q], axis=0, keepdims=True)
                sums[q, pl.ds(k * NP + p, 1), :] = row

    t_rho, g_x, g_y, g_z = (sums[q] for q in range(4))
    u_x, u_y, u_z = ang[0], ang[1], ang[2]
    inverse = geo[...]
    radial_part = t_rho - (u_x * g_x + u_y * g_y + u_z * g_z) * inverse
    grad[...] = jnp.zeros_like(grad)
    grad[0] = radial_part * u_x + g_x * inverse
    grad[1] = radial_part * u_y + g_y * inverse
    grad[2] = radial_part * u_z + g_z * inverse

    parts = []
    for p in range(NP):
        terms = jnp.concatenate([grad[:, k * NP + p, :] for k in range(NE)], axis=1)
        first, rest = split(terms)
        second, third_part = split(rest)
        parts.append(
            jnp.concatenate([first, second, third_part, jnp.zeros_like(first)], 0).astype(BF16)
        )

    def scatter(lo, hi):
        seen = {}
        for p in range(NP):
            out = dot(parts[p], oh[p, pl.ds(lo * S, (hi - lo) * S), :], (1, 1))
            out = (out[0:8] + out[8:16]) + out[16:24]
            for j in range(lo, hi):
                term = out[:, (j - lo) * S : (j - lo + 1) * S]
                at = near_slot(p, j)
                seen[at] = seen[at] - term if at in seen else -term
        for at, value in seen.items():
            extf[at] = value

    scatter(2, 9)
    force_copies = []
    for n, (dx, dy) in enumerate(DIRECTIONS):
        if dx == 0:
            here, there = pl.ds(0, 2), pl.ds(0, 2)
        elif dx == 1:
            here, there = pl.ds(2, 1), pl.ds(0, 1)
        else:
            here, there = pl.ds(3, 1), pl.ds(1, 1)
        copy = pltpu.make_async_remote_copy(
            src_ref=extf.at[PLACE[dy], here],
            dst_ref=frecv.at[n, there],
            send_sem=fo_send.at[n],
            recv_sem=fo_recv.at[n],
            device_id=device(dx, dy),
            device_id_type=MESH,
        )
        copy.start()
        force_copies.append(copy)

    scatter(0, 2)
    total = []
    for p in range(NP):
        mine = extf[0, p]
        for k in range(NE):
            mine = mine + grad[:, k * NP + p, :]
        total.append(mine)
    for n, (dx, dy) in enumerate(DIRECTIONS):
        force_copies[n].wait_recv()
        for p in range(NP):
            if dx == 0 or (dx == 1) == (p == 0):
                total[p] = total[p] + frecv[n, p]
    for p in range(NP):
        for m in range(3):
            forces[p, m] = total[p][m : m + 1]

    for copy in (*pos_copies, *force_copies):
        copy.wait_send()
    halo2.sent(range(len(GROUPS2)))
    write.wait()


def solution(mesh):
    gx_size, yz_size = mesh.shape["gx"], mesh.shape["yz"]

    def body(features, positions, *rest):
        args = (features, jnp.transpose(positions, (0, 2, 1, 3)), *rest)
        vmem = pl.BlockSpec(memory_space=pltpu.VMEM)
        anywhere = pl.BlockSpec(memory_space=pl.ANY)
        dma = pltpu.SemaphoreType.DMA
        n_dir = len(DIRECTIONS)

        def run_all(*refs):
            kernel(gx_size, yz_size, *refs)

        small = [pltpu.VMEM(x.shape, x.dtype) for x in args[1:]]
        new_features, force = pl.pallas_call(
            run_all,
            out_shape=(
                jax.ShapeDtypeStruct((NP, 1, S, BLOCKS * C), BF16),
                jax.ShapeDtypeStruct((NP, 3, 1, S), F32),
            ),
            in_specs=[pl.BlockSpec(memory_space=pltpu.HBM)] * 10,
            out_specs=(anywhere, vmem),
            scratch_shapes=small
            + [
                *[pltpu.VMEM((3, 4, hi - lo, S, C), BF16) for lo, hi in GROUPS + GROUPS2],
                pltpu.VMEM((3, 4, 8, S), F32),
                pltpu.VMEM((NP, NEAR, ROWS), BF16),
                pltpu.VMEM((7, C, NP * ROWS), F32),
                pltpu.VMEM((3, C, NP * ROWS), F32),
                pltpu.VMEM((9 * C, 32), BF16),
                pltpu.VMEM((4 * C, C), BF16),
                pltpu.VMEM((64, 8, S), F32),
                pltpu.VMEM((8, 8, S), F32),
                pltpu.VMEM((8, 8, S), F32),
                pltpu.VMEM((8, S), F32),
                pltpu.VMEM((2, 8, S), F32),
                pltpu.VMEM((BLOCKS, C, NP * S), F32),
                pltpu.VMEM((C, NP * S), F32),
                pltpu.VMEM((BLOCKS, C, NP * ROWS), F32),
                pltpu.VMEM((NP, 1, S, BLOCKS * C), BF16),
                pltpu.VMEM((NP, 1, S, BLOCKS * C), BF16),
                pltpu.VMEM((6, C, NP * ROWS), F32),
                pltpu.VMEM((4, 8, S), F32),
                pltpu.VMEM((8, 8, S), F32),
                pltpu.VMEM((3, 4, 8, S), F32),
                pltpu.VMEM((n_dir, NP, 8, S), F32),
                dma((len(small),)),
                dma,
                dma,
                dma((n_dir,)),
                dma((n_dir,)),
                dma((len(GROUPS), Halo.COUNT)),
                dma((len(GROUPS), Halo.COUNT)),
                dma((len(GROUPS2), Halo.COUNT)),
                dma((len(GROUPS2), Halo.COUNT)),
                dma((n_dir,)),
                dma((n_dir,)),
            ],
            compiler_params=pltpu.CompilerParams(
                collective_id=0, has_side_effects=True, vmem_limit_bytes=60 * 1024 * 1024
            ),
            cost_estimate=pl.CostEstimate(
                flops=4 * 10**9, bytes_accessed=2 * 10**6, transcendentals=10**5
            ),
        )(*args)
        return new_features, jnp.transpose(force, (0, 2, 1, 3))

    in_specs = (
        P("gx", "yz", None, None),
        P("gx", "yz", None, None),
        P(None, "gx", "yz", None),
        P(None, "gx", "yz", None),
        P(),
        P(),
        P(),
        P(),
        P(),
        P(),
    )
    out_specs = (P("gx", "yz", None, None), P("gx", "yz", None, None))
    return jax.shard_map(body, mesh=mesh, in_specs=in_specs, out_specs=out_specs, check_vma=False)
```

```python
import math

import jax
import jax.numpy as jnp
from jax import lax
from jax.experimental import pallas as pl
from jax.experimental.pallas import tpu as pltpu
from jax.sharding import PartitionSpec as P

MESH = pl.DeviceIdType.MESH
F32 = jnp.float32
BF16 = jnp.bfloat16
SOFTENING = 0.25
SPACING = 0.6
ROOT_THREE = math.sqrt(3.0)
C = 128
S = 128
NB = 8
NE = 3
NP = 2
BLOCKS = 9
READ_BLOCKS = 4
KP = NE * NP
ROWS = NE * S
NEAR = 9 * S
STEP = 16
GROUPS = ((0, 4), (4, 7), (7, 9))
GROUPS2 = ((0, 4),)
DIRECTIONS = tuple((dx, dy) for dx in (-1, 0, 1) for dy in (-1, 0, 1) if (dx, dy) != (0, 0))


def split(x):
    high = x.astype(BF16).astype(F32)
    return high, x - high


def dot(a, b, contract=(1, 0)):
    dims = (((contract[0],), (contract[1],)), ((), ()))
    return lax.dot_general(a, b, dims, preferred_element_type=F32)


PLACE = {0: 0, -1: 1, 1: 2}


def near_slot(p, j):
    y = (1, 2, 0, 0, 1, 2, 0, 1, 2)[j]
    return (y, (p, 1 - p, 3 - p)[j // 3])


def near_pillar(p, j):
    y, slot = near_slot(p, j)
    return (1, 2, 3, 0)[slot], (1, 0, 2)[y]


def block(bufs, c, *at):
    for buf in bufs:
        if c < buf.shape[2]:
            return buf.at[(*at, c)]
        c -= buf.shape[2]


class Halo:
    COUNT = 12

    def __init__(self, bufs, send, recv, device, low_wrap, high_wrap):
        self.copies = {}
        self.low_wrap, self.high_wrap = low_wrap, high_wrap
        for g, buf in enumerate(bufs):
            n = 0
            for own, ghost, dx in ((0, 2, -1), (1, 3, 1)):
                spans = {"x": (buf.at[0, own], buf.at[0, ghost], (dx, 0))}
                for sign, step, to in (("m", -1, 2), ("p", 1, 1)):
                    spans |= {
                        "y" + sign: (buf.at[0, own], buf.at[to, own], (0, step)),
                        "c" + sign: (buf.at[0, ghost], buf.at[to, ghost], (0, step)),
                        "w" + sign: (buf.at[0, own], buf.at[to, ghost], (dx, step)),
                    }
                for name, (src, dst, step) in spans.items():
                    if name[0] != "w":
                        slot = n
                        n += 1
                    else:
                        slot = n - 1
                    self.copies[name, own, g] = pltpu.make_async_remote_copy(
                        src_ref=src,
                        dst_ref=dst,
                        send_sem=send.at[g, slot],
                        recv_sem=recv.at[g, slot],
                        device_id=device(*step),
                        device_id_type=MESH,
                    )

    def start(self, own, g, *names):
        for name in names:
            self.copies[name, own, g].start()

    def arrived(self, own, g, *names):
        for name in names:
            self.copies[name, own, g].wait_recv()

    def sends(self, sign, plain, wrap):
        wraps = self.low_wrap if sign == "m" else self.high_wrap
        if wrap is not None:
            pl.when(wraps)(wrap)
        if plain is not None:
            pl.when(jnp.logical_not(wraps))(plain)

    def along_x(self, own, g):
        self.start(own, g, "x")
        for sign in "mp":
            self.sends(sign, None, lambda: self.start(own, g, "w" + sign))

    def along_y(self, own, g):
        self.start(own, g, "ym", "yp")

    def near(self, own, g):
        self.arrived(own, g, "ym", "yp")

    def corners(self, own, g):
        self.arrived(own, g, "x")
        for sign in "mp":
            self.sends(sign, lambda: self.start(own, g, "c" + sign), None)

    def rest(self, own, g):
        self.arrived(own, g, "cm", "cp")

    def sent(self, groups):
        for g in groups:
            for own in range(NP):
                for name in ("x", "ym", "yp", "cm", "cp"):
                    self.copies[name, own, g].wait_send()


def kernel(
    gx_size,
    yz_size,
    feat,
    *refs,
):
    small_in, refs = refs[:9], refs[9:]
    mixed, forces, *refs = refs
    small, refs = refs[:9], refs[9:]
    run(gx_size, yz_size, feat, small_in, small, mixed, forces, *refs)


def run(
    gx_size,
    yz_size,
    feat,
    small_in,
    small,
    mixed,
    forces,
    ext0,
    ext1,
    ext2,
    mix0,
    posx,
    oh,
    coef,
    qcoef,
    wide,
    w_turned,
    zf,
    ang,
    pj,
    geo,
    edges,
    acc,
    gate,
    gsc,
    raw,
    mix_out,
    side,
    sums,
    grad,
    extf,
    frecv,
    small_sem,
    load_sem,
    out_sem,
    pos_send,
    pos_recv,
    f1_send,
    f1_recv,
    f2_send,
    f2_recv,
    fo_send,
    fo_recv,
):
    ext, ext2 = (ext0, ext1, ext2), (mix0,)
    gx = lax.axis_index("gx")
    yz = lax.axis_index("yz")

    half = yz_size // 2
    low_wrap = lax.rem(yz, half) == 0
    high_wrap = lax.rem(yz, half) == half - 1

    def device(dx, dy):
        return (lax.rem(gx + dx + gx_size, gx_size), lax.rem(yz + dy + yz_size, yz_size))

    small_loads = [
        pltpu.make_async_copy(small_in[i], small[i], small_sem.at[i]) for i in range(len(small))
    ]
    for load in small_loads:
        load.start()
    pos, dst, shift, wr, wq, w_scalar, w_gate, w_vector, w_tensor = small
    feat_load = pltpu.make_async_copy(feat, raw, load_sem)
    feat_load.start()

    barrier = pltpu.get_barrier_semaphore()
    for step in DIRECTIONS:
        pl.semaphore_signal(barrier, inc=1, device_id=device(*step), device_id_type=MESH)

    for load in small_loads:
        load.wait()
    for p in range(NP):
        posx[0, p] = jnp.zeros((8, S), F32)
        for m in range(3):
            posx[0, p, pl.ds(m, 1), :] = pos[p, m]

    def turn(g):
        for c in range(*GROUPS[g]):
            for p in range(NP):
                tile = raw[p, 0, :, pl.ds(c * C, C)].astype(F32)
                block(ext, c, 0, p)[...] = jnp.transpose(tile).astype(BF16)

    feat_load.wait()
    turn(0)
    pl.semaphore_wait(barrier, len(DIRECTIONS))

    pos_copies = []
    for n, (dx, dy) in enumerate(DIRECTIONS):
        if dx == 0:
            here, there = pl.ds(0, 2), pl.ds(0, 2)
        elif dx == 1:
            here, there = pl.ds(1, 1), pl.ds(3, 1)
        else:
            here, there = pl.ds(0, 1), pl.ds(2, 1)
        copy = pltpu.make_async_remote_copy(
            src_ref=posx.at[0, here],
            dst_ref=posx.at[PLACE[-dy], there],
            send_sem=pos_send.at[n],
            recv_sem=pos_recv.at[n],
            device_id=device(dx, dy),
            device_id_type=MESH,
        )
        copy.start()
        pos_copies.append(copy)

    halo = Halo(ext, f1_send, f1_recv, device, low_wrap, high_wrap)
    for g in range(len(GROUPS)):
        if g > 0:
            turn(g)
        halo.along_x(1, g)
        halo.along_y(0, g)
        halo.along_y(1, g)

    atom = lax.broadcasted_iota(jnp.int32, (S, ROWS), 0).astype(F32)
    edges[...] = jnp.zeros_like(edges)
    for p in range(NP):
        rows = [dst[k, p].astype(F32) for k in range(NE)]
        for k in range(NE):
            edges[0, pl.ds(k * NP + p, 1), :] = rows[k]
            edges[1, pl.ds(k * NP + p, 1), :] = shift[k, p].astype(F32)
        place = jnp.concatenate(rows, axis=1) - atom
        for j in range(9):
            x, y = near_pillar(p, j)
            hit = place == float((3 * x + y) * S)
            oh[p, pl.ds(j * S, S), :] = jnp.where(hit, 1.0, 0.0).astype(BF16)

    for f in range(9):
        w = wr[:, pl.ds(f * C, C)] if f < 7 else wq[:, pl.ds((f - 7) * C, C)]
        high, low = split(w)
        rows = jnp.concatenate([high, low, high, jnp.zeros_like(w)], axis=0)
        wide[pl.ds(f * C, C), :] = jnp.transpose(rows).astype(BF16)
    for i, w in enumerate((w_scalar, w_gate, w_vector, w_tensor)):
        w_turned[pl.ds(i * C, C), :] = jnp.transpose(w[...].astype(F32)).astype(BF16)

    halo.along_x(0, 0)

    for copy in pos_copies:
        copy.wait_recv()
    for p in range(NP):
        places = jnp.concatenate([posx[near_slot(p, j)] for j in range(9)], axis=1)
        first, rest = split(places)
        second, third = split(rest)
        parts = jnp.concatenate([first, second, third, jnp.zeros_like(first)], 0).astype(BF16)
        found = dot(parts, oh[p])
        far = (found[0:8] + found[8:16]) + found[16:24]
        for k in range(NE):
            pj[k * NP + p] = far[:, k * S : (k + 1) * S] - posx[0, p]

    place = edges[0]
    pj[pl.ds(KP, 8 - KP)] = jnp.zeros((8 - KP, 8, S), F32)
    own_p = lax.rem(lax.broadcasted_iota(jnp.int32, (8, S), 0), NP).astype(F32)
    one = jnp.ones_like(place)
    nil = jnp.zeros_like(place)

    def at_least(x, bound):
        return jnp.where(x >= float(bound), one, nil)

    ext_x = at_least(place, 3 * S) + at_least(place, 6 * S) + at_least(place, 9 * S)
    left = place - ext_x * float(3 * S)
    ext_y = at_least(left, S) + at_least(left, 2 * S)
    disp_x = pj[:, 0, :] + (ext_x - 1.0 - own_p)
    disp_y = pj[:, 1, :] + (ext_y - 1.0)
    disp_z = pj[:, 2, :] + edges[1]
    rho = jnp.sqrt(disp_x * disp_x + disp_y * disp_y + disp_z * disp_z + SOFTENING)
    inverse = 1.0 / rho
    u_x, u_y, u_z = disp_x * inverse, disp_y * inverse, disp_z * inverse
    geo[...] = inverse
    length_sq = u_x * u_x + u_y * u_y + u_z * u_z
    angular = (
        u_x,
        u_y,
        u_z,
        ROOT_THREE * u_x * u_y,
        ROOT_THREE * u_y * u_z,
        0.5 * (3.0 * u_z * u_z - length_sq),
        ROOT_THREE * u_x * u_z,
        0.5 * ROOT_THREE * (u_x * u_x - u_y * u_y),
    )
    for f in range(8):
        ang[f] = angular[f]
    zf[...] = jnp.zeros_like(zf)
    for b in range(NB):
        off = (rho - (0.5 + SPACING * b)) / SPACING
        basis = jnp.exp(-(off * off))
        slope = basis * off * (-2.0 / SPACING)
        for i, value in enumerate((basis, slope)):
            high, low = split(value)
            zf[32 * i + b] = high
            zf[32 * i + 8 + b] = high
            zf[32 * i + 16 + b] = low

    def columns(p, k):
        return pl.ds((p * NE + k) * S, S)

    for p in range(NP):
        values = jnp.concatenate([zf[:, k * NP + p, :] for k in range(NE)], axis=1).astype(BF16)
        at = pl.ds(p * ROWS, ROWS)
        out = dot(wide[pl.ds(0, 7 * C), :], values[0:32])
        for f in range(7):
            coef[f, :, at] = out[f * C : (f + 1) * C]
        qcoef[0, :, at] = dot(wide[pl.ds(8 * C, C), :], values[0:32])
        out = dot(wide[pl.ds(7 * C, 2 * C), :], values[32:64])
        for f in range(2):
            qcoef[1 + f, :, at] = out[f * C : (f + 1) * C]

    halo.along_x(0, 1)
    halo.along_x(0, 2)

    def gather(bufs, g, lo, p, first, last):
        buf = bufs[g]
        n = buf.shape[2]
        tiles = [buf[near_slot(p, j)].reshape(n * C, S) for j in range(first, last)]
        out = dot(jnp.concatenate(tiles, axis=1), oh[p, pl.ds(first * S, (last - first) * S), :])
        at = pl.ds(p * ROWS, ROWS)
        for i in range(n):
            term = out[i * C : (i + 1) * C]
            gsc[lo + i, :, at] = term if first == 0 else gsc[lo + i, :, at] + term

    def each_row(p, fn):
        def run(i, carry):
            fn(p, pl.ds(pl.multiple_of(i * STEP, STEP), STEP))
            return carry

        lax.fori_loop(0, C // STEP, run, 0)

    def angle(f, p, k):
        return ang[f, pl.ds(k * NP + p, 1), :]

    def own_columns(p):
        return pl.ds(p * S, S)

    def message_sv(p, r):
        total = [jnp.zeros((STEP, S), F32) for _ in range(BLOCKS)]
        for k in range(NE):
            e = columns(p, k)
            s = gsc[0, r, e]
            v = [gsc[1 + m, r, e] for m in range(3)]
            u = [angle(m, p, k) for m in range(3)]
            along = u[0] * v[0] + u[1] * v[1] + u[2] * v[2]
            total[0] = total[0] + coef[0, r, e] * s + coef[1, r, e] * along
            r3s = coef[3, r, e] * s
            r4 = coef[4, r, e]
            for m in range(3):
                total[1 + m] = total[1 + m] + r3s * u[m] + r4 * v[m]
            r5s = coef[5, r, e] * s
            for n in range(5):
                total[4 + n] = total[4 + n] + r5s * angle(3 + n, p, k)
        for b in range(BLOCKS):
            acc[b, r, own_columns(p)] = total[b]

    def message_t(lo, hi):
        def fn(p, r):
            at = own_columns(p)
            total = [acc[b, r, at] for b in (0, *range(lo, hi))]
            for k in range(NE):
                e = columns(p, k)
                along = None
                r6 = coef[6, r, e]
                for n in range(lo, hi):
                    t = gsc[n, r, e]
                    term = angle(n - 1, p, k) * t
                    along = term if along is None else along + term
                    total[1 + n - lo] = total[1 + n - lo] + r6 * t
                total[0] = total[0] + coef[2, r, e] * along
            for i, b in enumerate((0, *range(lo, hi))):
                acc[b, r, at] = total[i]

        return fn

    third = 1.0 / NE

    def mix(p, lo, hi, w):
        at = own_columns(p)
        terms = jnp.concatenate([(acc[b, :, at] * third).astype(BF16) for b in range(lo, hi)], axis=1)
        out = dot(w_turned[pl.ds(w * C, C), :], terms)
        for b in range(lo, hi):
            acc[b, :, at] = out[:, (b - lo) * S : (b - lo + 1) * S]

    def update_sv(p, r):
        at = own_columns(p)
        g = gate[r, at]
        for b in range(READ_BLOCKS):
            old = block(ext, b, 0, p)[r, :].astype(F32)
            step = g * acc[b, r, at] if b > 0 else acc[0, r, at]
            block(ext2, b, 0, p)[r, :] = (old + step).astype(BF16)

    halo2 = Halo(ext2, f2_send, f2_recv, device, low_wrap, high_wrap)

    def finish(p):
        at = own_columns(p)
        out = dot(w_turned[pl.ds(0, 2 * C), :], (acc[0, :, at] * third).astype(BF16))
        pre = out[0:C]
        acc[0, :, at] = pre * jax.nn.sigmoid(pre)
        gate[:, at] = jax.nn.sigmoid(out[C : 2 * C])
        each_row(p, update_sv)
        halo2.along_x(p, 0)
        halo2.along_y(p, 0)

    def finish_tensors(p):
        mix(p, 4, 9, 3)
        at = own_columns(p)
        for b in range(BLOCKS):
            if b < READ_BLOCKS:
                new = block(ext2, b, 0, p)[...].astype(F32)
            else:
                new = block(ext, b, 0, p)[...].astype(F32) + gate[:, at] * acc[b, :, at]
            mix_out[p, 0, :, pl.ds(b * C, C)] = jnp.transpose(new).astype(BF16)

    starts = [lo for lo, _ in GROUPS]
    for g in range(3):
        halo.near(0, g)
        halo.near(1, g)
        gather(ext, g, starts[g], 0, 0, 6)
        halo.corners(1, g)
    for g in range(3):
        gather(ext, g, starts[g], 1, 0, 6)
    halo.rest(1, 0)
    gather(ext, 0, starts[0], 0, 6, 9)
    each_row(0, message_sv)
    mix(0, 1, 4, 2)
    halo.rest(1, 1)
    gather(ext, 1, starts[1], 0, 6, 9)
    each_row(0, message_t(4, 7))
    halo.rest(1, 2)
    gather(ext, 2, starts[2], 0, 6, 9)
    each_row(0, message_t(7, 9))
    finish(0)
    halo.corners(0, 0)
    halo.corners(0, 1)
    halo.rest(0, 0)
    gather(ext, 0, starts[0], 1, 6, 9)
    each_row(1, message_sv)
    mix(1, 1, 4, 2)
    halo.corners(0, 2)
    halo.rest(0, 1)
    gather(ext, 1, starts[1], 1, 6, 9)
    each_row(1, message_t(4, 7))
    halo.rest(0, 2)
    gather(ext, 2, starts[2], 1, 6, 9)
    each_row(1, message_t(7, 9))
    finish(1)

    def near_side(p, r):
        own = [block(ext2, b, 0, p)[r, :].astype(F32) for b in range(READ_BLOCKS)]
        for k in range(NE):
            e = columns(p, k)
            u = [angle(m, p, k) for m in range(3)]
            along = u[0] * own[1] + u[1] * own[2] + u[2] * own[3]
            q1 = qcoef[0, r, e]
            side[0, r, e] = qcoef[1, r, e] * own[0]
            side[1, r, e] = qcoef[2, r, e] * along
            side[2, r, e] = q1 * along
            for m in range(3):
                side[3 + m, r, e] = q1 * own[1 + m]

    halo2.corners(0, 0)
    halo2.near(0, 0)
    gather(ext2, 0, 0, 0, 0, 3)
    for p in range(NP):
        each_row(p, near_side)
        finish_tensors(p)
    write = pltpu.make_async_copy(mix_out, mixed, out_sem)
    write.start()
    halo2.corners(1, 0)
    halo2.near(1, 0)
    gather(ext2, 0, 0, 0, 3, 6)
    gather(ext2, 0, 0, 1, 0, 6)
    halo.sent(range(len(GROUPS)))
    halo2.rest(0, 0)
    gather(ext2, 0, 0, 1, 6, 9)
    halo2.rest(1, 0)
    gather(ext2, 0, 0, 0, 6, 9)

    sums[...] = jnp.zeros_like(sums)
    for p in range(NP):

        def pair(i, carry, p=p):
            r = pl.ds(pl.multiple_of(i * STEP, STEP), STEP)
            carry = list(carry)
            for k in range(NE):
                e = columns(p, k)
                far = [gsc[b, r, e] for b in range(READ_BLOCKS)]
                u = [angle(m, p, k) for m in range(3)]
                along = u[0] * far[1] + u[1] * far[2] + u[2] * far[3]
                carry[4 * k] = carry[4 * k] + side[0, r, e] * far[0] + side[1, r, e] * along
                own_q = side[2, r, e]
                for m in range(3):
                    term = side[3 + m, r, e] * along + own_q * far[1 + m]
                    carry[4 * k + 1 + m] = carry[4 * k + 1 + m] + term
            return tuple(carry)

        zero = jnp.zeros((STEP, S), F32)
        totals = lax.fori_loop(0, C // STEP, pair, (zero,) * (4 * NE))
        for k in range(NE):
            for q in range(4):
                row = jnp.sum(totals[4 * k + q], axis=0, keepdims=True)
                sums[q, pl.ds(k * NP + p, 1), :] = row

    t_rho, g_x, g_y, g_z = (sums[q] for q in range(4))
    u_x, u_y, u_z = ang[0], ang[1], ang[2]
    inverse = geo[...]
    radial_part = t_rho - (u_x * g_x + u_y * g_y + u_z * g_z) * inverse
    grad[...] = jnp.zeros_like(grad)
    grad[0] = radial_part * u_x + g_x * inverse
    grad[1] = radial_part * u_y + g_y * inverse
    grad[2] = radial_part * u_z + g_z * inverse

    parts = []
    for p in range(NP):
        terms = jnp.concatenate([grad[:, k * NP + p, :] for k in range(NE)], axis=1)
        first, rest = split(terms)
        second, third_part = split(rest)
        parts.append(
            jnp.concatenate([first, second, third_part, jnp.zeros_like(first)], 0).astype(BF16)
        )

    def scatter(*spans):
        seen = {}
        for p in range(NP):
            for lo, hi in spans:
                out = dot(parts[p], oh[p, pl.ds(lo * S, (hi - lo) * S), :], (1, 1))
                out = (out[0:8] + out[8:16]) + out[16:24]
                for j in range(lo, hi):
                    term = out[:, (j - lo) * S : (j - lo + 1) * S]
                    at = near_slot(p, j)
                    seen[at] = seen[at] - term if at in seen else -term
        for at, value in seen.items():
            extf[at] = value

    scatter((0, 2), (4, 9))
    force_copies = []
    for n, (dx, dy) in enumerate(DIRECTIONS):
        if dx == 0:
            here, there = pl.ds(0, 2), pl.ds(0, 2)
        elif dx == 1:
            here, there = pl.ds(2, 1), pl.ds(0, 1)
        else:
            here, there = pl.ds(3, 1), pl.ds(1, 1)
        copy = pltpu.make_async_remote_copy(
            src_ref=extf.at[PLACE[dy], here],
            dst_ref=frecv.at[n, there],
            send_sem=fo_send.at[n],
            recv_sem=fo_recv.at[n],
            device_id=device(dx, dy),
            device_id_type=MESH,
        )
        copy.start()
        force_copies.append(copy)

    scatter((2, 4))
    total = []
    for p in range(NP):
        mine = extf[0, p]
        for k in range(NE):
            mine = mine + grad[:, k * NP + p, :]
        total.append(mine)
    for n, (dx, dy) in enumerate(DIRECTIONS):
        force_copies[n].wait_recv()
        for p in range(NP):
            if dx == 0 or (dx == 1) == (p == 0):
                total[p] = total[p] + frecv[n, p]
    for p in range(NP):
        for m in range(3):
            forces[p, m] = total[p][m : m + 1]

    for copy in (*pos_copies, *force_copies):
        copy.wait_send()
    halo2.sent(range(len(GROUPS2)))
    write.wait()


def solution(mesh):
    gx_size, yz_size = mesh.shape["gx"], mesh.shape["yz"]

    def body(features, positions, *rest):
        args = (features, jnp.transpose(positions, (0, 2, 1, 3)), *rest)
        vmem = pl.BlockSpec(memory_space=pltpu.VMEM)
        anywhere = pl.BlockSpec(memory_space=pl.ANY)
        dma = pltpu.SemaphoreType.DMA
        n_dir = len(DIRECTIONS)

        def run_all(*refs):
            kernel(gx_size, yz_size, *refs)

        small = [pltpu.VMEM(x.shape, x.dtype) for x in args[1:]]
        new_features, force = pl.pallas_call(
            run_all,
            out_shape=(
                jax.ShapeDtypeStruct((NP, 1, S, BLOCKS * C), BF16),
                jax.ShapeDtypeStruct((NP, 3, 1, S), F32),
            ),
            in_specs=[pl.BlockSpec(memory_space=pltpu.HBM)] * 10,
            out_specs=(anywhere, vmem),
            scratch_shapes=small
            + [
                *[pltpu.VMEM((3, 4, hi - lo, S, C), BF16) for lo, hi in GROUPS + GROUPS2],
                pltpu.VMEM((3, 4, 8, S), F32),
                pltpu.VMEM((NP, NEAR, ROWS), BF16),
                pltpu.VMEM((7, C, NP * ROWS), F32),
                pltpu.VMEM((3, C, NP * ROWS), F32),
                pltpu.VMEM((9 * C, 32), BF16),
                pltpu.VMEM((4 * C, C), BF16),
                pltpu.VMEM((64, 8, S), F32),
                pltpu.VMEM((8, 8, S), F32),
                pltpu.VMEM((8, 8, S), F32),
                pltpu.VMEM((8, S), F32),
                pltpu.VMEM((2, 8, S), F32),
                pltpu.VMEM((BLOCKS, C, NP * S), F32),
                pltpu.VMEM((C, NP * S), F32),
                pltpu.VMEM((BLOCKS, C, NP * ROWS), F32),
                pltpu.VMEM((NP, 1, S, BLOCKS * C), BF16),
                pltpu.VMEM((NP, 1, S, BLOCKS * C), BF16),
                pltpu.VMEM((6, C, NP * ROWS), F32),
                pltpu.VMEM((4, 8, S), F32),
                pltpu.VMEM((8, 8, S), F32),
                pltpu.VMEM((3, 4, 8, S), F32),
                pltpu.VMEM((n_dir, NP, 8, S), F32),
                dma((len(small),)),
                dma,
                dma,
                dma((n_dir,)),
                dma((n_dir,)),
                dma((len(GROUPS), Halo.COUNT)),
                dma((len(GROUPS), Halo.COUNT)),
                dma((len(GROUPS2), Halo.COUNT)),
                dma((len(GROUPS2), Halo.COUNT)),
                dma((n_dir,)),
                dma((n_dir,)),
            ],
            compiler_params=pltpu.CompilerParams(
                collective_id=0, has_side_effects=True, vmem_limit_bytes=60 * 1024 * 1024
            ),
            cost_estimate=pl.CostEstimate(
                flops=4 * 10**9, bytes_accessed=2 * 10**6, transcendentals=10**5
            ),
        )(*args)
        return new_features, jnp.transpose(force, (0, 2, 1, 3))

    in_specs = (
        P("gx", "yz", None, None),
        P("gx", "yz", None, None),
        P(None, "gx", "yz", None),
        P(None, "gx", "yz", None),
        P(),
        P(),
        P(),
        P(),
        P(),
        P(),
    )
    out_specs = (P("gx", "yz", None, None), P("gx", "yz", None, None))
    return jax.shard_map(body, mesh=mesh, in_specs=in_specs, out_specs=out_specs, check_vma=False)
```

```python
import math

import jax
import jax.numpy as jnp
from jax import lax
from jax.experimental import pallas as pl
from jax.experimental.pallas import tpu as pltpu
from jax.sharding import PartitionSpec as P

MESH = pl.DeviceIdType.MESH
F32 = jnp.float32
BF16 = jnp.bfloat16
SOFTENING = 0.25
SPACING = 0.6
ROOT_THREE = math.sqrt(3.0)
C = 128
S = 128
NB = 8
NE = 3
NP = 2
BLOCKS = 9
READ_BLOCKS = 4
KP = NE * NP
ROWS = NE * S
NEAR = 9 * S
STEP = 16
GROUPS = ((0, 4), (4, 7), (7, 9))
GROUPS2 = ((0, 2), (2, 4))
DIRECTIONS = tuple((dx, dy) for dx in (-1, 0, 1) for dy in (-1, 0, 1) if (dx, dy) != (0, 0))


def split(x):
    high = x.astype(BF16).astype(F32)
    return high, x - high


def dot(a, b, contract=(1, 0)):
    dims = (((contract[0],), (contract[1],)), ((), ()))
    return lax.dot_general(a, b, dims, preferred_element_type=F32)


PLACE = {0: 0, -1: 1, 1: 2}


def near_slot(p, j):
    return (j // 2, j % 2) if j < 6 else (j - 6, 3 - p)


def near_pillar(p, j):
    y, slot = near_slot(p, j)
    return (1, 2, 3, 0)[slot], (1, 0, 2)[y]


def block(bufs, c, *at):
    for buf in bufs:
        if c < buf.shape[2]:
            return buf.at[(*at, c)]
        c -= buf.shape[2]


class Halo:
    COUNT = 10

    def __init__(self, bufs, send, recv, device, low_wrap, high_wrap):
        self.copies = {}
        self.low_wrap, self.high_wrap = low_wrap, high_wrap
        own, ghosts = pl.ds(0, 2), pl.ds(2, 2)
        for g, buf in enumerate(bufs):
            spans = {
                "x0": (buf.at[0, 0], buf.at[0, 2], (-1, 0)),
                "x1": (buf.at[0, 1], buf.at[0, 3], (1, 0)),
            }
            for sign, step, to in (("m", -1, 2), ("p", 1, 1)):
                spans |= {
                    "y" + sign: (buf.at[0, own], buf.at[to, own], (0, step)),
                    "c" + sign: (buf.at[0, ghosts], buf.at[to, ghosts], (0, step)),
                    "w0" + sign: (buf.at[0, 0], buf.at[to, 2], (-1, step)),
                    "w1" + sign: (buf.at[0, 1], buf.at[to, 3], (1, step)),
                }
            for n, (name, (src, dst, step)) in enumerate(spans.items()):
                self.copies[name, g] = pltpu.make_async_remote_copy(
                    src_ref=src,
                    dst_ref=dst,
                    send_sem=send.at[g, n],
                    recv_sem=recv.at[g, n],
                    device_id=device(*step),
                    device_id_type=MESH,
                )

    def start(self, g, *names):
        for name in names:
            self.copies[name, g].start()

    def arrived(self, g, *names):
        for name in names:
            self.copies[name, g].wait_recv()

    def sends(self, sign, plain, wrap):
        wraps = self.low_wrap if sign == "m" else self.high_wrap
        if wrap is not None:
            pl.when(wraps)(wrap)
        if plain is not None:
            pl.when(jnp.logical_not(wraps))(plain)

    def own(self, g):
        self.start(g, "x0", "x1", "ym", "yp")
        for sign in "mp":
            self.sends(sign, None, lambda: self.start(g, "w0" + sign, "w1" + sign))

    def near(self, g):
        self.arrived(g, "ym", "yp")

    def corners(self, g):
        self.arrived(g, "x0", "x1")
        for sign in "mp":
            self.sends(sign, lambda: self.start(g, "c" + sign), None)

    def rest(self, g):
        for sign, wraps in (("m", self.high_wrap), ("p", self.low_wrap)):
            pl.when(wraps)(lambda: self.arrived(g, "w0" + sign, "w1" + sign))
            pl.when(jnp.logical_not(wraps))(lambda: self.arrived(g, "c" + sign))

    def sent(self, groups):
        def done(*names):
            for g in groups:
                for name in names:
                    self.copies[name, g].wait_send()

        done("x0", "x1", "ym", "yp")
        for sign in "mp":
            self.sends(sign, lambda: done("c" + sign), lambda: done("w0" + sign, "w1" + sign))


def kernel(
    gx_size,
    yz_size,
    feat,
    *refs,
):
    small_in, refs = refs[:9], refs[9:]
    mixed, forces, *refs = refs
    small, refs = refs[:9], refs[9:]
    run(gx_size, yz_size, feat, small_in, small, mixed, forces, *refs)


def run(
    gx_size,
    yz_size,
    feat,
    small_in,
    small,
    mixed,
    forces,
    ext0,
    ext1,
    ext2,
    mix0,
    mix1,
    posx,
    oh,
    coef,
    wide,
    w_turned,
    zf,
    ang,
    pj,
    geo,
    edges,
    acc,
    gate,
    gsc,
    raw,
    mix_out,
    side,
    by_pillar,
    sums,
    grad,
    extf,
    frecv,
    small_sem,
    load_sem,
    out_sem,
    pos_send,
    pos_recv,
    f1_send,
    f1_recv,
    f2_send,
    f2_recv,
    fo_send,
    fo_recv,
):
    ext, ext2 = (ext0, ext1, ext2), (mix0, mix1)
    gx = lax.axis_index("gx")
    yz = lax.axis_index("yz")

    half = yz_size // 2
    low_wrap = lax.rem(yz, half) == 0
    high_wrap = lax.rem(yz, half) == half - 1

    def device(dx, dy):
        return (lax.rem(gx + dx + gx_size, gx_size), lax.rem(yz + dy + yz_size, yz_size))

    small_loads = [
        pltpu.make_async_copy(small_in[i], small[i], small_sem.at[i]) for i in range(len(small))
    ]
    for load in small_loads:
        load.start()
    pos, dst, shift, wr, wq, w_scalar, w_gate, w_vector, w_tensor = small
    feat_load = pltpu.make_async_copy(feat, raw, load_sem)
    feat_load.start()

    barrier = pltpu.get_barrier_semaphore()
    for step in DIRECTIONS:
        pl.semaphore_signal(barrier, inc=1, device_id=device(*step), device_id_type=MESH)

    for load in small_loads:
        load.wait()
    for p in range(NP):
        posx[0, p] = jnp.zeros((8, S), F32)
        for m in range(3):
            posx[0, p, pl.ds(m, 1), :] = pos[p, m]

    def turn(g):
        lo, hi = GROUPS[g]

        def run(i, carry):
            for p in range(NP):
                tile = raw[p, 0, :, pl.ds(pl.multiple_of((lo + i) * C, C), C)].astype(F32)
                ext[g][0, p, i] = jnp.transpose(tile).astype(BF16)
            return carry

        lax.fori_loop(0, hi - lo, run, 0)

    feat_load.wait()
    turn(0)
    pl.semaphore_wait(barrier, len(DIRECTIONS))

    pos_copies = []
    for n, (dx, dy) in enumerate(DIRECTIONS):
        if dx == 0:
            here, there = pl.ds(0, 2), pl.ds(0, 2)
        elif dx == 1:
            here, there = pl.ds(1, 1), pl.ds(3, 1)
        else:
            here, there = pl.ds(0, 1), pl.ds(2, 1)
        copy = pltpu.make_async_remote_copy(
            src_ref=posx.at[0, here],
            dst_ref=posx.at[PLACE[-dy], there],
            send_sem=pos_send.at[n],
            recv_sem=pos_recv.at[n],
            device_id=device(dx, dy),
            device_id_type=MESH,
        )
        copy.start()
        pos_copies.append(copy)

    halo = Halo(ext, f1_send, f1_recv, device, low_wrap, high_wrap)
    halo.own(0)
    for g in range(1, len(GROUPS)):
        turn(g)
        halo.own(g)

    atom = lax.broadcasted_iota(jnp.int32, (S, ROWS), 0).astype(F32)
    edges[...] = jnp.zeros_like(edges)
    places = []
    for p in range(NP):
        rows = [dst[k, p].astype(F32) for k in range(NE)]
        for k in range(NE):
            edges[0, pl.ds(k * NP + p, 1), :] = rows[k]
            edges[1, pl.ds(k * NP + p, 1), :] = shift[k, p].astype(F32)
        places.append(jnp.concatenate(rows, axis=1) - atom)

    def pick(y, carry):
        column = jnp.where(y == 0, 1, jnp.where(y == 1, 0, 2))
        for p in range(NP):
            for at, x in ((2 * y, 1), (2 * y + 1, 2), (6 + y, 3 * p)):
                hit = places[p] == ((3 * x + column) * S).astype(F32)
                rows = pl.ds(pl.multiple_of(at * S, S), S)
                oh[p, rows, :] = jnp.where(hit, 1.0, 0.0).astype(BF16)
        return carry

    lax.fori_loop(0, 3, pick, 0)

    def turned(w):
        high, low = split(w)
        rows = jnp.concatenate([high, low, high, jnp.zeros_like(w)], axis=0)
        return jnp.transpose(rows).astype(BF16)

    def widen(f, carry):
        wide[f] = turned(wr[:, pl.ds(pl.multiple_of(f * C, C), C)])
        return carry

    lax.fori_loop(0, 7, widen, 0)
    wide[8] = turned(wq[:, pl.ds(0, C)])
    last = turned(wq[:, pl.ds(C, C)])
    wide[7] = last
    wide[9] = last
    for i, w in enumerate((w_scalar, w_gate, w_vector, w_tensor)):
        w_turned[pl.ds(i * C, C), :] = jnp.transpose(w[...].astype(F32)).astype(BF16)

    for copy in pos_copies:
        copy.wait_recv()
    for p in range(NP):
        places = jnp.concatenate([posx[near_slot(p, j)] for j in range(9)], axis=1)
        first, rest = split(places)
        second, third = split(rest)
        parts = jnp.concatenate([first, second, third, jnp.zeros_like(first)], 0).astype(BF16)
        found = dot(parts, oh[p])
        far = (found[0:8] + found[8:16]) + found[16:24]
        for k in range(NE):
            pj[k * NP + p] = far[:, k * S : (k + 1) * S] - posx[0, p]

    place = edges[0]
    pj[pl.ds(KP, 8 - KP)] = jnp.zeros((8 - KP, 8, S), F32)
    own_p = lax.rem(lax.broadcasted_iota(jnp.int32, (8, S), 0), NP).astype(F32)
    one = jnp.ones_like(place)
    nil = jnp.zeros_like(place)

    def at_least(x, bound):
        return jnp.where(x >= float(bound), one, nil)

    ext_x = at_least(place, 3 * S) + at_least(place, 6 * S) + at_least(place, 9 * S)
    left = place - ext_x * float(3 * S)
    ext_y = at_least(left, S) + at_least(left, 2 * S)
    disp_x = pj[:, 0, :] + (ext_x - 1.0 - own_p)
    disp_y = pj[:, 1, :] + (ext_y - 1.0)
    disp_z = pj[:, 2, :] + edges[1]
    rho = jnp.sqrt(disp_x * disp_x + disp_y * disp_y + disp_z * disp_z + SOFTENING)
    inverse = 1.0 / rho
    u_x, u_y, u_z = disp_x * inverse, disp_y * inverse, disp_z * inverse
    geo[0] = u_x
    geo[1] = u_y
    geo[2] = u_z
    geo[3] = inverse
    length_sq = u_x * u_x + u_y * u_y + u_z * u_z
    angular = (
        u_x,
        u_y,
        u_z,
        ROOT_THREE * u_x * u_y,
        ROOT_THREE * u_y * u_z,
        0.5 * (3.0 * u_z * u_z - length_sq),
        ROOT_THREE * u_x * u_z,
        0.5 * ROOT_THREE * (u_x * u_x - u_y * u_y),
    )
    for f in range(8):
        for k in range(NE):
            for p in range(NP):
                ang[p, f, pl.ds(k, 1), :] = angular[f][k * NP + p : k * NP + p + 1]
    zf[...] = jnp.zeros_like(zf)
    for b in range(NB):
        off = (rho - (0.5 + SPACING * b)) / SPACING
        basis = jnp.exp(-(off * off))
        slope = basis * off * (-2.0 / SPACING)
        for i, value in enumerate((basis, slope)):
            high, low = split(value)
            zf[32 * i + b] = high
            zf[32 * i + 8 + b] = high
            zf[32 * i + 16 + b] = low

    def columns(k):
        return pl.ds(k * S, S)

    for p in range(NP):
        values = jnp.concatenate([zf[:, k * NP + p, :] for k in range(NE)], axis=1).astype(BF16)
        basis_rows, slope_rows = values[0:32], values[32:64]

        def expand(f, carry, p=p, rows=basis_rows):
            coef[f, p] = dot(wide[f], rows)
            return carry

        lax.fori_loop(0, 8, expand, 0)
        for f in (8, 9):
            coef[f, p] = dot(wide[f], slope_rows)

    def gather(bufs, g, lo, beyond):
        buf = bufs[g]
        n = buf.shape[2]

        def run(p, carry):
            if beyond:
                tiles = [buf[y, 3 - p].reshape(n * C, S) for y in range(3)]
                picks = oh[p, pl.ds(6 * S, 3 * S), :]
            else:
                tiles = [buf[y, slot].reshape(n * C, S) for y in range(3) for slot in range(2)]
                picks = oh[p, pl.ds(0, 6 * S), :]
            out = dot(jnp.concatenate(tiles, axis=1), picks)
            for i in range(n):
                term = out[i * C : (i + 1) * C]
                gsc[lo + i, p] = gsc[lo + i, p] + term if beyond else term
            return carry

        lax.fori_loop(0, NP, run, 0)

    def each_row(fn):
        steps = C // STEP

        def run(i, carry):
            p = i // steps
            fn(p, pl.ds(pl.multiple_of((i - p * steps) * STEP, STEP), STEP))
            return carry

        lax.fori_loop(0, NP * steps, run, 0)

    def angle(f, p, k):
        return ang[p, f, pl.ds(k, 1), :]

    def message_sv(p, r):
        total = [jnp.zeros((STEP, S), F32) for _ in range(BLOCKS)]
        for k in range(NE):
            e = columns(k)
            s = gsc[0, p, r, e]
            v = [gsc[1 + m, p, r, e] for m in range(3)]
            u = [angle(m, p, k) for m in range(3)]
            along = u[0] * v[0] + u[1] * v[1] + u[2] * v[2]
            total[0] = total[0] + coef[0, p, r, e] * s + coef[1, p, r, e] * along
            r3s = coef[3, p, r, e] * s
            r4 = coef[4, p, r, e]
            for m in range(3):
                total[1 + m] = total[1 + m] + r3s * u[m] + r4 * v[m]
            r5s = coef[5, p, r, e] * s
            for n in range(5):
                total[4 + n] = total[4 + n] + r5s * angle(3 + n, p, k)
        for b in range(BLOCKS):
            acc[b, p, r, :] = total[b]

    def message_t(lo, hi):
        def fn(p, r):
            total = [acc[b, p, r, :] for b in (0, *range(lo, hi))]
            for k in range(NE):
                e = columns(k)
                along = None
                r6 = coef[6, p, r, e]
                for n in range(lo, hi):
                    t = gsc[n, p, r, e]
                    term = angle(n - 1, p, k) * t
                    along = term if along is None else along + term
                    total[1 + n - lo] = total[1 + n - lo] + r6 * t
                total[0] = total[0] + coef[2, p, r, e] * along
            for i, b in enumerate((0, *range(lo, hi))):
                acc[b, p, r, :] = total[i]

        return fn

    third = 1.0 / NE

    def mix(lo, hi, w):
        def run(p, carry):
            terms = [(acc[b, p] * third).astype(BF16) for b in range(lo, hi)]
            out = dot(w_turned[pl.ds(w * C, C), :], jnp.concatenate(terms, axis=1))
            for b in range(lo, hi):
                acc[b, p] = out[:, (b - lo) * S : (b - lo + 1) * S]
            return carry

        lax.fori_loop(0, NP, run, 0)

    halo.near(0)
    gather(ext, 0, 0, False)
    halo.corners(0)
    halo.near(1)
    gather(ext, 1, 4, False)
    halo.near(2)
    gather(ext, 2, 7, False)
    halo.corners(1)
    halo.rest(0)
    gather(ext, 0, 0, True)
    each_row(message_sv)
    mix(1, 4, 2)
    halo.corners(2)
    halo.rest(1)
    gather(ext, 1, 4, True)
    each_row(message_t(4, 7))
    halo.rest(2)
    gather(ext, 2, 7, True)
    each_row(message_t(7, 9))

    def scalars(p, carry):
        out = dot(w_turned[pl.ds(0, 2 * C), :], (acc[0, p] * third).astype(BF16))
        pre = out[0:C]
        acc[0, p] = pre * jax.nn.sigmoid(pre)
        gate[p] = jax.nn.sigmoid(out[C : 2 * C])
        return carry

    lax.fori_loop(0, NP, scalars, 0)

    def update_sv(p, r):
        g = gate[p, r, :]
        for b in range(READ_BLOCKS):
            old = ext[0][0, p, b, r, :].astype(F32)
            step = g * acc[b, p, r, :] if b > 0 else acc[0, p, r, :]
            ext2[b // 2][0, p, b % 2, r, :] = (old + step).astype(BF16)

    each_row(update_sv)
    halo2 = Halo(ext2, f2_send, f2_recv, device, low_wrap, high_wrap)
    for g in range(len(GROUPS2)):
        halo2.own(g)

    mix(4, 9, 3)

    def results(lo, hi, value):
        def run(i, carry):
            for p in range(NP):
                at = pl.ds(pl.multiple_of((lo + i) * C, C), C)
                mix_out[p, 0, :, at] = jnp.transpose(value(p, i)).astype(BF16)
            return carry

        lax.fori_loop(0, hi - lo, run, 0)

    for g, (lo, hi) in enumerate(GROUPS2):
        results(lo, hi, lambda p, i: ext2[g][0, p, i].astype(F32))
    for g, (lo, hi) in enumerate(GROUPS):
        if g > 0:
            results(lo, hi, lambda p, i: ext[g][0, p, i].astype(F32) + gate[p] * acc[lo + i, p])
    write = pltpu.make_async_copy(mix_out, mixed, out_sem)
    write.start()

    def near_side(p, r):
        own = [ext2[b // 2][0, p, b % 2, r, :].astype(F32) for b in range(READ_BLOCKS)]
        for k in range(NE):
            e = columns(k)
            u = [angle(m, p, k) for m in range(3)]
            along = u[0] * own[1] + u[1] * own[2] + u[2] * own[3]
            q1 = coef[7, p, r, e]
            side[0, p, r, e] = coef[8, p, r, e] * own[0]
            side[1, p, r, e] = coef[9, p, r, e] * along
            side[2, p, r, e] = q1 * along
            for m in range(3):
                side[3 + m, p, r, e] = q1 * own[1 + m]

    halo2.near(0)
    gather(ext2, 0, 0, False)
    halo2.corners(0)
    each_row(near_side)
    halo2.near(1)
    gather(ext2, 1, 2, False)
    halo2.corners(1)
    halo.sent(range(len(GROUPS)))
    halo2.rest(0)
    gather(ext2, 0, 0, True)
    halo2.rest(1)
    gather(ext2, 1, 2, True)

    def pairs(p, outer):
        def pair(i, carry):
            r = pl.ds(pl.multiple_of(i * STEP, STEP), STEP)
            carry = list(carry)
            for k in range(NE):
                e = columns(k)
                far = [gsc[b, p, r, e] for b in range(READ_BLOCKS)]
                u = [angle(m, p, k) for m in range(3)]
                along = u[0] * far[1] + u[1] * far[2] + u[2] * far[3]
                carry[4 * k] = carry[4 * k] + side[0, p, r, e] * far[0] + side[1, p, r, e] * along
                own_q = side[2, p, r, e]
                for m in range(3):
                    term = side[3 + m, p, r, e] * along + own_q * far[1 + m]
                    carry[4 * k + 1 + m] = carry[4 * k + 1 + m] + term
            return tuple(carry)

        zero = jnp.zeros((STEP, S), F32)
        totals = lax.fori_loop(0, C // STEP, pair, (zero,) * (4 * NE))
        for k in range(NE):
            for q in range(4):
                row = jnp.sum(totals[4 * k + q], axis=0, keepdims=True)
                by_pillar[p, pl.ds(4 * k + q, 1), :] = row
        return outer

    lax.fori_loop(0, NP, pairs, 0)
    sums[...] = jnp.zeros_like(sums)
    for p in range(NP):
        for k in range(NE):
            for q in range(4):
                sums[q, pl.ds(k * NP + p, 1), :] = by_pillar[p, pl.ds(4 * k + q, 1), :]

    t_rho, g_x, g_y, g_z = (sums[q] for q in range(4))
    u_x, u_y, u_z, inverse = (geo[i] for i in range(4))
    radial_part = t_rho - (u_x * g_x + u_y * g_y + u_z * g_z) * inverse
    grad[...] = jnp.zeros_like(grad)
    grad[0] = radial_part * u_x + g_x * inverse
    grad[1] = radial_part * u_y + g_y * inverse
    grad[2] = radial_part * u_z + g_z * inverse

    parts = []
    for p in range(NP):
        terms = jnp.concatenate([grad[:, k * NP + p, :] for k in range(NE)], axis=1)
        first, rest = split(terms)
        second, third_part = split(rest)
        parts.append(
            jnp.concatenate([first, second, third_part, jnp.zeros_like(first)], 0).astype(BF16)
        )

    def scatter(lo, hi):
        seen = {}
        for p in range(NP):
            out = dot(parts[p], oh[p, pl.ds(lo * S, (hi - lo) * S), :], (1, 1))
            out = (out[0:8] + out[8:16]) + out[16:24]
            for j in range(lo, hi):
                term = out[:, (j - lo) * S : (j - lo + 1) * S]
                at = near_slot(p, j)
                seen[at] = seen[at] - term if at in seen else -term
        for at, value in seen.items():
            extf[at] = value

    scatter(2, 9)
    force_copies = []
    for n, (dx, dy) in enumerate(DIRECTIONS):
        if dx == 0:
            here, there = pl.ds(0, 2), pl.ds(0, 2)
        elif dx == 1:
            here, there = pl.ds(2, 1), pl.ds(0, 1)
        else:
            here, there = pl.ds(3, 1), pl.ds(1, 1)
        copy = pltpu.make_async_remote_copy(
            src_ref=extf.at[PLACE[dy], here],
            dst_ref=frecv.at[n, there],
            send_sem=fo_send.at[n],
            recv_sem=fo_recv.at[n],
            device_id=device(dx, dy),
            device_id_type=MESH,
        )
        copy.start()
        force_copies.append(copy)

    scatter(0, 2)
    total = []
    for p in range(NP):
        mine = extf[0, p]
        for k in range(NE):
            mine = mine + grad[:, k * NP + p, :]
        total.append(mine)
    for n, (dx, dy) in enumerate(DIRECTIONS):
        force_copies[n].wait_recv()
        for p in range(NP):
            if dx == 0 or (dx == 1) == (p == 0):
                total[p] = total[p] + frecv[n, p]
    for p in range(NP):
        for m in range(3):
            forces[p, m] = total[p][m : m + 1]

    for copy in (*pos_copies, *force_copies):
        copy.wait_send()
    halo2.sent(range(len(GROUPS2)))
    write.wait()


def solution(mesh):
    gx_size, yz_size = mesh.shape["gx"], mesh.shape["yz"]

    def body(features, positions, *rest):
        args = (features, jnp.transpose(positions, (0, 2, 1, 3)), *rest)
        vmem = pl.BlockSpec(memory_space=pltpu.VMEM)
        anywhere = pl.BlockSpec(memory_space=pl.ANY)
        dma = pltpu.SemaphoreType.DMA
        n_dir = len(DIRECTIONS)

        def run_all(*refs):
            kernel(gx_size, yz_size, *refs)

        small = [pltpu.VMEM(x.shape, x.dtype) for x in args[1:]]
        new_features, force = pl.pallas_call(
            run_all,
            out_shape=(
                jax.ShapeDtypeStruct((NP, 1, S, BLOCKS * C), BF16),
                jax.ShapeDtypeStruct((NP, 3, 1, S), F32),
            ),
            in_specs=[pl.BlockSpec(memory_space=pltpu.HBM)] * 10,
            out_specs=(anywhere, vmem),
            scratch_shapes=small
            + [
                *[pltpu.VMEM((3, 4, hi - lo, S, C), BF16) for lo, hi in GROUPS + GROUPS2],
                pltpu.VMEM((3, 4, 8, S), F32),
                pltpu.VMEM((NP, NEAR, ROWS), BF16),
                pltpu.VMEM((10, NP, C, ROWS), F32),
                pltpu.VMEM((10, C, 32), BF16),
                pltpu.VMEM((4 * C, C), BF16),
                pltpu.VMEM((64, 8, S), F32),
                pltpu.VMEM((NP, 8, NE, S), F32),
                pltpu.VMEM((8, 8, S), F32),
                pltpu.VMEM((4, 8, S), F32),
                pltpu.VMEM((2, 8, S), F32),
                pltpu.VMEM((BLOCKS, NP, C, S), F32),
                pltpu.VMEM((NP, C, S), F32),
                pltpu.VMEM((BLOCKS, NP, C, ROWS), F32),
                pltpu.VMEM((NP, 1, S, BLOCKS * C), BF16),
                pltpu.VMEM((NP, 1, S, BLOCKS * C), BF16),
                pltpu.VMEM((6, NP, C, ROWS), F32),
                pltpu.VMEM((NP, 4 * NE, S), F32),
                pltpu.VMEM((4, 8, S), F32),
                pltpu.VMEM((8, 8, S), F32),
                pltpu.VMEM((3, 4, 8, S), F32),
                pltpu.VMEM((n_dir, NP, 8, S), F32),
                dma((len(small),)),
                dma,
                dma,
                dma((n_dir,)),
                dma((n_dir,)),
                dma((len(GROUPS), Halo.COUNT)),
                dma((len(GROUPS), Halo.COUNT)),
                dma((len(GROUPS2), Halo.COUNT)),
                dma((len(GROUPS2), Halo.COUNT)),
                dma((n_dir,)),
                dma((n_dir,)),
            ],
            compiler_params=pltpu.CompilerParams(
                collective_id=0, has_side_effects=True, vmem_limit_bytes=60 * 1024 * 1024
            ),
            cost_estimate=pl.CostEstimate(
                flops=4 * 10**9, bytes_accessed=2 * 10**6, transcendentals=10**5
            ),
        )(*args)
        return new_features, jnp.transpose(force, (0, 2, 1, 3))

    in_specs = (
        P("gx", "yz", None, None),
        P("gx", "yz", None, None),
        P(None, "gx", "yz", None),
        P(None, "gx", "yz", None),
        P(),
        P(),
        P(),
        P(),
        P(),
        P(),
    )
    out_specs = (P("gx", "yz", None, None), P("gx", "yz", None, None))
    return jax.shard_map(body, mesh=mesh, in_specs=in_specs, out_specs=out_specs, check_vma=False)
```

```python
import math

import jax
import jax.numpy as jnp
from jax import lax
from jax.experimental import pallas as pl
from jax.experimental.pallas import tpu as pltpu
from jax.sharding import PartitionSpec as P

MESH = pl.DeviceIdType.MESH
F32 = jnp.float32
BF16 = jnp.bfloat16
SOFTENING = 0.25
SPACING = 0.6
ROOT_THREE = math.sqrt(3.0)
C = 128
S = 128
NB = 8
NE = 3
NP = 2
BLOCKS = 9
READ_BLOCKS = 4
ROWS = NE * S
NEAR = 9 * S
STEP = 16
GROUPS = ((0, 4), (4, 7), (7, 8), (8, 9))
GROUPS2 = ((0, 2), (2, 3), (3, 4))
PILLARS = {
    0: (1, 0),
    1: (1, 1),
    2: (2, 0),
    3: (2, 1),
    4: (0, 2),
    5: (0, 3),
    8: (0, 0),
    9: (0, 1),
    10: (1, 2),
    11: (1, 3),
    12: (2, 2),
    13: (2, 3),
}
OWN = 8
COUNT = 14
EDGE_ROWS = 48
DIRECTIONS = tuple((dx, dy) for dx in (-1, 0, 1) for dy in (-1, 0, 1) if (dx, dy) != (0, 0))


def split(x):
    high = x.astype(BF16).astype(F32)
    return high, x - high


def dot(a, b, contract=(1, 0)):
    dims = (((contract[0],), (contract[1],)), ((), ()))
    return lax.dot_general(a, b, dims, preferred_element_type=F32)


PLACE = {0: 0, -1: 1, 1: 2}


def near_slot(p, j):
    return (j // 2, j % 2) if j < 6 else (j - 6, 3 - p)


def near_pillar(p, j):
    y, slot = near_slot(p, j)
    return (1, 2, 3, 0)[slot], (1, 0, 2)[y]


def block(bufs, c, *at):
    for buf in bufs:
        if c < buf.shape[2]:
            return buf.at[(*at, c)]
        c -= buf.shape[2]


class Halo:
    COUNT = 10

    def __init__(self, bufs, send, recv, device, low_wrap, high_wrap):
        self.copies = {}
        self.low_wrap, self.high_wrap = low_wrap, high_wrap
        own, ghosts = pl.ds(0, 2), pl.ds(2, 2)
        for g, buf in enumerate(bufs):
            spans = {
                "x0": (buf.at[0, 0], buf.at[0, 2], (-1, 0)),
                "x1": (buf.at[0, 1], buf.at[0, 3], (1, 0)),
            }
            for sign, step, to in (("m", -1, 2), ("p", 1, 1)):
                spans |= {
                    "y" + sign: (buf.at[0, own], buf.at[to, own], (0, step)),
                    "c" + sign: (buf.at[0, ghosts], buf.at[to, ghosts], (0, step)),
                    "w0" + sign: (buf.at[0, 0], buf.at[to, 2], (-1, step)),
                    "w1" + sign: (buf.at[0, 1], buf.at[to, 3], (1, step)),
                }
            for n, (name, (src, dst, step)) in enumerate(spans.items()):
                self.copies[name, g] = pltpu.make_async_remote_copy(
                    src_ref=src,
                    dst_ref=dst,
                    send_sem=send.at[g, n],
                    recv_sem=recv.at[g, n],
                    device_id=device(*step),
                    device_id_type=MESH,
                )

    def start(self, g, *names):
        for name in names:
            self.copies[name, g].start()

    def arrived(self, g, *names):
        for name in names:
            self.copies[name, g].wait_recv()

    def sends(self, sign, plain, wrap):
        wraps = self.low_wrap if sign == "m" else self.high_wrap
        if wrap is not None:
            pl.when(wraps)(wrap)
        if plain is not None:
            pl.when(jnp.logical_not(wraps))(plain)

    def own(self, g):
        self.start(g, "x0", "x1", "ym", "yp")
        for sign in "mp":
            self.sends(sign, None, lambda: self.start(g, "w0" + sign, "w1" + sign))

    def near(self, g):
        self.arrived(g, "ym", "yp")

    def corners(self, g):
        self.arrived(g, "x0", "x1")
        for sign in "mp":
            self.sends(sign, lambda: self.start(g, "c" + sign), None)

    def rest(self, g):
        for sign, wraps in (("m", self.high_wrap), ("p", self.low_wrap)):
            pl.when(wraps)(lambda: self.arrived(g, "w0" + sign, "w1" + sign))
            pl.when(jnp.logical_not(wraps))(lambda: self.arrived(g, "c" + sign))

    def sent(self, groups):
        def done(*names):
            for g in groups:
                for name in names:
                    self.copies[name, g].wait_send()

        done("x0", "x1", "ym", "yp")
        for sign in "mp":
            self.sends(sign, lambda: done("c" + sign), lambda: done("w0" + sign, "w1" + sign))


def kernel(
    gx_size,
    yz_size,
    feat,
    *refs,
):
    small_in, refs = refs[:9], refs[9:]
    mixed, forces, *refs = refs
    small, refs = refs[:9], refs[9:]
    run(gx_size, yz_size, feat, small_in, small, mixed, forces, *refs)


def run(
    gx_size,
    yz_size,
    feat,
    small_in,
    small,
    mixed,
    forces,
    ext0,
    ext1,
    ext2,
    ext3,
    mix0,
    mix1,
    mix2,
    posx,
    oh,
    oh_own,
    coef,
    readout,
    wide,
    w_turned,
    zf,
    ang,
    pj,
    inverses,
    target,
    edges,
    acc,
    gate,
    gsc,
    ends,
    raw,
    mix_out,
    side,
    sums,
    grad,
    small_sem,
    load_sem,
    out_sem,
    pos_send,
    pos_recv,
    f1_send,
    f1_recv,
    f2_send,
    f2_recv,
):
    ext, ext2 = (ext0, ext1, ext2, ext3), (mix0, mix1, mix2)
    gx = lax.axis_index("gx")
    yz = lax.axis_index("yz")

    half = yz_size // 2
    low_wrap = lax.rem(yz, half) == 0
    high_wrap = lax.rem(yz, half) == half - 1

    def device(dx, dy):
        return (lax.rem(gx + dx + gx_size, gx_size), lax.rem(yz + dy + yz_size, yz_size))

    small_loads = [
        pltpu.make_async_copy(small_in[i], small[i], small_sem.at[i]) for i in range(len(small))
    ]
    for load in small_loads:
        load.start()
    pos, dst, shift, wr, wq, w_scalar, w_gate, w_vector, w_tensor = small
    feat_load = pltpu.make_async_copy(feat, raw, load_sem)
    feat_load.start()

    barrier = pltpu.get_barrier_semaphore()
    for step in DIRECTIONS:
        pl.semaphore_signal(barrier, inc=1, device_id=device(*step), device_id_type=MESH)

    for load in small_loads:
        load.wait()
    for p in range(NP):
        posx[0, p] = jnp.zeros((16, S), F32)
        for m in range(3):
            posx[0, p, pl.ds(m, 1), :] = pos[p, m]
        for k in range(NE):
            posx[0, p, pl.ds(3 + k, 1), :] = dst[k, p].astype(F32)
            posx[0, p, pl.ds(6 + k, 1), :] = shift[k, p].astype(F32)

    def turn(g):
        lo, hi = GROUPS[g]

        def run(i, carry):
            for p in range(NP):
                tile = raw[p, 0, :, pl.ds(pl.multiple_of((lo + i) * C, C), C)].astype(F32)
                ext[g][0, p, i] = jnp.transpose(tile).astype(BF16)
            return carry

        lax.fori_loop(0, hi - lo, run, 0)

    feat_load.wait()
    turn(0)
    pl.semaphore_wait(barrier, len(DIRECTIONS))

    pos_copies = []
    for n, (dx, dy) in enumerate(DIRECTIONS):
        if dx == 0:
            here, there = pl.ds(0, 2), pl.ds(0, 2)
        elif dx == 1:
            here, there = pl.ds(1, 1), pl.ds(3, 1)
        else:
            here, there = pl.ds(0, 1), pl.ds(2, 1)
        copy = pltpu.make_async_remote_copy(
            src_ref=posx.at[0, here],
            dst_ref=posx.at[PLACE[-dy], there],
            send_sem=pos_send.at[n],
            recv_sem=pos_recv.at[n],
            device_id=device(dx, dy),
            device_id_type=MESH,
        )
        copy.start()
        pos_copies.append(copy)

    halo = Halo(ext, f1_send, f1_recv, device, low_wrap, high_wrap)
    halo.own(0)
    for g in range(1, len(GROUPS)):
        turn(g)
        halo.own(g)

    atom = lax.broadcasted_iota(jnp.int32, (S, ROWS), 0).astype(F32)
    places = []
    for p in range(NP):
        rows = [posx[0, p, pl.ds(3 + k, 1), :] for k in range(NE)]
        places.append(jnp.concatenate(rows, axis=1) - atom)

    def pick(y, carry):
        column = jnp.where(y == 0, 1, jnp.where(y == 1, 0, 2))
        for p in range(NP):
            for at, x in ((2 * y, 1), (2 * y + 1, 2), (6 + y, 3 * p)):
                hit = places[p] == ((3 * x + column) * S).astype(F32)
                rows = pl.ds(pl.multiple_of(at * S, S), S)
                oh[p, rows, :] = jnp.where(hit, 1.0, 0.0).astype(BF16)
        return carry

    lax.fori_loop(0, 3, pick, 0)

    def turned(w):
        high, low = split(w)
        rows = jnp.concatenate([high, low, high, jnp.zeros_like(w)], axis=0)
        return jnp.transpose(rows).astype(BF16)

    def widen(f, carry):
        wide[f] = turned(wr[:, pl.ds(pl.multiple_of(f * C, C), C)])
        return carry

    lax.fori_loop(0, 7, widen, 0)
    wide[8] = turned(wq[:, pl.ds(0, C)])
    last = turned(wq[:, pl.ds(C, C)])
    wide[7] = last
    wide[9] = last
    for i, w in enumerate((w_scalar, w_gate, w_vector, w_tensor)):
        w_turned[pl.ds(i * C, C), :] = jnp.transpose(w[...].astype(F32)).astype(BF16)

    for copy in pos_copies:
        copy.wait_recv()
    edges[...] = jnp.zeros_like(edges)
    for q, (y, slot) in PILLARS.items():
        at = pl.ds(NE * q, NE)
        edges[0, at, :] = posx[y, slot, pl.ds(3, NE), :]
        edges[1, at, :] = posx[y, slot, pl.ds(6, NE), :]
        for i, value in ((2, slot % NP), (3, (1, 2, 3, 0)[slot]), (4, (1, 0, 2)[y])):
            edges[i, at, :] = jnp.full((NE, S), value, F32)
    place = edges[0]
    one = jnp.ones_like(place)
    nil = jnp.zeros_like(place)

    def at_least(x, bound):
        return jnp.where(x >= float(bound), one, nil)

    ext_x = at_least(place, 3 * S) + at_least(place, 6 * S) + at_least(place, 9 * S)
    left = place - ext_x * float(3 * S)
    ext_y = at_least(left, S) + at_least(left, 2 * S)
    step_x = ext_x - 1.0 - edges[2]
    step_y = ext_y - 1.0
    to_x = edges[3] + step_x - 1.0
    mine = (edges[4] + step_y == 1.0) & (to_x >= 0.0) & (to_x <= 1.0)
    target[...] = jnp.where(mine, to_x * S + (left - ext_y * S), -1.0)

    atom = lax.broadcasted_iota(jnp.int32, (NP * S, ROWS), 0).astype(F32)

    def own_pick(q, carry):
        rows = [target[pl.ds(NE * q + k, 1), :] for k in range(NE)]
        hit = jnp.concatenate(rows, axis=1) == atom
        oh_own[:, pl.ds(pl.multiple_of(q * ROWS, ROWS), ROWS)] = jnp.where(hit, 1.0, 0.0).astype(BF16)
        return carry

    lax.fori_loop(0, 6, own_pick, 0)
    lax.fori_loop(OWN, COUNT, own_pick, 0)

    def in_parts(x):
        first, rest = split(x)
        second, third = split(rest)
        return jnp.concatenate([first, second, third, jnp.zeros_like(first)], 0).astype(BF16)

    def whole(x):
        return (x[0:8] + x[8:16]) + x[16:24]

    pj[...] = jnp.zeros_like(pj)
    own_parts = in_parts(jnp.concatenate([posx[0, p, pl.ds(0, 8), :] for p in range(NP)], axis=1))
    for q, (y, slot) in PILLARS.items():
        if q in (OWN, OWN + 1):
            near = [near_slot(slot, j) for j in range(9)]
            parts = in_parts(jnp.concatenate([posx[b, a, pl.ds(0, 8), :] for b, a in near], axis=1))
            far = whole(dot(parts, oh[slot]))
        else:
            far = whole(dot(own_parts, oh_own[:, pl.ds(q * ROWS, ROWS)]))
        for k in range(NE):
            pj[NE * q + k] = far[:, k * S : (k + 1) * S] - posx[y, slot, pl.ds(0, 8), :]

    disp_x = pj[:, 0, :] + step_x
    disp_y = pj[:, 1, :] + step_y
    disp_z = pj[:, 2, :] + edges[1]
    rho = jnp.sqrt(disp_x * disp_x + disp_y * disp_y + disp_z * disp_z + SOFTENING)
    inverse = 1.0 / rho
    u_x, u_y, u_z = disp_x * inverse, disp_y * inverse, disp_z * inverse
    inverses[...] = inverse
    length_sq = u_x * u_x + u_y * u_y + u_z * u_z
    angular = (
        u_x,
        u_y,
        u_z,
        ROOT_THREE * u_x * u_y,
        ROOT_THREE * u_y * u_z,
        0.5 * (3.0 * u_z * u_z - length_sq),
        ROOT_THREE * u_x * u_z,
        0.5 * ROOT_THREE * (u_x * u_x - u_y * u_y),
    )
    for f in range(8):
        ang[f] = angular[f]
    zf[...] = jnp.zeros_like(zf)
    for b in range(NB):
        off = (rho - (0.5 + SPACING * b)) / SPACING
        basis = jnp.exp(-(off * off))
        slope = basis * off * (-2.0 / SPACING)
        for i, value in enumerate((basis, slope)):
            high, low = split(value)
            zf[32 * i + b] = high
            zf[32 * i + 8 + b] = high
            zf[32 * i + 16 + b] = low

    def columns(k):
        return pl.ds(k * S, S)

    for q in PILLARS:
        values = jnp.concatenate([zf[:, NE * q + k, :] for k in range(NE)], axis=1).astype(BF16)
        basis_rows, slope_rows = values[0:32], values[32:64]
        if q in (OWN, OWN + 1):

            def expand(f, carry, p=q - OWN, rows=basis_rows):
                coef[f, p] = dot(wide[f], rows)
                return carry

            lax.fori_loop(0, 7, expand, 0)
        readout[q, 0] = dot(wide[7], basis_rows)
        readout[q, 1] = dot(wide[8], slope_rows)
        readout[q, 2] = dot(wide[9], slope_rows)

    def gather(bufs, g, lo, beyond):
        buf = bufs[g]
        n = buf.shape[2]

        def run(p, carry):
            if beyond:
                tiles = [buf[y, 3 - p].reshape(n * C, S) for y in range(3)]
                picks = oh[p, pl.ds(6 * S, 3 * S), :]
            else:
                tiles = [buf[y, slot].reshape(n * C, S) for y in range(3) for slot in range(2)]
                picks = oh[p, pl.ds(0, 6 * S), :]
            out = dot(jnp.concatenate(tiles, axis=1), picks)
            for i in range(n):
                term = out[i * C : (i + 1) * C]
                gsc[lo + i, p] = gsc[lo + i, p] + term if beyond else term
            return carry

        lax.fori_loop(0, NP, run, 0)

    def each_row(fn):
        steps = C // STEP

        def run(i, carry):
            p = i // steps
            fn(p, pl.ds(pl.multiple_of((i - p * steps) * STEP, STEP), STEP))
            return carry

        lax.fori_loop(0, NP * steps, run, 0)

    def angle(f, q, k):
        return ang[f, pl.ds(NE * q + k, 1), :]

    def message_sv(p, r):
        total = [jnp.zeros((STEP, S), F32) for _ in range(BLOCKS)]
        for k in range(NE):
            e = columns(k)
            s = gsc[0, p, r, e]
            v = [gsc[1 + m, p, r, e] for m in range(3)]
            u = [angle(m, OWN + p, k) for m in range(3)]
            along = u[0] * v[0] + u[1] * v[1] + u[2] * v[2]
            total[0] = total[0] + coef[0, p, r, e] * s + coef[1, p, r, e] * along
            r3s = coef[3, p, r, e] * s
            r4 = coef[4, p, r, e]
            for m in range(3):
                total[1 + m] = total[1 + m] + r3s * u[m] + r4 * v[m]
            r5s = coef[5, p, r, e] * s
            for n in range(5):
                total[4 + n] = total[4 + n] + r5s * angle(3 + n, OWN + p, k)
        for b in range(BLOCKS):
            acc[b, p, r, :] = total[b]

    def message_t(lo, hi):
        def fn(p, r):
            total = [acc[b, p, r, :] for b in (0, *range(lo, hi))]
            for k in range(NE):
                e = columns(k)
                along = None
                r6 = coef[6, p, r, e]
                for n in range(lo, hi):
                    t = gsc[n, p, r, e]
                    term = angle(n - 1, OWN + p, k) * t
                    along = term if along is None else along + term
                    total[1 + n - lo] = total[1 + n - lo] + r6 * t
                total[0] = total[0] + coef[2, p, r, e] * along
            for i, b in enumerate((0, *range(lo, hi))):
                acc[b, p, r, :] = total[i]

        return fn

    third = 1.0 / NE

    def mix(lo, hi, w):
        def run(p, carry):
            terms = [(acc[b, p] * third).astype(BF16) for b in range(lo, hi)]
            out = dot(w_turned[pl.ds(w * C, C), :], jnp.concatenate(terms, axis=1))
            for b in range(lo, hi):
                acc[b, p] = out[:, (b - lo) * S : (b - lo + 1) * S]
            return carry

        lax.fori_loop(0, NP, run, 0)

    halo.near(0)
    gather(ext, 0, 0, False)
    halo.corners(0)
    for g in range(1, len(GROUPS)):
        halo.near(g)
        gather(ext, g, GROUPS[g][0], False)
    halo.corners(1)
    halo.rest(0)
    gather(ext, 0, 0, True)
    each_row(message_sv)
    mix(1, 4, 2)
    halo.corners(2)
    halo.rest(1)
    gather(ext, 1, 4, True)
    each_row(message_t(4, 7))
    halo.corners(3)
    halo.rest(2)
    gather(ext, 2, 7, True)
    each_row(message_t(7, 8))
    halo.rest(3)
    gather(ext, 3, 8, True)
    each_row(message_t(8, 9))

    def scalars(p, carry):
        out = dot(w_turned[pl.ds(0, 2 * C), :], (acc[0, p] * third).astype(BF16))
        pre = out[0:C]
        acc[0, p] = pre * jax.nn.sigmoid(pre)
        gate[p] = jax.nn.sigmoid(out[C : 2 * C])
        return carry

    lax.fori_loop(0, NP, scalars, 0)

    def read_block(b, y, slot):
        g = (0, 0, 1, 2)[b]
        return ext2[g].at[y, slot, b - GROUPS2[g][0]]

    def update_sv(p, r):
        g = gate[p, r, :]
        for b in range(READ_BLOCKS):
            old = ext[0][0, p, b, r, :].astype(F32)
            step = g * acc[b, p, r, :] if b > 0 else acc[0, p, r, :]
            read_block(b, 0, p)[r, :] = (old + step).astype(BF16)

    each_row(update_sv)
    halo2 = Halo(ext2, f2_send, f2_recv, device, low_wrap, high_wrap)
    for g in range(len(GROUPS2)):
        halo2.own(g)

    mix(4, 9, 3)

    def results(lo, hi, value):
        def run(i, carry):
            for p in range(NP):
                at = pl.ds(pl.multiple_of((lo + i) * C, C), C)
                mix_out[p, 0, :, at] = jnp.transpose(value(p, i)).astype(BF16)
            return carry

        lax.fori_loop(0, hi - lo, run, 0)

    for g, (lo, hi) in enumerate(GROUPS2):
        results(lo, hi, lambda p, i: ext2[g][0, p, i].astype(F32))
    for g, (lo, hi) in enumerate(GROUPS):
        if g > 0:
            results(lo, hi, lambda p, i: ext[g][0, p, i].astype(F32) + gate[p] * acc[lo + i, p])
    write = pltpu.make_async_copy(mix_out, mixed, out_sem)
    write.start()

    def near_side(q, r, end):
        for k in range(NE):
            e = columns(k)
            s, v = end(k)
            u = [angle(m, q, k) for m in range(3)]
            along = u[0] * v[0] + u[1] * v[1] + u[2] * v[2]
            q1 = readout[q, 0, r, e]
            side[q, 0, r, e] = readout[q, 1, r, e] * s
            side[q, 1, r, e] = readout[q, 2, r, e] * along
            side[q, 2, r, e] = q1 * along
            for m in range(3):
                side[q, 3 + m, r, e] = q1 * v[m]

    def own_side(p, r):
        own = [read_block(b, 0, p)[r, :].astype(F32) for b in range(READ_BLOCKS)]
        near_side(OWN + p, r, lambda k: (own[0], own[1:]))

    def ghost_sides(lo, hi):
        def run(q, carry):
            tiles = []
            for p in range(NP):
                parts = [ext2[g][0, p].reshape((b - a) * C, S) for g, (a, b) in enumerate(GROUPS2)]
                tiles.append(jnp.concatenate(parts, axis=0))
            picks = oh_own[:, pl.ds(pl.multiple_of(q * ROWS, ROWS), ROWS)]
            ends[...] = dot(jnp.concatenate(tiles, axis=1), picks)

            def rows(i, inner):
                at = pl.multiple_of(i * STEP, STEP)

                def end(k):
                    far = [ends[pl.ds(b * C + at, STEP), columns(k)] for b in range(READ_BLOCKS)]
                    return far[0], far[1:]

                near_side(q, pl.ds(at, STEP), end)
                return inner

            lax.fori_loop(0, C // STEP, rows, 0)
            return carry

        lax.fori_loop(lo, hi, run, 0)

    def pairs(lo, hi, far_rows):
        def run(q, outer):
            def pair(i, carry):
                r = pl.ds(pl.multiple_of(i * STEP, STEP), STEP)
                carry = list(carry)
                get = far_rows(q, r)
                for k in range(NE):
                    e = columns(k)
                    far = get(k)
                    u = [angle(m, q, k) for m in range(3)]
                    along = u[0] * far[1] + u[1] * far[2] + u[2] * far[3]
                    carry[4 * k] = carry[4 * k] + side[q, 0, r, e] * far[0] + side[q, 1, r, e] * along
                    own_q = side[q, 2, r, e]
                    for m in range(3):
                        term = side[q, 3 + m, r, e] * along + own_q * far[1 + m]
                        carry[4 * k + 1 + m] = carry[4 * k + 1 + m] + term
                return tuple(carry)

            zero = jnp.zeros((STEP, S), F32)
            totals = lax.fori_loop(0, C // STEP, pair, (zero,) * (4 * NE))
            for k in range(NE):
                for i in range(4):
                    row = jnp.sum(totals[4 * k + i], axis=0, keepdims=True)
                    sums[i, pl.ds(NE * q + k, 1), :] = row
            return outer

        lax.fori_loop(lo, hi, run, 0)

    def own_far(q, r):
        return lambda k: [gsc[b, q - OWN, r, columns(k)] for b in range(READ_BLOCKS)]

    def ghost_far(place_of):
        def rows(q, r):
            y, slot = place_of(q)
            far = [read_block(b, y, slot)[r, :].astype(F32) for b in range(READ_BLOCKS)]
            return lambda k: far

        return rows

    def gradient(lo, hi):
        rows = pl.ds(lo, hi - lo)
        t_rho, g_x, g_y, g_z = (sums[i, rows, :] for i in range(4))
        u_x, u_y, u_z, inverse = ang[0, rows, :], ang[1, rows, :], ang[2, rows, :], inverses[rows, :]
        radial_part = t_rho - (u_x * g_x + u_y * g_y + u_z * g_z) * inverse
        grad[0, rows, :] = radial_part * u_x + g_x * inverse
        grad[1, rows, :] = radial_part * u_y + g_y * inverse
        grad[2, rows, :] = radial_part * u_z + g_z * inverse
        used = [NE * q + k for q in PILLARS for k in range(NE) if lo <= NE * q < hi]
        parts = in_parts(jnp.concatenate([grad[:, row, :] for row in used], axis=1))
        at = pl.ds(used[0] * S, len(used) * S)
        return whole(dot(parts, oh_own[:, at], (1, 1)))

    sums[...] = jnp.zeros_like(sums)
    grad[...] = jnp.zeros_like(grad)
    each_row(own_side)
    for g, (lo, hi) in enumerate(GROUPS2):
        halo2.near(g)
        gather(ext2, g, lo, False)
    halo2.corners(0)
    ghost_sides(0, 4)
    pairs(0, 4, ghost_far(lambda q: (1 + q // 2, q % 2)))
    halo2.corners(1)
    halo2.corners(2)
    ghost_sides(4, 6)
    pairs(4, 6, ghost_far(lambda q: (0, q - 2)))
    ghost_sides(10, 14)
    early = gradient(0, 24)
    halo.sent(range(len(GROUPS)))
    for g, (lo, hi) in enumerate(GROUPS2):
        halo2.rest(g)
        gather(ext2, g, lo, True)
    pairs(OWN, OWN + 2, own_far)
    pairs(10, 14, ghost_far(lambda q: (q // 2 - 4, 2 + q % 2)))
    back = early + gradient(24, EDGE_ROWS)
    for p in range(NP):
        total = -back[:, p * S : (p + 1) * S]
        for k in range(NE):
            total = total + grad[:, NE * (OWN + p) + k, :]
        for m in range(3):
            forces[p, m] = total[m : m + 1]

    for copy in pos_copies:
        copy.wait_send()
    halo2.sent(range(len(GROUPS2)))
    write.wait()


def solution(mesh):
    gx_size, yz_size = mesh.shape["gx"], mesh.shape["yz"]

    def body(features, positions, *rest):
        args = (features, jnp.transpose(positions, (0, 2, 1, 3)), *rest)
        vmem = pl.BlockSpec(memory_space=pltpu.VMEM)
        anywhere = pl.BlockSpec(memory_space=pl.ANY)
        dma = pltpu.SemaphoreType.DMA
        n_dir = len(DIRECTIONS)

        def run_all(*refs):
            kernel(gx_size, yz_size, *refs)

        small = [pltpu.VMEM(x.shape, x.dtype) for x in args[1:]]
        new_features, force = pl.pallas_call(
            run_all,
            out_shape=(
                jax.ShapeDtypeStruct((NP, 1, S, BLOCKS * C), BF16),
                jax.ShapeDtypeStruct((NP, 3, 1, S), F32),
            ),
            in_specs=[pl.BlockSpec(memory_space=pltpu.HBM)] * 10,
            out_specs=(anywhere, vmem),
            scratch_shapes=small
            + [
                *[pltpu.VMEM((3, 4, hi - lo, S, C), BF16) for lo, hi in GROUPS + GROUPS2],
                pltpu.VMEM((3, 4, 16, S), F32),
                pltpu.VMEM((NP, NEAR, ROWS), BF16),
                pltpu.VMEM((NP * S, COUNT * ROWS), BF16),
                pltpu.VMEM((7, NP, C, ROWS), F32),
                pltpu.VMEM((COUNT, 3, C, ROWS), F32),
                pltpu.VMEM((10, C, 32), BF16),
                pltpu.VMEM((4 * C, C), BF16),
                pltpu.VMEM((64, EDGE_ROWS, S), F32),
                pltpu.VMEM((8, EDGE_ROWS, S), F32),
                pltpu.VMEM((EDGE_ROWS, 8, S), F32),
                pltpu.VMEM((EDGE_ROWS, S), F32),
                pltpu.VMEM((EDGE_ROWS, S), F32),
                pltpu.VMEM((5, EDGE_ROWS, S), F32),
                pltpu.VMEM((BLOCKS, NP, C, S), F32),
                pltpu.VMEM((NP, C, S), F32),
                pltpu.VMEM((BLOCKS, NP, C, ROWS), F32),
                pltpu.VMEM((READ_BLOCKS * C, ROWS), F32),
                pltpu.VMEM((NP, 1, S, BLOCKS * C), BF16),
                pltpu.VMEM((NP, 1, S, BLOCKS * C), BF16),
                pltpu.VMEM((COUNT, 6, C, ROWS), F32),
                pltpu.VMEM((4, EDGE_ROWS, S), F32),
                pltpu.VMEM((8, EDGE_ROWS, S), F32),
                dma((len(small),)),
                dma,
                dma,
                dma((n_dir,)),
                dma((n_dir,)),
                dma((len(GROUPS), Halo.COUNT)),
                dma((len(GROUPS), Halo.COUNT)),
                dma((len(GROUPS2), Halo.COUNT)),
                dma((len(GROUPS2), Halo.COUNT)),
            ],
            compiler_params=pltpu.CompilerParams(
                collective_id=0, has_side_effects=True, vmem_limit_bytes=60 * 1024 * 1024
            ),
            cost_estimate=pl.CostEstimate(
                flops=6 * 10**9, bytes_accessed=2 * 10**6, transcendentals=10**5
            ),
        )(*args)
        return new_features, jnp.transpose(force, (0, 2, 1, 3))

    in_specs = (
        P("gx", "yz", None, None),
        P("gx", "yz", None, None),
        P(None, "gx", "yz", None),
        P(None, "gx", "yz", None),
        P(),
        P(),
        P(),
        P(),
        P(),
        P(),
    )
    out_specs = (P("gx", "yz", None, None), P("gx", "yz", None, None))
    return jax.shard_map(body, mesh=mesh, in_specs=in_specs, out_specs=out_specs, check_vma=False)
```

```python
import math

import jax
import jax.numpy as jnp
from jax import lax
from jax.experimental import pallas as pl
from jax.experimental.pallas import tpu as pltpu
from jax.sharding import PartitionSpec as P

MESH = pl.DeviceIdType.MESH
F32 = jnp.float32
BF16 = jnp.bfloat16
SOFTENING = 0.25
SPACING = 0.6
ROOT_THREE = math.sqrt(3.0)
C = 128
S = 128
NB = 8
NE = 3
NP = 2
BLOCKS = 9
READ_BLOCKS = 4
KP = NE * NP
ROWS = NE * S
NEAR = 9 * S
STEP = 32
GROUPS = ((0, 4), (4, 7), (7, 9))
GROUPS2 = ((0, 4),)
DIRECTIONS = ((-1, -1), (-1, 1), (1, -1), (1, 1), (-1, 0), (1, 0), (0, -1), (0, 1))


def split(x):
    high = x.astype(BF16).astype(F32)
    return high, x - high


def dot(a, b, contract=(1, 0)):
    dims = (((contract[0],), (contract[1],)), ((), ()))
    return lax.dot_general(a, b, dims, preferred_element_type=F32)


PLACE = {0: 0, -1: 1, 1: 2}


def near_slot(p, j):
    y = (1, 2, 0, 0, 1, 2, 0, 1, 2)[j]
    return (y, (p, 1 - p, 3 - p)[j // 3])


def near_pillar(p, j):
    y, slot = near_slot(p, j)
    return (1, 2, 3, 0)[slot], (1, 0, 2)[y]


def block(bufs, c, *at):
    for buf in bufs:
        if c < buf.shape[2]:
            return buf.at[(*at, c)]
        c -= buf.shape[2]


def deliver(mixed, forces, mixed_out, forces_out, held, held_forces, sems):
    parts = [(forces, held_forces, forces_out)]
    parts += [(mixed.at[p], held.at[p], mixed_out.at[p]) for p in range(NP)]
    reads = [pltpu.make_async_copy(a, b, sems.at[0, i]) for i, (a, b, _) in enumerate(parts)]
    writes = [pltpu.make_async_copy(b, c, sems.at[1, i]) for i, (_, b, c) in enumerate(parts)]
    for copy in reads:
        copy.start()
    for read, write in zip(reads, writes):
        read.wait()
        write.start()
    for copy in writes:
        copy.wait()


class Halo:
    COUNT = 12

    def __init__(self, bufs, send, recv, device, low_wrap, high_wrap):
        self.copies = {}
        self.low_wrap, self.high_wrap = low_wrap, high_wrap
        for g, buf in enumerate(bufs):
            n = 0
            for own, ghost, dx in ((0, 2, -1), (1, 3, 1)):
                spans = {"x": (buf.at[0, own], buf.at[0, ghost], (dx, 0))}
                for sign, step, to in (("m", -1, 2), ("p", 1, 1)):
                    spans |= {
                        "y" + sign: (buf.at[0, own], buf.at[to, own], (0, step)),
                        "c" + sign: (buf.at[0, ghost], buf.at[to, ghost], (0, step)),
                        "w" + sign: (buf.at[0, own], buf.at[to, ghost], (dx, step)),
                    }
                for name, (src, dst, step) in spans.items():
                    if name[0] != "w":
                        slot = n
                        n += 1
                    else:
                        slot = n - 1
                    self.copies[name, own, g] = pltpu.make_async_remote_copy(
                        src_ref=src,
                        dst_ref=dst,
                        send_sem=send.at[g, slot],
                        recv_sem=recv.at[g, slot],
                        device_id=device(*step),
                        device_id_type=MESH,
                    )

    def start(self, own, g, *names):
        for name in names:
            self.copies[name, own, g].start()

    def arrived(self, own, g, *names):
        for name in names:
            self.copies[name, own, g].wait_recv()

    def sends(self, sign, plain, wrap):
        wraps = self.low_wrap if sign == "m" else self.high_wrap
        if wrap is not None:
            pl.when(wraps)(wrap)
        if plain is not None:
            pl.when(jnp.logical_not(wraps))(plain)

    def along_x(self, own, g):
        self.start(own, g, "x")
        for sign in "mp":
            self.sends(sign, None, lambda: self.start(own, g, "w" + sign))

    def along_y(self, own, g):
        self.start(own, g, "ym", "yp")

    def near(self, own, g):
        self.arrived(own, g, "ym", "yp")

    def corners(self, own, g):
        self.arrived(own, g, "x")
        for sign in "mp":
            self.sends(sign, lambda: self.start(own, g, "c" + sign), None)

    def rest(self, own, g):
        self.arrived(own, g, "cm", "cp")

    def sent(self, groups):
        for g in groups:
            for own in range(NP):
                for name in ("x", "ym", "yp", "cm", "cp"):
                    self.copies[name, own, g].wait_send()


def kernel(
    gx_size,
    yz_size,
    feat,
    *refs,
):
    small_in, refs = refs[:9], refs[9:]
    mixed, forces, *refs = refs
    small, refs = refs[:9], refs[9:]
    run(gx_size, yz_size, feat, small_in, small, mixed, forces, *refs)


def run(
    gx_size,
    yz_size,
    feat,
    small_in,
    small,
    mixed,
    forces,
    ext0,
    ext1,
    ext2,
    mix0,
    posx,
    oh,
    coef,
    qcoef,
    wide,
    w_turned,
    zf,
    ang,
    pj,
    geo,
    edges,
    acc,
    gate,
    gsc,
    raw,
    mix_out,
    side,
    sums,
    grad,
    extf,
    frecv,
    small_sem,
    load_sem,
    out_sem,
    pos_send,
    pos_recv,
    f1_send,
    f1_recv,
    f2_send,
    f2_recv,
    fo_send,
    fo_recv,
):
    ext, ext2 = (ext0, ext1, ext2), (mix0,)
    gx = lax.axis_index("gx")
    yz = lax.axis_index("yz")

    half = yz_size // 2
    low_wrap = lax.rem(yz, half) == 0
    high_wrap = lax.rem(yz, half) == half - 1

    def device(dx, dy):
        return (lax.rem(gx + dx + gx_size, gx_size), lax.rem(yz + dy + yz_size, yz_size))

    small_loads = [
        pltpu.make_async_copy(small_in[i], small[i], small_sem.at[i]) for i in range(len(small))
    ]
    for load in small_loads:
        load.start()
    pos, dst, shift, wr, wq, w_scalar, w_gate, w_vector, w_tensor = small
    feat_load = pltpu.make_async_copy(feat, raw, load_sem)
    feat_load.start()

    barrier = pltpu.get_barrier_semaphore()
    for step in DIRECTIONS:
        pl.semaphore_signal(barrier, inc=1, device_id=device(*step), device_id_type=MESH)

    for load in small_loads:
        load.wait()
    for p in range(NP):
        posx[0, p] = jnp.zeros((8, S), F32)
        for m in range(3):
            posx[0, p, pl.ds(m, 1), :] = pos[p, m]

    def turn(g):
        for c in range(*GROUPS[g]):
            for p in range(NP):
                tile = raw[p, 0, :, pl.ds(c * C, C)].astype(F32)
                block(ext, c, 0, p)[...] = jnp.transpose(tile).astype(BF16)

    feat_load.wait()
    turn(0)
    pl.semaphore_wait(barrier, len(DIRECTIONS))

    halo = Halo(ext, f1_send, f1_recv, device, low_wrap, high_wrap)
    halo.along_x(1, 0)
    halo.along_y(0, 0)
    halo.along_y(1, 0)
    pos_copies = []
    for n, (dx, dy) in enumerate(DIRECTIONS):
        if dx == 0:
            here, there = pl.ds(0, 2), pl.ds(0, 2)
        elif dx == 1:
            here, there = pl.ds(1, 1), pl.ds(3, 1)
        else:
            here, there = pl.ds(0, 1), pl.ds(2, 1)
        copy = pltpu.make_async_remote_copy(
            src_ref=posx.at[0, here],
            dst_ref=posx.at[PLACE[-dy], there],
            send_sem=pos_send.at[n],
            recv_sem=pos_recv.at[n],
            device_id=device(dx, dy),
            device_id_type=MESH,
        )
        copy.start()
        pos_copies.append(copy)

    for g in range(1, len(GROUPS)):
        turn(g)
        halo.along_x(1, g)
        halo.along_y(0, g)
        halo.along_y(1, g)

    atom = lax.broadcasted_iota(jnp.int32, (S, ROWS), 0).astype(F32)
    edges[...] = jnp.zeros_like(edges)
    for p in range(NP):
        rows = [dst[k, p].astype(F32) for k in range(NE)]
        for k in range(NE):
            edges[0, pl.ds(k * NP + p, 1), :] = rows[k]
            edges[1, pl.ds(k * NP + p, 1), :] = shift[k, p].astype(F32)
        place = jnp.concatenate(rows, axis=1) - atom
        for j in range(9):
            x, y = near_pillar(p, j)
            hit = place == float((3 * x + y) * S)
            oh[p, pl.ds(j * S, S), :] = jnp.where(hit, 1.0, 0.0).astype(BF16)

    for f in range(9):
        w = wr[:, pl.ds(f * C, C)] if f < 7 else wq[:, pl.ds((f - 7) * C, C)]
        high, low = split(w)
        rows = jnp.concatenate([high, low, high, jnp.zeros_like(w)], axis=0)
        wide[pl.ds(f * C, C), :] = jnp.transpose(rows).astype(BF16)
    for i, w in enumerate((w_scalar, w_gate, w_vector, w_tensor)):
        w_turned[pl.ds(i * C, C), :] = jnp.transpose(w[...].astype(F32)).astype(BF16)

    halo.along_x(0, 0)

    for copy in pos_copies:
        copy.wait_recv()
    for p in range(NP):
        places = jnp.concatenate([posx[near_slot(p, j)] for j in range(9)], axis=1)
        first, rest = split(places)
        second, third = split(rest)
        parts = jnp.concatenate([first, second, third, jnp.zeros_like(first)], 0).astype(BF16)
        found = dot(parts, oh[p])
        far = (found[0:8] + found[8:16]) + found[16:24]
        for k in range(NE):
            pj[k * NP + p] = far[:, k * S : (k + 1) * S] - posx[0, p]

    place = edges[0]
    pj[pl.ds(KP, 8 - KP)] = jnp.zeros((8 - KP, 8, S), F32)
    own_p = lax.rem(lax.broadcasted_iota(jnp.int32, (8, S), 0), NP).astype(F32)
    one = jnp.ones_like(place)
    nil = jnp.zeros_like(place)

    def at_least(x, bound):
        return jnp.where(x >= float(bound), one, nil)

    ext_x = at_least(place, 3 * S) + at_least(place, 6 * S) + at_least(place, 9 * S)
    left = place - ext_x * float(3 * S)
    ext_y = at_least(left, S) + at_least(left, 2 * S)
    disp_x = pj[:, 0, :] + (ext_x - 1.0 - own_p)
    disp_y = pj[:, 1, :] + (ext_y - 1.0)
    disp_z = pj[:, 2, :] + edges[1]
    rho = jnp.sqrt(disp_x * disp_x + disp_y * disp_y + disp_z * disp_z + SOFTENING)
    inverse = 1.0 / rho
    u_x, u_y, u_z = disp_x * inverse, disp_y * inverse, disp_z * inverse
    geo[...] = inverse
    length_sq = u_x * u_x + u_y * u_y + u_z * u_z
    angular = (
        u_x,
        u_y,
        u_z,
        ROOT_THREE * u_x * u_y,
        ROOT_THREE * u_y * u_z,
        0.5 * (3.0 * u_z * u_z - length_sq),
        ROOT_THREE * u_x * u_z,
        0.5 * ROOT_THREE * (u_x * u_x - u_y * u_y),
    )
    for f in range(8):
        ang[f] = angular[f]
    zf[...] = jnp.zeros_like(zf)
    for b in range(NB):
        off = (rho - (0.5 + SPACING * b)) / SPACING
        basis = jnp.exp(-(off * off))
        slope = basis * off * (-2.0 / SPACING)
        for i, value in enumerate((basis, slope)):
            high, low = split(value)
            zf[32 * i + b] = high
            zf[32 * i + 8 + b] = high
            zf[32 * i + 16 + b] = low

    def columns(p, k):
        return pl.ds((p * NE + k) * S, S)

    for p in range(NP):
        values = jnp.concatenate([zf[:, k * NP + p, :] for k in range(NE)], axis=1).astype(BF16)
        at = pl.ds(p * ROWS, ROWS)
        out = dot(wide[pl.ds(0, 7 * C), :], values[0:32])
        for f in range(7):
            coef[f, :, at] = out[f * C : (f + 1) * C]
        qcoef[0, :, at] = dot(wide[pl.ds(8 * C, C), :], values[0:32])
        out = dot(wide[pl.ds(7 * C, 2 * C), :], values[32:64])
        for f in range(2):
            qcoef[1 + f, :, at] = out[f * C : (f + 1) * C]

    halo.along_x(0, 1)
    halo.along_x(0, 2)

    def gather(bufs, g, lo, p, first, last):
        buf = bufs[g]
        n = buf.shape[2]
        tiles = [buf[near_slot(p, j)].reshape(n * C, S) for j in range(first, last)]
        out = dot(jnp.concatenate(tiles, axis=1), oh[p, pl.ds(first * S, (last - first) * S), :])
        at = pl.ds(p * ROWS, ROWS)
        for i in range(n):
            term = out[i * C : (i + 1) * C]
            gsc[lo + i, :, at] = term if first == 0 else gsc[lo + i, :, at] + term

    def each_row(p, fn):
        def run(i, carry):
            fn(p, pl.ds(pl.multiple_of(i * STEP, STEP), STEP))
            return carry

        lax.fori_loop(0, C // STEP, run, 0)

    def angle(f, p, k):
        return ang[f, pl.ds(k * NP + p, 1), :]

    def own_columns(p):
        return pl.ds(p * S, S)

    def message_sv(p, r):
        total = [jnp.zeros((STEP, S), F32) for _ in range(BLOCKS)]
        for k in range(NE):
            e = columns(p, k)
            s = gsc[0, r, e]
            v = [gsc[1 + m, r, e] for m in range(3)]
            u = [angle(m, p, k) for m in range(3)]
            along = u[0] * v[0] + u[1] * v[1] + u[2] * v[2]
            total[0] = total[0] + coef[0, r, e] * s + coef[1, r, e] * along
            r3s = coef[3, r, e] * s
            r4 = coef[4, r, e]
            for m in range(3):
                total[1 + m] = total[1 + m] + r3s * u[m] + r4 * v[m]
            r5s = coef[5, r, e] * s
            for n in range(5):
                total[4 + n] = total[4 + n] + r5s * angle(3 + n, p, k)
        for b in range(BLOCKS):
            acc[b, r, own_columns(p)] = total[b]

    def message_t(lo, hi):
        def fn(p, r):
            at = own_columns(p)
            total = [acc[b, r, at] for b in (0, *range(lo, hi))]
            for k in range(NE):
                e = columns(p, k)
                along = None
                r6 = coef[6, r, e]
                for n in range(lo, hi):
                    t = gsc[n, r, e]
                    term = angle(n - 1, p, k) * t
                    along = term if along is None else along + term
                    total[1 + n - lo] = total[1 + n - lo] + r6 * t
                total[0] = total[0] + coef[2, r, e] * along
            for i, b in enumerate((0, *range(lo, hi))):
                acc[b, r, at] = total[i]

        return fn

    third = 1.0 / NE

    def mix(p, lo, hi, w):
        at = own_columns(p)
        terms = jnp.concatenate([(acc[b, :, at] * third).astype(BF16) for b in range(lo, hi)], axis=1)
        out = dot(w_turned[pl.ds(w * C, C), :], terms)
        for b in range(lo, hi):
            acc[b, :, at] = out[:, (b - lo) * S : (b - lo + 1) * S]

    def update_sv(p, r):
        at = own_columns(p)
        g = gate[r, at]
        for b in range(READ_BLOCKS):
            old = block(ext, b, 0, p)[r, :].astype(F32)
            step = g * acc[b, r, at] if b > 0 else acc[0, r, at]
            block(ext2, b, 0, p)[r, :] = (old + step).astype(BF16)

    halo2 = Halo(ext2, f2_send, f2_recv, device, low_wrap, high_wrap)

    def finish(p):
        at = own_columns(p)
        out = dot(w_turned[pl.ds(0, 2 * C), :], (acc[0, :, at] * third).astype(BF16))
        pre = out[0:C]
        acc[0, :, at] = pre * jax.nn.sigmoid(pre)
        gate[:, at] = jax.nn.sigmoid(out[C : 2 * C])
        each_row(p, update_sv)
        halo2.along_x(p, 0)
        halo2.along_y(p, 0)

    def finish_tensors(p):
        mix(p, 4, 9, 3)
        at = own_columns(p)
        for b in range(BLOCKS):
            if b < READ_BLOCKS:
                new = block(ext2, b, 0, p)[...].astype(F32)
            else:
                new = block(ext, b, 0, p)[...].astype(F32) + gate[:, at] * acc[b, :, at]
            mix_out[p, 0, :, pl.ds(b * C, C)] = jnp.transpose(new).astype(BF16)

    starts = [lo for lo, _ in GROUPS]
    for g in range(3):
        halo.near(0, g)
        halo.near(1, g)
        gather(ext, g, starts[g], 0, 0, 6)
        halo.corners(1, g)
    for g in range(3):
        gather(ext, g, starts[g], 1, 0, 6)
    halo.rest(1, 0)
    gather(ext, 0, starts[0], 0, 6, 9)
    each_row(0, message_sv)
    mix(0, 1, 4, 2)
    halo.rest(1, 1)
    gather(ext, 1, starts[1], 0, 6, 9)
    each_row(0, message_t(4, 7))
    halo.rest(1, 2)
    gather(ext, 2, starts[2], 0, 6, 9)
    each_row(0, message_t(7, 9))
    finish(0)
    halo.corners(0, 0)
    halo.corners(0, 1)
    halo.rest(0, 0)
    gather(ext, 0, starts[0], 1, 6, 9)
    each_row(1, message_sv)
    mix(1, 1, 4, 2)
    halo.corners(0, 2)
    halo.rest(0, 1)
    gather(ext, 1, starts[1], 1, 6, 9)
    each_row(1, message_t(4, 7))
    halo.rest(0, 2)
    gather(ext, 2, starts[2], 1, 6, 9)
    each_row(1, message_t(7, 9))
    finish(1)

    def near_side(p, r):
        own = [block(ext2, b, 0, p)[r, :].astype(F32) for b in range(READ_BLOCKS)]
        for k in range(NE):
            e = columns(p, k)
            u = [angle(m, p, k) for m in range(3)]
            along = u[0] * own[1] + u[1] * own[2] + u[2] * own[3]
            q1 = qcoef[0, r, e]
            side[0, r, e] = qcoef[1, r, e] * own[0]
            side[1, r, e] = qcoef[2, r, e] * along
            side[2, r, e] = q1 * along
            for m in range(3):
                side[3 + m, r, e] = q1 * own[1 + m]

    halo2.corners(0, 0)
    halo2.near(0, 0)
    gather(ext2, 0, 0, 0, 0, 3)
    for p in range(NP):
        each_row(p, near_side)
        finish_tensors(p)
    write = pltpu.make_async_copy(mix_out, mixed, out_sem)
    write.start()
    halo2.corners(1, 0)
    halo2.near(1, 0)
    gather(ext2, 0, 0, 0, 3, 6)
    gather(ext2, 0, 0, 1, 0, 6)
    halo.sent(range(len(GROUPS)))
    halo2.rest(0, 0)
    gather(ext2, 0, 0, 1, 6, 9)
    halo2.rest(1, 0)
    gather(ext2, 0, 0, 0, 6, 9)

    def fold(x):
        return sum(x[8 * i : 8 * i + 8] for i in range(1, STEP // 8)) + x[0:8]

    sums[...] = jnp.zeros_like(sums)
    for p in range(NP):

        def pair(i, carry, p=p):
            r = pl.ds(pl.multiple_of(i * STEP, STEP), STEP)
            carry = list(carry)
            for k in range(NE):
                e = columns(p, k)
                far = [gsc[b, r, e] for b in range(READ_BLOCKS)]
                u = [angle(m, p, k) for m in range(3)]
                along = u[0] * far[1] + u[1] * far[2] + u[2] * far[3]
                carry[4 * k] = carry[4 * k] + fold(side[0, r, e] * far[0] + side[1, r, e] * along)
                own_q = side[2, r, e]
                for m in range(3):
                    term = side[3 + m, r, e] * along + own_q * far[1 + m]
                    carry[4 * k + 1 + m] = carry[4 * k + 1 + m] + fold(term)
            return tuple(carry)

        zero = jnp.zeros((8, S), F32)
        totals = lax.fori_loop(0, C // STEP, pair, (zero,) * (4 * NE))
        for k in range(NE):
            for q in range(4):
                row = jnp.sum(totals[4 * k + q], axis=0, keepdims=True)
                sums[q, pl.ds(k * NP + p, 1), :] = row

    t_rho, g_x, g_y, g_z = (sums[q] for q in range(4))
    u_x, u_y, u_z = ang[0], ang[1], ang[2]
    inverse = geo[...]
    radial_part = t_rho - (u_x * g_x + u_y * g_y + u_z * g_z) * inverse
    grad[...] = jnp.zeros_like(grad)
    grad[0] = radial_part * u_x + g_x * inverse
    grad[1] = radial_part * u_y + g_y * inverse
    grad[2] = radial_part * u_z + g_z * inverse

    parts = []
    for p in range(NP):
        terms = jnp.concatenate([grad[:, k * NP + p, :] for k in range(NE)], axis=1)
        first, rest = split(terms)
        second, third_part = split(rest)
        parts.append(
            jnp.concatenate([first, second, third_part, jnp.zeros_like(first)], 0).astype(BF16)
        )

    def scatter(*spans):
        seen = {}
        for p in range(NP):
            for lo, hi in spans:
                out = dot(parts[p], oh[p, pl.ds(lo * S, (hi - lo) * S), :], (1, 1))
                out = (out[0:8] + out[8:16]) + out[16:24]
                for j in range(lo, hi):
                    term = out[:, (j - lo) * S : (j - lo + 1) * S]
                    at = near_slot(p, j)
                    seen[at] = seen[at] - term if at in seen else -term
        for at, value in seen.items():
            extf[at] = value

    scatter((0, 2), (4, 9))
    force_copies = []
    for n, (dx, dy) in enumerate(DIRECTIONS):
        if dx == 0:
            here, there = pl.ds(0, 2), pl.ds(0, 2)
        elif dx == 1:
            here, there = pl.ds(2, 1), pl.ds(0, 1)
        else:
            here, there = pl.ds(3, 1), pl.ds(1, 1)
        copy = pltpu.make_async_remote_copy(
            src_ref=extf.at[PLACE[dy], here],
            dst_ref=frecv.at[n, there],
            send_sem=fo_send.at[n],
            recv_sem=fo_recv.at[n],
            device_id=device(dx, dy),
            device_id_type=MESH,
        )
        copy.start()
        force_copies.append(copy)

    scatter((2, 4))
    total = []
    for p in range(NP):
        mine = extf[0, p]
        for k in range(NE):
            mine = mine + grad[:, k * NP + p, :]
        total.append(mine)
    for n, (dx, dy) in enumerate(DIRECTIONS):
        force_copies[n].wait_recv()
        for p in range(NP):
            if dx == 0 or (dx == 1) == (p == 0):
                total[p] = total[p] + frecv[n, p]
    for p in range(NP):
        for m in range(3):
            forces[p, m] = total[p][m : m + 1]

    for copy in (*pos_copies, *force_copies):
        copy.wait_send()
    halo2.sent(range(len(GROUPS2)))
    write.wait()


def solution(mesh):
    gx_size, yz_size = mesh.shape["gx"], mesh.shape["yz"]

    def body(features, positions, *rest):
        args = (features, jnp.transpose(positions, (0, 2, 1, 3)), *rest)
        vmem = pl.BlockSpec(memory_space=pltpu.VMEM)
        anywhere = pl.BlockSpec(memory_space=pl.ANY)
        dma = pltpu.SemaphoreType.DMA
        n_dir = len(DIRECTIONS)

        def run_all(*refs):
            kernel(gx_size, yz_size, *refs)

        small = [pltpu.VMEM(x.shape, x.dtype) for x in args[1:]]
        new_features, force = pl.pallas_call(
            run_all,
            out_shape=(
                jax.ShapeDtypeStruct((NP, 1, S, BLOCKS * C), BF16),
                jax.ShapeDtypeStruct((NP, 3, 1, S), F32),
            ),
            in_specs=[pl.BlockSpec(memory_space=pltpu.HBM)] * 10,
            out_specs=(anywhere, vmem),
            scratch_shapes=small
            + [
                *[pltpu.VMEM((3, 4, hi - lo, S, C), BF16) for lo, hi in GROUPS + GROUPS2],
                pltpu.VMEM((3, 4, 8, S), F32),
                pltpu.VMEM((NP, NEAR, ROWS), BF16),
                pltpu.VMEM((7, C, NP * ROWS), F32),
                pltpu.VMEM((3, C, NP * ROWS), F32),
                pltpu.VMEM((9 * C, 32), BF16),
                pltpu.VMEM((4 * C, C), BF16),
                pltpu.VMEM((64, 8, S), F32),
                pltpu.VMEM((8, 8, S), F32),
                pltpu.VMEM((8, 8, S), F32),
                pltpu.VMEM((8, S), F32),
                pltpu.VMEM((2, 8, S), F32),
                pltpu.VMEM((BLOCKS, C, NP * S), F32),
                pltpu.VMEM((C, NP * S), F32),
                pltpu.VMEM((BLOCKS, C, NP * ROWS), F32),
                pltpu.VMEM((NP, 1, S, BLOCKS * C), BF16),
                pltpu.VMEM((NP, 1, S, BLOCKS * C), BF16),
                pltpu.VMEM((6, C, NP * ROWS), F32),
                pltpu.VMEM((4, 8, S), F32),
                pltpu.VMEM((8, 8, S), F32),
                pltpu.VMEM((3, 4, 8, S), F32),
                pltpu.VMEM((n_dir, NP, 8, S), F32),
                dma((len(small),)),
                dma,
                dma,
                dma((n_dir,)),
                dma((n_dir,)),
                dma((len(GROUPS), Halo.COUNT)),
                dma((len(GROUPS), Halo.COUNT)),
                dma((len(GROUPS2), Halo.COUNT)),
                dma((len(GROUPS2), Halo.COUNT)),
                dma((n_dir,)),
                dma((n_dir,)),
            ],
            compiler_params=pltpu.CompilerParams(
                collective_id=0, has_side_effects=True, vmem_limit_bytes=60 * 1024 * 1024
            ),
            cost_estimate=pl.CostEstimate(
                flops=4 * 10**9, bytes_accessed=2 * 10**6, transcendentals=10**5
            ),
        )(*args)
        new_features, force = pl.pallas_call(
            deliver,
            out_shape=(
                jax.ShapeDtypeStruct((NP, 1, S, BLOCKS * C), BF16),
                jax.ShapeDtypeStruct((NP, 3, 1, S), F32),
            ),
            in_specs=[anywhere] * 2,
            out_specs=(anywhere, anywhere),
            scratch_shapes=[
                pltpu.VMEM((NP, 1, S, BLOCKS * C), BF16),
                pltpu.VMEM((NP, 3, 1, S), F32),
                dma((2, 1 + NP)),
            ],
            compiler_params=pltpu.CompilerParams(vmem_limit_bytes=60 * 1024 * 1024),
            cost_estimate=pl.CostEstimate(flops=0, bytes_accessed=12 * 10**5, transcendentals=0),
        )(new_features, force)
        return new_features, jnp.transpose(force, (0, 2, 1, 3))

    in_specs = (
        P("gx", "yz", None, None),
        P("gx", "yz", None, None),
        P(None, "gx", "yz", None),
        P(None, "gx", "yz", None),
        P(),
        P(),
        P(),
        P(),
        P(),
        P(),
    )
    out_specs = (P("gx", "yz", None, None), P("gx", "yz", None, None))
    return jax.shard_map(body, mesh=mesh, in_specs=in_specs, out_specs=out_specs, check_vma=False)
```

```python
import math

import jax
import jax.numpy as jnp
from jax import lax
from jax.experimental import pallas as pl
from jax.experimental.pallas import tpu as pltpu
from jax.sharding import PartitionSpec as P

MESH = pl.DeviceIdType.MESH
F32 = jnp.float32
BF16 = jnp.bfloat16
SOFTENING = 0.25
SPACING = 0.6
ROOT_THREE = math.sqrt(3.0)
C = 128
S = 128
NB = 8
NE = 3
NP = 2
BLOCKS = 9
READ_BLOCKS = 4
ROWS = NE * S
STEP = 32
GROUPS = ((0, 4), (4, 7), (7, 9))
SUMS = ((1, 2, 3), (4, 5, 6), (7, 8, 0))
GROUPS2 = ((0, 2), (2, 4))
COUNT = 6
EDGE_ROWS = 24
NEIGHBOURS = ((-1, 0), (1, 0), (0, -1), (0, 1))


def split(x):
    high = x.astype(BF16).astype(F32)
    return high, x - high


def dot(a, b, contract=(1, 0)):
    dims = (((contract[0],), (contract[1],)), ((), ()))
    return lax.dot_general(a, b, dims, preferred_element_type=F32)


def deliver(mixed, forces, mixed_out, forces_out, held, held_forces, sems):
    parts = [(forces, held_forces, forces_out)]
    parts += [(mixed.at[p], held.at[p], mixed_out.at[p]) for p in range(NP)]
    reads = [pltpu.make_async_copy(a, b, sems.at[0, i]) for i, (a, b, _) in enumerate(parts)]
    writes = [pltpu.make_async_copy(b, c, sems.at[1, i]) for i, (_, b, c) in enumerate(parts)]
    for copy in reads:
        copy.start()
    for read, write in zip(reads, writes):
        read.wait()
        write.start()
    for copy in writes:
        copy.wait()


def kernel(
    gx_size,
    yz_size,
    feat,
    *refs,
):
    small_in, refs = refs[:9], refs[9:]
    mixed, forces, *refs = refs
    small, refs = refs[:9], refs[9:]
    run(gx_size, yz_size, feat, small_in, small, mixed, forces, *refs)


def run(
    gx_size,
    yz_size,
    feat,
    small_in,
    small,
    mixed,
    forces,
    ext0,
    ext1,
    ext2,
    mix0,
    mix1,
    part_out,
    part_in,
    posx,
    oh,
    coef,
    readout,
    wide,
    w_turned,
    zf,
    ang,
    pj,
    inverses,
    target,
    edges,
    acc,
    gate,
    gsc,
    raw,
    mix_out,
    side,
    sums,
    grad,
    force_y,
    force_y_in,
    force_x,
    force_x_in,
    small_sem,
    load_sem,
    out_sem,
    pos_send,
    pos_recv,
    x_send,
    x_recv,
    part_send,
    part_recv,
    mix_send,
    mix_recv,
    force_send,
    force_recv,
):
    ext, ext2 = (ext0, ext1, ext2), (mix0, mix1)
    gx = lax.axis_index("gx")
    yz = lax.axis_index("yz")

    def device(dx, dy):
        return (lax.rem(gx + dx + gx_size, gx_size), lax.rem(yz + dy + yz_size, yz_size))

    def remote(src, dst, send, recv, step):
        return pltpu.make_async_remote_copy(
            src_ref=src,
            dst_ref=dst,
            send_sem=send,
            recv_sem=recv,
            device_id=device(*step),
            device_id_type=MESH,
        )

    small_loads = [
        pltpu.make_async_copy(small_in[i], small[i], small_sem.at[i]) for i in range(len(small))
    ]
    feat_load = pltpu.make_async_copy(feat, raw, load_sem)
    feat_load.start()
    for load in small_loads:
        load.start()
    pos, dst, shift, wr, wq, w_scalar, w_gate, w_vector, w_tensor = small

    barrier = pltpu.get_barrier_semaphore()
    for step in NEIGHBOURS:
        pl.semaphore_signal(barrier, inc=1, device_id=device(*step), device_id_type=MESH)

    def turn(g):
        lo, hi = GROUPS[g]
        for i in range(hi - lo):
            for p in range(NP):
                tile = raw[p, 0, :, pl.ds((lo + i) * C, C)].astype(F32)
                ext[g][p, i] = jnp.transpose(tile).astype(BF16)

    feat_load.wait()
    turn(0)
    pl.semaphore_wait(barrier, len(NEIGHBOURS))

    x_copies = []
    for g in range(len(GROUPS)):
        for own, ghost, dx in ((0, 2, -1), (1, 3, 1)):
            x_copies.append(
                remote(ext[g].at[own], ext[g].at[ghost], x_send.at[g, own], x_recv.at[g, own], (dx, 0))
            )
    x_copies[0].start()
    x_copies[1].start()

    for load in small_loads:
        load.wait()
    for p in range(NP):
        posx[0, p] = jnp.zeros((16, S), F32)
        for m in range(3):
            posx[0, p, pl.ds(m, 1), :] = pos[p, m]
        for k in range(NE):
            posx[0, p, pl.ds(3 + k, 1), :] = dst[k, p].astype(F32)
            posx[0, p, pl.ds(6 + k, 1), :] = shift[k, p].astype(F32)
    own = pl.ds(0, NP)
    pos_copies = [
        remote(posx.at[0, 0], posx.at[0, 2], pos_send.at[0], pos_recv.at[0], (-1, 0)),
        remote(posx.at[0, 1], posx.at[0, 3], pos_send.at[1], pos_recv.at[1], (1, 0)),
        remote(posx.at[0, own], posx.at[2, own], pos_send.at[2], pos_recv.at[2], (0, -1)),
        remote(posx.at[0, own], posx.at[1, own], pos_send.at[3], pos_recv.at[3], (0, 1)),
    ]
    for copy in pos_copies:
        copy.start()
    for g in range(1, len(GROUPS)):
        turn(g)
        x_copies[2 * g].start()
        x_copies[2 * g + 1].start()

    def turned(w):
        high, low = split(w)
        rows = jnp.concatenate([high, low, high, jnp.zeros_like(w)], axis=0)
        return jnp.transpose(rows).astype(BF16)

    def widen(f, carry):
        at = pl.ds(pl.multiple_of(f * C, C), C)
        wide[at, :] = turned(wr[:, at])
        return carry

    lax.fori_loop(0, 7, widen, 0)
    wide[pl.ds(8 * C, C), :] = turned(wq[:, pl.ds(0, C)])
    last = turned(wq[:, pl.ds(C, C)])
    wide[pl.ds(7 * C, C), :] = last
    wide[pl.ds(9 * C, C), :] = last
    for i, w in enumerate((w_scalar, w_gate, w_vector, w_tensor)):
        w_turned[pl.ds(i * C, C), :] = jnp.transpose(w[...].astype(F32)).astype(BF16)

    for copy in pos_copies:
        copy.wait_recv()
    edges[...] = jnp.zeros_like(edges)
    for q in range(COUNT):
        y, p = q // NP, q % NP
        at = pl.ds(NE * q, NE)
        edges[0, at, :] = posx[y, p, pl.ds(3, NE), :]
        edges[1, at, :] = posx[y, p, pl.ds(6, NE), :]
        edges[2, at, :] = jnp.full((NE, S), p, F32)
        edges[3, at, :] = jnp.full((NE, S), (1, 0, 2)[y], F32)
    place = edges[0]
    one = jnp.ones_like(place)
    nil = jnp.zeros_like(place)

    def at_least(x, bound):
        return jnp.where(x >= float(bound), one, nil)

    ext_x = at_least(place, 3 * S) + at_least(place, 6 * S) + at_least(place, 9 * S)
    left = place - ext_x * float(3 * S)
    ext_y = at_least(left, S) + at_least(left, 2 * S)
    step_x = ext_x - 1.0 - edges[2]
    step_y = ext_y - 1.0
    target[...] = jnp.where(edges[3] + step_y == 1.0, ext_x * S + (left - ext_y * S), -1.0)

    atom = lax.broadcasted_iota(jnp.int32, (S, ROWS), 0).astype(F32)

    def pick(y, carry):
        for p in range(NP):
            rows = [target[pl.ds(NE * (NP * y + p) + k, 1), :] for k in range(NE)]
            ends = jnp.concatenate(rows, axis=1) - atom
            for i, x in enumerate((1, 2, 3 * p)):
                hit = jnp.where(ends == float(x * S), 1.0, 0.0).astype(BF16)
                oh[p, pl.ds(i * S, S), pl.ds(pl.multiple_of(y * ROWS, ROWS), ROWS)] = hit
        return carry

    lax.fori_loop(0, 3, pick, 0)

    def in_parts(x):
        first, rest = split(x)
        second, third = split(rest)
        return jnp.concatenate([first, second, third, jnp.zeros_like(first)], 0).astype(BF16)

    def whole(x):
        return (x[0:8] + x[8:16]) + x[16:24]

    pj[...] = jnp.zeros_like(pj)
    for p in range(NP):
        near = [posx[0, slot, pl.ds(0, 8), :] for slot in (0, 1, 3 - p)]
        far = whole(dot(in_parts(jnp.concatenate(near, axis=1)), oh[p]))
        for y in range(3):
            for k in range(NE):
                at = (NE * y + k) * S
                pj[NE * (NP * y + p) + k] = far[:, at : at + S] - posx[y, p, pl.ds(0, 8), :]

    disp_x = pj[:, 0, :] + step_x
    disp_y = pj[:, 1, :] + step_y
    disp_z = pj[:, 2, :] + edges[1]
    rho = jnp.sqrt(disp_x * disp_x + disp_y * disp_y + disp_z * disp_z + SOFTENING)
    inverse = 1.0 / rho
    u_x, u_y, u_z = disp_x * inverse, disp_y * inverse, disp_z * inverse
    inverses[...] = inverse
    length_sq = u_x * u_x + u_y * u_y + u_z * u_z
    angular = (
        u_x,
        u_y,
        u_z,
        ROOT_THREE * u_x * u_y,
        ROOT_THREE * u_y * u_z,
        0.5 * (3.0 * u_z * u_z - length_sq),
        ROOT_THREE * u_x * u_z,
        0.5 * ROOT_THREE * (u_x * u_x - u_y * u_y),
    )
    for f in range(8):
        ang[f] = angular[f]
    zf[...] = jnp.zeros_like(zf)
    for b in range(NB):
        off = (rho - (0.5 + SPACING * b)) / SPACING
        basis = jnp.exp(-(off * off))
        slope = basis * off * (-2.0 / SPACING)
        for i, value in enumerate((basis, slope)):
            high, low = split(value)
            zf[32 * i + b] = high
            zf[32 * i + 8 + b] = high
            zf[32 * i + 16 + b] = low

    def columns(k):
        return pl.ds(k * S, S)

    for q in range(COUNT):
        values = jnp.concatenate([zf[:, NE * q + k, :] for k in range(NE)], axis=1).astype(BF16)
        out = dot(wide[pl.ds(0, 8 * C), :], values[0:32])
        for f in range(7):
            coef[f, q] = out[f * C : (f + 1) * C]
        readout[q, 0] = out[7 * C : 8 * C]
        out = dot(wide[pl.ds(8 * C, 2 * C), :], values[32:64])
        readout[q, 1] = out[0:C]
        readout[q, 2] = out[C : 2 * C]

    def columns(k):
        return pl.ds(k * S, S)

    def gather(bufs, g, to, first, last):
        buf = bufs[g]
        n = buf.shape[1]

        def run(y, carry):
            for p in range(NP):
                tiles = [buf[slot].reshape(n * C, S) for slot in (0, 1, 3 - p)[first:last]]
                rows = pl.ds(first * S, (last - first) * S)
                picks = oh[p, rows, pl.ds(pl.multiple_of(y * ROWS, ROWS), ROWS)]
                out = dot(jnp.concatenate(tiles, axis=1), picks)
                for i in range(n):
                    gsc[to + i, NP * y + p] = out[i * C : (i + 1) * C]
            return carry

        lax.fori_loop(0, 3, run, 0)

    def each_row(fn, lo, hi):
        steps = C // STEP

        def run(i, carry):
            q = i // steps
            fn(q, pl.ds(pl.multiple_of((i - q * steps) * STEP, STEP), STEP))
            return carry

        lax.fori_loop(lo * steps, hi * steps, run, 0)

    def angle(f, q, k):
        return ang[f, pl.ds(NE * q + k, 1), :]

    def message_sv(p, r):
        total = [jnp.zeros((STEP, S), F32) for _ in range(BLOCKS)]
        for k in range(NE):
            e = columns(k)
            s = gsc[0, p, r, e]
            v = [gsc[1 + m, p, r, e] for m in range(3)]
            u = [angle(m, p, k) for m in range(3)]
            along = u[0] * v[0] + u[1] * v[1] + u[2] * v[2]
            total[0] = total[0] + coef[0, p, r, e] * s + coef[1, p, r, e] * along
            r3s = coef[3, p, r, e] * s
            r4 = coef[4, p, r, e]
            for m in range(3):
                total[1 + m] = total[1 + m] + r3s * u[m] + r4 * v[m]
            r5s = coef[5, p, r, e] * s
            for n in range(5):
                total[4 + n] = total[4 + n] + r5s * angle(3 + n, p, k)
        for b in range(BLOCKS):
            acc[b, p, r, :] = total[b]

    def message_t(lo, hi):
        def fn(p, r):
            total = [acc[b, p, r, :] for b in (0, *range(lo, hi))]
            for k in range(NE):
                e = columns(k)
                along = None
                r6 = coef[6, p, r, e]
                for n in range(lo, hi):
                    t = gsc[n, p, r, e]
                    term = angle(n - 1, p, k) * t
                    along = term if along is None else along + term
                    total[1 + n - lo] = total[1 + n - lo] + r6 * t
                total[0] = total[0] + coef[2, p, r, e] * along
            for i, b in enumerate((0, *range(lo, hi))):
                acc[b, p, r, :] = total[i]

        return fn

    third = 1.0 / NE

    def mix(lo, hi, w):
        def run(p, carry):
            terms = [(acc[b, p] * third).astype(BF16) for b in range(lo, hi)]
            out = dot(w_turned[pl.ds(w * C, C), :], jnp.concatenate(terms, axis=1))
            for b in range(lo, hi):
                acc[b, p] = out[:, (b - lo) * S : (b - lo + 1) * S]
            return carry

        lax.fori_loop(0, NP, run, 0)

    part_copies = []
    for h in range(len(SUMS)):
        for i, dy in ((0, -1), (1, 1)):
            part_copies.append(
                remote(
                    part_out.at[h, i],
                    part_in.at[h, 1 - i],
                    part_send.at[h, i],
                    part_recv.at[h, i],
                    (0, dy),
                )
            )

    def send_sums(h):
        for i in range(2):
            for p in range(NP):
                for j, b in enumerate(SUMS[h]):
                    part_out[h, i, p, j] = acc[b, NP * (1 + i) + p].astype(BF16)
            part_copies[2 * h + i].start()

    def add_sums(h):
        for i in range(2):
            part_copies[2 * h + i].wait_recv()
        for p in range(NP):
            for j, b in enumerate(SUMS[h]):
                acc[b, p] = acc[b, p] + part_in[h, 0, p, j].astype(F32) + part_in[h, 1, p, j].astype(F32)

    for g, (lo, hi) in enumerate(GROUPS):
        x_copies[2 * g].wait_recv()
        x_copies[2 * g + 1].wait_recv()
        gather(ext, g, lo, 0, 3)
        if g == 0:
            each_row(message_sv, 0, COUNT)
        else:
            each_row(message_t(lo, hi), 0, COUNT)
        send_sums(g)
    add_sums(0)
    mix(1, 4, 2)
    add_sums(1)
    add_sums(2)

    def scalars(p, carry):
        out = dot(w_turned[pl.ds(0, 2 * C), :], (acc[0, p] * third).astype(BF16))
        pre = out[0:C]
        acc[0, p] = pre * jax.nn.sigmoid(pre)
        gate[p] = jax.nn.sigmoid(out[C : 2 * C])
        return carry

    lax.fori_loop(0, NP, scalars, 0)

    def read_block(b, y, slot):
        g = b // 2
        return ext2[g].at[y, slot, b - GROUPS2[g][0]]

    def read_block(b, at):
        return ext2[b // 2].at[at, b % 2]

    def update_sv(p, r):
        g = gate[p, r, :]
        for b in range(READ_BLOCKS):
            old = ext[0][p, b, r, :].astype(F32)
            step = g * acc[b, p, r, :] if b > 0 else acc[0, p, r, :]
            read_block(b, p)[r, :] = (old + step).astype(BF16)

    each_row(update_sv, 0, NP)
    mix_x, mix_y = [], []
    for g, buf in enumerate(ext2):
        spans = (
            (mix_x, buf.at[0], buf.at[2], (-1, 0)),
            (mix_x, buf.at[1], buf.at[3], (1, 0)),
            (mix_y, buf.at[own], buf.at[pl.ds(6, NP)], (0, -1)),
            (mix_y, buf.at[own], buf.at[pl.ds(4, NP)], (0, 1)),
        )
        for n, (into, src, to, step) in enumerate(spans):
            into.append(remote(src, to, mix_send.at[g, n], mix_recv.at[g, n], step))
    for copy in (*mix_x, *mix_y):
        copy.start()

    def results(lo, hi, value):
        for i in range(hi - lo):
            for p in range(NP):
                mix_out[p, 0, :, pl.ds((lo + i) * C, C)] = jnp.transpose(value(p, i)).astype(BF16)

    mix(4, 9, 3)
    for g, (lo, hi) in enumerate(GROUPS2):
        results(lo, hi, lambda p, i: ext2[g][p, i].astype(F32))
    for g, (lo, hi) in enumerate(GROUPS):
        if g > 0:
            results(lo, hi, lambda p, i: ext[g][p, i].astype(F32) + gate[p] * acc[lo + i, p])
    write = pltpu.make_async_copy(mix_out, mixed, out_sem)
    write.start()

    def near_side(q, r):
        at = jnp.where(q < NP, q, q + 2)
        row = [read_block(b, at)[r, :].astype(F32) for b in range(READ_BLOCKS)]
        s, v = row[0], row[1:]
        for k in range(NE):
            e = columns(k)
            u = [angle(m, q, k) for m in range(3)]
            along = u[0] * v[0] + u[1] * v[1] + u[2] * v[2]
            q1 = readout[q, 0, r, e]
            side[q, 0, r, e] = readout[q, 1, r, e] * s
            side[q, 1, r, e] = readout[q, 2, r, e] * along
            side[q, 2, r, e] = q1 * along
            for m in range(3):
                side[q, 3 + m, r, e] = q1 * v[m]

    for g, (lo, hi) in enumerate(GROUPS2):
        gather(ext2, g, lo, 0, 2)
    each_row(near_side, 0, NP)
    for copy in mix_y:
        copy.wait_recv()
    each_row(near_side, NP, COUNT)
    for copy in (*pos_copies, *x_copies, *part_copies):
        copy.wait_send()
    for g, (lo, hi) in enumerate(GROUPS2):
        mix_x[2 * g].wait_recv()
        mix_x[2 * g + 1].wait_recv()
        gather(ext2, g, READ_BLOCKS + lo, 2, 3)

    def fold(x):
        return sum(x[8 * i : 8 * i + 8] for i in range(1, STEP // 8)) + x[0:8]

    sums[...] = jnp.zeros_like(sums)

    def pairs(q, outer):
        def pair(i, carry):
            r = pl.ds(pl.multiple_of(i * STEP, STEP), STEP)
            carry = list(carry)
            for k in range(NE):
                e = columns(k)
                far = [gsc[b, q, r, e] + gsc[READ_BLOCKS + b, q, r, e] for b in range(READ_BLOCKS)]
                u = [angle(m, q, k) for m in range(3)]
                along = u[0] * far[1] + u[1] * far[2] + u[2] * far[3]
                term = side[q, 0, r, e] * far[0] + side[q, 1, r, e] * along
                carry[4 * k] = carry[4 * k] + fold(term)
                own_q = side[q, 2, r, e]
                for m in range(3):
                    term = side[q, 3 + m, r, e] * along + own_q * far[1 + m]
                    carry[4 * k + 1 + m] = carry[4 * k + 1 + m] + fold(term)
            return tuple(carry)

        zero = jnp.zeros((8, S), F32)
        totals = lax.fori_loop(0, C // STEP, pair, (zero,) * (4 * NE))
        for k in range(NE):
            for i in range(4):
                row = jnp.sum(totals[4 * k + i], axis=0, keepdims=True)
                sums[i, pl.ds(NE * q + k, 1), :] = row
        return outer

    lax.fori_loop(0, COUNT, pairs, 0)

    t_rho, g_x, g_y, g_z = (sums[i] for i in range(4))
    u_x, u_y, u_z, inverse = ang[0], ang[1], ang[2], inverses[...]
    radial_part = t_rho - (u_x * g_x + u_y * g_y + u_z * g_z) * inverse
    grad[...] = jnp.zeros_like(grad)
    grad[0] = radial_part * u_x + g_x * inverse
    grad[1] = radial_part * u_y + g_y * inverse
    grad[2] = radial_part * u_z + g_z * inverse

    def at_atoms(q):
        return (grad[:, NE * q, :] + grad[:, NE * q + 1, :]) + grad[:, NE * q + 2, :]

    force_copies = []
    for i, dy in ((0, -1), (1, 1)):
        force_copies.append(
            remote(force_y.at[i], force_y_in.at[1 - i], force_send.at[i], force_recv.at[i], (0, dy))
        )
    for i, (p, dx) in enumerate(((0, 1), (1, -1))):
        force_copies.append(
            remote(force_x.at[p], force_x_in.at[p], force_send.at[2 + i], force_recv.at[2 + i], (dx, 0))
        )
    parts = []
    for p in range(NP):
        used = [NE * (NP * y + p) + k for y in range(3) for k in range(NE)]
        parts.append(in_parts(jnp.concatenate([grad[:, row, :] for row in used], axis=1)))
    total = [at_atoms(p) for p in range(NP)]
    for p in range(NP):
        out = whole(jnp.transpose(dot(oh[p], parts[p], (1, 1))))
        force_x[1 - p] = -out[:, 2 * S :]
        force_copies[3 - p].start()
        for i in range(NP):
            total[i] = total[i] - out[:, i * S : (i + 1) * S]
    for i in range(2):
        for p in range(NP):
            force_y[i, p] = at_atoms(NP * (1 + i) + p)
        force_copies[i].start()
    for copy in force_copies:
        copy.wait_recv()
    for p in range(NP):
        value = (total[p] + force_x_in[p]) + (force_y_in[0, p] + force_y_in[1, p])
        for m in range(3):
            forces[p, m] = value[m : m + 1]

    for copy in (*mix_x, *mix_y, *force_copies):
        copy.wait_send()
    write.wait()


def solution(mesh):
    gx_size, yz_size = mesh.shape["gx"], mesh.shape["yz"]

    def body(features, positions, *rest):
        args = (features, jnp.transpose(positions, (0, 2, 1, 3)), *rest)
        vmem = pl.BlockSpec(memory_space=pltpu.VMEM)
        anywhere = pl.BlockSpec(memory_space=pl.ANY)
        dma = pltpu.SemaphoreType.DMA

        def run_all(*refs):
            kernel(gx_size, yz_size, *refs)

        small = [pltpu.VMEM(x.shape, x.dtype) for x in args[1:]]
        new_features, force = pl.pallas_call(
            run_all,
            out_shape=(
                jax.ShapeDtypeStruct((NP, 1, S, BLOCKS * C), BF16),
                jax.ShapeDtypeStruct((NP, 3, 1, S), F32),
            ),
            in_specs=[anywhere] * 10,
            out_specs=(anywhere, vmem),
            scratch_shapes=small
            + [
                *[pltpu.VMEM((4, hi - lo, C, S), BF16) for lo, hi in GROUPS],
                *[pltpu.VMEM((8, hi - lo, C, S), BF16) for lo, hi in GROUPS2],
                pltpu.VMEM((len(SUMS), 2, NP, 3, C, S), BF16),
                pltpu.VMEM((len(SUMS), 2, NP, 3, C, S), BF16),
                pltpu.VMEM((3, 4, 16, S), F32),
                pltpu.VMEM((NP, 3 * S, 3 * ROWS), BF16),
                pltpu.VMEM((7, COUNT, C, ROWS), F32),
                pltpu.VMEM((COUNT, 3, C, ROWS), F32),
                pltpu.VMEM((10 * C, 32), BF16),
                pltpu.VMEM((4 * C, C), BF16),
                pltpu.VMEM((64, EDGE_ROWS, S), F32),
                pltpu.VMEM((8, EDGE_ROWS, S), F32),
                pltpu.VMEM((EDGE_ROWS, 8, S), F32),
                pltpu.VMEM((EDGE_ROWS, S), F32),
                pltpu.VMEM((EDGE_ROWS, S), F32),
                pltpu.VMEM((4, EDGE_ROWS, S), F32),
                pltpu.VMEM((BLOCKS, COUNT, C, S), F32),
                pltpu.VMEM((NP, C, S), F32),
                pltpu.VMEM((BLOCKS, COUNT, C, ROWS), F32),
                pltpu.VMEM((NP, 1, S, BLOCKS * C), BF16),
                pltpu.VMEM((NP, 1, S, BLOCKS * C), BF16),
                pltpu.VMEM((COUNT, 6, C, ROWS), F32),
                pltpu.VMEM((4, EDGE_ROWS, S), F32),
                pltpu.VMEM((8, EDGE_ROWS, S), F32),
                pltpu.VMEM((2, NP, 8, S), F32),
                pltpu.VMEM((2, NP, 8, S), F32),
                pltpu.VMEM((NP, 8, S), F32),
                pltpu.VMEM((NP, 8, S), F32),
                dma((len(small),)),
                dma,
                dma,
                dma((4,)),
                dma((4,)),
                dma((len(GROUPS), 2)),
                dma((len(GROUPS), 2)),
                dma((len(SUMS), 2)),
                dma((len(SUMS), 2)),
                dma((len(GROUPS2), 4)),
                dma((len(GROUPS2), 4)),
                dma((4,)),
                dma((4,)),
            ],
            compiler_params=pltpu.CompilerParams(
                collective_id=0, has_side_effects=True, vmem_limit_bytes=60 * 1024 * 1024
            ),
            cost_estimate=pl.CostEstimate(
                flops=6 * 10**9, bytes_accessed=2 * 10**6, transcendentals=10**5
            ),
        )(*args)
        new_features, force = pl.pallas_call(
            deliver,
            out_shape=(
                jax.ShapeDtypeStruct((NP, 1, S, BLOCKS * C), BF16),
                jax.ShapeDtypeStruct((NP, 3, 1, S), F32),
            ),
            in_specs=[anywhere] * 2,
            out_specs=(anywhere, anywhere),
            scratch_shapes=[
                pltpu.VMEM((NP, 1, S, BLOCKS * C), BF16),
                pltpu.VMEM((NP, 3, 1, S), F32),
                dma((2, 1 + NP)),
            ],
            compiler_params=pltpu.CompilerParams(vmem_limit_bytes=60 * 1024 * 1024),
            cost_estimate=pl.CostEstimate(flops=0, bytes_accessed=12 * 10**5, transcendentals=0),
        )(new_features, force)
        return new_features, jnp.transpose(force, (0, 2, 1, 3))

    in_specs = (
        P("gx", "yz", None, None),
        P("gx", "yz", None, None),
        P(None, "gx", "yz", None),
        P(None, "gx", "yz", None),
        P(),
        P(),
        P(),
        P(),
        P(),
        P(),
    )
    out_specs = (P("gx", "yz", None, None), P("gx", "yz", None, None))
    return jax.shard_map(body, mesh=mesh, in_specs=in_specs, out_specs=out_specs, check_vma=False)
```

```python
import math

import jax
import jax.numpy as jnp
from jax import lax
from jax.experimental import pallas as pl
from jax.experimental.pallas import tpu as pltpu
from jax.sharding import PartitionSpec as P

MESH = pl.DeviceIdType.MESH
F32 = jnp.float32
BF16 = jnp.bfloat16
SOFTENING = 0.25
SPACING = 0.6
ROOT_THREE = math.sqrt(3.0)
C = 128
S = 128
NB = 8
NE = 3
NP = 2
BLOCKS = 9
READ_BLOCKS = 4
ROWS = NE * S
STEP = 32
GROUPS = ((0, 4), (4, 6), (6, 8), (8, 9))
SUMS = ((1, 2, 3), (4, 5), (6, 7), (8, 0))
GROUPS2 = ((0, 2), (2, 4))
COUNT = 6
EDGE_ROWS = 24
NEIGHBOURS = ((-1, 0), (1, 0), (0, -1), (0, 1))


def split(x):
    high = x.astype(BF16).astype(F32)
    return high, x - high


def dot(a, b, contract=(1, 0)):
    dims = (((contract[0],), (contract[1],)), ((), ()))
    return lax.dot_general(a, b, dims, preferred_element_type=F32)


def deliver(mixed, forces, mixed_out, forces_out, held, held_forces, sems):
    parts = [(forces, held_forces, forces_out)]
    parts += [(mixed.at[p], held.at[p], mixed_out.at[p]) for p in range(NP)]
    reads = [pltpu.make_async_copy(a, b, sems.at[0, i]) for i, (a, b, _) in enumerate(parts)]
    writes = [pltpu.make_async_copy(b, c, sems.at[1, i]) for i, (_, b, c) in enumerate(parts)]
    for copy in reads:
        copy.start()
    for read, write in zip(reads, writes):
        read.wait()
        write.start()
    for copy in writes:
        copy.wait()


def kernel(
    gx_size,
    yz_size,
    feat,
    *refs,
):
    small_in, refs = refs[:9], refs[9:]
    mixed, forces, *refs = refs
    small, refs = refs[:9], refs[9:]
    run(gx_size, yz_size, feat, small_in, small, mixed, forces, *refs)


def run(
    gx_size,
    yz_size,
    feat,
    small_in,
    small,
    mixed,
    forces,
    ext0,
    ext1,
    ext2,
    ext3,
    mix0,
    mix1,
    *refs,
):
    n = len(SUMS)
    part_out, part_in, refs = refs[:n], refs[n : 2 * n], refs[2 * n :]
    (
        posx,
        oh,
        coef,
        readout,
        wide,
        w_turned,
        zf,
        ang,
        pj,
        inverses,
        target,
        edges,
        acc,
        gate,
        gsc,
        raw,
        mix_out,
        side,
        sums,
        grad,
        force_y,
        force_y_in,
        force_x,
        force_x_in,
        small_sem,
        load_sem,
        out_sem,
        pos_send,
        pos_recv,
        x_send,
        x_recv,
        part_send,
        part_recv,
        mix_send,
        mix_recv,
        force_send,
        force_recv,
    ) = refs
    ext, ext2 = (ext0, ext1, ext2, ext3), (mix0, mix1)
    gx = lax.axis_index("gx")
    yz = lax.axis_index("yz")

    def device(dx, dy):
        return (lax.rem(gx + dx + gx_size, gx_size), lax.rem(yz + dy + yz_size, yz_size))

    def remote(src, dst, send, recv, step):
        return pltpu.make_async_remote_copy(
            src_ref=src,
            dst_ref=dst,
            send_sem=send,
            recv_sem=recv,
            device_id=device(*step),
            device_id_type=MESH,
        )

    small_loads = [
        pltpu.make_async_copy(small_in[i], small[i], small_sem.at[i]) for i in range(len(small))
    ]
    feat_load = pltpu.make_async_copy(feat, raw, load_sem)
    feat_load.start()
    for load in small_loads:
        load.start()
    pos, dst, shift, wr, wq, w_scalar, w_gate, w_vector, w_tensor = small

    barrier = pltpu.get_barrier_semaphore()
    for step in NEIGHBOURS:
        pl.semaphore_signal(barrier, inc=1, device_id=device(*step), device_id_type=MESH)

    def turn(g):
        lo, hi = GROUPS[g]
        for i in range(hi - lo):
            for p in range(NP):
                tile = raw[p, 0, :, pl.ds((lo + i) * C, C)].astype(F32)
                ext[g][p, i] = jnp.transpose(tile).astype(BF16)

    feat_load.wait()
    turn(0)
    pl.semaphore_wait(barrier, len(NEIGHBOURS))

    x_copies = []
    for g in range(len(GROUPS)):
        for own, ghost, dx in ((0, 2, -1), (1, 3, 1)):
            x_copies.append(
                remote(ext[g].at[own], ext[g].at[ghost], x_send.at[g, own], x_recv.at[g, own], (dx, 0))
            )
    x_copies[0].start()
    x_copies[1].start()

    for load in small_loads:
        load.wait()
    for p in range(NP):
        posx[0, p] = jnp.zeros((16, S), F32)
        for m in range(3):
            posx[0, p, pl.ds(m, 1), :] = pos[p, m]
        for k in range(NE):
            posx[0, p, pl.ds(3 + k, 1), :] = dst[k, p].astype(F32)
            posx[0, p, pl.ds(6 + k, 1), :] = shift[k, p].astype(F32)
    own = pl.ds(0, NP)
    pos_copies = [
        remote(posx.at[0, 0], posx.at[0, 2], pos_send.at[0], pos_recv.at[0], (-1, 0)),
        remote(posx.at[0, 1], posx.at[0, 3], pos_send.at[1], pos_recv.at[1], (1, 0)),
        remote(posx.at[0, own], posx.at[2, own], pos_send.at[2], pos_recv.at[2], (0, -1)),
        remote(posx.at[0, own], posx.at[1, own], pos_send.at[3], pos_recv.at[3], (0, 1)),
    ]
    for copy in pos_copies:
        copy.start()
    for g in range(1, len(GROUPS)):
        turn(g)
        x_copies[2 * g].start()
        x_copies[2 * g + 1].start()

    def turned(w):
        high, low = split(w)
        rows = jnp.concatenate([high, low, high, jnp.zeros_like(w)], axis=0)
        return jnp.transpose(rows).astype(BF16)

    def widen(f, carry):
        at = pl.ds(pl.multiple_of(f * C, C), C)
        wide[at, :] = turned(wr[:, at])
        return carry

    lax.fori_loop(0, 7, widen, 0)

    for copy in pos_copies:
        copy.wait_recv()
    edges[...] = jnp.zeros_like(edges)
    for q in range(COUNT):
        y, p = q // NP, q % NP
        at = pl.ds(NE * q, NE)
        edges[0, at, :] = posx[y, p, pl.ds(3, NE), :]
        edges[1, at, :] = posx[y, p, pl.ds(6, NE), :]
        edges[2, at, :] = jnp.full((NE, S), p, F32)
        edges[3, at, :] = jnp.full((NE, S), (1, 0, 2)[y], F32)
    place = edges[0]
    one = jnp.ones_like(place)
    nil = jnp.zeros_like(place)

    def at_least(x, bound):
        return jnp.where(x >= float(bound), one, nil)

    ext_x = at_least(place, 3 * S) + at_least(place, 6 * S) + at_least(place, 9 * S)
    left = place - ext_x * float(3 * S)
    ext_y = at_least(left, S) + at_least(left, 2 * S)
    step_x = ext_x - 1.0 - edges[2]
    step_y = ext_y - 1.0
    target[...] = jnp.where(edges[3] + step_y == 1.0, ext_x * S + (left - ext_y * S), -1.0)

    atom = lax.broadcasted_iota(jnp.int32, (S, ROWS), 0).astype(F32)

    def pick(y, carry):
        for p in range(NP):
            rows = [target[pl.ds(NE * (NP * y + p) + k, 1), :] for k in range(NE)]
            ends = jnp.concatenate(rows, axis=1) - atom
            for i, x in enumerate((1, 2, 3 * p)):
                hit = jnp.where(ends == float(x * S), 1.0, 0.0).astype(BF16)
                oh[p, pl.ds(i * S, S), pl.ds(pl.multiple_of(y * ROWS, ROWS), ROWS)] = hit
        return carry

    lax.fori_loop(0, 3, pick, 0)

    def in_parts(x):
        first, rest = split(x)
        second, third = split(rest)
        return jnp.concatenate([first, second, third, jnp.zeros_like(first)], 0).astype(BF16)

    def whole(x):
        return (x[0:8] + x[8:16]) + x[16:24]

    pj[...] = jnp.zeros_like(pj)
    for p in range(NP):
        near = [posx[0, slot, pl.ds(0, 8), :] for slot in (0, 1, 3 - p)]
        far = whole(dot(in_parts(jnp.concatenate(near, axis=1)), oh[p]))
        for y in range(3):
            for k in range(NE):
                at = (NE * y + k) * S
                pj[NE * (NP * y + p) + k] = far[:, at : at + S] - posx[y, p, pl.ds(0, 8), :]

    disp_x = pj[:, 0, :] + step_x
    disp_y = pj[:, 1, :] + step_y
    disp_z = pj[:, 2, :] + edges[1]
    rho = jnp.sqrt(disp_x * disp_x + disp_y * disp_y + disp_z * disp_z + SOFTENING)
    inverse = 1.0 / rho
    u_x, u_y, u_z = disp_x * inverse, disp_y * inverse, disp_z * inverse
    inverses[...] = inverse
    length_sq = u_x * u_x + u_y * u_y + u_z * u_z
    angular = (
        u_x,
        u_y,
        u_z,
        ROOT_THREE * u_x * u_y,
        ROOT_THREE * u_y * u_z,
        0.5 * (3.0 * u_z * u_z - length_sq),
        ROOT_THREE * u_x * u_z,
        0.5 * ROOT_THREE * (u_x * u_x - u_y * u_y),
    )
    for f in range(8):
        ang[f] = angular[f]
    zf[...] = jnp.zeros_like(zf)
    for b in range(NB):
        off = (rho - (0.5 + SPACING * b)) / SPACING
        basis = jnp.exp(-(off * off))
        slope = basis * off * (-2.0 / SPACING)
        for i, value in enumerate((basis, slope)):
            high, low = split(value)
            zf[32 * i + b] = high
            zf[32 * i + 8 + b] = high
            zf[32 * i + 16 + b] = low

    def columns(k):
        return pl.ds(k * S, S)

    def expanded(q, part, rows):
        edge_rows = [zf[pl.ds(32 * part, 32), NE * q + k, :] for k in range(NP * NE)]
        return dot(rows, jnp.concatenate(edge_rows, axis=1).astype(BF16))

    for q in range(0, COUNT, NP):
        out = expanded(q, 0, wide[pl.ds(0, 7 * C), :])
        for f in range(7):
            for p in range(NP):
                coef[f, q + p] = out[f * C : (f + 1) * C, p * ROWS : (p + 1) * ROWS]

    def columns(k):
        return pl.ds(k * S, S)

    def gather(bufs, g, to, first, last):
        buf = bufs[g]
        n = buf.shape[1]

        for p in range(NP):
            tiles = [buf[slot].reshape(n * C, S) for slot in (0, 1, 3 - p)[first:last]]
            out = dot(jnp.concatenate(tiles, axis=1), oh[p, pl.ds(first * S, (last - first) * S), :])
            for i in range(n):
                for y in range(3):
                    gsc[to + i, NP * y + p] = out[i * C : (i + 1) * C, y * ROWS : (y + 1) * ROWS]

    def each_row(fn, lo, hi):
        steps = C // STEP

        def run(i, carry):
            q = i // steps
            fn(q, pl.ds(pl.multiple_of((i - q * steps) * STEP, STEP), STEP))
            return carry

        lax.fori_loop(lo * steps, hi * steps, run, 0)

    def angle(f, q, k):
        return ang[f, pl.ds(NE * q + k, 1), :]

    def message_sv(p, r):
        total = [jnp.zeros((STEP, S), F32) for _ in range(BLOCKS)]
        for k in range(NE):
            e = columns(k)
            s = gsc[0, p, r, e]
            v = [gsc[1 + m, p, r, e] for m in range(3)]
            u = [angle(m, p, k) for m in range(3)]
            along = u[0] * v[0] + u[1] * v[1] + u[2] * v[2]
            total[0] = total[0] + coef[0, p, r, e] * s + coef[1, p, r, e] * along
            r3s = coef[3, p, r, e] * s
            r4 = coef[4, p, r, e]
            for m in range(3):
                total[1 + m] = total[1 + m] + r3s * u[m] + r4 * v[m]
            r5s = coef[5, p, r, e] * s
            for n in range(5):
                total[4 + n] = total[4 + n] + r5s * angle(3 + n, p, k)
        for b in range(BLOCKS):
            acc[b, p, r, :] = total[b]

    def message_t(lo, hi):
        def fn(p, r):
            total = [acc[b, p, r, :] for b in (0, *range(lo, hi))]
            for k in range(NE):
                e = columns(k)
                along = None
                r6 = coef[6, p, r, e]
                for n in range(lo, hi):
                    t = gsc[n, p, r, e]
                    term = angle(n - 1, p, k) * t
                    along = term if along is None else along + term
                    total[1 + n - lo] = total[1 + n - lo] + r6 * t
                total[0] = total[0] + coef[2, p, r, e] * along
            for i, b in enumerate((0, *range(lo, hi))):
                acc[b, p, r, :] = total[i]

        return fn

    third = 1.0 / NE

    def mix(lo, hi, w):
        def run(p, carry):
            terms = [(acc[b, p] * third).astype(BF16) for b in range(lo, hi)]
            out = dot(w_turned[pl.ds(w * C, C), :], jnp.concatenate(terms, axis=1))
            for b in range(lo, hi):
                acc[b, p] = out[:, (b - lo) * S : (b - lo + 1) * S]
            return carry

        lax.fori_loop(0, NP, run, 0)

    part_copies = []
    for h in range(len(SUMS)):
        for i, dy in ((0, -1), (1, 1)):
            part_copies.append(
                remote(
                    part_out[h].at[i],
                    part_in[h].at[1 - i],
                    part_send.at[h, i],
                    part_recv.at[h, i],
                    (0, dy),
                )
            )

    def send_sums(h):
        for i in range(2):
            for p in range(NP):
                for j, b in enumerate(SUMS[h]):
                    part_out[h][i, p, j] = acc[b, NP * (1 + i) + p].astype(BF16)
            part_copies[2 * h + i].start()

    def add_sums(h):
        for i in range(2):
            part_copies[2 * h + i].wait_recv()
        for p in range(NP):
            for j, b in enumerate(SUMS[h]):
                acc[b, p] = acc[b, p] + part_in[h][0, p, j].astype(F32) + part_in[h][1, p, j].astype(F32)

    for g, (lo, hi) in enumerate(GROUPS):
        x_copies[2 * g].wait_recv()
        x_copies[2 * g + 1].wait_recv()
        gather(ext, g, lo, 0, 3)
        if g == 0:
            each_row(message_sv, 0, COUNT)
        else:
            each_row(message_t(lo, hi), 0, COUNT)
        send_sums(g)

    wide[pl.ds(8 * C, C), :] = turned(wq[:, pl.ds(0, C)])
    last = turned(wq[:, pl.ds(C, C)])
    wide[pl.ds(7 * C, C), :] = last
    wide[pl.ds(9 * C, C), :] = last
    for i, w in enumerate((w_scalar, w_gate, w_vector, w_tensor)):
        w_turned[pl.ds(i * C, C), :] = jnp.transpose(w[...].astype(F32)).astype(BF16)
    for q in range(0, COUNT, NP):
        outs = [expanded(q, 0, wide[pl.ds(7 * C, C), :]), expanded(q, 1, wide[pl.ds(8 * C, 2 * C), :])]
        for p in range(NP):
            at = slice(p * ROWS, (p + 1) * ROWS)
            readout[q + p, 0] = outs[0][:, at]
            readout[q + p, 1] = outs[1][0:C, at]
            readout[q + p, 2] = outs[1][C : 2 * C, at]
    add_sums(0)
    mix(1, 4, 2)
    add_sums(1)
    add_sums(2)
    add_sums(3)

    def scalars(p, carry):
        out = dot(w_turned[pl.ds(0, 2 * C), :], (acc[0, p] * third).astype(BF16))
        pre = out[0:C]
        acc[0, p] = pre * jax.nn.sigmoid(pre)
        gate[p] = jax.nn.sigmoid(out[C : 2 * C])
        return carry

    lax.fori_loop(0, NP, scalars, 0)

    def read_block(b, y, slot):
        g = b // 2
        return ext2[g].at[y, slot, b - GROUPS2[g][0]]

    def read_block(b, at):
        return ext2[b // 2].at[at, b % 2]

    def update_sv(p, r):
        g = gate[p, r, :]
        for b in range(READ_BLOCKS):
            old = ext[0][p, b, r, :].astype(F32)
            step = g * acc[b, p, r, :] if b > 0 else acc[0, p, r, :]
            read_block(b, p)[r, :] = (old + step).astype(BF16)

    each_row(update_sv, 0, NP)
    mix_x, mix_y = [], []
    for g, buf in enumerate(ext2):
        spans = (
            (mix_x, buf.at[0], buf.at[2], (-1, 0)),
            (mix_x, buf.at[1], buf.at[3], (1, 0)),
            (mix_y, buf.at[own], buf.at[pl.ds(6, NP)], (0, -1)),
            (mix_y, buf.at[own], buf.at[pl.ds(4, NP)], (0, 1)),
        )
        for n, (into, src, to, step) in enumerate(spans):
            into.append(remote(src, to, mix_send.at[g, n], mix_recv.at[g, n], step))
    for copy in (*mix_x, *mix_y):
        copy.start()

    def results(lo, hi, value):
        for i in range(hi - lo):
            for p in range(NP):
                mix_out[p, 0, :, pl.ds((lo + i) * C, C)] = jnp.transpose(value(p, i)).astype(BF16)

    mix(4, 9, 3)
    for g, (lo, hi) in enumerate(GROUPS2):
        results(lo, hi, lambda p, i: ext2[g][p, i].astype(F32))
    for g, (lo, hi) in enumerate(GROUPS):
        if g > 0:
            results(lo, hi, lambda p, i: ext[g][p, i].astype(F32) + gate[p] * acc[lo + i, p])
    write = pltpu.make_async_copy(mix_out, mixed, out_sem)
    write.start()

    def near_side(q, r):
        at = jnp.where(q < NP, q, q + 2)
        row = [read_block(b, at)[r, :].astype(F32) for b in range(READ_BLOCKS)]
        s, v = row[0], row[1:]
        for k in range(NE):
            e = columns(k)
            u = [angle(m, q, k) for m in range(3)]
            along = u[0] * v[0] + u[1] * v[1] + u[2] * v[2]
            q1 = readout[q, 0, r, e]
            side[q, 0, r, e] = readout[q, 1, r, e] * s
            side[q, 1, r, e] = readout[q, 2, r, e] * along
            side[q, 2, r, e] = q1 * along
            for m in range(3):
                side[q, 3 + m, r, e] = q1 * v[m]

    for g, (lo, hi) in enumerate(GROUPS2):
        gather(ext2, g, lo, 0, 2)
    each_row(near_side, 0, NP)
    for copy in mix_y:
        copy.wait_recv()
    each_row(near_side, NP, COUNT)
    for copy in (*pos_copies, *x_copies, *part_copies):
        copy.wait_send()
    for g, (lo, hi) in enumerate(GROUPS2):
        mix_x[2 * g].wait_recv()
        mix_x[2 * g + 1].wait_recv()
        gather(ext2, g, READ_BLOCKS + lo, 2, 3)

    def fold(x):
        return sum(x[8 * i : 8 * i + 8] for i in range(1, STEP // 8)) + x[0:8]

    sums[...] = jnp.zeros_like(sums)

    def pairs(q, outer):
        def pair(i, carry):
            r = pl.ds(pl.multiple_of(i * STEP, STEP), STEP)
            carry = list(carry)
            for k in range(NE):
                e = columns(k)
                far = [gsc[b, q, r, e] + gsc[READ_BLOCKS + b, q, r, e] for b in range(READ_BLOCKS)]
                u = [angle(m, q, k) for m in range(3)]
                along = u[0] * far[1] + u[1] * far[2] + u[2] * far[3]
                term = side[q, 0, r, e] * far[0] + side[q, 1, r, e] * along
                carry[4 * k] = carry[4 * k] + fold(term)
                own_q = side[q, 2, r, e]
                for m in range(3):
                    term = side[q, 3 + m, r, e] * along + own_q * far[1 + m]
                    carry[4 * k + 1 + m] = carry[4 * k + 1 + m] + fold(term)
            return tuple(carry)

        zero = jnp.zeros((8, S), F32)
        totals = lax.fori_loop(0, C // STEP, pair, (zero,) * (4 * NE))
        for k in range(NE):
            for i in range(4):
                row = jnp.sum(totals[4 * k + i], axis=0, keepdims=True)
                sums[i, pl.ds(NE * q + k, 1), :] = row
        return outer

    lax.fori_loop(0, COUNT, pairs, 0)

    t_rho, g_x, g_y, g_z = (sums[i] for i in range(4))
    u_x, u_y, u_z, inverse = ang[0], ang[1], ang[2], inverses[...]
    radial_part = t_rho - (u_x * g_x + u_y * g_y + u_z * g_z) * inverse
    grad[...] = jnp.zeros_like(grad)
    grad[0] = radial_part * u_x + g_x * inverse
    grad[1] = radial_part * u_y + g_y * inverse
    grad[2] = radial_part * u_z + g_z * inverse

    def at_atoms(q):
        return (grad[:, NE * q, :] + grad[:, NE * q + 1, :]) + grad[:, NE * q + 2, :]

    force_copies = []
    for i, dy in ((0, -1), (1, 1)):
        force_copies.append(
            remote(force_y.at[i], force_y_in.at[1 - i], force_send.at[i], force_recv.at[i], (0, dy))
        )
    for i, (p, dx) in enumerate(((0, 1), (1, -1))):
        force_copies.append(
            remote(force_x.at[p], force_x_in.at[p], force_send.at[2 + i], force_recv.at[2 + i], (dx, 0))
        )
    parts = []
    for p in range(NP):
        used = [NE * (NP * y + p) + k for y in range(3) for k in range(NE)]
        parts.append(in_parts(jnp.concatenate([grad[:, row, :] for row in used], axis=1)))
    total = [at_atoms(p) for p in range(NP)]
    for p in range(NP):
        out = whole(jnp.transpose(dot(oh[p], parts[p], (1, 1))))
        force_x[1 - p] = -out[:, 2 * S :]
        force_copies[3 - p].start()
        for i in range(NP):
            total[i] = total[i] - out[:, i * S : (i + 1) * S]
    for i in range(2):
        for p in range(NP):
            force_y[i, p] = at_atoms(NP * (1 + i) + p)
        force_copies[i].start()
    for copy in force_copies:
        copy.wait_recv()
    for p in range(NP):
        value = (total[p] + force_x_in[p]) + (force_y_in[0, p] + force_y_in[1, p])
        for m in range(3):
            forces[p, m] = value[m : m + 1]

    for copy in (*mix_x, *mix_y, *force_copies):
        copy.wait_send()
    write.wait()


def solution(mesh):
    gx_size, yz_size = mesh.shape["gx"], mesh.shape["yz"]

    def body(features, positions, *rest):
        args = (features, jnp.transpose(positions, (0, 2, 1, 3)), *rest)
        vmem = pl.BlockSpec(memory_space=pltpu.VMEM)
        anywhere = pl.BlockSpec(memory_space=pl.ANY)
        dma = pltpu.SemaphoreType.DMA

        def run_all(*refs):
            kernel(gx_size, yz_size, *refs)

        small = [pltpu.VMEM(x.shape, x.dtype) for x in args[1:]]
        new_features, force = pl.pallas_call(
            run_all,
            out_shape=(
                jax.ShapeDtypeStruct((NP, 1, S, BLOCKS * C), BF16),
                jax.ShapeDtypeStruct((NP, 3, 1, S), F32),
            ),
            in_specs=[anywhere] * 10,
            out_specs=(anywhere, vmem),
            scratch_shapes=small
            + [
                *[pltpu.VMEM((4, hi - lo, C, S), BF16) for lo, hi in GROUPS],
                *[pltpu.VMEM((8, hi - lo, C, S), BF16) for lo, hi in GROUPS2],
                *[pltpu.VMEM((2, NP, len(blocks), C, S), BF16) for blocks in SUMS],
                *[pltpu.VMEM((2, NP, len(blocks), C, S), BF16) for blocks in SUMS],
                pltpu.VMEM((3, 4, 16, S), F32),
                pltpu.VMEM((NP, 3 * S, 3 * ROWS), BF16),
                pltpu.VMEM((7, COUNT, C, ROWS), F32),
                pltpu.VMEM((COUNT, 3, C, ROWS), F32),
                pltpu.VMEM((10 * C, 32), BF16),
                pltpu.VMEM((4 * C, C), BF16),
                pltpu.VMEM((64, EDGE_ROWS, S), F32),
                pltpu.VMEM((8, EDGE_ROWS, S), F32),
                pltpu.VMEM((EDGE_ROWS, 8, S), F32),
                pltpu.VMEM((EDGE_ROWS, S), F32),
                pltpu.VMEM((EDGE_ROWS, S), F32),
                pltpu.VMEM((4, EDGE_ROWS, S), F32),
                pltpu.VMEM((BLOCKS, COUNT, C, S), F32),
                pltpu.VMEM((NP, C, S), F32),
                pltpu.VMEM((BLOCKS, COUNT, C, ROWS), F32),
                pltpu.VMEM((NP, 1, S, BLOCKS * C), BF16),
                pltpu.VMEM((NP, 1, S, BLOCKS * C), BF16),
                pltpu.VMEM((COUNT, 6, C, ROWS), F32),
                pltpu.VMEM((4, EDGE_ROWS, S), F32),
                pltpu.VMEM((8, EDGE_ROWS, S), F32),
                pltpu.VMEM((2, NP, 8, S), F32),
                pltpu.VMEM((2, NP, 8, S), F32),
                pltpu.VMEM((NP, 8, S), F32),
                pltpu.VMEM((NP, 8, S), F32),
                dma((len(small),)),
                dma,
                dma,
                dma((4,)),
                dma((4,)),
                dma((len(GROUPS), 2)),
                dma((len(GROUPS), 2)),
                dma((len(SUMS), 2)),
                dma((len(SUMS), 2)),
                dma((len(GROUPS2), 4)),
                dma((len(GROUPS2), 4)),
                dma((4,)),
                dma((4,)),
            ],
            compiler_params=pltpu.CompilerParams(
                collective_id=0, has_side_effects=True, vmem_limit_bytes=60 * 1024 * 1024
            ),
            cost_estimate=pl.CostEstimate(
                flops=6 * 10**9, bytes_accessed=2 * 10**6, transcendentals=10**5
            ),
        )(*args)
        new_features, force = pl.pallas_call(
            deliver,
            out_shape=(
                jax.ShapeDtypeStruct((NP, 1, S, BLOCKS * C), BF16),
                jax.ShapeDtypeStruct((NP, 3, 1, S), F32),
            ),
            in_specs=[anywhere] * 2,
            out_specs=(anywhere, anywhere),
            scratch_shapes=[
                pltpu.VMEM((NP, 1, S, BLOCKS * C), BF16),
                pltpu.VMEM((NP, 3, 1, S), F32),
                dma((2, 1 + NP)),
            ],
            compiler_params=pltpu.CompilerParams(vmem_limit_bytes=60 * 1024 * 1024),
            cost_estimate=pl.CostEstimate(flops=0, bytes_accessed=12 * 10**5, transcendentals=0),
        )(new_features, force)
        return new_features, jnp.transpose(force, (0, 2, 1, 3))

    in_specs = (
        P("gx", "yz", None, None),
        P("gx", "yz", None, None),
        P(None, "gx", "yz", None),
        P(None, "gx", "yz", None),
        P(),
        P(),
        P(),
        P(),
        P(),
        P(),
    )
    out_specs = (P("gx", "yz", None, None), P("gx", "yz", None, None))
    return jax.shard_map(body, mesh=mesh, in_specs=in_specs, out_specs=out_specs, check_vma=False)
```

```python
import math

import jax
import jax.numpy as jnp
from jax import lax
from jax.experimental import pallas as pl
from jax.experimental.pallas import tpu as pltpu
from jax.sharding import PartitionSpec as P

MESH = pl.DeviceIdType.MESH
F32 = jnp.float32
BF16 = jnp.bfloat16
SOFTENING = 0.25
SPACING = 0.6
ROOT_THREE = math.sqrt(3.0)
C = 128
S = 128
NB = 8
NE = 3
NP = 2
BLOCKS = 9
READ_BLOCKS = 4
ROWS = NE * S
STEP = 32
GROUPS = ((0, 4), (4, 6), (6, 8), (8, 9))
SUMS = ((1, 2, 3), (4, 5), (6, 7), (8, 0))
GROUPS2 = ((0, 2), (2, 4))
COUNT = 6
EDGE_ROWS = 24
NEIGHBOURS = ((-1, 0), (1, 0), (0, -1), (0, 1))


def split(x):
    high = x.astype(BF16).astype(F32)
    return high, x - high


def dot(a, b, contract=(1, 0)):
    dims = (((contract[0],), (contract[1],)), ((), ()))
    return lax.dot_general(a, b, dims, preferred_element_type=F32)


def deliver(mixed, forces, mixed_out, forces_out, held, held_forces, sems):
    parts = [(forces, held_forces, forces_out)]
    for i in range(8):
        at = (i // 4, 0, pl.ds(i % 4 * (S // 4), S // 4))
        parts.append((mixed.at[at], held.at[at], mixed_out.at[at]))
    reads = [pltpu.make_async_copy(a, b, sems.at[0, i]) for i, (a, b, _) in enumerate(parts)]
    writes = [pltpu.make_async_copy(b, c, sems.at[1, i]) for i, (_, b, c) in enumerate(parts)]
    for copy in reads:
        copy.start()
    for read, write in zip(reads, writes):
        read.wait()
        write.start()
    for copy in writes:
        copy.wait()


def kernel(
    gx_size,
    yz_size,
    feat,
    *refs,
):
    small_in, refs = refs[:9], refs[9:]
    mixed, forces, *refs = refs
    small, refs = refs[:9], refs[9:]
    run(gx_size, yz_size, feat, small_in, small, mixed, forces, *refs)


def run(
    gx_size,
    yz_size,
    feat,
    small_in,
    small,
    mixed,
    forces,
    ext0,
    ext1,
    ext2,
    ext3,
    mix0,
    mix1,
    *refs,
):
    n = len(SUMS)
    part_out, part_in, refs = refs[:n], refs[n : 2 * n], refs[2 * n :]
    (
        posx,
        oh,
        coef,
        readout,
        wide,
        w_turned,
        zf,
        ang,
        pj,
        inverses,
        target,
        edges,
        acc,
        gate,
        gsc,
        raw,
        mix_out,
        side,
        sums,
        grad,
        force_y,
        force_y_in,
        force_x,
        force_x_in,
        small_sem,
        load_sem,
        out_sem,
        pos_send,
        pos_recv,
        x_send,
        x_recv,
        part_send,
        part_recv,
        mix_send,
        mix_recv,
        force_send,
        force_recv,
    ) = refs
    ext, ext2 = (ext0, ext1, ext2, ext3), (mix0, mix1)
    gx = lax.axis_index("gx")
    yz = lax.axis_index("yz")

    def device(dx, dy):
        return (lax.rem(gx + dx + gx_size, gx_size), lax.rem(yz + dy + yz_size, yz_size))

    def remote(src, dst, send, recv, step):
        return pltpu.make_async_remote_copy(
            src_ref=src,
            dst_ref=dst,
            send_sem=send,
            recv_sem=recv,
            device_id=device(*step),
            device_id_type=MESH,
        )

    barrier = pltpu.get_barrier_semaphore()
    for step in NEIGHBOURS:
        pl.semaphore_signal(barrier, inc=1, device_id=device(*step), device_id_type=MESH)

    small_loads = [
        pltpu.make_async_copy(small_in[i], small[i], small_sem.at[i]) for i in range(len(small))
    ]
    feat_load = pltpu.make_async_copy(feat, raw, load_sem)
    feat_load.start()
    for load in small_loads:
        load.start()
    pos, dst, shift, wr, wq, w_scalar, w_gate, w_vector, w_tensor = small

    def turn(g):
        lo, hi = GROUPS[g]
        for i in range(hi - lo):
            for p in range(NP):
                ext[g][p, i] = jnp.transpose(raw[p, 0, :, pl.ds((lo + i) * C, C)])

    feat_load.wait()
    turn(0)
    pl.semaphore_wait(barrier, len(NEIGHBOURS))

    x_copies = []
    for g in range(len(GROUPS)):
        for own, ghost, dx in ((0, 2, -1), (1, 3, 1)):
            x_copies.append(
                remote(ext[g].at[own], ext[g].at[ghost], x_send.at[g, own], x_recv.at[g, own], (dx, 0))
            )
    x_copies[0].start()
    x_copies[1].start()

    for load in small_loads:
        load.wait()
    for p in range(NP):
        posx[0, p] = jnp.zeros((16, S), F32)
        for m in range(3):
            posx[0, p, pl.ds(m, 1), :] = pos[p, m]
        for k in range(NE):
            posx[0, p, pl.ds(3 + k, 1), :] = dst[k, p].astype(F32)
            posx[0, p, pl.ds(6 + k, 1), :] = shift[k, p].astype(F32)
    own = pl.ds(0, NP)
    pos_copies = [
        remote(posx.at[0, 0], posx.at[0, 2], pos_send.at[0], pos_recv.at[0], (-1, 0)),
        remote(posx.at[0, 1], posx.at[0, 3], pos_send.at[1], pos_recv.at[1], (1, 0)),
        remote(posx.at[0, own], posx.at[2, own], pos_send.at[2], pos_recv.at[2], (0, -1)),
        remote(posx.at[0, own], posx.at[1, own], pos_send.at[3], pos_recv.at[3], (0, 1)),
    ]
    for copy in pos_copies:
        copy.start()
    for g in range(1, len(GROUPS)):
        turn(g)
        x_copies[2 * g].start()
        x_copies[2 * g + 1].start()

    def turned(w):
        high, low = split(w)
        rows = jnp.concatenate([high, low, high, jnp.zeros_like(w)], axis=0)
        return jnp.transpose(rows).astype(BF16)

    def widen(f, carry):
        at = pl.ds(pl.multiple_of(f * C, C), C)
        wide[at, :] = turned(wr[:, at])
        return carry

    lax.fori_loop(0, 7, widen, 0)

    for copy in pos_copies:
        copy.wait_recv()
    edges[...] = jnp.zeros_like(edges)
    for q in range(COUNT):
        y, p = q // NP, q % NP
        at = pl.ds(NE * q, NE)
        edges[0, at, :] = posx[y, p, pl.ds(3, NE), :]
        edges[1, at, :] = posx[y, p, pl.ds(6, NE), :]
        edges[2, at, :] = jnp.full((NE, S), p, F32)
        edges[3, at, :] = jnp.full((NE, S), (1, 0, 2)[y], F32)
    place = edges[0]
    one = jnp.ones_like(place)
    nil = jnp.zeros_like(place)

    def at_least(x, bound):
        return jnp.where(x >= float(bound), one, nil)

    ext_x = at_least(place, 3 * S) + at_least(place, 6 * S) + at_least(place, 9 * S)
    left = place - ext_x * float(3 * S)
    ext_y = at_least(left, S) + at_least(left, 2 * S)
    step_x = ext_x - 1.0 - edges[2]
    step_y = ext_y - 1.0
    target[...] = jnp.where(edges[3] + step_y == 1.0, ext_x * S + (left - ext_y * S), -1.0)

    atom = lax.broadcasted_iota(jnp.int32, (S, ROWS), 0).astype(F32)

    def pick(y, carry):
        for p in range(NP):
            rows = [target[pl.ds(NE * (NP * y + p) + k, 1), :] for k in range(NE)]
            ends = jnp.concatenate(rows, axis=1) - atom
            for i, x in enumerate((1, 2, 3 * p)):
                hit = jnp.where(ends == float(x * S), 1.0, 0.0).astype(BF16)
                oh[p, pl.ds(i * S, S), pl.ds(pl.multiple_of(y * ROWS, ROWS), ROWS)] = hit
        return carry

    lax.fori_loop(0, 3, pick, 0)

    def in_parts(x):
        first, rest = split(x)
        second, third = split(rest)
        return jnp.concatenate([first, second, third, jnp.zeros_like(first)], 0).astype(BF16)

    def whole(x):
        return (x[0:8] + x[8:16]) + x[16:24]

    pj[...] = jnp.zeros_like(pj)
    for p in range(NP):
        near = [posx[0, slot, pl.ds(0, 8), :] for slot in (0, 1, 3 - p)]
        far = whole(dot(in_parts(jnp.concatenate(near, axis=1)), oh[p]))
        for y in range(3):
            for k in range(NE):
                at = (NE * y + k) * S
                pj[NE * (NP * y + p) + k] = far[:, at : at + S] - posx[y, p, pl.ds(0, 8), :]

    disp_x = pj[:, 0, :] + step_x
    disp_y = pj[:, 1, :] + step_y
    disp_z = pj[:, 2, :] + edges[1]
    rho = jnp.sqrt(disp_x * disp_x + disp_y * disp_y + disp_z * disp_z + SOFTENING)
    inverse = 1.0 / rho
    u_x, u_y, u_z = disp_x * inverse, disp_y * inverse, disp_z * inverse
    inverses[...] = inverse
    length_sq = u_x * u_x + u_y * u_y + u_z * u_z
    angular = (
        u_x,
        u_y,
        u_z,
        ROOT_THREE * u_x * u_y,
        ROOT_THREE * u_y * u_z,
        0.5 * (3.0 * u_z * u_z - length_sq),
        ROOT_THREE * u_x * u_z,
        0.5 * ROOT_THREE * (u_x * u_x - u_y * u_y),
    )
    for f in range(8):
        ang[f] = angular[f]
    zf[...] = jnp.zeros_like(zf)
    for b in range(NB):
        off = (rho - (0.5 + SPACING * b)) / SPACING
        basis = jnp.exp(-(off * off))
        slope = basis * off * (-2.0 / SPACING)
        for i, value in enumerate((basis, slope)):
            high, low = split(value)
            zf[32 * i + b] = high
            zf[32 * i + 8 + b] = high
            zf[32 * i + 16 + b] = low

    def columns(k):
        return pl.ds(k * S, S)

    def expanded(q, part, rows):
        edge_rows = [zf[pl.ds(32 * part, 32), NE * q + k, :] for k in range(NP * NE)]
        return dot(rows, jnp.concatenate(edge_rows, axis=1).astype(BF16))

    for q in range(0, COUNT, NP):
        out = expanded(q, 0, wide[pl.ds(0, 7 * C), :])
        for f in range(7):
            for p in range(NP):
                coef[f, q + p] = out[f * C : (f + 1) * C, p * ROWS : (p + 1) * ROWS]

    def columns(k):
        return pl.ds(k * S, S)

    def gather(bufs, g, to, first, last):
        buf = bufs[g]
        n = buf.shape[1]

        for p in range(NP):
            tiles = [buf[slot].reshape(n * C, S) for slot in (0, 1, 3 - p)[first:last]]
            out = dot(jnp.concatenate(tiles, axis=1), oh[p, pl.ds(first * S, (last - first) * S), :])
            for i in range(n):
                for y in range(3):
                    gsc[to + i, NP * y + p] = out[i * C : (i + 1) * C, y * ROWS : (y + 1) * ROWS]

    def each_row(fn, lo, hi):
        steps = C // STEP

        def run(i, carry):
            q = i // steps
            fn(q, pl.ds(pl.multiple_of((i - q * steps) * STEP, STEP), STEP))
            return carry

        lax.fori_loop(lo * steps, hi * steps, run, 0)

    def angle(f, q, k):
        return ang[f, pl.ds(NE * q + k, 1), :]

    def message_sv(p, r):
        total = [jnp.zeros((STEP, S), F32) for _ in range(BLOCKS)]
        for k in range(NE):
            e = columns(k)
            s = gsc[0, p, r, e]
            v = [gsc[1 + m, p, r, e] for m in range(3)]
            u = [angle(m, p, k) for m in range(3)]
            along = u[0] * v[0] + u[1] * v[1] + u[2] * v[2]
            total[0] = total[0] + coef[0, p, r, e] * s + coef[1, p, r, e] * along
            r3s = coef[3, p, r, e] * s
            r4 = coef[4, p, r, e]
            for m in range(3):
                total[1 + m] = total[1 + m] + r3s * u[m] + r4 * v[m]
            r5s = coef[5, p, r, e] * s
            for n in range(5):
                total[4 + n] = total[4 + n] + r5s * angle(3 + n, p, k)
        for b in range(BLOCKS):
            acc[b, p, r, :] = total[b]

    def message_t(lo, hi):
        def fn(p, r):
            total = [acc[b, p, r, :] for b in (0, *range(lo, hi))]
            for k in range(NE):
                e = columns(k)
                along = None
                r6 = coef[6, p, r, e]
                for n in range(lo, hi):
                    t = gsc[n, p, r, e]
                    term = angle(n - 1, p, k) * t
                    along = term if along is None else along + term
                    total[1 + n - lo] = total[1 + n - lo] + r6 * t
                total[0] = total[0] + coef[2, p, r, e] * along
            for i, b in enumerate((0, *range(lo, hi))):
                acc[b, p, r, :] = total[i]

        return fn

    third = 1.0 / NE

    def mix(lo, hi, w):
        def run(p, carry):
            terms = [(acc[b, p] * third).astype(BF16) for b in range(lo, hi)]
            out = dot(w_turned[pl.ds(w * C, C), :], jnp.concatenate(terms, axis=1))
            for b in range(lo, hi):
                acc[b, p] = out[:, (b - lo) * S : (b - lo + 1) * S]
            return carry

        lax.fori_loop(0, NP, run, 0)

    part_copies = []
    for h in range(len(SUMS)):
        for i, dy in ((0, -1), (1, 1)):
            part_copies.append(
                remote(
                    part_out[h].at[i],
                    part_in[h].at[1 - i],
                    part_send.at[h, i],
                    part_recv.at[h, i],
                    (0, dy),
                )
            )

    def send_sums(h):
        for i in range(2):
            for p in range(NP):
                for j, b in enumerate(SUMS[h]):
                    part_out[h][i, p, j] = acc[b, NP * (1 + i) + p].astype(BF16)
            part_copies[2 * h + i].start()

    def add_sums(h):
        for i in range(2):
            part_copies[2 * h + i].wait_recv()
        for p in range(NP):
            for j, b in enumerate(SUMS[h]):
                acc[b, p] = acc[b, p] + part_in[h][0, p, j].astype(F32) + part_in[h][1, p, j].astype(F32)

    for g, (lo, hi) in enumerate(GROUPS):
        x_copies[2 * g].wait_recv()
        x_copies[2 * g + 1].wait_recv()
        gather(ext, g, lo, 0, 3)
        if g == 0:
            each_row(message_sv, 0, COUNT)
        else:
            each_row(message_t(lo, hi), 0, COUNT)
        send_sums(g)

    wide[pl.ds(8 * C, C), :] = turned(wq[:, pl.ds(0, C)])
    last = turned(wq[:, pl.ds(C, C)])
    wide[pl.ds(7 * C, C), :] = last
    wide[pl.ds(9 * C, C), :] = last
    for i, w in enumerate((w_scalar, w_gate, w_vector, w_tensor)):
        w_turned[pl.ds(i * C, C), :] = jnp.transpose(w[...])
    for q in range(0, COUNT, NP):
        outs = [expanded(q, 0, wide[pl.ds(7 * C, C), :]), expanded(q, 1, wide[pl.ds(8 * C, 2 * C), :])]
        for p in range(NP):
            at = slice(p * ROWS, (p + 1) * ROWS)
            readout[q + p, 0] = outs[0][:, at]
            readout[q + p, 1] = outs[1][0:C, at]
            readout[q + p, 2] = outs[1][C : 2 * C, at]
    add_sums(0)
    mix(1, 4, 2)
    add_sums(1)
    add_sums(2)
    add_sums(3)

    def scalars(p, carry):
        out = dot(w_turned[pl.ds(0, 2 * C), :], (acc[0, p] * third).astype(BF16))
        pre = out[0:C]
        acc[0, p] = pre * jax.nn.sigmoid(pre)
        gate[p] = jax.nn.sigmoid(out[C : 2 * C])
        return carry

    lax.fori_loop(0, NP, scalars, 0)

    def read_block(b, y, slot):
        g = b // 2
        return ext2[g].at[y, slot, b - GROUPS2[g][0]]

    def read_block(b, at):
        return ext2[b // 2].at[at, b % 2]

    def update_sv(p, r):
        g = gate[p, r, :]
        for b in range(READ_BLOCKS):
            old = ext[0][p, b, r, :].astype(F32)
            step = g * acc[b, p, r, :] if b > 0 else acc[0, p, r, :]
            read_block(b, p)[r, :] = (old + step).astype(BF16)

    each_row(update_sv, 0, NP)
    mix_x, mix_y = [], []
    for g, buf in enumerate(ext2):
        spans = (
            (mix_x, buf.at[0], buf.at[2], (-1, 0)),
            (mix_x, buf.at[1], buf.at[3], (1, 0)),
            (mix_y, buf.at[own], buf.at[pl.ds(6, NP)], (0, -1)),
            (mix_y, buf.at[own], buf.at[pl.ds(4, NP)], (0, 1)),
        )
        for n, (into, src, to, step) in enumerate(spans):
            into.append(remote(src, to, mix_send.at[g, n], mix_recv.at[g, n], step))
    for copy in (*mix_x, *mix_y):
        copy.start()

    def results(lo, hi, value):
        for i in range(hi - lo):
            for p in range(NP):
                mix_out[p, 0, :, pl.ds((lo + i) * C, C)] = jnp.transpose(value(p, i).astype(BF16))

    mix(4, 9, 3)
    for g, (lo, hi) in enumerate(GROUPS2):
        results(lo, hi, lambda p, i: ext2[g][p, i])
    for g, (lo, hi) in enumerate(GROUPS):
        if g > 0:
            results(lo, hi, lambda p, i: ext[g][p, i].astype(F32) + gate[p] * acc[lo + i, p])
    write = pltpu.make_async_copy(mix_out, mixed, out_sem)
    write.start()

    def near_side(q, r):
        at = jnp.where(q < NP, q, q + 2)
        row = [read_block(b, at)[r, :].astype(F32) for b in range(READ_BLOCKS)]
        s, v = row[0], row[1:]
        for k in range(NE):
            e = columns(k)
            u = [angle(m, q, k) for m in range(3)]
            along = u[0] * v[0] + u[1] * v[1] + u[2] * v[2]
            q1 = readout[q, 0, r, e]
            side[q, 0, r, e] = readout[q, 1, r, e] * s
            side[q, 1, r, e] = readout[q, 2, r, e] * along
            side[q, 2, r, e] = q1 * along
            for m in range(3):
                side[q, 3 + m, r, e] = q1 * v[m]

    for g, (lo, hi) in enumerate(GROUPS2):
        gather(ext2, g, lo, 0, 2)
    each_row(near_side, 0, NP)
    for copy in mix_y:
        copy.wait_recv()
    each_row(near_side, NP, COUNT)

    def fold(x):
        return sum(x[8 * i : 8 * i + 8] for i in range(1, STEP // 8)) + x[0:8]

    sums[...] = jnp.zeros_like(sums)

    def pairs(q, lo, first):
        def pair(i, carry):
            r = pl.ds(pl.multiple_of(i * STEP, STEP), STEP)
            carry = list(carry)
            for k in range(NE):
                e = columns(k)
                far = [gsc[lo + b, q, r, e] for b in range(READ_BLOCKS)]
                u = [angle(m, q, k) for m in range(3)]
                along = u[0] * far[1] + u[1] * far[2] + u[2] * far[3]
                term = side[q, 0, r, e] * far[0] + side[q, 1, r, e] * along
                carry[4 * k] = carry[4 * k] + fold(term)
                own_q = side[q, 2, r, e]
                for m in range(3):
                    term = side[q, 3 + m, r, e] * along + own_q * far[1 + m]
                    carry[4 * k + 1 + m] = carry[4 * k + 1 + m] + fold(term)
            return tuple(carry)

        zero = jnp.zeros((8, S), F32)
        totals = lax.fori_loop(0, C // STEP, pair, (zero,) * (4 * NE))
        for k in range(NE):
            for i in range(4):
                row = jnp.sum(totals[4 * k + i], axis=0, keepdims=True)
                at = pl.ds(NE * q + k, 1)
                sums[i, at, :] = row if first else sums[i, at, :] + row

    def each_pairs(lo, first):
        def run(q, carry):
            pairs(q, lo, first)
            return carry

        lax.fori_loop(0, COUNT, run, 0)

    each_pairs(0, True)
    for copy in (*pos_copies, *x_copies, *part_copies):
        copy.wait_send()
    for g, (lo, hi) in enumerate(GROUPS2):
        mix_x[2 * g].wait_recv()
        mix_x[2 * g + 1].wait_recv()
        gather(ext2, g, READ_BLOCKS + lo, 2, 3)
    each_pairs(READ_BLOCKS, False)

    t_rho, g_x, g_y, g_z = (sums[i] for i in range(4))
    u_x, u_y, u_z, inverse = ang[0], ang[1], ang[2], inverses[...]
    radial_part = t_rho - (u_x * g_x + u_y * g_y + u_z * g_z) * inverse
    grad[...] = jnp.zeros_like(grad)
    grad[0] = radial_part * u_x + g_x * inverse
    grad[1] = radial_part * u_y + g_y * inverse
    grad[2] = radial_part * u_z + g_z * inverse

    def at_atoms(q):
        return (grad[:, NE * q, :] + grad[:, NE * q + 1, :]) + grad[:, NE * q + 2, :]

    force_copies = []
    for i, dy in ((0, -1), (1, 1)):
        force_copies.append(
            remote(force_y.at[i], force_y_in.at[1 - i], force_send.at[i], force_recv.at[i], (0, dy))
        )
    for i, (p, dx) in enumerate(((0, 1), (1, -1))):
        force_copies.append(
            remote(force_x.at[p], force_x_in.at[p], force_send.at[2 + i], force_recv.at[2 + i], (dx, 0))
        )
    parts = []
    for p in range(NP):
        used = [NE * (NP * y + p) + k for y in range(3) for k in range(NE)]
        parts.append(in_parts(jnp.concatenate([grad[:, row, :] for row in used], axis=1)))
    total = [at_atoms(p) for p in range(NP)]
    def scatter(p, lo, hi):
        return whole(jnp.transpose(dot(oh[p, pl.ds(lo * S, (hi - lo) * S), :], parts[p], (1, 1))))

    for p in range(NP):
        force_x[1 - p] = -scatter(p, 2, 3)
        force_copies[3 - p].start()
    for i in range(2):
        for p in range(NP):
            force_y[i, p] = at_atoms(NP * (1 + i) + p)
        force_copies[i].start()
    for p in range(NP):
        out = scatter(p, 0, 2)
        for i in range(NP):
            total[i] = total[i] - out[:, i * S : (i + 1) * S]
    for copy in force_copies:
        copy.wait_recv()
    for p in range(NP):
        value = (total[p] + force_x_in[p]) + (force_y_in[0, p] + force_y_in[1, p])
        for m in range(3):
            forces[p, m] = value[m : m + 1]

    for copy in (*mix_x, *mix_y, *force_copies):
        copy.wait_send()
    write.wait()


def solution(mesh):
    gx_size, yz_size = mesh.shape["gx"], mesh.shape["yz"]

    def body(features, positions, *rest):
        args = (features, jnp.transpose(positions, (0, 2, 1, 3)), *rest)
        vmem = pl.BlockSpec(memory_space=pltpu.VMEM)
        anywhere = pl.BlockSpec(memory_space=pl.ANY)
        dma = pltpu.SemaphoreType.DMA

        def run_all(*refs):
            kernel(gx_size, yz_size, *refs)

        small = [pltpu.VMEM(x.shape, x.dtype) for x in args[1:]]
        new_features, force = pl.pallas_call(
            run_all,
            out_shape=(
                jax.ShapeDtypeStruct((NP, 1, S, BLOCKS * C), BF16),
                jax.ShapeDtypeStruct((NP, 3, 1, S), F32),
            ),
            in_specs=[anywhere] * 10,
            out_specs=(anywhere, vmem),
            scratch_shapes=small
            + [
                *[pltpu.VMEM((4, hi - lo, C, S), BF16) for lo, hi in GROUPS],
                *[pltpu.VMEM((8, hi - lo, C, S), BF16) for lo, hi in GROUPS2],
                *[pltpu.VMEM((2, NP, len(blocks), C, S), BF16) for blocks in SUMS],
                *[pltpu.VMEM((2, NP, len(blocks), C, S), BF16) for blocks in SUMS],
                pltpu.VMEM((3, 4, 16, S), F32),
                pltpu.VMEM((NP, 3 * S, 3 * ROWS), BF16),
                pltpu.VMEM((7, COUNT, C, ROWS), F32),
                pltpu.VMEM((COUNT, 3, C, ROWS), F32),
                pltpu.VMEM((10 * C, 32), BF16),
                pltpu.VMEM((4 * C, C), BF16),
                pltpu.VMEM((64, EDGE_ROWS, S), F32),
                pltpu.VMEM((8, EDGE_ROWS, S), F32),
                pltpu.VMEM((EDGE_ROWS, 8, S), F32),
                pltpu.VMEM((EDGE_ROWS, S), F32),
                pltpu.VMEM((EDGE_ROWS, S), F32),
                pltpu.VMEM((4, EDGE_ROWS, S), F32),
                pltpu.VMEM((BLOCKS, COUNT, C, S), F32),
                pltpu.VMEM((NP, C, S), F32),
                pltpu.VMEM((BLOCKS, COUNT, C, ROWS), F32),
                pltpu.VMEM((NP, 1, S, BLOCKS * C), BF16),
                pltpu.VMEM((NP, 1, S, BLOCKS * C), BF16),
                pltpu.VMEM((COUNT, 6, C, ROWS), F32),
                pltpu.VMEM((4, EDGE_ROWS, S), F32),
                pltpu.VMEM((8, EDGE_ROWS, S), F32),
                pltpu.VMEM((2, NP, 8, S), F32),
                pltpu.VMEM((2, NP, 8, S), F32),
                pltpu.VMEM((NP, 8, S), F32),
                pltpu.VMEM((NP, 8, S), F32),
                dma((len(small),)),
                dma,
                dma,
                dma((4,)),
                dma((4,)),
                dma((len(GROUPS), 2)),
                dma((len(GROUPS), 2)),
                dma((len(SUMS), 2)),
                dma((len(SUMS), 2)),
                dma((len(GROUPS2), 4)),
                dma((len(GROUPS2), 4)),
                dma((4,)),
                dma((4,)),
            ],
            compiler_params=pltpu.CompilerParams(
                collective_id=0, has_side_effects=True, vmem_limit_bytes=60 * 1024 * 1024
            ),
            cost_estimate=pl.CostEstimate(
                flops=6 * 10**9, bytes_accessed=2 * 10**6, transcendentals=10**5
            ),
        )(*args)
        new_features, force = pl.pallas_call(
            deliver,
            out_shape=(
                jax.ShapeDtypeStruct((NP, 1, S, BLOCKS * C), BF16),
                jax.ShapeDtypeStruct((NP, 3, 1, S), F32),
            ),
            in_specs=[anywhere] * 2,
            out_specs=(anywhere, anywhere),
            scratch_shapes=[
                pltpu.VMEM((NP, 1, S, BLOCKS * C), BF16),
                pltpu.VMEM((NP, 3, 1, S), F32),
                dma((2, 9)),
            ],
            compiler_params=pltpu.CompilerParams(vmem_limit_bytes=60 * 1024 * 1024),
            cost_estimate=pl.CostEstimate(flops=0, bytes_accessed=12 * 10**5, transcendentals=0),
        )(new_features, force)
        return new_features, jnp.transpose(force, (0, 2, 1, 3))

    in_specs = (
        P("gx", "yz", None, None),
        P("gx", "yz", None, None),
        P(None, "gx", "yz", None),
        P(None, "gx", "yz", None),
        P(),
        P(),
        P(),
        P(),
        P(),
        P(),
    )
    out_specs = (P("gx", "yz", None, None), P("gx", "yz", None, None))
    return jax.shard_map(body, mesh=mesh, in_specs=in_specs, out_specs=out_specs, check_vma=False)
```

```python
import math

import jax
import jax.numpy as jnp
from jax import lax
from jax.experimental import pallas as pl
from jax.experimental.pallas import tpu as pltpu
from jax.sharding import PartitionSpec as P

MESH = pl.DeviceIdType.MESH
F32 = jnp.float32
BF16 = jnp.bfloat16
SOFTENING = 0.25
SPACING = 0.6
ROOT_THREE = math.sqrt(3.0)
C = 128
S = 128
NB = 8
NE = 3
NP = 2
BLOCKS = 9
READ_BLOCKS = 4
ROWS = NE * S
STEP = 32
GROUPS = ((0, 4), (4, 6), (6, 8), (8, 9))
SUMS = ((1, 2, 3), (4, 5), (6, 7), (8, 0))
GROUPS2 = ((0, 2), (2, 4))
COUNT = 6
EDGE_ROWS = 24
NEIGHBOURS = ((-1, 0), (1, 0), (0, -1), (0, 1))


def split(x):
    high = x.astype(BF16).astype(F32)
    return high, x - high


def dot(a, b, contract=(1, 0)):
    dims = (((contract[0],), (contract[1],)), ((), ()))
    return lax.dot_general(a, b, dims, preferred_element_type=F32)


def deliver(mixed, forces, mixed_out, forces_out, held, held_forces, sems):
    parts = [(forces, held_forces, forces_out)]
    parts += [(mixed.at[p], held.at[p], mixed_out.at[p]) for p in range(NP)]
    reads = [pltpu.make_async_copy(a, b, sems.at[0, i]) for i, (a, b, _) in enumerate(parts)]
    writes = [pltpu.make_async_copy(b, c, sems.at[1, i]) for i, (_, b, c) in enumerate(parts)]
    for copy in reads:
        copy.start()
    for read, write in zip(reads, writes):
        read.wait()
        write.start()
    for copy in writes:
        copy.wait()


def kernel(
    gx_size,
    yz_size,
    feat,
    *refs,
):
    small_in, refs = refs[:9], refs[9:]
    mixed, forces, *refs = refs
    small, refs = refs[:9], refs[9:]
    run(gx_size, yz_size, feat, small_in, small, mixed, forces, *refs)


def run(
    gx_size,
    yz_size,
    feat,
    small_in,
    small,
    mixed,
    forces,
    ext0,
    ext1,
    ext2,
    ext3,
    mix0,
    mix1,
    *refs,
):
    n = len(SUMS)
    part_out, part_in, refs = refs[:n], refs[n : 2 * n], refs[2 * n :]
    (
        posx,
        oh,
        coef,
        readout,
        wide,
        w_turned,
        zf,
        ang,
        inverses,
        target,
        edges,
        acc,
        gate,
        gsc,
        raw,
        mix_out,
        side,
        sums,
        grad,
        force_y,
        force_y_in,
        force_x,
        force_x_in,
        small_sem,
        load_sem,
        out_sem,
        pos_send,
        pos_recv,
        x_send,
        x_recv,
        part_send,
        part_recv,
        mix_send,
        mix_recv,
        force_send,
        force_recv,
    ) = refs
    ext, ext2 = (ext0, ext1, ext2, ext3), (mix0, mix1)
    gx = lax.axis_index("gx")
    yz = lax.axis_index("yz")

    def device(dx, dy):
        return (lax.rem(gx + dx + gx_size, gx_size), lax.rem(yz + dy + yz_size, yz_size))

    def remote(src, dst, send, recv, step):
        return pltpu.make_async_remote_copy(
            src_ref=src,
            dst_ref=dst,
            send_sem=send,
            recv_sem=recv,
            device_id=device(*step),
            device_id_type=MESH,
        )

    barrier = pltpu.get_barrier_semaphore()
    for step in NEIGHBOURS:
        pl.semaphore_signal(barrier, inc=1, device_id=device(*step), device_id_type=MESH)

    small_loads = [
        pltpu.make_async_copy(small_in[i], small[i], small_sem.at[i]) for i in range(len(small))
    ]
    feat_load = pltpu.make_async_copy(feat, raw, load_sem)
    feat_load.start()
    for load in small_loads:
        load.start()
    pos, dst, shift, wr, wq, w_scalar, w_gate, w_vector, w_tensor = small

    def turn(g):
        lo, hi = GROUPS[g]
        for i in range(hi - lo):
            for p in range(NP):
                ext[g][p, i] = jnp.transpose(raw[p, 0, :, pl.ds((lo + i) * C, C)])

    feat_load.wait()
    turn(0)
    pl.semaphore_wait(barrier, len(NEIGHBOURS))

    x_copies = []
    for g in range(len(GROUPS)):
        for own, ghost, dx in ((0, 2, -1), (1, 3, 1)):
            x_copies.append(
                remote(ext[g].at[own], ext[g].at[ghost], x_send.at[g, own], x_recv.at[g, own], (dx, 0))
            )
    x_copies[0].start()
    x_copies[1].start()

    for load in small_loads:
        load.wait()
    for p in range(NP):
        posx[0, p] = jnp.zeros((16, S), F32)
        for m in range(3):
            posx[0, p, pl.ds(m, 1), :] = pos[p, m]
        for k in range(NE):
            posx[0, p, pl.ds(3 + k, 1), :] = dst[k, p].astype(F32)
            posx[0, p, pl.ds(6 + k, 1), :] = shift[k, p].astype(F32)
    own = pl.ds(0, NP)
    pos_copies = [
        remote(posx.at[0, 0], posx.at[0, 2], pos_send.at[0], pos_recv.at[0], (-1, 0)),
        remote(posx.at[0, 1], posx.at[0, 3], pos_send.at[1], pos_recv.at[1], (1, 0)),
        remote(posx.at[0, own], posx.at[2, own], pos_send.at[2], pos_recv.at[2], (0, -1)),
        remote(posx.at[0, own], posx.at[1, own], pos_send.at[3], pos_recv.at[3], (0, 1)),
    ]
    for copy in pos_copies:
        copy.start()
    for g in range(1, len(GROUPS)):
        turn(g)
        x_copies[2 * g].start()
        x_copies[2 * g + 1].start()

    def turned(w):
        high, low = split(w)
        rows = jnp.concatenate([high, low, high, jnp.zeros_like(w)], axis=0)
        return jnp.transpose(rows).astype(BF16)

    def widen(f, carry):
        at = pl.ds(pl.multiple_of(f * C, C), C)
        wide[at, :] = turned(wr[:, at])
        return carry

    lax.fori_loop(0, 7, widen, 0)

    for copy in pos_copies:
        copy.wait_recv()
    edges[...] = jnp.zeros_like(edges)
    for q in range(COUNT):
        y, p = q // NP, q % NP
        at = pl.ds(NE * q, NE)
        edges[0, at, :] = posx[y, p, pl.ds(3, NE), :]
        edges[1, at, :] = posx[y, p, pl.ds(6, NE), :]
        edges[2, at, :] = jnp.full((NE, S), p, F32)
        edges[3, at, :] = jnp.full((NE, S), (1, 0, 2)[y], F32)
        for m in range(3):
            edges[4 + m, at, :] = jnp.broadcast_to(posx[y, p, pl.ds(m, 1), :], (NE, S))
    place = edges[0]
    one = jnp.ones_like(place)
    nil = jnp.zeros_like(place)

    def at_least(x, bound):
        return jnp.where(x >= float(bound), one, nil)

    ext_x = at_least(place, 3 * S) + at_least(place, 6 * S) + at_least(place, 9 * S)
    left = place - ext_x * float(3 * S)
    ext_y = at_least(left, S) + at_least(left, 2 * S)
    step_x = ext_x - 1.0 - edges[2]
    step_y = ext_y - 1.0
    far_slot = left - ext_y * S
    target[...] = jnp.where(edges[3] + step_y == 1.0, ext_x * S + far_slot, -1.0)

    atom = lax.broadcasted_iota(jnp.int32, (S, ROWS), 0).astype(F32)

    def pick(y, carry):
        for p in range(NP):
            rows = [target[pl.ds(NE * (NP * y + p) + k, 1), :] for k in range(NE)]
            ends = jnp.concatenate(rows, axis=1) - atom
            for i, x in enumerate((1, 2, 3 * p)):
                hit = jnp.where(ends == float(x * S), 1.0, 0.0).astype(BF16)
                oh[p, pl.ds(i * S, S), pl.ds(pl.multiple_of(y * ROWS, ROWS), ROWS)] = hit
        return carry

    lax.fori_loop(0, 3, pick, 0)

    def in_parts(x):
        first, rest = split(x)
        second, third = split(rest)
        return jnp.concatenate([first, second, third, jnp.zeros_like(first)], 0).astype(BF16)

    def whole(x):
        return (x[0:8] + x[8:16]) + x[16:24]

    lanes = far_slot.astype(jnp.int32)

    def far_place(m):
        found = []
        for slot in (3, 0, 1, 2):
            row = jnp.broadcast_to(posx[0, slot, pl.ds(m, 1), :], (EDGE_ROWS, S))
            found.append(jnp.take_along_axis(row, lanes, axis=1, mode="promise_in_bounds"))
        low = jnp.where(ext_x == 0.0, found[0], found[1])
        high = jnp.where(ext_x == 2.0, found[2], found[3])
        return jnp.where(ext_x < 2.0, low, high)

    disp_x = far_place(0) - edges[4] + step_x
    disp_y = far_place(1) - edges[5] + step_y
    disp_z = far_place(2) - edges[6] + edges[1]
    rho = jnp.sqrt(disp_x * disp_x + disp_y * disp_y + disp_z * disp_z + SOFTENING)
    inverse = 1.0 / rho
    u_x, u_y, u_z = disp_x * inverse, disp_y * inverse, disp_z * inverse
    inverses[...] = inverse
    length_sq = u_x * u_x + u_y * u_y + u_z * u_z
    angular = (
        u_x,
        u_y,
        u_z,
        ROOT_THREE * u_x * u_y,
        ROOT_THREE * u_y * u_z,
        0.5 * (3.0 * u_z * u_z - length_sq),
        ROOT_THREE * u_x * u_z,
        0.5 * ROOT_THREE * (u_x * u_x - u_y * u_y),
    )
    for f in range(8):
        ang[f] = angular[f]
    zf[...] = jnp.zeros_like(zf)
    for b in range(NB):
        off = (rho - (0.5 + SPACING * b)) / SPACING
        basis = jnp.exp(-(off * off))
        slope = basis * off * (-2.0 / SPACING)
        for i, value in enumerate((basis, slope)):
            high, low = split(value)
            zf[32 * i + b] = high
            zf[32 * i + 8 + b] = high
            zf[32 * i + 16 + b] = low

    def columns(k):
        return pl.ds(k * S, S)

    def expanded(q, part, rows):
        edge_rows = [zf[pl.ds(32 * part, 32), NE * q + k, :] for k in range(NP * NE)]
        return dot(rows, jnp.concatenate(edge_rows, axis=1).astype(BF16))

    for q in range(0, COUNT, NP):
        out = expanded(q, 0, wide[pl.ds(0, 7 * C), :])
        for f in range(7):
            for p in range(NP):
                coef[f, q + p] = out[f * C : (f + 1) * C, p * ROWS : (p + 1) * ROWS]

    def columns(k):
        return pl.ds(k * S, S)

    def gather(bufs, g, to, first, last):
        buf = bufs[g]
        n = buf.shape[1]

        for p in range(NP):
            tiles = [buf[slot].reshape(n * C, S) for slot in (0, 1, 3 - p)[first:last]]
            out = dot(jnp.concatenate(tiles, axis=1), oh[p, pl.ds(first * S, (last - first) * S), :])
            for i in range(n):
                for y in range(3):
                    gsc[to + i, NP * y + p] = out[i * C : (i + 1) * C, y * ROWS : (y + 1) * ROWS]

    def each_row(fn, lo, hi):
        steps = C // STEP

        def run(i, carry):
            q = i // steps
            fn(q, pl.ds(pl.multiple_of((i - q * steps) * STEP, STEP), STEP))
            return carry

        lax.fori_loop(lo * steps, hi * steps, run, 0)

    def angle(f, q, k):
        return ang[f, pl.ds(NE * q + k, 1), :]

    def message_sv(p, r):
        total = [jnp.zeros((STEP, S), F32) for _ in range(BLOCKS)]
        for k in range(NE):
            e = columns(k)
            s = gsc[0, p, r, e]
            v = [gsc[1 + m, p, r, e] for m in range(3)]
            u = [angle(m, p, k) for m in range(3)]
            along = u[0] * v[0] + u[1] * v[1] + u[2] * v[2]
            total[0] = total[0] + coef[0, p, r, e] * s + coef[1, p, r, e] * along
            r3s = coef[3, p, r, e] * s
            r4 = coef[4, p, r, e]
            for m in range(3):
                total[1 + m] = total[1 + m] + r3s * u[m] + r4 * v[m]
            r5s = coef[5, p, r, e] * s
            for n in range(5):
                total[4 + n] = total[4 + n] + r5s * angle(3 + n, p, k)
        for b in range(BLOCKS):
            acc[b, p, r, :] = total[b]

    def message_t(lo, hi):
        def fn(p, r):
            total = [acc[b, p, r, :] for b in (0, *range(lo, hi))]
            for k in range(NE):
                e = columns(k)
                along = None
                r6 = coef[6, p, r, e]
                for n in range(lo, hi):
                    t = gsc[n, p, r, e]
                    term = angle(n - 1, p, k) * t
                    along = term if along is None else along + term
                    total[1 + n - lo] = total[1 + n - lo] + r6 * t
                total[0] = total[0] + coef[2, p, r, e] * along
            for i, b in enumerate((0, *range(lo, hi))):
                acc[b, p, r, :] = total[i]

        return fn

    third = 1.0 / NE

    def mix(lo, hi, w):
        def run(p, carry):
            terms = [(acc[b, p] * third).astype(BF16) for b in range(lo, hi)]
            out = dot(w_turned[pl.ds(w * C, C), :], jnp.concatenate(terms, axis=1))
            for b in range(lo, hi):
                acc[b, p] = out[:, (b - lo) * S : (b - lo + 1) * S]
            return carry

        lax.fori_loop(0, NP, run, 0)

    part_copies = []
    for h in range(len(SUMS)):
        for i, dy in ((0, -1), (1, 1)):
            part_copies.append(
                remote(
                    part_out[h].at[i],
                    part_in[h].at[1 - i],
                    part_send.at[h, i],
                    part_recv.at[h, i],
                    (0, dy),
                )
            )

    def send_sums(h):
        for i in range(2):
            for p in range(NP):
                for j, b in enumerate(SUMS[h]):
                    part_out[h][i, p, j] = acc[b, NP * (1 + i) + p].astype(BF16)
            part_copies[2 * h + i].start()

    def add_sums(h):
        for i in range(2):
            part_copies[2 * h + i].wait_recv()
        for p in range(NP):
            for j, b in enumerate(SUMS[h]):
                acc[b, p] = acc[b, p] + part_in[h][0, p, j].astype(F32) + part_in[h][1, p, j].astype(F32)

    for g, (lo, hi) in enumerate(GROUPS):
        x_copies[2 * g].wait_recv()
        x_copies[2 * g + 1].wait_recv()
        gather(ext, g, lo, 0, 3)
        if g == 0:
            each_row(message_sv, 0, COUNT)
        else:
            each_row(message_t(lo, hi), 0, COUNT)
        send_sums(g)

    wide[pl.ds(8 * C, C), :] = turned(wq[:, pl.ds(0, C)])
    last = turned(wq[:, pl.ds(C, C)])
    wide[pl.ds(7 * C, C), :] = last
    wide[pl.ds(9 * C, C), :] = last
    for i, w in enumerate((w_scalar, w_gate, w_vector, w_tensor)):
        w_turned[pl.ds(i * C, C), :] = jnp.transpose(w[...])
    for q in range(0, COUNT, NP):
        outs = [expanded(q, 0, wide[pl.ds(7 * C, C), :]), expanded(q, 1, wide[pl.ds(8 * C, 2 * C), :])]
        for p in range(NP):
            at = slice(p * ROWS, (p + 1) * ROWS)
            readout[q + p, 0] = outs[0][:, at]
            readout[q + p, 1] = outs[1][0:C, at]
            readout[q + p, 2] = outs[1][C : 2 * C, at]
    add_sums(0)
    mix(1, 4, 2)
    add_sums(1)
    add_sums(2)
    add_sums(3)

    def scalars(p, carry):
        out = dot(w_turned[pl.ds(0, 2 * C), :], (acc[0, p] * third).astype(BF16))
        pre = out[0:C]
        acc[0, p] = pre * jax.nn.sigmoid(pre)
        gate[p] = jax.nn.sigmoid(out[C : 2 * C])
        return carry

    lax.fori_loop(0, NP, scalars, 0)

    def read_block(b, y, slot):
        g = b // 2
        return ext2[g].at[y, slot, b - GROUPS2[g][0]]

    def read_block(b, at):
        return ext2[b // 2].at[at, b % 2]

    def update_sv(p, r):
        g = gate[p, r, :]
        for b in range(READ_BLOCKS):
            old = ext[0][p, b, r, :].astype(F32)
            step = g * acc[b, p, r, :] if b > 0 else acc[0, p, r, :]
            read_block(b, p)[r, :] = (old + step).astype(BF16)

    each_row(update_sv, 0, NP)
    mix_x, mix_y = [], []
    for g, buf in enumerate(ext2):
        spans = (
            (mix_x, buf.at[0], buf.at[2], (-1, 0)),
            (mix_x, buf.at[1], buf.at[3], (1, 0)),
            (mix_y, buf.at[own], buf.at[pl.ds(6, NP)], (0, -1)),
            (mix_y, buf.at[own], buf.at[pl.ds(4, NP)], (0, 1)),
        )
        for n, (into, src, to, step) in enumerate(spans):
            into.append(remote(src, to, mix_send.at[g, n], mix_recv.at[g, n], step))
    for copy in (*mix_x, *mix_y):
        copy.start()

    def results(lo, hi, value):
        for i in range(hi - lo):
            for p in range(NP):
                mix_out[p, 0, :, pl.ds((lo + i) * C, C)] = jnp.transpose(value(p, i).astype(BF16))

    mix(4, 9, 3)
    for g, (lo, hi) in enumerate(GROUPS2):
        results(lo, hi, lambda p, i: ext2[g][p, i])
    for g, (lo, hi) in enumerate(GROUPS):
        if g > 0:
            results(lo, hi, lambda p, i: ext[g][p, i].astype(F32) + gate[p] * acc[lo + i, p])
    write = pltpu.make_async_copy(mix_out, mixed, out_sem)
    write.start()

    def near_side(q, r):
        at = jnp.where(q < NP, q, q + 2)
        row = [read_block(b, at)[r, :].astype(F32) for b in range(READ_BLOCKS)]
        s, v = row[0], row[1:]
        for k in range(NE):
            e = columns(k)
            u = [angle(m, q, k) for m in range(3)]
            along = u[0] * v[0] + u[1] * v[1] + u[2] * v[2]
            q1 = readout[q, 0, r, e]
            side[q, 0, r, e] = readout[q, 1, r, e] * s
            side[q, 1, r, e] = readout[q, 2, r, e] * along
            side[q, 2, r, e] = q1 * along
            for m in range(3):
                side[q, 3 + m, r, e] = q1 * v[m]

    for g, (lo, hi) in enumerate(GROUPS2):
        gather(ext2, g, lo, 0, 2)
    each_row(near_side, 0, NP)
    for copy in mix_y:
        copy.wait_recv()
    each_row(near_side, NP, COUNT)

    def fold(x):
        return sum(x[8 * i : 8 * i + 8] for i in range(1, STEP // 8)) + x[0:8]

    sums[...] = jnp.zeros_like(sums)

    def pairs(q, lo, first):
        def pair(i, carry):
            r = pl.ds(pl.multiple_of(i * STEP, STEP), STEP)
            carry = list(carry)
            for k in range(NE):
                e = columns(k)
                far = [gsc[lo + b, q, r, e] for b in range(READ_BLOCKS)]
                u = [angle(m, q, k) for m in range(3)]
                along = u[0] * far[1] + u[1] * far[2] + u[2] * far[3]
                term = side[q, 0, r, e] * far[0] + side[q, 1, r, e] * along
                carry[4 * k] = carry[4 * k] + fold(term)
                own_q = side[q, 2, r, e]
                for m in range(3):
                    term = side[q, 3 + m, r, e] * along + own_q * far[1 + m]
                    carry[4 * k + 1 + m] = carry[4 * k + 1 + m] + fold(term)
            return tuple(carry)

        zero = jnp.zeros((8, S), F32)
        totals = lax.fori_loop(0, C // STEP, pair, (zero,) * (4 * NE))
        for k in range(NE):
            for i in range(4):
                row = jnp.sum(totals[4 * k + i], axis=0, keepdims=True)
                at = pl.ds(NE * q + k, 1)
                sums[i, at, :] = row if first else sums[i, at, :] + row

    def each_pairs(lo, first):
        def run(q, carry):
            pairs(q, lo, first)
            return carry

        lax.fori_loop(0, COUNT, run, 0)

    each_pairs(0, True)
    for copy in (*pos_copies, *x_copies, *part_copies):
        copy.wait_send()
    for g, (lo, hi) in enumerate(GROUPS2):
        mix_x[2 * g].wait_recv()
        mix_x[2 * g + 1].wait_recv()
        gather(ext2, g, READ_BLOCKS + lo, 2, 3)
    each_pairs(READ_BLOCKS, False)

    t_rho, g_x, g_y, g_z = (sums[i] for i in range(4))
    u_x, u_y, u_z, inverse = ang[0], ang[1], ang[2], inverses[...]
    radial_part = t_rho - (u_x * g_x + u_y * g_y + u_z * g_z) * inverse
    grad[...] = jnp.zeros_like(grad)
    grad[0] = radial_part * u_x + g_x * inverse
    grad[1] = radial_part * u_y + g_y * inverse
    grad[2] = radial_part * u_z + g_z * inverse

    def at_atoms(q):
        return (grad[:, NE * q, :] + grad[:, NE * q + 1, :]) + grad[:, NE * q + 2, :]

    force_copies = []
    for i, dy in ((0, -1), (1, 1)):
        force_copies.append(
            remote(force_y.at[i], force_y_in.at[1 - i], force_send.at[i], force_recv.at[i], (0, dy))
        )
    for i, (p, dx) in enumerate(((0, 1), (1, -1))):
        force_copies.append(
            remote(force_x.at[p], force_x_in.at[p], force_send.at[2 + i], force_recv.at[2 + i], (dx, 0))
        )
    parts = []
    for p in range(NP):
        used = [NE * (NP * y + p) + k for y in range(3) for k in range(NE)]
        parts.append(in_parts(jnp.concatenate([grad[:, row, :] for row in used], axis=1)))
    total = [at_atoms(p) for p in range(NP)]
    def scatter(p, lo, hi):
        return whole(jnp.transpose(dot(oh[p, pl.ds(lo * S, (hi - lo) * S), :], parts[p], (1, 1))))

    for p in range(NP):
        force_x[1 - p] = -scatter(p, 2, 3)
        force_copies[3 - p].start()
    for i in range(2):
        for p in range(NP):
            force_y[i, p] = at_atoms(NP * (1 + i) + p)
        force_copies[i].start()
    for p in range(NP):
        out = scatter(p, 0, 2)
        for i in range(NP):
            total[i] = total[i] - out[:, i * S : (i + 1) * S]
    for copy in force_copies:
        copy.wait_recv()
    for p in range(NP):
        value = (total[p] + force_x_in[p]) + (force_y_in[0, p] + force_y_in[1, p])
        for m in range(3):
            forces[p, m] = value[m : m + 1]

    for copy in (*mix_x, *mix_y, *force_copies):
        copy.wait_send()
    write.wait()


def solution(mesh):
    gx_size, yz_size = mesh.shape["gx"], mesh.shape["yz"]

    def body(features, positions, *rest):
        args = (features, jnp.transpose(positions, (0, 2, 1, 3)), *rest)
        vmem = pl.BlockSpec(memory_space=pltpu.VMEM)
        anywhere = pl.BlockSpec(memory_space=pl.ANY)
        dma = pltpu.SemaphoreType.DMA

        def run_all(*refs):
            kernel(gx_size, yz_size, *refs)

        small = [pltpu.VMEM(x.shape, x.dtype) for x in args[1:]]
        new_features, force = pl.pallas_call(
            run_all,
            out_shape=(
                jax.ShapeDtypeStruct((NP, 1, S, BLOCKS * C), BF16),
                jax.ShapeDtypeStruct((NP, 3, 1, S), F32),
            ),
            in_specs=[anywhere] * 10,
            out_specs=(anywhere, vmem),
            scratch_shapes=small
            + [
                *[pltpu.VMEM((4, hi - lo, C, S), BF16) for lo, hi in GROUPS],
                *[pltpu.VMEM((8, hi - lo, C, S), BF16) for lo, hi in GROUPS2],
                *[pltpu.VMEM((2, NP, len(blocks), C, S), BF16) for blocks in SUMS],
                *[pltpu.VMEM((2, NP, len(blocks), C, S), BF16) for blocks in SUMS],
                pltpu.VMEM((3, 4, 16, S), F32),
                pltpu.VMEM((NP, 3 * S, 3 * ROWS), BF16),
                pltpu.VMEM((7, COUNT, C, ROWS), F32),
                pltpu.VMEM((COUNT, 3, C, ROWS), F32),
                pltpu.VMEM((10 * C, 32), BF16),
                pltpu.VMEM((4 * C, C), BF16),
                pltpu.VMEM((64, EDGE_ROWS, S), F32),
                pltpu.VMEM((8, EDGE_ROWS, S), F32),
                pltpu.VMEM((EDGE_ROWS, S), F32),
                pltpu.VMEM((EDGE_ROWS, S), F32),
                pltpu.VMEM((7, EDGE_ROWS, S), F32),
                pltpu.VMEM((BLOCKS, COUNT, C, S), F32),
                pltpu.VMEM((NP, C, S), F32),
                pltpu.VMEM((BLOCKS, COUNT, C, ROWS), F32),
                pltpu.VMEM((NP, 1, S, BLOCKS * C), BF16),
                pltpu.VMEM((NP, 1, S, BLOCKS * C), BF16),
                pltpu.VMEM((COUNT, 6, C, ROWS), F32),
                pltpu.VMEM((4, EDGE_ROWS, S), F32),
                pltpu.VMEM((8, EDGE_ROWS, S), F32),
                pltpu.VMEM((2, NP, 8, S), F32),
                pltpu.VMEM((2, NP, 8, S), F32),
                pltpu.VMEM((NP, 8, S), F32),
                pltpu.VMEM((NP, 8, S), F32),
                dma((len(small),)),
                dma,
                dma,
                dma((4,)),
                dma((4,)),
                dma((len(GROUPS), 2)),
                dma((len(GROUPS), 2)),
                dma((len(SUMS), 2)),
                dma((len(SUMS), 2)),
                dma((len(GROUPS2), 4)),
                dma((len(GROUPS2), 4)),
                dma((4,)),
                dma((4,)),
            ],
            compiler_params=pltpu.CompilerParams(
                collective_id=0, has_side_effects=True, vmem_limit_bytes=60 * 1024 * 1024
            ),
            cost_estimate=pl.CostEstimate(
                flops=6 * 10**9, bytes_accessed=2 * 10**6, transcendentals=10**5
            ),
        )(*args)
        new_features, force = pl.pallas_call(
            deliver,
            out_shape=(
                jax.ShapeDtypeStruct((NP, 1, S, BLOCKS * C), BF16),
                jax.ShapeDtypeStruct((NP, 3, 1, S), F32),
            ),
            in_specs=[anywhere] * 2,
            out_specs=(anywhere, anywhere),
            scratch_shapes=[
                pltpu.VMEM((NP, 1, S, BLOCKS * C), BF16),
                pltpu.VMEM((NP, 3, 1, S), F32),
                dma((2, 1 + NP)),
            ],
            compiler_params=pltpu.CompilerParams(vmem_limit_bytes=60 * 1024 * 1024),
            cost_estimate=pl.CostEstimate(flops=0, bytes_accessed=12 * 10**5, transcendentals=0),
        )(new_features, force)
        return new_features, jnp.transpose(force, (0, 2, 1, 3))

    in_specs = (
        P("gx", "yz", None, None),
        P("gx", "yz", None, None),
        P(None, "gx", "yz", None),
        P(None, "gx", "yz", None),
        P(),
        P(),
        P(),
        P(),
        P(),
        P(),
    )
    out_specs = (P("gx", "yz", None, None), P("gx", "yz", None, None))
    return jax.shard_map(body, mesh=mesh, in_specs=in_specs, out_specs=out_specs, check_vma=False)
```

```python
import math

import jax
import jax.numpy as jnp
from jax import lax
from jax.experimental import pallas as pl
from jax.experimental.pallas import tpu as pltpu
from jax.sharding import PartitionSpec as P

MESH = pl.DeviceIdType.MESH
F32 = jnp.float32
BF16 = jnp.bfloat16
SOFTENING = 0.25
SPACING = 0.6
ROOT_THREE = math.sqrt(3.0)
C = 128
S = 128
NB = 8
NE = 3
NP = 2
BLOCKS = 9
READ_BLOCKS = 4
ROWS = NE * S
STEP = 32
GROUPS = ((0, 4), (4, 6), (6, 8), (8, 9))
SUMS = ((1, 2, 3), (4, 5), (6, 7), (8, 0))
GROUPS2 = ((0, 2), (2, 4))
COUNT = 6
EDGE_ROWS = 24
NEIGHBOURS = ((-1, 0), (1, 0), (0, -1), (0, 1))


def split(x):
    high = x.astype(BF16).astype(F32)
    return high, x - high


def dot(a, b, contract=(1, 0)):
    dims = (((contract[0],), (contract[1],)), ((), ()))
    return lax.dot_general(a, b, dims, preferred_element_type=F32)


def deliver(mixed, forces, mixed_out, forces_out, held, held_forces, sems):
    parts = [(forces, held_forces, forces_out)]
    parts += [(mixed.at[p], held.at[p], mixed_out.at[p]) for p in range(NP)]
    reads = [pltpu.make_async_copy(a, b, sems.at[0, i]) for i, (a, b, _) in enumerate(parts)]
    writes = [pltpu.make_async_copy(b, c, sems.at[1, i]) for i, (_, b, c) in enumerate(parts)]
    for copy in reads:
        copy.start()
    for read, write in zip(reads, writes):
        read.wait()
        write.start()
    for copy in writes:
        copy.wait()


def kernel(
    gx_size,
    yz_size,
    feat,
    *refs,
):
    small_in, refs = refs[:9], refs[9:]
    mixed, forces, *refs = refs
    small, refs = refs[:9], refs[9:]
    run(gx_size, yz_size, feat, small_in, small, mixed, forces, *refs)


def run(
    gx_size,
    yz_size,
    feat,
    small_in,
    small,
    mixed,
    forces,
    ext0,
    ext1,
    ext2,
    ext3,
    mix0,
    mix1,
    *refs,
):
    n = len(SUMS)
    part_out, part_in, refs = refs[:n], refs[n : 2 * n], refs[2 * n :]
    (
        posx,
        oh,
        coef,
        readout,
        wide,
        w_turned,
        zf,
        ang,
        inverses,
        target,
        edges,
        acc,
        gate,
        gsc,
        raw,
        mix_out,
        side,
        sums,
        grad,
        force_y,
        force_y_in,
        force_x,
        force_x_in,
        small_sem,
        load_sem,
        out_sem,
        pos_send,
        pos_recv,
        x_send,
        x_recv,
        part_send,
        part_recv,
        mix_send,
        mix_recv,
        force_send,
        force_recv,
    ) = refs
    ext, ext2 = (ext0, ext1, ext2, ext3), (mix0, mix1)
    gx = lax.axis_index("gx")
    yz = lax.axis_index("yz")

    def device(dx, dy):
        return (lax.rem(gx + dx + gx_size, gx_size), lax.rem(yz + dy + yz_size, yz_size))

    def remote(src, dst, send, recv, step):
        return pltpu.make_async_remote_copy(
            src_ref=src,
            dst_ref=dst,
            send_sem=send,
            recv_sem=recv,
            device_id=device(*step),
            device_id_type=MESH,
        )

    barrier = pltpu.get_barrier_semaphore()
    for step in NEIGHBOURS:
        pl.semaphore_signal(barrier, inc=1, device_id=device(*step), device_id_type=MESH)

    small_loads = [
        pltpu.make_async_copy(small_in[i], small[i], small_sem.at[i]) for i in range(len(small))
    ]
    feat_load = pltpu.make_async_copy(feat, raw, load_sem)
    feat_load.start()
    for load in small_loads:
        load.start()
    pos, dst, shift, wr, wq, w_scalar, w_gate, w_vector, w_tensor = small

    def turn(g):
        lo, hi = GROUPS[g]
        for i in range(hi - lo):
            for p in range(NP):
                ext[g][p, i] = jnp.transpose(raw[p, 0, :, pl.ds((lo + i) * C, C)])

    feat_load.wait()
    turn(0)
    pl.semaphore_wait(barrier, len(NEIGHBOURS))

    x_copies = []
    for g in range(len(GROUPS)):
        for own, ghost, dx in ((0, 2, -1), (1, 3, 1)):
            x_copies.append(
                remote(ext[g].at[own], ext[g].at[ghost], x_send.at[g, own], x_recv.at[g, own], (dx, 0))
            )
    x_copies[0].start()
    x_copies[1].start()

    for load in small_loads:
        load.wait()
    for p in range(NP):
        posx[0, p] = jnp.zeros((16, S), F32)
        for m in range(3):
            posx[0, p, pl.ds(m, 1), :] = pos[p, m]
        for k in range(NE):
            posx[0, p, pl.ds(3 + k, 1), :] = dst[k, p].astype(F32)
            posx[0, p, pl.ds(6 + k, 1), :] = shift[k, p].astype(F32)
    own = pl.ds(0, NP)
    pos_copies = [
        remote(posx.at[0, 0], posx.at[0, 2], pos_send.at[0], pos_recv.at[0], (-1, 0)),
        remote(posx.at[0, 1], posx.at[0, 3], pos_send.at[1], pos_recv.at[1], (1, 0)),
        remote(posx.at[0, own], posx.at[2, own], pos_send.at[2], pos_recv.at[2], (0, -1)),
        remote(posx.at[0, own], posx.at[1, own], pos_send.at[3], pos_recv.at[3], (0, 1)),
    ]
    for copy in pos_copies:
        copy.start()
    for g in range(1, len(GROUPS)):
        turn(g)
        x_copies[2 * g].start()
        x_copies[2 * g + 1].start()

    def turned(w):
        high, low = split(w)
        rows = jnp.concatenate([high, low, high, jnp.zeros_like(w)], axis=0)
        return jnp.transpose(rows).astype(BF16)

    def widen(f, carry):
        at = pl.ds(pl.multiple_of(f * C, C), C)
        wide[at, :] = turned(wr[:, at])
        return carry

    lax.fori_loop(0, 7, widen, 0)

    for copy in pos_copies:
        copy.wait_recv()
    edges[...] = jnp.zeros_like(edges)
    for q in range(COUNT):
        y, p = q // NP, q % NP
        at = pl.ds(NE * q, NE)
        edges[0, at, :] = posx[y, p, pl.ds(3, NE), :]
        edges[1, at, :] = posx[y, p, pl.ds(6, NE), :]
        edges[2, at, :] = jnp.full((NE, S), p, F32)
        edges[3, at, :] = jnp.full((NE, S), (1, 0, 2)[y], F32)
        for m in range(3):
            edges[4 + m, at, :] = jnp.broadcast_to(posx[y, p, pl.ds(m, 1), :], (NE, S))
    place = edges[0]
    one = jnp.ones_like(place)
    nil = jnp.zeros_like(place)

    def at_least(x, bound):
        return jnp.where(x >= float(bound), one, nil)

    ext_x = at_least(place, 3 * S) + at_least(place, 6 * S) + at_least(place, 9 * S)
    left = place - ext_x * float(3 * S)
    ext_y = at_least(left, S) + at_least(left, 2 * S)
    step_x = ext_x - 1.0 - edges[2]
    step_y = ext_y - 1.0
    far_slot = left - ext_y * S
    target[...] = jnp.where(edges[3] + step_y == 1.0, ext_x * S + far_slot, -1.0)

    atom = lax.broadcasted_iota(jnp.int32, (S, ROWS), 0).astype(F32)

    def pick(y, carry):
        for p in range(NP):
            rows = [target[pl.ds(NE * (NP * y + p) + k, 1), :] for k in range(NE)]
            ends = jnp.concatenate(rows, axis=1) - atom
            for i, x in enumerate((1, 2, 3 * p)):
                hit = jnp.where(ends == float(x * S), 1.0, 0.0).astype(BF16)
                oh[p, pl.ds(i * S, S), pl.ds(pl.multiple_of(y * ROWS, ROWS), ROWS)] = hit
        return carry

    lax.fori_loop(0, 3, pick, 0)

    def in_parts(x):
        first, rest = split(x)
        second, third = split(rest)
        return jnp.concatenate([first, second, third, jnp.zeros_like(first)], 0).astype(BF16)

    def whole(x):
        return (x[0:8] + x[8:16]) + x[16:24]

    lanes = far_slot.astype(jnp.int32)

    def far_place(m):
        found = []
        for slot in (3, 0, 1, 2):
            row = jnp.broadcast_to(posx[0, slot, pl.ds(m, 1), :], (EDGE_ROWS, S))
            found.append(jnp.take_along_axis(row, lanes, axis=1, mode="promise_in_bounds"))
        low = jnp.where(ext_x == 0.0, found[0], found[1])
        high = jnp.where(ext_x == 2.0, found[2], found[3])
        return jnp.where(ext_x < 2.0, low, high)

    disp_x = far_place(0) - edges[4] + step_x
    disp_y = far_place(1) - edges[5] + step_y
    disp_z = far_place(2) - edges[6] + edges[1]
    rho = jnp.sqrt(disp_x * disp_x + disp_y * disp_y + disp_z * disp_z + SOFTENING)
    inverse = 1.0 / rho
    u_x, u_y, u_z = disp_x * inverse, disp_y * inverse, disp_z * inverse
    inverses[...] = inverse
    length_sq = u_x * u_x + u_y * u_y + u_z * u_z
    angular = (
        u_x,
        u_y,
        u_z,
        ROOT_THREE * u_x * u_y,
        ROOT_THREE * u_y * u_z,
        0.5 * (3.0 * u_z * u_z - length_sq),
        ROOT_THREE * u_x * u_z,
        0.5 * ROOT_THREE * (u_x * u_x - u_y * u_y),
    )
    for f in range(8):
        ang[f] = angular[f]
    zf[...] = jnp.zeros_like(zf)
    for b in range(NB):
        off = (rho - (0.5 + SPACING * b)) / SPACING
        basis = jnp.exp(-(off * off))
        slope = basis * off * (-2.0 / SPACING)
        for i, value in enumerate((basis, slope)):
            high, low = split(value)
            zf[32 * i + b] = high
            zf[32 * i + 8 + b] = high
            zf[32 * i + 16 + b] = low

    def columns(k):
        return pl.ds(k * S, S)

    def expanded(q, part, rows):
        edge_rows = [zf[pl.ds(32 * part, 32), NE * q + k, :] for k in range(NP * NE)]
        return dot(rows, jnp.concatenate(edge_rows, axis=1).astype(BF16))

    for q in range(0, COUNT, NP):
        out = expanded(q, 0, wide[pl.ds(0, 7 * C), :])
        for f in range(7):
            for p in range(NP):
                coef[f, q + p] = out[f * C : (f + 1) * C, p * ROWS : (p + 1) * ROWS]

    def columns(k):
        return pl.ds(k * S, S)

    def gather(bufs, g, to, first, last):
        buf = bufs[g]
        n = buf.shape[1]

        for p in range(NP):
            tiles = [buf[slot].reshape(n * C, S) for slot in (0, 1, 3 - p)[first:last]]
            out = dot(jnp.concatenate(tiles, axis=1), oh[p, pl.ds(first * S, (last - first) * S), :])
            for i in range(n):
                for y in range(3):
                    gsc[to + i, NP * y + p] = out[i * C : (i + 1) * C, y * ROWS : (y + 1) * ROWS]

    def each_row(fn, lo, hi):
        steps = C // STEP

        def run(i, carry):
            q = i // steps
            fn(q, pl.ds(pl.multiple_of((i - q * steps) * STEP, STEP), STEP))
            return carry

        lax.fori_loop(lo * steps, hi * steps, run, 0)

    def angle(f, q, k):
        return ang[f, pl.ds(NE * q + k, 1), :]

    def message_sv(p, r):
        total = [jnp.zeros((STEP, S), F32) for _ in range(READ_BLOCKS)]
        for k in range(NE):
            e = columns(k)
            s = gsc[0, p, r, e]
            v = [gsc[1 + m, p, r, e] for m in range(3)]
            u = [angle(m, p, k) for m in range(3)]
            along = u[0] * v[0] + u[1] * v[1] + u[2] * v[2]
            total[0] = total[0] + coef[0, p, r, e] * s + coef[1, p, r, e] * along
            r3s = coef[3, p, r, e] * s
            r4 = coef[4, p, r, e]
            for m in range(3):
                total[1 + m] = total[1 + m] + r3s * u[m] + r4 * v[m]
        for b in range(READ_BLOCKS):
            acc[b, p, r, :] = total[b]

    def message_st(p, r):
        total = [jnp.zeros((STEP, S), F32) for _ in range(5)]
        for k in range(NE):
            e = columns(k)
            r5s = coef[5, p, r, e] * gsc[0, p, r, e]
            for n in range(5):
                total[n] = total[n] + r5s * angle(3 + n, p, k)
        for n in range(5):
            acc[READ_BLOCKS + n, p, r, :] = total[n]

    def message_t(lo, hi):
        def fn(p, r):
            total = [acc[b, p, r, :] for b in (0, *range(lo, hi))]
            for k in range(NE):
                e = columns(k)
                along = None
                r6 = coef[6, p, r, e]
                for n in range(lo, hi):
                    t = gsc[n, p, r, e]
                    term = angle(n - 1, p, k) * t
                    along = term if along is None else along + term
                    total[1 + n - lo] = total[1 + n - lo] + r6 * t
                total[0] = total[0] + coef[2, p, r, e] * along
            for i, b in enumerate((0, *range(lo, hi))):
                acc[b, p, r, :] = total[i]

        return fn

    third = 1.0 / NE

    def mix(lo, hi, w):
        def run(p, carry):
            terms = [(acc[b, p] * third).astype(BF16) for b in range(lo, hi)]
            out = dot(w_turned[pl.ds(w * C, C), :], jnp.concatenate(terms, axis=1))
            for b in range(lo, hi):
                acc[b, p] = out[:, (b - lo) * S : (b - lo + 1) * S]
            return carry

        lax.fori_loop(0, NP, run, 0)

    part_copies = []
    for h in range(len(SUMS)):
        for i, dy in ((0, -1), (1, 1)):
            part_copies.append(
                remote(
                    part_out[h].at[i],
                    part_in[h].at[1 - i],
                    part_send.at[h, i],
                    part_recv.at[h, i],
                    (0, dy),
                )
            )

    def send_sums(h):
        for i in range(2):
            for p in range(NP):
                for j, b in enumerate(SUMS[h]):
                    part_out[h][i, p, j] = acc[b, NP * (1 + i) + p].astype(BF16)
            part_copies[2 * h + i].start()

    def add_sums(h):
        for i in range(2):
            part_copies[2 * h + i].wait_recv()
        for p in range(NP):
            for j, b in enumerate(SUMS[h]):
                acc[b, p] = acc[b, p] + part_in[h][0, p, j].astype(F32) + part_in[h][1, p, j].astype(F32)

    for g, (lo, hi) in enumerate(GROUPS):
        x_copies[2 * g].wait_recv()
        x_copies[2 * g + 1].wait_recv()
        gather(ext, g, lo, 0, 3)
        message = message_sv if g == 0 else message_t(lo, hi)
        each_row(message, NP, COUNT)
        send_sums(g)
        each_row(message, 0, NP)
        if g == 0:
            each_row(message_st, 0, COUNT)

    wide[pl.ds(8 * C, C), :] = turned(wq[:, pl.ds(0, C)])
    last = turned(wq[:, pl.ds(C, C)])
    wide[pl.ds(7 * C, C), :] = last
    wide[pl.ds(9 * C, C), :] = last
    for i, w in enumerate((w_scalar, w_gate, w_vector, w_tensor)):
        w_turned[pl.ds(i * C, C), :] = jnp.transpose(w[...])
    for q in range(0, COUNT, NP):
        outs = [expanded(q, 0, wide[pl.ds(7 * C, C), :]), expanded(q, 1, wide[pl.ds(8 * C, 2 * C), :])]
        for p in range(NP):
            at = slice(p * ROWS, (p + 1) * ROWS)
            readout[q + p, 0] = outs[0][:, at]
            readout[q + p, 1] = outs[1][0:C, at]
            readout[q + p, 2] = outs[1][C : 2 * C, at]
    add_sums(0)
    mix(1, 4, 2)
    add_sums(1)
    add_sums(2)
    add_sums(3)

    def scalars(p, carry):
        out = dot(w_turned[pl.ds(0, 2 * C), :], (acc[0, p] * third).astype(BF16))
        pre = out[0:C]
        acc[0, p] = pre * jax.nn.sigmoid(pre)
        gate[p] = jax.nn.sigmoid(out[C : 2 * C])
        return carry

    lax.fori_loop(0, NP, scalars, 0)

    def read_block(b, y, slot):
        g = b // 2
        return ext2[g].at[y, slot, b - GROUPS2[g][0]]

    def read_block(b, at):
        return ext2[b // 2].at[at, b % 2]

    def update_sv(p, r):
        g = gate[p, r, :]
        for b in range(READ_BLOCKS):
            old = ext[0][p, b, r, :].astype(F32)
            step = g * acc[b, p, r, :] if b > 0 else acc[0, p, r, :]
            read_block(b, p)[r, :] = (old + step).astype(BF16)

    each_row(update_sv, 0, NP)
    mix_x, mix_y = [], []
    for g, buf in enumerate(ext2):
        spans = (
            (mix_x, buf.at[0], buf.at[2], (-1, 0)),
            (mix_x, buf.at[1], buf.at[3], (1, 0)),
            (mix_y, buf.at[own], buf.at[pl.ds(6, NP)], (0, -1)),
            (mix_y, buf.at[own], buf.at[pl.ds(4, NP)], (0, 1)),
        )
        for n, (into, src, to, step) in enumerate(spans):
            into.append(remote(src, to, mix_send.at[g, n], mix_recv.at[g, n], step))
    for copy in (*mix_x, *mix_y):
        copy.start()

    def results(lo, hi, value):
        for i in range(hi - lo):
            for p in range(NP):
                mix_out[p, 0, :, pl.ds((lo + i) * C, C)] = jnp.transpose(value(p, i).astype(BF16))

    mix(4, 9, 3)
    for g, (lo, hi) in enumerate(GROUPS2):
        results(lo, hi, lambda p, i: ext2[g][p, i])
    for g, (lo, hi) in enumerate(GROUPS):
        if g > 0:
            results(lo, hi, lambda p, i: ext[g][p, i].astype(F32) + gate[p] * acc[lo + i, p])
    write = pltpu.make_async_copy(mix_out, mixed, out_sem)
    write.start()

    def near_side(q, r):
        at = jnp.where(q < NP, q, q + 2)
        row = [read_block(b, at)[r, :].astype(F32) for b in range(READ_BLOCKS)]
        s, v = row[0], row[1:]
        for k in range(NE):
            e = columns(k)
            u = [angle(m, q, k) for m in range(3)]
            along = u[0] * v[0] + u[1] * v[1] + u[2] * v[2]
            q1 = readout[q, 0, r, e]
            side[q, 0, r, e] = readout[q, 1, r, e] * s
            side[q, 1, r, e] = readout[q, 2, r, e] * along
            side[q, 2, r, e] = q1 * along
            for m in range(3):
                side[q, 3 + m, r, e] = q1 * v[m]

    for g, (lo, hi) in enumerate(GROUPS2):
        gather(ext2, g, lo, 0, 2)
    each_row(near_side, 0, NP)
    for copy in mix_y:
        copy.wait_recv()
    each_row(near_side, NP, COUNT)

    def fold(x):
        return sum(x[8 * i : 8 * i + 8] for i in range(1, STEP // 8)) + x[0:8]

    sums[...] = jnp.zeros_like(sums)

    def pairs(q, lo, first):
        def pair(i, carry):
            r = pl.ds(pl.multiple_of(i * STEP, STEP), STEP)
            carry = list(carry)
            for k in range(NE):
                e = columns(k)
                far = [gsc[lo + b, q, r, e] for b in range(READ_BLOCKS)]
                u = [angle(m, q, k) for m in range(3)]
                along = u[0] * far[1] + u[1] * far[2] + u[2] * far[3]
                term = side[q, 0, r, e] * far[0] + side[q, 1, r, e] * along
                carry[4 * k] = carry[4 * k] + fold(term)
                own_q = side[q, 2, r, e]
                for m in range(3):
                    term = side[q, 3 + m, r, e] * along + own_q * far[1 + m]
                    carry[4 * k + 1 + m] = carry[4 * k + 1 + m] + fold(term)
            return tuple(carry)

        zero = jnp.zeros((8, S), F32)
        totals = lax.fori_loop(0, C // STEP, pair, (zero,) * (4 * NE))
        for k in range(NE):
            for i in range(4):
                row = jnp.sum(totals[4 * k + i], axis=0, keepdims=True)
                at = pl.ds(NE * q + k, 1)
                sums[i, at, :] = row if first else sums[i, at, :] + row

    def each_pairs(lo, first):
        def run(q, carry):
            pairs(q, lo, first)
            return carry

        lax.fori_loop(0, COUNT, run, 0)

    each_pairs(0, True)
    for copy in (*pos_copies, *x_copies, *part_copies):
        copy.wait_send()
    for g, (lo, hi) in enumerate(GROUPS2):
        mix_x[2 * g].wait_recv()
        mix_x[2 * g + 1].wait_recv()
        gather(ext2, g, READ_BLOCKS + lo, 2, 3)
    each_pairs(READ_BLOCKS, False)

    t_rho, g_x, g_y, g_z = (sums[i] for i in range(4))
    u_x, u_y, u_z, inverse = ang[0], ang[1], ang[2], inverses[...]
    radial_part = t_rho - (u_x * g_x + u_y * g_y + u_z * g_z) * inverse
    grad[...] = jnp.zeros_like(grad)
    grad[0] = radial_part * u_x + g_x * inverse
    grad[1] = radial_part * u_y + g_y * inverse
    grad[2] = radial_part * u_z + g_z * inverse

    def at_atoms(q):
        return (grad[:, NE * q, :] + grad[:, NE * q + 1, :]) + grad[:, NE * q + 2, :]

    force_copies = []
    for i, dy in ((0, -1), (1, 1)):
        force_copies.append(
            remote(force_y.at[i], force_y_in.at[1 - i], force_send.at[i], force_recv.at[i], (0, dy))
        )
    for i, (p, dx) in enumerate(((0, 1), (1, -1))):
        force_copies.append(
            remote(force_x.at[p], force_x_in.at[p], force_send.at[2 + i], force_recv.at[2 + i], (dx, 0))
        )
    parts = []
    for p in range(NP):
        used = [NE * (NP * y + p) + k for y in range(3) for k in range(NE)]
        parts.append(in_parts(jnp.concatenate([grad[:, row, :] for row in used], axis=1)))
    total = [at_atoms(p) for p in range(NP)]
    def scatter(p, lo, hi):
        return whole(jnp.transpose(dot(oh[p, pl.ds(lo * S, (hi - lo) * S), :], parts[p], (1, 1))))

    for p in range(NP):
        force_x[1 - p] = -scatter(p, 2, 3)
        force_copies[3 - p].start()
    for i in range(2):
        for p in range(NP):
            force_y[i, p] = at_atoms(NP * (1 + i) + p)
        force_copies[i].start()
    for p in range(NP):
        out = scatter(p, 0, 2)
        for i in range(NP):
            total[i] = total[i] - out[:, i * S : (i + 1) * S]
    for copy in force_copies:
        copy.wait_recv()
    for p in range(NP):
        value = (total[p] + force_x_in[p]) + (force_y_in[0, p] + force_y_in[1, p])
        for m in range(3):
            forces[p, m] = value[m : m + 1]

    for copy in (*mix_x, *mix_y, *force_copies):
        copy.wait_send()
    write.wait()


def solution(mesh):
    gx_size, yz_size = mesh.shape["gx"], mesh.shape["yz"]

    def body(features, positions, *rest):
        args = (features, jnp.transpose(positions, (0, 2, 1, 3)), *rest)
        vmem = pl.BlockSpec(memory_space=pltpu.VMEM)
        anywhere = pl.BlockSpec(memory_space=pl.ANY)
        dma = pltpu.SemaphoreType.DMA

        def run_all(*refs):
            kernel(gx_size, yz_size, *refs)

        small = [pltpu.VMEM(x.shape, x.dtype) for x in args[1:]]
        new_features, force = pl.pallas_call(
            run_all,
            out_shape=(
                jax.ShapeDtypeStruct((NP, 1, S, BLOCKS * C), BF16),
                jax.ShapeDtypeStruct((NP, 3, 1, S), F32),
            ),
            in_specs=[anywhere] * 10,
            out_specs=(anywhere, vmem),
            scratch_shapes=small
            + [
                *[pltpu.VMEM((4, hi - lo, C, S), BF16) for lo, hi in GROUPS],
                *[pltpu.VMEM((8, hi - lo, C, S), BF16) for lo, hi in GROUPS2],
                *[pltpu.VMEM((2, NP, len(blocks), C, S), BF16) for blocks in SUMS],
                *[pltpu.VMEM((2, NP, len(blocks), C, S), BF16) for blocks in SUMS],
                pltpu.VMEM((3, 4, 16, S), F32),
                pltpu.VMEM((NP, 3 * S, 3 * ROWS), BF16),
                pltpu.VMEM((7, COUNT, C, ROWS), F32),
                pltpu.VMEM((COUNT, 3, C, ROWS), F32),
                pltpu.VMEM((10 * C, 32), BF16),
                pltpu.VMEM((4 * C, C), BF16),
                pltpu.VMEM((64, EDGE_ROWS, S), F32),
                pltpu.VMEM((8, EDGE_ROWS, S), F32),
                pltpu.VMEM((EDGE_ROWS, S), F32),
                pltpu.VMEM((EDGE_ROWS, S), F32),
                pltpu.VMEM((7, EDGE_ROWS, S), F32),
                pltpu.VMEM((BLOCKS, COUNT, C, S), F32),
                pltpu.VMEM((NP, C, S), F32),
                pltpu.VMEM((BLOCKS, COUNT, C, ROWS), F32),
                pltpu.VMEM((NP, 1, S, BLOCKS * C), BF16),
                pltpu.VMEM((NP, 1, S, BLOCKS * C), BF16),
                pltpu.VMEM((COUNT, 6, C, ROWS), F32),
                pltpu.VMEM((4, EDGE_ROWS, S), F32),
                pltpu.VMEM((8, EDGE_ROWS, S), F32),
                pltpu.VMEM((2, NP, 8, S), F32),
                pltpu.VMEM((2, NP, 8, S), F32),
                pltpu.VMEM((NP, 8, S), F32),
                pltpu.VMEM((NP, 8, S), F32),
                dma((len(small),)),
                dma,
                dma,
                dma((4,)),
                dma((4,)),
                dma((len(GROUPS), 2)),
                dma((len(GROUPS), 2)),
                dma((len(SUMS), 2)),
                dma((len(SUMS), 2)),
                dma((len(GROUPS2), 4)),
                dma((len(GROUPS2), 4)),
                dma((4,)),
                dma((4,)),
            ],
            compiler_params=pltpu.CompilerParams(
                collective_id=0, has_side_effects=True, vmem_limit_bytes=60 * 1024 * 1024
            ),
            cost_estimate=pl.CostEstimate(
                flops=6 * 10**9, bytes_accessed=2 * 10**6, transcendentals=10**5
            ),
        )(*args)
        new_features, force = pl.pallas_call(
            deliver,
            out_shape=(
                jax.ShapeDtypeStruct((NP, 1, S, BLOCKS * C), BF16),
                jax.ShapeDtypeStruct((NP, 3, 1, S), F32),
            ),
            in_specs=[anywhere] * 2,
            out_specs=(anywhere, anywhere),
            scratch_shapes=[
                pltpu.VMEM((NP, 1, S, BLOCKS * C), BF16),
                pltpu.VMEM((NP, 3, 1, S), F32),
                dma((2, 1 + NP)),
            ],
            compiler_params=pltpu.CompilerParams(vmem_limit_bytes=60 * 1024 * 1024),
            cost_estimate=pl.CostEstimate(flops=0, bytes_accessed=12 * 10**5, transcendentals=0),
        )(new_features, force)
        return new_features, jnp.transpose(force, (0, 2, 1, 3))

    in_specs = (
        P("gx", "yz", None, None),
        P("gx", "yz", None, None),
        P(None, "gx", "yz", None),
        P(None, "gx", "yz", None),
        P(),
        P(),
        P(),
        P(),
        P(),
        P(),
    )
    out_specs = (P("gx", "yz", None, None), P("gx", "yz", None, None))
    return jax.shard_map(body, mesh=mesh, in_specs=in_specs, out_specs=out_specs, check_vma=False)
```

```python
import math

import jax
import jax.numpy as jnp
from jax import lax
from jax.experimental import pallas as pl
from jax.experimental.pallas import tpu as pltpu
from jax.sharding import PartitionSpec as P

MESH = pl.DeviceIdType.MESH
F32 = jnp.float32
BF16 = jnp.bfloat16
SOFTENING = 0.25
SPACING = 0.6
ROOT_THREE = math.sqrt(3.0)
C = 128
S = 128
NB = 8
NE = 3
NP = 2
BLOCKS = 9
READ_BLOCKS = 4
ROWS = NE * S
STEP = 32
GROUPS = ((0, 4), (4, 6), (6, 8), (8, 9))
SUMS = ((1, 2, 3), (4, 5), (6, 7), (8, 0))
GROUPS2 = ((0, 2), (2, 4))
COUNT = 6
EDGE_ROWS = 24
NEIGHBOURS = ((-1, 0), (1, 0), (0, -1), (0, 1))


def split(x):
    high = x.astype(BF16).astype(F32)
    return high, x - high


def dot(a, b, contract=(1, 0)):
    dims = (((contract[0],), (contract[1],)), ((), ()))
    return lax.dot_general(a, b, dims, preferred_element_type=F32)


def deliver(mixed, forces, mixed_out, forces_out, held, held_forces, sems):
    parts = [(forces, held_forces, forces_out)]
    parts += [(mixed.at[p], held.at[p], mixed_out.at[p]) for p in range(NP)]
    reads = [pltpu.make_async_copy(a, b, sems.at[0, i]) for i, (a, b, _) in enumerate(parts)]
    writes = [pltpu.make_async_copy(b, c, sems.at[1, i]) for i, (_, b, c) in enumerate(parts)]
    for copy in reads:
        copy.start()
    for read, write in zip(reads, writes):
        read.wait()
        write.start()
    for copy in writes:
        copy.wait()


def kernel(
    gx_size,
    yz_size,
    feat,
    *refs,
):
    small_in, refs = refs[:9], refs[9:]
    mixed, forces, *refs = refs
    small, refs = refs[:9], refs[9:]
    run(gx_size, yz_size, feat, small_in, small, mixed, forces, *refs)


def run(
    gx_size,
    yz_size,
    feat,
    small_in,
    small,
    mixed,
    forces,
    ext0,
    ext1,
    ext2,
    ext3,
    mix0,
    mix1,
    *refs,
):
    n = len(SUMS)
    part_out, part_in, refs = refs[:n], refs[n : 2 * n], refs[2 * n :]
    (
        posx,
        oh,
        coef,
        readout,
        wide,
        w_turned,
        zf,
        ang,
        inverses,
        target,
        edges,
        acc,
        gate,
        gsc,
        raw,
        mix_out,
        side,
        sums,
        grad,
        force_y,
        force_y_in,
        force_x,
        force_x_in,
        small_sem,
        load_sem,
        out_sem,
        pos_send,
        pos_recv,
        x_send,
        x_recv,
        part_send,
        part_recv,
        mix_send,
        mix_recv,
        force_send,
        force_recv,
    ) = refs
    ext, ext2 = (ext0, ext1, ext2, ext3), (mix0, mix1)
    gx = lax.axis_index("gx")
    yz = lax.axis_index("yz")

    def device(dx, dy):
        return (lax.rem(gx + dx + gx_size, gx_size), lax.rem(yz + dy + yz_size, yz_size))

    def remote(src, dst, send, recv, step):
        return pltpu.make_async_remote_copy(
            src_ref=src,
            dst_ref=dst,
            send_sem=send,
            recv_sem=recv,
            device_id=device(*step),
            device_id_type=MESH,
        )

    barrier = pltpu.get_barrier_semaphore()
    for step in NEIGHBOURS:
        pl.semaphore_signal(barrier, inc=1, device_id=device(*step), device_id_type=MESH)

    small_loads = [
        pltpu.make_async_copy(small_in[i], small[i], small_sem.at[i]) for i in range(len(small))
    ]
    feat_load = pltpu.make_async_copy(feat, raw, load_sem)
    feat_load.start()
    for load in small_loads:
        load.start()
    pos, dst, shift, wr, wq, w_scalar, w_gate, w_vector, w_tensor = small

    def turn(g):
        lo, hi = GROUPS[g]
        for i in range(hi - lo):
            for p in range(NP):
                ext[g][p, i] = jnp.transpose(raw[p, 0, :, pl.ds((lo + i) * C, C)])

    feat_load.wait()
    turn(0)
    pl.semaphore_wait(barrier, len(NEIGHBOURS))

    x_copies = []
    for g in range(len(GROUPS)):
        for own, ghost, dx in ((0, 2, -1), (1, 3, 1)):
            x_copies.append(
                remote(ext[g].at[own], ext[g].at[ghost], x_send.at[g, own], x_recv.at[g, own], (dx, 0))
            )
    x_copies[0].start()
    x_copies[1].start()

    for load in small_loads:
        load.wait()
    for p in range(NP):
        posx[0, p] = jnp.zeros((16, S), F32)
        for m in range(3):
            posx[0, p, pl.ds(m, 1), :] = pos[p, m]
        for k in range(NE):
            posx[0, p, pl.ds(3 + k, 1), :] = dst[k, p].astype(F32)
            posx[0, p, pl.ds(6 + k, 1), :] = shift[k, p].astype(F32)
    own = pl.ds(0, NP)
    pos_copies = [
        remote(posx.at[0, 0], posx.at[0, 2], pos_send.at[0], pos_recv.at[0], (-1, 0)),
        remote(posx.at[0, 1], posx.at[0, 3], pos_send.at[1], pos_recv.at[1], (1, 0)),
        remote(posx.at[0, own], posx.at[2, own], pos_send.at[2], pos_recv.at[2], (0, -1)),
        remote(posx.at[0, own], posx.at[1, own], pos_send.at[3], pos_recv.at[3], (0, 1)),
    ]
    for copy in pos_copies:
        copy.start()
    for g in range(1, len(GROUPS)):
        turn(g)
        x_copies[2 * g].start()
        x_copies[2 * g + 1].start()

    def turned(w):
        high, low = split(w)
        rows = jnp.concatenate([high, low, high, jnp.zeros_like(w)], axis=0)
        return jnp.transpose(rows).astype(BF16)

    def widen(f, carry):
        at = pl.ds(pl.multiple_of(f * C, C), C)
        wide[at, :] = turned(wr[:, at])
        return carry

    lax.fori_loop(0, 7, widen, 0)

    for copy in pos_copies:
        copy.wait_recv()
    edges[...] = jnp.zeros_like(edges)
    for q in range(COUNT):
        y, p = q // NP, q % NP
        at = pl.ds(NE * q, NE)
        edges[0, at, :] = posx[y, p, pl.ds(3, NE), :]
        edges[1, at, :] = posx[y, p, pl.ds(6, NE), :]
        edges[2, at, :] = jnp.full((NE, S), p, F32)
        edges[3, at, :] = jnp.full((NE, S), (1, 0, 2)[y], F32)
        for m in range(3):
            edges[4 + m, at, :] = jnp.broadcast_to(posx[y, p, pl.ds(m, 1), :], (NE, S))
    place = edges[0]
    one = jnp.ones_like(place)
    nil = jnp.zeros_like(place)

    def at_least(x, bound):
        return jnp.where(x >= float(bound), one, nil)

    ext_x = at_least(place, 3 * S) + at_least(place, 6 * S) + at_least(place, 9 * S)
    left = place - ext_x * float(3 * S)
    ext_y = at_least(left, S) + at_least(left, 2 * S)
    step_x = ext_x - 1.0 - edges[2]
    step_y = ext_y - 1.0
    far_slot = left - ext_y * S
    target[...] = jnp.where(edges[3] + step_y == 1.0, ext_x * S + far_slot, -1.0)

    atom = lax.broadcasted_iota(jnp.int32, (S, ROWS), 0).astype(F32)

    def pick(y, carry):
        for p in range(NP):
            rows = [target[pl.ds(NE * (NP * y + p) + k, 1), :] for k in range(NE)]
            ends = jnp.concatenate(rows, axis=1) - atom
            for i, x in enumerate((1, 2, 3 * p)):
                hit = jnp.where(ends == float(x * S), 1.0, 0.0).astype(BF16)
                oh[p, pl.ds(i * S, S), pl.ds(pl.multiple_of(y * ROWS, ROWS), ROWS)] = hit
        return carry

    lax.fori_loop(0, 3, pick, 0)

    def in_parts(x):
        first, rest = split(x)
        second, third = split(rest)
        return jnp.concatenate([first, second, third, jnp.zeros_like(first)], 0).astype(BF16)

    def whole(x):
        return (x[0:8] + x[8:16]) + x[16:24]

    lanes = far_slot.astype(jnp.int32)

    def far_place(m):
        found = []
        for slot in (3, 0, 1, 2):
            row = jnp.broadcast_to(posx[0, slot, pl.ds(m, 1), :], (EDGE_ROWS, S))
            found.append(jnp.take_along_axis(row, lanes, axis=1, mode="promise_in_bounds"))
        low = jnp.where(ext_x == 0.0, found[0], found[1])
        high = jnp.where(ext_x == 2.0, found[2], found[3])
        return jnp.where(ext_x < 2.0, low, high)

    disp_x = far_place(0) - edges[4] + step_x
    disp_y = far_place(1) - edges[5] + step_y
    disp_z = far_place(2) - edges[6] + edges[1]
    rho = jnp.sqrt(disp_x * disp_x + disp_y * disp_y + disp_z * disp_z + SOFTENING)
    inverse = 1.0 / rho
    u_x, u_y, u_z = disp_x * inverse, disp_y * inverse, disp_z * inverse
    inverses[...] = inverse
    length_sq = u_x * u_x + u_y * u_y + u_z * u_z
    angular = (
        u_x,
        u_y,
        u_z,
        ROOT_THREE * u_x * u_y,
        ROOT_THREE * u_y * u_z,
        0.5 * (3.0 * u_z * u_z - length_sq),
        ROOT_THREE * u_x * u_z,
        0.5 * ROOT_THREE * (u_x * u_x - u_y * u_y),
    )
    for f in range(8):
        ang[f] = angular[f]
    zf[...] = jnp.zeros_like(zf)
    for b in range(NB):
        off = (rho - (0.5 + SPACING * b)) / SPACING
        basis = jnp.exp(-(off * off))
        slope = basis * off * (-2.0 / SPACING)
        for i, value in enumerate((basis, slope)):
            high, low = split(value)
            zf[32 * i + b] = high
            zf[32 * i + 8 + b] = high
            zf[32 * i + 16 + b] = low

    def columns(k):
        return pl.ds(k * S, S)

    def expanded(q, part, rows):
        edge_rows = [zf[pl.ds(32 * part, 32), NE * q + k, :] for k in range(NP * NE)]
        return dot(rows, jnp.concatenate(edge_rows, axis=1).astype(BF16))

    for q in range(0, COUNT, NP):
        out = expanded(q, 0, wide[pl.ds(0, 7 * C), :])
        for f in range(7):
            for p in range(NP):
                coef[f, q + p] = out[f * C : (f + 1) * C, p * ROWS : (p + 1) * ROWS]

    def columns(k):
        return pl.ds(k * S, S)

    def gather(bufs, g, to, first, last):
        buf = bufs[g]
        n = buf.shape[1]

        for p in range(NP):
            tiles = [buf[slot].reshape(n * C, S) for slot in (0, 1, 3 - p)[first:last]]
            out = dot(jnp.concatenate(tiles, axis=1), oh[p, pl.ds(first * S, (last - first) * S), :])
            for i in range(n):
                for y in range(3):
                    gsc[to + i, NP * y + p] = out[i * C : (i + 1) * C, y * ROWS : (y + 1) * ROWS]

    def each_row(fn, lo, hi):
        steps = C // STEP

        def run(i, carry):
            q = i // steps
            fn(q, pl.ds(pl.multiple_of((i - q * steps) * STEP, STEP), STEP))
            return carry

        lax.fori_loop(lo * steps, hi * steps, run, 0)

    def angle(f, q, k):
        return ang[f, pl.ds(NE * q + k, 1), :]

    def message_sv(p, r):
        total = [jnp.zeros((STEP, S), F32) for _ in range(READ_BLOCKS)]
        for k in range(NE):
            e = columns(k)
            s = gsc[0, p, r, e]
            v = [gsc[1 + m, p, r, e] for m in range(3)]
            u = [angle(m, p, k) for m in range(3)]
            along = u[0] * v[0] + u[1] * v[1] + u[2] * v[2]
            total[0] = total[0] + coef[0, p, r, e] * s + coef[1, p, r, e] * along
            r3s = coef[3, p, r, e] * s
            r4 = coef[4, p, r, e]
            for m in range(3):
                total[1 + m] = total[1 + m] + r3s * u[m] + r4 * v[m]
        for b in range(READ_BLOCKS):
            acc[b, p, r, :] = total[b]

    def message_st(p, r):
        total = [jnp.zeros((STEP, S), F32) for _ in range(5)]
        for k in range(NE):
            e = columns(k)
            r5s = coef[5, p, r, e] * gsc[0, p, r, e]
            for n in range(5):
                total[n] = total[n] + r5s * angle(3 + n, p, k)
        for n in range(5):
            acc[READ_BLOCKS + n, p, r, :] = total[n]

    def message_t(lo, hi):
        def fn(p, r):
            total = [acc[b, p, r, :] for b in (0, *range(lo, hi))]
            for k in range(NE):
                e = columns(k)
                along = None
                r6 = coef[6, p, r, e]
                for n in range(lo, hi):
                    t = gsc[n, p, r, e]
                    term = angle(n - 1, p, k) * t
                    along = term if along is None else along + term
                    total[1 + n - lo] = total[1 + n - lo] + r6 * t
                total[0] = total[0] + coef[2, p, r, e] * along
            for i, b in enumerate((0, *range(lo, hi))):
                acc[b, p, r, :] = total[i]

        return fn

    third = 1.0 / NE

    def mix(lo, hi, w):
        def run(p, carry):
            terms = [(acc[b, p] * third).astype(BF16) for b in range(lo, hi)]
            out = dot(w_turned[pl.ds(w * C, C), :], jnp.concatenate(terms, axis=1))
            for b in range(lo, hi):
                acc[b, p] = out[:, (b - lo) * S : (b - lo + 1) * S]
            return carry

        lax.fori_loop(0, NP, run, 0)

    part_copies = []
    for h in range(len(SUMS)):
        for i, dy in ((0, -1), (1, 1)):
            part_copies.append(
                remote(
                    part_out[h].at[i],
                    part_in[h].at[1 - i],
                    part_send.at[h, i],
                    part_recv.at[h, i],
                    (0, dy),
                )
            )

    def send_sums(h):
        for i in range(2):
            for p in range(NP):
                for j, b in enumerate(SUMS[h]):
                    part_out[h][i, p, j] = acc[b, NP * (1 + i) + p].astype(BF16)
            part_copies[2 * h + i].start()

    def add_sums(h):
        for i in range(2):
            part_copies[2 * h + i].wait_recv()
        for p in range(NP):
            for j, b in enumerate(SUMS[h]):
                acc[b, p] = acc[b, p] + part_in[h][0, p, j].astype(F32) + part_in[h][1, p, j].astype(F32)

    for g, (lo, hi) in enumerate(GROUPS):
        x_copies[2 * g].wait_recv()
        x_copies[2 * g + 1].wait_recv()
        gather(ext, g, lo, 0, 3)
        message = message_sv if g == 0 else message_t(lo, hi)
        each_row(message, NP, COUNT)
        send_sums(g)
        each_row(message, 0, NP)
        if g == 0:
            each_row(message_st, 0, COUNT)

    wide[pl.ds(8 * C, C), :] = turned(wq[:, pl.ds(0, C)])
    last = turned(wq[:, pl.ds(C, C)])
    wide[pl.ds(7 * C, C), :] = last
    wide[pl.ds(9 * C, C), :] = last
    for i, w in enumerate((w_scalar, w_gate, w_vector, w_tensor)):
        w_turned[pl.ds(i * C, C), :] = jnp.transpose(w[...])
    for q in range(0, COUNT, NP):
        outs = [expanded(q, 0, wide[pl.ds(7 * C, C), :]), expanded(q, 1, wide[pl.ds(8 * C, 2 * C), :])]
        for p in range(NP):
            at = slice(p * ROWS, (p + 1) * ROWS)
            readout[q + p, 0] = outs[0][:, at]
            readout[q + p, 1] = outs[1][0:C, at]
            readout[q + p, 2] = outs[1][C : 2 * C, at]
    add_sums(0)
    mix(1, 4, 2)
    add_sums(1)
    add_sums(2)
    add_sums(3)

    def scalars(p, carry):
        out = dot(w_turned[pl.ds(0, 2 * C), :], (acc[0, p] * third).astype(BF16))
        pre = out[0:C]
        acc[0, p] = pre * jax.nn.sigmoid(pre)
        gate[p] = jax.nn.sigmoid(out[C : 2 * C])
        return carry

    lax.fori_loop(0, NP, scalars, 0)

    def read_block(b, y, slot):
        g = b // 2
        return ext2[g].at[y, slot, b - GROUPS2[g][0]]

    def read_block(b, at):
        return ext2[b // 2].at[at, b % 2]

    def update_sv(p, r):
        g = gate[p, r, :]
        for b in range(READ_BLOCKS):
            old = ext[0][p, b, r, :].astype(F32)
            step = g * acc[b, p, r, :] if b > 0 else acc[0, p, r, :]
            read_block(b, p)[r, :] = (old + step).astype(BF16)

    each_row(update_sv, 0, NP)
    mix_x, mix_y = [], []
    for g, buf in enumerate(ext2):
        spans = (
            (mix_x, buf.at[0], buf.at[2], (-1, 0)),
            (mix_x, buf.at[1], buf.at[3], (1, 0)),
            (mix_y, buf.at[own], buf.at[pl.ds(6, NP)], (0, -1)),
            (mix_y, buf.at[own], buf.at[pl.ds(4, NP)], (0, 1)),
        )
        for n, (into, src, to, step) in enumerate(spans):
            into.append(remote(src, to, mix_send.at[g, n], mix_recv.at[g, n], step))
    for copy in (*mix_x[:2], *mix_y, *mix_x[2:]):
        copy.start()

    def near_side(q, r):
        at = jnp.where(q < NP, q, q + 2)
        row = [read_block(b, at)[r, :].astype(F32) for b in range(READ_BLOCKS)]
        s, v = row[0], row[1:]
        for k in range(NE):
            e = columns(k)
            u = [angle(m, q, k) for m in range(3)]
            along = u[0] * v[0] + u[1] * v[1] + u[2] * v[2]
            q1 = readout[q, 0, r, e]
            side[q, 0, r, e] = readout[q, 1, r, e] * s
            side[q, 1, r, e] = readout[q, 2, r, e] * along
            side[q, 2, r, e] = q1 * along
            for m in range(3):
                side[q, 3 + m, r, e] = q1 * v[m]

    for g, (lo, hi) in enumerate(GROUPS2):
        gather(ext2, g, lo, 0, 2)
    each_row(near_side, 0, NP)

    def fold(x):
        return sum(x[8 * i : 8 * i + 8] for i in range(1, STEP // 8)) + x[0:8]

    sums[...] = jnp.zeros_like(sums)

    def pairs(q, lo, first):
        def pair(i, carry):
            r = pl.ds(pl.multiple_of(i * STEP, STEP), STEP)
            carry = list(carry)
            for k in range(NE):
                e = columns(k)
                far = [gsc[lo + b, q, r, e] for b in range(READ_BLOCKS)]
                u = [angle(m, q, k) for m in range(3)]
                along = u[0] * far[1] + u[1] * far[2] + u[2] * far[3]
                term = side[q, 0, r, e] * far[0] + side[q, 1, r, e] * along
                carry[4 * k] = carry[4 * k] + fold(term)
                own_q = side[q, 2, r, e]
                for m in range(3):
                    term = side[q, 3 + m, r, e] * along + own_q * far[1 + m]
                    carry[4 * k + 1 + m] = carry[4 * k + 1 + m] + fold(term)
            return tuple(carry)

        zero = jnp.zeros((8, S), F32)
        totals = lax.fori_loop(0, C // STEP, pair, (zero,) * (4 * NE))
        for k in range(NE):
            for i in range(4):
                row = jnp.sum(totals[4 * k + i], axis=0, keepdims=True)
                at = pl.ds(NE * q + k, 1)
                sums[i, at, :] = row if first else sums[i, at, :] + row

    def each_pairs(lo, first, pillars):
        def run(q, carry):
            pairs(q, lo, first)
            return carry

        lax.fori_loop(*pillars, run, 0)

    each_pairs(0, True, (0, NP))
    for copy in mix_y:
        copy.wait_recv()
    each_row(near_side, NP, COUNT)
    each_pairs(0, True, (NP, COUNT))
    for copy in (*pos_copies, *x_copies, *part_copies):
        copy.wait_send()
    for g, (lo, hi) in enumerate(GROUPS2):
        mix_x[2 * g].wait_recv()
        mix_x[2 * g + 1].wait_recv()
        gather(ext2, g, READ_BLOCKS + lo, 2, 3)
    each_pairs(READ_BLOCKS, False, (0, COUNT))

    t_rho, g_x, g_y, g_z = (sums[i] for i in range(4))
    u_x, u_y, u_z, inverse = ang[0], ang[1], ang[2], inverses[...]
    radial_part = t_rho - (u_x * g_x + u_y * g_y + u_z * g_z) * inverse
    grad[...] = jnp.zeros_like(grad)
    grad[0] = radial_part * u_x + g_x * inverse
    grad[1] = radial_part * u_y + g_y * inverse
    grad[2] = radial_part * u_z + g_z * inverse

    def at_atoms(q):
        return (grad[:, NE * q, :] + grad[:, NE * q + 1, :]) + grad[:, NE * q + 2, :]

    force_copies = []
    for i, dy in ((0, -1), (1, 1)):
        force_copies.append(
            remote(force_y.at[i], force_y_in.at[1 - i], force_send.at[i], force_recv.at[i], (0, dy))
        )
    for i, (p, dx) in enumerate(((0, 1), (1, -1))):
        force_copies.append(
            remote(force_x.at[p], force_x_in.at[p], force_send.at[2 + i], force_recv.at[2 + i], (dx, 0))
        )
    parts = []
    for p in range(NP):
        used = [NE * (NP * y + p) + k for y in range(3) for k in range(NE)]
        parts.append(in_parts(jnp.concatenate([grad[:, row, :] for row in used], axis=1)))
    total = [at_atoms(p) for p in range(NP)]
    def scatter(p, lo, hi):
        return whole(jnp.transpose(dot(oh[p, pl.ds(lo * S, (hi - lo) * S), :], parts[p], (1, 1))))

    for p in range(NP):
        force_x[1 - p] = -scatter(p, 2, 3)
        force_copies[3 - p].start()
    for i in range(2):
        for p in range(NP):
            force_y[i, p] = at_atoms(NP * (1 + i) + p)
        force_copies[i].start()
    for p in range(NP):
        out = scatter(p, 0, 2)
        for i in range(NP):
            total[i] = total[i] - out[:, i * S : (i + 1) * S]
    def results(lo, hi, value):
        for i in range(hi - lo):
            for p in range(NP):
                mix_out[p, 0, :, pl.ds((lo + i) * C, C)] = jnp.transpose(value(p, i).astype(BF16))

    mix(4, 9, 3)
    for g, (lo, hi) in enumerate(GROUPS2):
        results(lo, hi, lambda p, i: ext2[g][p, i])
    for g, (lo, hi) in enumerate(GROUPS):
        if g > 0:
            results(lo, hi, lambda p, i: ext[g][p, i].astype(F32) + gate[p] * acc[lo + i, p])
    write = pltpu.make_async_copy(mix_out, mixed, out_sem)
    write.start()

    for copy in force_copies:
        copy.wait_recv()
    for p in range(NP):
        value = (total[p] + force_x_in[p]) + (force_y_in[0, p] + force_y_in[1, p])
        for m in range(3):
            forces[p, m] = value[m : m + 1]

    for copy in (*mix_x, *mix_y, *force_copies):
        copy.wait_send()
    write.wait()


def solution(mesh):
    gx_size, yz_size = mesh.shape["gx"], mesh.shape["yz"]

    def body(features, positions, *rest):
        args = (features, jnp.transpose(positions, (0, 2, 1, 3)), *rest)
        vmem = pl.BlockSpec(memory_space=pltpu.VMEM)
        anywhere = pl.BlockSpec(memory_space=pl.ANY)
        dma = pltpu.SemaphoreType.DMA

        def run_all(*refs):
            kernel(gx_size, yz_size, *refs)

        small = [pltpu.VMEM(x.shape, x.dtype) for x in args[1:]]
        new_features, force = pl.pallas_call(
            run_all,
            out_shape=(
                jax.ShapeDtypeStruct((NP, 1, S, BLOCKS * C), BF16),
                jax.ShapeDtypeStruct((NP, 3, 1, S), F32),
            ),
            in_specs=[anywhere] * 10,
            out_specs=(anywhere, vmem),
            scratch_shapes=small
            + [
                *[pltpu.VMEM((4, hi - lo, C, S), BF16) for lo, hi in GROUPS],
                *[pltpu.VMEM((8, hi - lo, C, S), BF16) for lo, hi in GROUPS2],
                *[pltpu.VMEM((2, NP, len(blocks), C, S), BF16) for blocks in SUMS],
                *[pltpu.VMEM((2, NP, len(blocks), C, S), BF16) for blocks in SUMS],
                pltpu.VMEM((3, 4, 16, S), F32),
                pltpu.VMEM((NP, 3 * S, 3 * ROWS), BF16),
                pltpu.VMEM((7, COUNT, C, ROWS), F32),
                pltpu.VMEM((COUNT, 3, C, ROWS), F32),
                pltpu.VMEM((10 * C, 32), BF16),
                pltpu.VMEM((4 * C, C), BF16),
                pltpu.VMEM((64, EDGE_ROWS, S), F32),
                pltpu.VMEM((8, EDGE_ROWS, S), F32),
                pltpu.VMEM((EDGE_ROWS, S), F32),
                pltpu.VMEM((EDGE_ROWS, S), F32),
                pltpu.VMEM((7, EDGE_ROWS, S), F32),
                pltpu.VMEM((BLOCKS, COUNT, C, S), F32),
                pltpu.VMEM((NP, C, S), F32),
                pltpu.VMEM((BLOCKS, COUNT, C, ROWS), F32),
                pltpu.VMEM((NP, 1, S, BLOCKS * C), BF16),
                pltpu.VMEM((NP, 1, S, BLOCKS * C), BF16),
                pltpu.VMEM((COUNT, 6, C, ROWS), F32),
                pltpu.VMEM((4, EDGE_ROWS, S), F32),
                pltpu.VMEM((8, EDGE_ROWS, S), F32),
                pltpu.VMEM((2, NP, 8, S), F32),
                pltpu.VMEM((2, NP, 8, S), F32),
                pltpu.VMEM((NP, 8, S), F32),
                pltpu.VMEM((NP, 8, S), F32),
                dma((len(small),)),
                dma,
                dma,
                dma((4,)),
                dma((4,)),
                dma((len(GROUPS), 2)),
                dma((len(GROUPS), 2)),
                dma((len(SUMS), 2)),
                dma((len(SUMS), 2)),
                dma((len(GROUPS2), 4)),
                dma((len(GROUPS2), 4)),
                dma((4,)),
                dma((4,)),
            ],
            compiler_params=pltpu.CompilerParams(
                collective_id=0, has_side_effects=True, vmem_limit_bytes=60 * 1024 * 1024
            ),
            cost_estimate=pl.CostEstimate(
                flops=6 * 10**9, bytes_accessed=2 * 10**6, transcendentals=10**5
            ),
        )(*args)
        new_features, force = pl.pallas_call(
            deliver,
            out_shape=(
                jax.ShapeDtypeStruct((NP, 1, S, BLOCKS * C), BF16),
                jax.ShapeDtypeStruct((NP, 3, 1, S), F32),
            ),
            in_specs=[anywhere] * 2,
            out_specs=(anywhere, anywhere),
            scratch_shapes=[
                pltpu.VMEM((NP, 1, S, BLOCKS * C), BF16),
                pltpu.VMEM((NP, 3, 1, S), F32),
                dma((2, 1 + NP)),
            ],
            compiler_params=pltpu.CompilerParams(vmem_limit_bytes=60 * 1024 * 1024),
            cost_estimate=pl.CostEstimate(flops=0, bytes_accessed=12 * 10**5, transcendentals=0),
        )(new_features, force)
        return new_features, jnp.transpose(force, (0, 2, 1, 3))

    in_specs = (
        P("gx", "yz", None, None),
        P("gx", "yz", None, None),
        P(None, "gx", "yz", None),
        P(None, "gx", "yz", None),
        P(),
        P(),
        P(),
        P(),
        P(),
        P(),
    )
    out_specs = (P("gx", "yz", None, None), P("gx", "yz", None, None))
    return jax.shard_map(body, mesh=mesh, in_specs=in_specs, out_specs=out_specs, check_vma=False)
```

```python
import math

import jax
import jax.numpy as jnp
from jax import lax
from jax.experimental import pallas as pl
from jax.experimental.pallas import tpu as pltpu
from jax.sharding import PartitionSpec as P

MESH = pl.DeviceIdType.MESH
F32 = jnp.float32
BF16 = jnp.bfloat16
SOFTENING = 0.25
SPACING = 0.6
ROOT_THREE = math.sqrt(3.0)
C = 128
S = 128
NB = 8
NE = 3
NP = 2
BLOCKS = 9
READ_BLOCKS = 4
ROWS = NE * S
STEP = 32
GROUPS = ((0, 4), (4, 6), (6, 8), (8, 9))
SUMS = ((1, 2, 3), (4, 5), (6, 7), (8, 0))
GROUPS2 = ((0, 2), (2, 4))
COUNT = 6
EDGE_ROWS = 24
NEIGHBOURS = ((-1, 0), (1, 0), (0, -1), (0, 1))


def split(x):
    high = x.astype(BF16).astype(F32)
    return high, x - high


def dot(a, b, contract=(1, 0)):
    dims = (((contract[0],), (contract[1],)), ((), ()))
    return lax.dot_general(a, b, dims, preferred_element_type=F32)


def deliver(mixed, forces, mixed_out, forces_out, held, held_forces, sems):
    parts = [(forces, held_forces, forces_out)]
    parts += [(mixed.at[p], held.at[p], mixed_out.at[p]) for p in range(NP)]
    reads = [pltpu.make_async_copy(a, b, sems.at[0, i]) for i, (a, b, _) in enumerate(parts)]
    writes = [pltpu.make_async_copy(b, c, sems.at[1, i]) for i, (_, b, c) in enumerate(parts)]
    for copy in reads:
        copy.start()
    for read, write in zip(reads, writes):
        read.wait()
        write.start()
    for copy in writes:
        copy.wait()


def kernel(
    gx_size,
    yz_size,
    feat,
    *refs,
):
    small_in, refs = refs[:9], refs[9:]
    mixed, forces, *refs = refs
    small, refs = refs[:9], refs[9:]
    run(gx_size, yz_size, feat, small_in, small, mixed, forces, *refs)


def run(
    gx_size,
    yz_size,
    feat,
    small_in,
    small,
    mixed,
    forces,
    ext0,
    ext1,
    ext2,
    ext3,
    mix0,
    mix1,
    *refs,
):
    n = len(SUMS)
    part_out, part_in, refs = refs[:n], refs[n : 2 * n], refs[2 * n :]
    (
        posx,
        oh,
        coef,
        readout,
        wide,
        w_turned,
        zf,
        ang,
        inverses,
        target,
        edges,
        acc,
        gate,
        gsc,
        raw,
        mix_out,
        side,
        sums,
        grad,
        force_y,
        force_y_in,
        force_x,
        force_x_in,
        small_sem,
        load_sem,
        out_sem,
        pos_send,
        pos_recv,
        x_send,
        x_recv,
        part_send,
        part_recv,
        mix_send,
        mix_recv,
        force_send,
        force_recv,
    ) = refs
    ext, ext2 = (ext0, ext1, ext2, ext3), (mix0, mix1)
    gx = lax.axis_index("gx")
    yz = lax.axis_index("yz")

    def device(dx, dy):
        return (lax.rem(gx + dx + gx_size, gx_size), lax.rem(yz + dy + yz_size, yz_size))

    def remote(src, dst, send, recv, step):
        return pltpu.make_async_remote_copy(
            src_ref=src,
            dst_ref=dst,
            send_sem=send,
            recv_sem=recv,
            device_id=device(*step),
            device_id_type=MESH,
        )

    barrier = pltpu.get_barrier_semaphore()
    for step in NEIGHBOURS:
        pl.semaphore_signal(barrier, inc=1, device_id=device(*step), device_id_type=MESH)

    small_loads = [
        pltpu.make_async_copy(small_in[i], small[i], small_sem.at[i]) for i in range(len(small))
    ]
    feat_load = pltpu.make_async_copy(feat, raw, load_sem)
    feat_load.start()
    for load in small_loads:
        load.start()
    pos, dst, shift, wr, wq, w_scalar, w_gate, w_vector, w_tensor = small

    def turn(g):
        lo, hi = GROUPS[g]
        for i in range(hi - lo):
            for p in range(NP):
                ext[g][p, i] = jnp.transpose(raw[p, 0, :, pl.ds((lo + i) * C, C)])

    feat_load.wait()
    turn(0)
    pl.semaphore_wait(barrier, len(NEIGHBOURS))

    x_copies = []
    for g in range(len(GROUPS)):
        for own, ghost, dx in ((0, 2, -1), (1, 3, 1)):
            x_copies.append(
                remote(ext[g].at[own], ext[g].at[ghost], x_send.at[g, own], x_recv.at[g, own], (dx, 0))
            )
    x_copies[0].start()
    x_copies[1].start()

    for load in small_loads:
        load.wait()
    for p in range(NP):
        posx[0, p] = jnp.zeros((16, S), F32)
        for m in range(3):
            posx[0, p, pl.ds(m, 1), :] = pos[p, m]
        for k in range(NE):
            posx[0, p, pl.ds(3 + k, 1), :] = dst[k, p].astype(F32)
            posx[0, p, pl.ds(6 + k, 1), :] = shift[k, p].astype(F32)
    own = pl.ds(0, NP)
    pos_copies = [
        remote(posx.at[0, 0], posx.at[0, 2], pos_send.at[0], pos_recv.at[0], (-1, 0)),
        remote(posx.at[0, 1], posx.at[0, 3], pos_send.at[1], pos_recv.at[1], (1, 0)),
        remote(posx.at[0, own], posx.at[2, own], pos_send.at[2], pos_recv.at[2], (0, -1)),
        remote(posx.at[0, own], posx.at[1, own], pos_send.at[3], pos_recv.at[3], (0, 1)),
    ]
    for copy in pos_copies:
        copy.start()
    for g in range(1, len(GROUPS)):
        turn(g)
        x_copies[2 * g].start()
        x_copies[2 * g + 1].start()

    def turned(w):
        high, low = split(w)
        rows = jnp.concatenate([high, low, high, jnp.zeros_like(w)], axis=0)
        return jnp.transpose(rows).astype(BF16)

    def widen(f, carry):
        at = pl.ds(pl.multiple_of(f * C, C), C)
        wide[at, :] = turned(wr[:, at])
        return carry

    lax.fori_loop(0, 7, widen, 0)

    for copy in pos_copies:
        copy.wait_recv()
    edges[...] = jnp.zeros_like(edges)
    for q in range(COUNT):
        y, p = q // NP, q % NP
        at = pl.ds(NE * q, NE)
        edges[0, at, :] = posx[y, p, pl.ds(3, NE), :]
        edges[1, at, :] = posx[y, p, pl.ds(6, NE), :]
        edges[2, at, :] = jnp.full((NE, S), p, F32)
        edges[3, at, :] = jnp.full((NE, S), (1, 0, 2)[y], F32)
        for m in range(3):
            edges[4 + m, at, :] = jnp.broadcast_to(posx[y, p, pl.ds(m, 1), :], (NE, S))
    place = edges[0]
    one = jnp.ones_like(place)
    nil = jnp.zeros_like(place)

    def at_least(x, bound):
        return jnp.where(x >= float(bound), one, nil)

    ext_x = at_least(place, 3 * S) + at_least(place, 6 * S) + at_least(place, 9 * S)
    left = place - ext_x * float(3 * S)
    ext_y = at_least(left, S) + at_least(left, 2 * S)
    step_x = ext_x - 1.0 - edges[2]
    step_y = ext_y - 1.0
    far_slot = left - ext_y * S
    target[...] = jnp.where(edges[3] + step_y == 1.0, ext_x * S + far_slot, -1.0)

    atom = lax.broadcasted_iota(jnp.int32, (S, ROWS), 0).astype(F32)

    def pick(y, carry):
        for p in range(NP):
            rows = [target[pl.ds(NE * (NP * y + p) + k, 1), :] for k in range(NE)]
            ends = jnp.concatenate(rows, axis=1) - atom
            for i, x in enumerate((1, 2, 3 * p)):
                hit = jnp.where(ends == float(x * S), 1.0, 0.0).astype(BF16)
                oh[p, pl.ds(i * S, S), pl.ds(pl.multiple_of(y * ROWS, ROWS), ROWS)] = hit
        return carry

    lax.fori_loop(0, 3, pick, 0)

    def in_parts(x):
        first, rest = split(x)
        second, third = split(rest)
        return jnp.concatenate([first, second, third, jnp.zeros_like(first)], 0).astype(BF16)

    def whole(x):
        return (x[0:8] + x[8:16]) + x[16:24]

    lanes = far_slot.astype(jnp.int32)

    def far_place(m):
        found = []
        for slot in (3, 0, 1, 2):
            row = jnp.broadcast_to(posx[0, slot, pl.ds(m, 1), :], (EDGE_ROWS, S))
            found.append(jnp.take_along_axis(row, lanes, axis=1, mode="promise_in_bounds"))
        low = jnp.where(ext_x == 0.0, found[0], found[1])
        high = jnp.where(ext_x == 2.0, found[2], found[3])
        return jnp.where(ext_x < 2.0, low, high)

    disp_x = far_place(0) - edges[4] + step_x
    disp_y = far_place(1) - edges[5] + step_y
    disp_z = far_place(2) - edges[6] + edges[1]
    rho = jnp.sqrt(disp_x * disp_x + disp_y * disp_y + disp_z * disp_z + SOFTENING)
    inverse = 1.0 / rho
    u_x, u_y, u_z = disp_x * inverse, disp_y * inverse, disp_z * inverse
    inverses[...] = inverse
    length_sq = u_x * u_x + u_y * u_y + u_z * u_z
    angular = (
        u_x,
        u_y,
        u_z,
        ROOT_THREE * u_x * u_y,
        ROOT_THREE * u_y * u_z,
        0.5 * (3.0 * u_z * u_z - length_sq),
        ROOT_THREE * u_x * u_z,
        0.5 * ROOT_THREE * (u_x * u_x - u_y * u_y),
    )
    for f in range(8):
        ang[f] = angular[f]
    zf[...] = jnp.zeros_like(zf)
    for b in range(NB):
        off = (rho - (0.5 + SPACING * b)) / SPACING
        basis = jnp.exp(-(off * off))
        slope = basis * off * (-2.0 / SPACING)
        for i, value in enumerate((basis, slope)):
            high, low = split(value)
            zf[32 * i + b] = high
            zf[32 * i + 8 + b] = high
            zf[32 * i + 16 + b] = low

    def columns(k):
        return pl.ds(k * S, S)

    def expanded(q, part, rows):
        edge_rows = [zf[pl.ds(32 * part, 32), NE * q + k, :] for k in range(NP * NE)]
        return dot(rows, jnp.concatenate(edge_rows, axis=1).astype(BF16))

    for q in range(0, COUNT, NP):
        out = expanded(q, 0, wide[pl.ds(0, 7 * C), :])
        for f in range(7):
            for p in range(NP):
                coef[f, q + p] = out[f * C : (f + 1) * C, p * ROWS : (p + 1) * ROWS]

    def columns(k):
        return pl.ds(k * S, S)

    def gather(bufs, g, to, first, last):
        buf = bufs[g]
        n = buf.shape[1]

        for p in range(NP):
            tiles = [buf[slot].reshape(n * C, S) for slot in (0, 1, 3 - p)[first:last]]
            out = dot(jnp.concatenate(tiles, axis=1), oh[p, pl.ds(first * S, (last - first) * S), :])
            for i in range(n):
                for y in range(3):
                    gsc[to + i, NP * y + p] = out[i * C : (i + 1) * C, y * ROWS : (y + 1) * ROWS]

    def each_row(fn, lo, hi):
        steps = C // (2 * STEP)

        def run(i, carry):
            q = i // steps
            for j in range(2):
                fn(q, pl.ds(pl.multiple_of((i - q * steps) * (2 * STEP) + j * STEP, STEP), STEP))
            return carry

        lax.fori_loop(lo * steps, hi * steps, run, 0)

    def angle(f, q, k):
        return ang[f, pl.ds(NE * q + k, 1), :]

    def message_sv(p, r):
        total = [jnp.zeros((STEP, S), F32) for _ in range(READ_BLOCKS)]
        for k in range(NE):
            e = columns(k)
            s = gsc[0, p, r, e]
            v = [gsc[1 + m, p, r, e] for m in range(3)]
            u = [angle(m, p, k) for m in range(3)]
            along = u[0] * v[0] + u[1] * v[1] + u[2] * v[2]
            total[0] = total[0] + coef[0, p, r, e] * s + coef[1, p, r, e] * along
            r3s = coef[3, p, r, e] * s
            r4 = coef[4, p, r, e]
            for m in range(3):
                total[1 + m] = total[1 + m] + r3s * u[m] + r4 * v[m]
        for b in range(READ_BLOCKS):
            acc[b, p, r, :] = total[b]

    def message_st(p, r):
        total = [jnp.zeros((STEP, S), F32) for _ in range(5)]
        for k in range(NE):
            e = columns(k)
            r5s = coef[5, p, r, e] * gsc[0, p, r, e]
            for n in range(5):
                total[n] = total[n] + r5s * angle(3 + n, p, k)
        for n in range(5):
            acc[READ_BLOCKS + n, p, r, :] = total[n]

    def message_t(lo, hi):
        def fn(p, r):
            total = [acc[b, p, r, :] for b in (0, *range(lo, hi))]
            for k in range(NE):
                e = columns(k)
                along = None
                r6 = coef[6, p, r, e]
                for n in range(lo, hi):
                    t = gsc[n, p, r, e]
                    term = angle(n - 1, p, k) * t
                    along = term if along is None else along + term
                    total[1 + n - lo] = total[1 + n - lo] + r6 * t
                total[0] = total[0] + coef[2, p, r, e] * along
            for i, b in enumerate((0, *range(lo, hi))):
                acc[b, p, r, :] = total[i]

        return fn

    third = 1.0 / NE

    def mix(lo, hi, w):
        def run(p, carry):
            terms = [(acc[b, p] * third).astype(BF16) for b in range(lo, hi)]
            out = dot(w_turned[pl.ds(w * C, C), :], jnp.concatenate(terms, axis=1))
            for b in range(lo, hi):
                acc[b, p] = out[:, (b - lo) * S : (b - lo + 1) * S]
            return carry

        lax.fori_loop(0, NP, run, 0)

    part_copies = []
    for h in range(len(SUMS)):
        for i, dy in ((0, -1), (1, 1)):
            part_copies.append(
                remote(
                    part_out[h].at[i],
                    part_in[h].at[1 - i],
                    part_send.at[h, i],
                    part_recv.at[h, i],
                    (0, dy),
                )
            )

    def send_sums(h):
        for i in range(2):
            for p in range(NP):
                for j, b in enumerate(SUMS[h]):
                    part_out[h][i, p, j] = acc[b, NP * (1 + i) + p].astype(BF16)
            part_copies[2 * h + i].start()

    def add_sums(h):
        for i in range(2):
            part_copies[2 * h + i].wait_recv()
        for p in range(NP):
            for j, b in enumerate(SUMS[h]):
                acc[b, p] = acc[b, p] + part_in[h][0, p, j].astype(F32) + part_in[h][1, p, j].astype(F32)

    for g, (lo, hi) in enumerate(GROUPS):
        x_copies[2 * g].wait_recv()
        x_copies[2 * g + 1].wait_recv()
        gather(ext, g, lo, 0, 3)
        message = message_sv if g == 0 else message_t(lo, hi)
        each_row(message, NP, COUNT)
        send_sums(g)
        each_row(message, 0, NP)
        if g == 0:
            each_row(message_st, 0, COUNT)

    wide[pl.ds(8 * C, C), :] = turned(wq[:, pl.ds(0, C)])
    last = turned(wq[:, pl.ds(C, C)])
    wide[pl.ds(7 * C, C), :] = last
    wide[pl.ds(9 * C, C), :] = last
    for i, w in enumerate((w_scalar, w_gate, w_vector, w_tensor)):
        w_turned[pl.ds(i * C, C), :] = jnp.transpose(w[...])
    for q in range(0, COUNT, NP):
        outs = [expanded(q, 0, wide[pl.ds(7 * C, C), :]), expanded(q, 1, wide[pl.ds(8 * C, 2 * C), :])]
        for p in range(NP):
            at = slice(p * ROWS, (p + 1) * ROWS)
            readout[q + p, 0] = outs[0][:, at]
            readout[q + p, 1] = outs[1][0:C, at]
            readout[q + p, 2] = outs[1][C : 2 * C, at]
    add_sums(0)
    mix(1, 4, 2)
    add_sums(1)
    add_sums(2)
    add_sums(3)

    def scalars(p, carry):
        out = dot(w_turned[pl.ds(0, 2 * C), :], (acc[0, p] * third).astype(BF16))
        pre = out[0:C]
        acc[0, p] = pre * jax.nn.sigmoid(pre)
        gate[p] = jax.nn.sigmoid(out[C : 2 * C])
        return carry

    lax.fori_loop(0, NP, scalars, 0)

    def read_block(b, y, slot):
        g = b // 2
        return ext2[g].at[y, slot, b - GROUPS2[g][0]]

    def read_block(b, at):
        return ext2[b // 2].at[at, b % 2]

    def update_sv(p, r):
        g = gate[p, r, :]
        for b in range(READ_BLOCKS):
            old = ext[0][p, b, r, :].astype(F32)
            step = g * acc[b, p, r, :] if b > 0 else acc[0, p, r, :]
            read_block(b, p)[r, :] = (old + step).astype(BF16)

    each_row(update_sv, 0, NP)
    mix_x, mix_y = [], []
    for g, buf in enumerate(ext2):
        spans = (
            (mix_x, buf.at[0], buf.at[2], (-1, 0)),
            (mix_x, buf.at[1], buf.at[3], (1, 0)),
            (mix_y, buf.at[own], buf.at[pl.ds(6, NP)], (0, -1)),
            (mix_y, buf.at[own], buf.at[pl.ds(4, NP)], (0, 1)),
        )
        for n, (into, src, to, step) in enumerate(spans):
            into.append(remote(src, to, mix_send.at[g, n], mix_recv.at[g, n], step))
    for copy in (*mix_x[:2], *mix_y, *mix_x[2:]):
        copy.start()

    def near_side(q, r):
        at = jnp.where(q < NP, q, q + 2)
        row = [read_block(b, at)[r, :].astype(F32) for b in range(READ_BLOCKS)]
        s, v = row[0], row[1:]
        for k in range(NE):
            e = columns(k)
            u = [angle(m, q, k) for m in range(3)]
            along = u[0] * v[0] + u[1] * v[1] + u[2] * v[2]
            q1 = readout[q, 0, r, e]
            side[q, 0, r, e] = readout[q, 1, r, e] * s
            side[q, 1, r, e] = readout[q, 2, r, e] * along
            side[q, 2, r, e] = q1 * along
            for m in range(3):
                side[q, 3 + m, r, e] = q1 * v[m]

    for g, (lo, hi) in enumerate(GROUPS2):
        gather(ext2, g, lo, 0, 2)
    each_row(near_side, 0, NP)

    def fold(x):
        return sum(x[8 * i : 8 * i + 8] for i in range(1, STEP // 8)) + x[0:8]

    sums[...] = jnp.zeros_like(sums)

    def pairs(q, lo, first):
        totals = [None if first else sums[i % 4, NE * q + i // 4] for i in range(4 * NE)]

        def add(i, term):
            totals[i] = fold(term) if totals[i] is None else totals[i] + fold(term)

        for start in range(0, C, STEP):
            r = pl.ds(start, STEP)
            for k in range(NE):
                e = columns(k)
                far = [gsc[lo + b, q, r, e] for b in range(READ_BLOCKS)]
                u = [angle(m, q, k) for m in range(3)]
                along = u[0] * far[1] + u[1] * far[2] + u[2] * far[3]
                add(4 * k, side[q, 0, r, e] * far[0] + side[q, 1, r, e] * along)
                own_q = side[q, 2, r, e]
                for m in range(3):
                    add(4 * k + 1 + m, side[q, 3 + m, r, e] * along + own_q * far[1 + m])
        for i in range(4 * NE):
            sums[i % 4, NE * q + i // 4] = totals[i]

    def each_pairs(lo, first, pillars):
        def run(q, carry):
            pairs(q, lo, first)
            return carry

        lax.fori_loop(*pillars, run, 0)

    each_pairs(0, True, (0, NP))
    for copy in mix_y:
        copy.wait_recv()
    each_row(near_side, NP, COUNT)
    each_pairs(0, True, (NP, COUNT))
    for copy in (*pos_copies, *x_copies, *part_copies):
        copy.wait_send()
    for g, (lo, hi) in enumerate(GROUPS2):
        mix_x[2 * g].wait_recv()
        mix_x[2 * g + 1].wait_recv()
        gather(ext2, g, READ_BLOCKS + lo, 2, 3)
    each_pairs(READ_BLOCKS, False, (0, COUNT))

    t_rho, g_x, g_y, g_z = (jnp.sum(sums[i], axis=1) for i in range(4))
    u_x, u_y, u_z, inverse = ang[0], ang[1], ang[2], inverses[...]
    radial_part = t_rho - (u_x * g_x + u_y * g_y + u_z * g_z) * inverse
    grad[...] = jnp.zeros_like(grad)
    grad[0] = radial_part * u_x + g_x * inverse
    grad[1] = radial_part * u_y + g_y * inverse
    grad[2] = radial_part * u_z + g_z * inverse

    def at_atoms(q):
        return (grad[:, NE * q, :] + grad[:, NE * q + 1, :]) + grad[:, NE * q + 2, :]

    force_copies = []
    for i, dy in ((0, -1), (1, 1)):
        force_copies.append(
            remote(force_y.at[i], force_y_in.at[1 - i], force_send.at[i], force_recv.at[i], (0, dy))
        )
    for i, (p, dx) in enumerate(((0, 1), (1, -1))):
        force_copies.append(
            remote(force_x.at[p], force_x_in.at[p], force_send.at[2 + i], force_recv.at[2 + i], (dx, 0))
        )
    parts = []
    for p in range(NP):
        used = [NE * (NP * y + p) + k for y in range(3) for k in range(NE)]
        parts.append(in_parts(jnp.concatenate([grad[:, row, :] for row in used], axis=1)))
    total = [at_atoms(p) for p in range(NP)]
    def scatter(p, lo, hi):
        return whole(jnp.transpose(dot(oh[p, pl.ds(lo * S, (hi - lo) * S), :], parts[p], (1, 1))))

    for p in range(NP):
        force_x[1 - p] = -scatter(p, 2, 3)
        force_copies[3 - p].start()
    for i in range(2):
        for p in range(NP):
            force_y[i, p] = at_atoms(NP * (1 + i) + p)
        force_copies[i].start()
    for p in range(NP):
        out = scatter(p, 0, 2)
        for i in range(NP):
            total[i] = total[i] - out[:, i * S : (i + 1) * S]
    def results(lo, hi, value):
        for i in range(hi - lo):
            for p in range(NP):
                mix_out[p, 0, :, pl.ds((lo + i) * C, C)] = jnp.transpose(value(p, i).astype(BF16))

    mix(4, 9, 3)
    for g, (lo, hi) in enumerate(GROUPS2):
        results(lo, hi, lambda p, i: ext2[g][p, i])
    for g, (lo, hi) in enumerate(GROUPS):
        if g > 0:
            results(lo, hi, lambda p, i: ext[g][p, i].astype(F32) + gate[p] * acc[lo + i, p])
    write = pltpu.make_async_copy(mix_out, mixed, out_sem)
    write.start()

    for copy in force_copies:
        copy.wait_recv()
    for p in range(NP):
        value = (total[p] + force_x_in[p]) + (force_y_in[0, p] + force_y_in[1, p])
        for m in range(3):
            forces[p, m] = value[m : m + 1]

    for copy in (*mix_x, *mix_y, *force_copies):
        copy.wait_send()
    write.wait()


def solution(mesh):
    gx_size, yz_size = mesh.shape["gx"], mesh.shape["yz"]

    def body(features, positions, *rest):
        args = (features, jnp.transpose(positions, (0, 2, 1, 3)), *rest)
        vmem = pl.BlockSpec(memory_space=pltpu.VMEM)
        anywhere = pl.BlockSpec(memory_space=pl.ANY)
        dma = pltpu.SemaphoreType.DMA

        def run_all(*refs):
            kernel(gx_size, yz_size, *refs)

        small = [pltpu.VMEM(x.shape, x.dtype) for x in args[1:]]
        new_features, force = pl.pallas_call(
            run_all,
            out_shape=(
                jax.ShapeDtypeStruct((NP, 1, S, BLOCKS * C), BF16),
                jax.ShapeDtypeStruct((NP, 3, 1, S), F32),
            ),
            in_specs=[anywhere] * 10,
            out_specs=(anywhere, vmem),
            scratch_shapes=small
            + [
                *[pltpu.VMEM((4, hi - lo, C, S), BF16) for lo, hi in GROUPS],
                *[pltpu.VMEM((8, hi - lo, C, S), BF16) for lo, hi in GROUPS2],
                *[pltpu.VMEM((2, NP, len(blocks), C, S), BF16) for blocks in SUMS],
                *[pltpu.VMEM((2, NP, len(blocks), C, S), BF16) for blocks in SUMS],
                pltpu.VMEM((3, 4, 16, S), F32),
                pltpu.VMEM((NP, 3 * S, 3 * ROWS), BF16),
                pltpu.VMEM((7, COUNT, C, ROWS), F32),
                pltpu.VMEM((COUNT, 3, C, ROWS), F32),
                pltpu.VMEM((10 * C, 32), BF16),
                pltpu.VMEM((4 * C, C), BF16),
                pltpu.VMEM((64, EDGE_ROWS, S), F32),
                pltpu.VMEM((8, EDGE_ROWS, S), F32),
                pltpu.VMEM((EDGE_ROWS, S), F32),
                pltpu.VMEM((EDGE_ROWS, S), F32),
                pltpu.VMEM((7, EDGE_ROWS, S), F32),
                pltpu.VMEM((BLOCKS, COUNT, C, S), F32),
                pltpu.VMEM((NP, C, S), F32),
                pltpu.VMEM((BLOCKS, COUNT, C, ROWS), F32),
                pltpu.VMEM((NP, 1, S, BLOCKS * C), BF16),
                pltpu.VMEM((NP, 1, S, BLOCKS * C), BF16),
                pltpu.VMEM((COUNT, 6, C, ROWS), F32),
                pltpu.VMEM((4, EDGE_ROWS, 8, S), F32),
                pltpu.VMEM((8, EDGE_ROWS, S), F32),
                pltpu.VMEM((2, NP, 8, S), F32),
                pltpu.VMEM((2, NP, 8, S), F32),
                pltpu.VMEM((NP, 8, S), F32),
                pltpu.VMEM((NP, 8, S), F32),
                dma((len(small),)),
                dma,
                dma,
                dma((4,)),
                dma((4,)),
                dma((len(GROUPS), 2)),
                dma((len(GROUPS), 2)),
                dma((len(SUMS), 2)),
                dma((len(SUMS), 2)),
                dma((len(GROUPS2), 4)),
                dma((len(GROUPS2), 4)),
                dma((4,)),
                dma((4,)),
            ],
            compiler_params=pltpu.CompilerParams(
                collective_id=0, has_side_effects=True, vmem_limit_bytes=60 * 1024 * 1024
            ),
            cost_estimate=pl.CostEstimate(
                flops=6 * 10**9, bytes_accessed=2 * 10**6, transcendentals=10**5
            ),
        )(*args)
        new_features, force = pl.pallas_call(
            deliver,
            out_shape=(
                jax.ShapeDtypeStruct((NP, 1, S, BLOCKS * C), BF16),
                jax.ShapeDtypeStruct((NP, 3, 1, S), F32),
            ),
            in_specs=[anywhere] * 2,
            out_specs=(anywhere, anywhere),
            scratch_shapes=[
                pltpu.VMEM((NP, 1, S, BLOCKS * C), BF16),
                pltpu.VMEM((NP, 3, 1, S), F32),
                dma((2, 1 + NP)),
            ],
            compiler_params=pltpu.CompilerParams(vmem_limit_bytes=60 * 1024 * 1024),
            cost_estimate=pl.CostEstimate(flops=0, bytes_accessed=12 * 10**5, transcendentals=0),
        )(new_features, force)
        return new_features, jnp.transpose(force, (0, 2, 1, 3))

    in_specs = (
        P("gx", "yz", None, None),
        P("gx", "yz", None, None),
        P(None, "gx", "yz", None),
        P(None, "gx", "yz", None),
        P(),
        P(),
        P(),
        P(),
        P(),
        P(),
    )
    out_specs = (P("gx", "yz", None, None), P("gx", "yz", None, None))
    return jax.shard_map(body, mesh=mesh, in_specs=in_specs, out_specs=out_specs, check_vma=False)
```

```python
import math

import jax
import jax.numpy as jnp
from jax import lax
from jax.experimental import pallas as pl
from jax.experimental.pallas import tpu as pltpu
from jax.sharding import PartitionSpec as P

MESH = pl.DeviceIdType.MESH
F32 = jnp.float32
BF16 = jnp.bfloat16
SOFTENING = 0.25
SPACING = 0.6
ROOT_THREE = math.sqrt(3.0)
C = 128
S = 128
NB = 8
NE = 3
NP = 2
BLOCKS = 9
READ_BLOCKS = 4
ROWS = NE * S
STEP = 32
GROUPS = ((0, 4), (4, 6), (6, 8), (8, 9))
SUMS = ((1, 2, 3), (4, 5), (6, 7), (8, 0))
GROUPS2 = ((0, 2), (2, 4))
COUNT = 6
EDGE_ROWS = 24
NEIGHBOURS = ((-1, 0), (1, 0), (0, -1), (0, 1))


def split(x):
    high = x.astype(BF16).astype(F32)
    return high, x - high


def dot(a, b, contract=(1, 0)):
    dims = (((contract[0],), (contract[1],)), ((), ()))
    return lax.dot_general(a, b, dims, preferred_element_type=F32)


def deliver(mixed, forces, mixed_out, forces_out, held, held_forces, sems):
    parts = [(forces, held_forces, forces_out)]
    parts += [(mixed.at[p], held.at[p], mixed_out.at[p]) for p in range(NP)]
    reads = [pltpu.make_async_copy(a, b, sems.at[0, i]) for i, (a, b, _) in enumerate(parts)]
    writes = [pltpu.make_async_copy(b, c, sems.at[1, i]) for i, (_, b, c) in enumerate(parts)]
    for copy in reads:
        copy.start()
    for read, write in zip(reads, writes):
        read.wait()
        write.start()
    for copy in writes:
        copy.wait()


def kernel(
    gx_size,
    yz_size,
    feat,
    *refs,
):
    small_in, refs = refs[:9], refs[9:]
    mixed, forces, *refs = refs
    small, refs = refs[:9], refs[9:]
    run(gx_size, yz_size, feat, small_in, small, mixed, forces, *refs)


def run(
    gx_size,
    yz_size,
    feat,
    small_in,
    small,
    mixed,
    forces,
    ext0,
    ext1,
    ext2,
    ext3,
    mix0,
    mix1,
    *refs,
):
    n = len(SUMS)
    part_out, part_in, refs = refs[:n], refs[n : 2 * n], refs[2 * n :]
    (
        posx,
        oh,
        coef,
        readout,
        wide,
        w_turned,
        zf,
        ang,
        inverses,
        target,
        edges,
        acc,
        gate,
        gsc,
        raw,
        mix_out,
        side,
        sums,
        grad,
        force_y,
        force_y_in,
        force_x,
        force_x_in,
        small_sem,
        load_sem,
        out_sem,
        pos_send,
        pos_recv,
        x_send,
        x_recv,
        part_send,
        part_recv,
        mix_send,
        mix_recv,
        force_send,
        force_recv,
    ) = refs
    ext, ext2 = (ext0, ext1, ext2, ext3), (mix0, mix1)
    gx = lax.axis_index("gx")
    yz = lax.axis_index("yz")

    def device(dx, dy):
        return (lax.rem(gx + dx + gx_size, gx_size), lax.rem(yz + dy + yz_size, yz_size))

    def remote(src, dst, send, recv, step):
        return pltpu.make_async_remote_copy(
            src_ref=src,
            dst_ref=dst,
            send_sem=send,
            recv_sem=recv,
            device_id=device(*step),
            device_id_type=MESH,
        )

    barrier = pltpu.get_barrier_semaphore()
    for step in NEIGHBOURS:
        pl.semaphore_signal(barrier, inc=1, device_id=device(*step), device_id_type=MESH)

    small_loads = [
        pltpu.make_async_copy(small_in[i], small[i], small_sem.at[i]) for i in range(len(small))
    ]
    feat_load = pltpu.make_async_copy(feat, raw, load_sem)
    feat_load.start()
    for load in small_loads:
        load.start()
    pos, dst, shift, wr, wq, w_scalar, w_gate, w_vector, w_tensor = small

    def turn(g):
        lo, hi = GROUPS[g]
        for i in range(hi - lo):
            for p in range(NP):
                ext[g][p, i] = jnp.transpose(raw[p, 0, :, pl.ds((lo + i) * C, C)])

    feat_load.wait()
    turn(0)
    pl.semaphore_wait(barrier, len(NEIGHBOURS))

    x_copies = []
    for g in range(len(GROUPS)):
        for own, ghost, dx in ((0, 2, -1), (1, 3, 1)):
            x_copies.append(
                remote(ext[g].at[own], ext[g].at[ghost], x_send.at[g, own], x_recv.at[g, own], (dx, 0))
            )
    x_copies[0].start()
    x_copies[1].start()

    for load in small_loads:
        load.wait()
    for p in range(NP):
        posx[0, p] = jnp.zeros((16, S), F32)
        for m in range(3):
            posx[0, p, pl.ds(m, 1), :] = pos[p, m]
        for k in range(NE):
            posx[0, p, pl.ds(3 + k, 1), :] = dst[k, p].astype(F32)
            posx[0, p, pl.ds(6 + k, 1), :] = shift[k, p].astype(F32)
    own = pl.ds(0, NP)
    pos_copies = [
        remote(posx.at[0, 0], posx.at[0, 2], pos_send.at[0], pos_recv.at[0], (-1, 0)),
        remote(posx.at[0, 1], posx.at[0, 3], pos_send.at[1], pos_recv.at[1], (1, 0)),
        remote(posx.at[0, own], posx.at[2, own], pos_send.at[2], pos_recv.at[2], (0, -1)),
        remote(posx.at[0, own], posx.at[1, own], pos_send.at[3], pos_recv.at[3], (0, 1)),
    ]
    for copy in pos_copies:
        copy.start()
    for g in range(1, len(GROUPS)):
        turn(g)
        x_copies[2 * g].start()
        x_copies[2 * g + 1].start()

    def turned(w):
        high, low = split(w)
        rows = jnp.concatenate([high, low, high, jnp.zeros_like(w)], axis=0)
        return jnp.transpose(rows).astype(BF16)

    def widen(f, carry):
        at = pl.ds(pl.multiple_of(f * C, C), C)
        wide[at, :] = turned(wr[:, at])
        return carry

    lax.fori_loop(0, 7, widen, 0)

    for copy in pos_copies:
        copy.wait_recv()
    edges[...] = jnp.zeros_like(edges)
    for q in range(COUNT):
        y, p = q // NP, q % NP
        at = pl.ds(NE * q, NE)
        edges[0, at, :] = posx[y, p, pl.ds(3, NE), :]
        edges[1, at, :] = posx[y, p, pl.ds(6, NE), :]
        edges[2, at, :] = jnp.full((NE, S), p, F32)
        edges[3, at, :] = jnp.full((NE, S), (1, 0, 2)[y], F32)
        for m in range(3):
            edges[4 + m, at, :] = jnp.broadcast_to(posx[y, p, pl.ds(m, 1), :], (NE, S))
    place = edges[0]
    one = jnp.ones_like(place)
    nil = jnp.zeros_like(place)

    def at_least(x, bound):
        return jnp.where(x >= float(bound), one, nil)

    ext_x = at_least(place, 3 * S) + at_least(place, 6 * S) + at_least(place, 9 * S)
    left = place - ext_x * float(3 * S)
    ext_y = at_least(left, S) + at_least(left, 2 * S)
    step_x = ext_x - 1.0 - edges[2]
    step_y = ext_y - 1.0
    far_slot = left - ext_y * S
    target[...] = jnp.where(edges[3] + step_y == 1.0, ext_x * S + far_slot, -1.0)

    atom = lax.broadcasted_iota(jnp.int32, (S, ROWS), 0).astype(F32)

    def pick(y, carry):
        for p in range(NP):
            rows = [target[pl.ds(NE * (NP * y + p) + k, 1), :] for k in range(NE)]
            ends = jnp.concatenate(rows, axis=1) - atom
            for i, x in enumerate((1, 2, 3 * p)):
                hit = jnp.where(ends == float(x * S), 1.0, 0.0).astype(BF16)
                oh[p, pl.ds(i * S, S), pl.ds(pl.multiple_of(y * ROWS, ROWS), ROWS)] = hit
        return carry

    lax.fori_loop(0, 3, pick, 0)

    def in_parts(x):
        first, rest = split(x)
        second, third = split(rest)
        return jnp.concatenate([first, second, third, jnp.zeros_like(first)], 0).astype(BF16)

    def whole(x):
        return (x[0:8] + x[8:16]) + x[16:24]

    lanes = far_slot.astype(jnp.int32)

    def far_place(m):
        found = []
        for slot in (3, 0, 1, 2):
            row = jnp.broadcast_to(posx[0, slot, pl.ds(m, 1), :], (EDGE_ROWS, S))
            found.append(jnp.take_along_axis(row, lanes, axis=1, mode="promise_in_bounds"))
        low = jnp.where(ext_x == 0.0, found[0], found[1])
        high = jnp.where(ext_x == 2.0, found[2], found[3])
        return jnp.where(ext_x < 2.0, low, high)

    disp_x = far_place(0) - edges[4] + step_x
    disp_y = far_place(1) - edges[5] + step_y
    disp_z = far_place(2) - edges[6] + edges[1]
    rho = jnp.sqrt(disp_x * disp_x + disp_y * disp_y + disp_z * disp_z + SOFTENING)
    inverse = 1.0 / rho
    u_x, u_y, u_z = disp_x * inverse, disp_y * inverse, disp_z * inverse
    inverses[...] = inverse
    length_sq = u_x * u_x + u_y * u_y + u_z * u_z
    angular = (
        u_x,
        u_y,
        u_z,
        ROOT_THREE * u_x * u_y,
        ROOT_THREE * u_y * u_z,
        0.5 * (3.0 * u_z * u_z - length_sq),
        ROOT_THREE * u_x * u_z,
        0.5 * ROOT_THREE * (u_x * u_x - u_y * u_y),
    )
    for f in range(8):
        ang[f] = angular[f]
    zf[...] = jnp.zeros_like(zf)
    for b in range(NB):
        off = (rho - (0.5 + SPACING * b)) / SPACING
        basis = jnp.exp(-(off * off))
        slope = basis * off * (-2.0 / SPACING)
        for i, value in enumerate((basis, slope)):
            high, low = split(value)
            zf[32 * i + b] = high
            zf[32 * i + 8 + b] = high
            zf[32 * i + 16 + b] = low

    def columns(k):
        return pl.ds(k * S, S)

    def expanded(q, part, rows):
        edge_rows = [zf[pl.ds(32 * part, 32), NE * q + k, :] for k in range(NP * NE)]
        return dot(rows, jnp.concatenate(edge_rows, axis=1).astype(BF16))

    for q in range(0, COUNT, NP):
        out = expanded(q, 0, wide[pl.ds(0, 7 * C), :])
        for f in range(7):
            for p in range(NP):
                coef[f, q + p] = out[f * C : (f + 1) * C, p * ROWS : (p + 1) * ROWS]

    def columns(k):
        return pl.ds(k * S, S)

    def gather(bufs, g, to, first, last):
        buf = bufs[g]
        n = buf.shape[1]

        for p in range(NP):
            tiles = [buf[slot].reshape(n * C, S) for slot in (0, 1, 3 - p)[first:last]]
            out = dot(jnp.concatenate(tiles, axis=1), oh[p, pl.ds(first * S, (last - first) * S), :])
            for i in range(n):
                for y in range(3):
                    gsc[to + i, NP * y + p] = out[i * C : (i + 1) * C, y * ROWS : (y + 1) * ROWS]

    def each_row(fn, lo, hi):
        def run(q, carry):
            for start in range(0, C, STEP):
                fn(q, pl.ds(start, STEP))
            return carry

        lax.fori_loop(lo, hi, run, 0)

    def angle(f, q, k):
        return ang[f, pl.ds(NE * q + k, 1), :]

    def message_sv(p, r):
        total = [jnp.zeros((STEP, S), F32) for _ in range(READ_BLOCKS)]
        for k in range(NE):
            e = columns(k)
            s = gsc[0, p, r, e]
            v = [gsc[1 + m, p, r, e] for m in range(3)]
            u = [angle(m, p, k) for m in range(3)]
            along = u[0] * v[0] + u[1] * v[1] + u[2] * v[2]
            total[0] = total[0] + coef[0, p, r, e] * s + coef[1, p, r, e] * along
            r3s = coef[3, p, r, e] * s
            r4 = coef[4, p, r, e]
            for m in range(3):
                total[1 + m] = total[1 + m] + r3s * u[m] + r4 * v[m]
        for b in range(READ_BLOCKS):
            acc[b, p, r, :] = total[b]

    def message_st(p, r):
        total = [jnp.zeros((STEP, S), F32) for _ in range(5)]
        for k in range(NE):
            e = columns(k)
            r5s = coef[5, p, r, e] * gsc[0, p, r, e]
            for n in range(5):
                total[n] = total[n] + r5s * angle(3 + n, p, k)
        for n in range(5):
            acc[READ_BLOCKS + n, p, r, :] = total[n]

    def message_t(lo, hi):
        def fn(p, r):
            total = [acc[b, p, r, :] for b in (0, *range(lo, hi))]
            for k in range(NE):
                e = columns(k)
                along = None
                r6 = coef[6, p, r, e]
                for n in range(lo, hi):
                    t = gsc[n, p, r, e]
                    term = angle(n - 1, p, k) * t
                    along = term if along is None else along + term
                    total[1 + n - lo] = total[1 + n - lo] + r6 * t
                total[0] = total[0] + coef[2, p, r, e] * along
            for i, b in enumerate((0, *range(lo, hi))):
                acc[b, p, r, :] = total[i]

        return fn

    third = 1.0 / NE

    def mix(lo, hi, w):
        def run(p, carry):
            terms = [(acc[b, p] * third).astype(BF16) for b in range(lo, hi)]
            out = dot(w_turned[pl.ds(w * C, C), :], jnp.concatenate(terms, axis=1))
            for b in range(lo, hi):
                acc[b, p] = out[:, (b - lo) * S : (b - lo + 1) * S]
            return carry

        for p in range(NP):
            run(p, 0)

    part_copies = []
    for h in range(len(SUMS)):
        for i, dy in ((0, -1), (1, 1)):
            part_copies.append(
                remote(
                    part_out[h].at[i],
                    part_in[h].at[1 - i],
                    part_send.at[h, i],
                    part_recv.at[h, i],
                    (0, dy),
                )
            )

    def send_sums(h):
        for i in range(2):
            for p in range(NP):
                for j, b in enumerate(SUMS[h]):
                    part_out[h][i, p, j] = acc[b, NP * (1 + i) + p].astype(BF16)
            part_copies[2 * h + i].start()

    def add_sums(h):
        for i in range(2):
            part_copies[2 * h + i].wait_recv()
        for p in range(NP):
            for j, b in enumerate(SUMS[h]):
                acc[b, p] = acc[b, p] + part_in[h][0, p, j].astype(F32) + part_in[h][1, p, j].astype(F32)

    for g, (lo, hi) in enumerate(GROUPS):
        x_copies[2 * g].wait_recv()
        x_copies[2 * g + 1].wait_recv()
        gather(ext, g, lo, 0, 3)
        message = message_sv if g == 0 else message_t(lo, hi)
        each_row(message, NP, COUNT)
        send_sums(g)
        each_row(message, 0, NP)
        if g == 0:
            each_row(message_st, 0, COUNT)

    wide[pl.ds(8 * C, C), :] = turned(wq[:, pl.ds(0, C)])
    last = turned(wq[:, pl.ds(C, C)])
    wide[pl.ds(7 * C, C), :] = last
    wide[pl.ds(9 * C, C), :] = last
    for i, w in enumerate((w_scalar, w_gate, w_vector, w_tensor)):
        w_turned[pl.ds(i * C, C), :] = jnp.transpose(w[...])
    for q in range(0, COUNT, NP):
        outs = [expanded(q, 0, wide[pl.ds(7 * C, C), :]), expanded(q, 1, wide[pl.ds(8 * C, 2 * C), :])]
        for p in range(NP):
            at = slice(p * ROWS, (p + 1) * ROWS)
            readout[q + p, 0] = outs[0][:, at]
            readout[q + p, 1] = outs[1][0:C, at]
            readout[q + p, 2] = outs[1][C : 2 * C, at]
    add_sums(0)
    mix(1, 4, 2)
    add_sums(1)
    add_sums(2)
    add_sums(3)

    def scalars(p, carry):
        out = dot(w_turned[pl.ds(0, 2 * C), :], (acc[0, p] * third).astype(BF16))
        pre = out[0:C]
        acc[0, p] = pre * jax.nn.sigmoid(pre)
        gate[p] = jax.nn.sigmoid(out[C : 2 * C])
        return carry

    for p in range(NP):
        scalars(p, 0)

    def read_block(b, y, slot):
        g = b // 2
        return ext2[g].at[y, slot, b - GROUPS2[g][0]]

    def read_block(b, at):
        return ext2[b // 2].at[at, b % 2]

    def update_sv(p, r):
        g = gate[p, r, :]
        for b in range(READ_BLOCKS):
            old = ext[0][p, b, r, :].astype(F32)
            step = g * acc[b, p, r, :] if b > 0 else acc[0, p, r, :]
            read_block(b, p)[r, :] = (old + step).astype(BF16)

    each_row(update_sv, 0, NP)
    mix_x, mix_y = [], []
    for g, buf in enumerate(ext2):
        spans = (
            (mix_x, buf.at[0], buf.at[2], (-1, 0)),
            (mix_x, buf.at[1], buf.at[3], (1, 0)),
            (mix_y, buf.at[own], buf.at[pl.ds(6, NP)], (0, -1)),
            (mix_y, buf.at[own], buf.at[pl.ds(4, NP)], (0, 1)),
        )
        for n, (into, src, to, step) in enumerate(spans):
            into.append(remote(src, to, mix_send.at[g, n], mix_recv.at[g, n], step))
    for copy in (*mix_x[:2], *mix_y, *mix_x[2:]):
        copy.start()

    def near_side(q, r):
        at = jnp.where(q < NP, q, q + 2)
        row = [read_block(b, at)[r, :].astype(F32) for b in range(READ_BLOCKS)]
        s, v = row[0], row[1:]
        for k in range(NE):
            e = columns(k)
            u = [angle(m, q, k) for m in range(3)]
            along = u[0] * v[0] + u[1] * v[1] + u[2] * v[2]
            q1 = readout[q, 0, r, e]
            side[q, 0, r, e] = readout[q, 1, r, e] * s
            side[q, 1, r, e] = readout[q, 2, r, e] * along
            side[q, 2, r, e] = q1 * along
            for m in range(3):
                side[q, 3 + m, r, e] = q1 * v[m]

    for g, (lo, hi) in enumerate(GROUPS2):
        gather(ext2, g, lo, 0, 2)
    each_row(near_side, 0, NP)

    def fold(x):
        return sum(x[8 * i : 8 * i + 8] for i in range(1, STEP // 8)) + x[0:8]

    sums[...] = jnp.zeros_like(sums)

    def pairs(q, lo, first):
        totals = [None if first else sums[i % 4, NE * q + i // 4] for i in range(4 * NE)]

        def add(i, term):
            totals[i] = fold(term) if totals[i] is None else totals[i] + fold(term)

        for start in range(0, C, STEP):
            r = pl.ds(start, STEP)
            for k in range(NE):
                e = columns(k)
                far = [gsc[lo + b, q, r, e] for b in range(READ_BLOCKS)]
                u = [angle(m, q, k) for m in range(3)]
                along = u[0] * far[1] + u[1] * far[2] + u[2] * far[3]
                add(4 * k, side[q, 0, r, e] * far[0] + side[q, 1, r, e] * along)
                own_q = side[q, 2, r, e]
                for m in range(3):
                    add(4 * k + 1 + m, side[q, 3 + m, r, e] * along + own_q * far[1 + m])
        for i in range(4 * NE):
            sums[i % 4, NE * q + i // 4] = totals[i]

    def each_pairs(lo, first, pillars):
        def run(q, carry):
            pairs(q, lo, first)
            return carry

        lax.fori_loop(*pillars, run, 0)

    each_pairs(0, True, (0, NP))
    for copy in mix_y:
        copy.wait_recv()
    each_row(near_side, NP, COUNT)
    each_pairs(0, True, (NP, COUNT))
    for copy in (*pos_copies, *x_copies, *part_copies):
        copy.wait_send()
    for g, (lo, hi) in enumerate(GROUPS2):
        mix_x[2 * g].wait_recv()
        mix_x[2 * g + 1].wait_recv()
        gather(ext2, g, READ_BLOCKS + lo, 2, 3)
    each_pairs(READ_BLOCKS, False, (0, COUNT))

    t_rho, g_x, g_y, g_z = (jnp.sum(sums[i], axis=1) for i in range(4))
    u_x, u_y, u_z, inverse = ang[0], ang[1], ang[2], inverses[...]
    radial_part = t_rho - (u_x * g_x + u_y * g_y + u_z * g_z) * inverse
    grad[...] = jnp.zeros_like(grad)
    grad[0] = radial_part * u_x + g_x * inverse
    grad[1] = radial_part * u_y + g_y * inverse
    grad[2] = radial_part * u_z + g_z * inverse

    def at_atoms(q):
        return (grad[:, NE * q, :] + grad[:, NE * q + 1, :]) + grad[:, NE * q + 2, :]

    force_copies = []
    for i, dy in ((0, -1), (1, 1)):
        force_copies.append(
            remote(force_y.at[i], force_y_in.at[1 - i], force_send.at[i], force_recv.at[i], (0, dy))
        )
    for i, (p, dx) in enumerate(((0, 1), (1, -1))):
        force_copies.append(
            remote(force_x.at[p], force_x_in.at[p], force_send.at[2 + i], force_recv.at[2 + i], (dx, 0))
        )
    parts = []
    for p in range(NP):
        used = [NE * (NP * y + p) + k for y in range(3) for k in range(NE)]
        parts.append(in_parts(jnp.concatenate([grad[:, row, :] for row in used], axis=1)))
    total = [at_atoms(p) for p in range(NP)]
    def scatter(p, lo, hi):
        return whole(jnp.transpose(dot(oh[p, pl.ds(lo * S, (hi - lo) * S), :], parts[p], (1, 1))))

    for p in range(NP):
        force_x[1 - p] = -scatter(p, 2, 3)
        force_copies[3 - p].start()
    for i in range(2):
        for p in range(NP):
            force_y[i, p] = at_atoms(NP * (1 + i) + p)
        force_copies[i].start()
    for p in range(NP):
        out = scatter(p, 0, 2)
        for i in range(NP):
            total[i] = total[i] - out[:, i * S : (i + 1) * S]
    def results(lo, hi, value):
        for i in range(hi - lo):
            for p in range(NP):
                mix_out[p, 0, :, pl.ds((lo + i) * C, C)] = jnp.transpose(value(p, i).astype(BF16))

    mix(4, 9, 3)
    for g, (lo, hi) in enumerate(GROUPS2):
        results(lo, hi, lambda p, i: ext2[g][p, i])
    for g, (lo, hi) in enumerate(GROUPS):
        if g > 0:
            results(lo, hi, lambda p, i: ext[g][p, i].astype(F32) + gate[p] * acc[lo + i, p])
    write = pltpu.make_async_copy(mix_out, mixed, out_sem)
    write.start()

    for copy in force_copies:
        copy.wait_recv()
    for p in range(NP):
        value = (total[p] + force_x_in[p]) + (force_y_in[0, p] + force_y_in[1, p])
        for m in range(3):
            forces[p, m] = value[m : m + 1]

    for copy in (*mix_x, *mix_y, *force_copies):
        copy.wait_send()
    write.wait()


def solution(mesh):
    gx_size, yz_size = mesh.shape["gx"], mesh.shape["yz"]

    def body(features, positions, *rest):
        args = (features, jnp.transpose(positions, (0, 2, 1, 3)), *rest)
        vmem = pl.BlockSpec(memory_space=pltpu.VMEM)
        anywhere = pl.BlockSpec(memory_space=pl.ANY)
        dma = pltpu.SemaphoreType.DMA

        def run_all(*refs):
            kernel(gx_size, yz_size, *refs)

        small = [pltpu.VMEM(x.shape, x.dtype) for x in args[1:]]
        new_features, force = pl.pallas_call(
            run_all,
            out_shape=(
                jax.ShapeDtypeStruct((NP, 1, S, BLOCKS * C), BF16),
                jax.ShapeDtypeStruct((NP, 3, 1, S), F32),
            ),
            in_specs=[anywhere] * 10,
            out_specs=(anywhere, vmem),
            scratch_shapes=small
            + [
                *[pltpu.VMEM((4, hi - lo, C, S), BF16) for lo, hi in GROUPS],
                *[pltpu.VMEM((8, hi - lo, C, S), BF16) for lo, hi in GROUPS2],
                *[pltpu.VMEM((2, NP, len(blocks), C, S), BF16) for blocks in SUMS],
                *[pltpu.VMEM((2, NP, len(blocks), C, S), BF16) for blocks in SUMS],
                pltpu.VMEM((3, 4, 16, S), F32),
                pltpu.VMEM((NP, 3 * S, 3 * ROWS), BF16),
                pltpu.VMEM((7, COUNT, C, ROWS), F32),
                pltpu.VMEM((COUNT, 3, C, ROWS), F32),
                pltpu.VMEM((10 * C, 32), BF16),
                pltpu.VMEM((4 * C, C), BF16),
                pltpu.VMEM((64, EDGE_ROWS, S), F32),
                pltpu.VMEM((8, EDGE_ROWS, S), F32),
                pltpu.VMEM((EDGE_ROWS, S), F32),
                pltpu.VMEM((EDGE_ROWS, S), F32),
                pltpu.VMEM((7, EDGE_ROWS, S), F32),
                pltpu.VMEM((BLOCKS, COUNT, C, S), F32),
                pltpu.VMEM((NP, C, S), F32),
                pltpu.VMEM((BLOCKS, COUNT, C, ROWS), F32),
                pltpu.VMEM((NP, 1, S, BLOCKS * C), BF16),
                pltpu.VMEM((NP, 1, S, BLOCKS * C), BF16),
                pltpu.VMEM((COUNT, 6, C, ROWS), F32),
                pltpu.VMEM((4, EDGE_ROWS, 8, S), F32),
                pltpu.VMEM((8, EDGE_ROWS, S), F32),
                pltpu.VMEM((2, NP, 8, S), F32),
                pltpu.VMEM((2, NP, 8, S), F32),
                pltpu.VMEM((NP, 8, S), F32),
                pltpu.VMEM((NP, 8, S), F32),
                dma((len(small),)),
                dma,
                dma,
                dma((4,)),
                dma((4,)),
                dma((len(GROUPS), 2)),
                dma((len(GROUPS), 2)),
                dma((len(SUMS), 2)),
                dma((len(SUMS), 2)),
                dma((len(GROUPS2), 4)),
                dma((len(GROUPS2), 4)),
                dma((4,)),
                dma((4,)),
            ],
            compiler_params=pltpu.CompilerParams(
                collective_id=0, has_side_effects=True, vmem_limit_bytes=60 * 1024 * 1024
            ),
            cost_estimate=pl.CostEstimate(
                flops=6 * 10**9, bytes_accessed=2 * 10**6, transcendentals=10**5
            ),
        )(*args)
        new_features, force = pl.pallas_call(
            deliver,
            out_shape=(
                jax.ShapeDtypeStruct((NP, 1, S, BLOCKS * C), BF16),
                jax.ShapeDtypeStruct((NP, 3, 1, S), F32),
            ),
            in_specs=[anywhere] * 2,
            out_specs=(anywhere, anywhere),
            scratch_shapes=[
                pltpu.VMEM((NP, 1, S, BLOCKS * C), BF16),
                pltpu.VMEM((NP, 3, 1, S), F32),
                dma((2, 1 + NP)),
            ],
            compiler_params=pltpu.CompilerParams(vmem_limit_bytes=60 * 1024 * 1024),
            cost_estimate=pl.CostEstimate(flops=0, bytes_accessed=12 * 10**5, transcendentals=0),
        )(new_features, force)
        return new_features, jnp.transpose(force, (0, 2, 1, 3))

    in_specs = (
        P("gx", "yz", None, None),
        P("gx", "yz", None, None),
        P(None, "gx", "yz", None),
        P(None, "gx", "yz", None),
        P(),
        P(),
        P(),
        P(),
        P(),
        P(),
    )
    out_specs = (P("gx", "yz", None, None), P("gx", "yz", None, None))
    return jax.shard_map(body, mesh=mesh, in_specs=in_specs, out_specs=out_specs, check_vma=False)
```

```python
import math

import jax
import jax.numpy as jnp
from jax import lax
from jax.experimental import pallas as pl
from jax.experimental.pallas import tpu as pltpu
from jax.sharding import PartitionSpec as P

MESH = pl.DeviceIdType.MESH
F32 = jnp.float32
BF16 = jnp.bfloat16
SOFTENING = 0.25
SPACING = 0.6
ROOT_THREE = math.sqrt(3.0)
C = 128
S = 128
NB = 8
NE = 3
NP = 2
BLOCKS = 9
READ_BLOCKS = 4
ROWS = NE * S
STEP = 32
GROUPS = ((0, 4), (4, 6), (6, 8), (8, 9))
SUMS = ((1, 2, 3), (4, 5), (6, 7), (8, 0))
GROUPS2 = ((0, 2), (2, 4))
COUNT = 6
EDGE_ROWS = 24
NEIGHBOURS = ((-1, 0), (1, 0), (0, -1), (0, 1))


def split(x):
    high = x.astype(BF16).astype(F32)
    return high, x - high


def dot(a, b, contract=(1, 0)):
    dims = (((contract[0],), (contract[1],)), ((), ()))
    return lax.dot_general(a, b, dims, preferred_element_type=F32)


def deliver(mixed, forces, mixed_out, forces_out, held, held_forces, sems):
    parts = [(forces, held_forces, forces_out)]
    parts += [(mixed.at[p], held.at[p], mixed_out.at[p]) for p in range(NP)]
    reads = [pltpu.make_async_copy(a, b, sems.at[0, i]) for i, (a, b, _) in enumerate(parts)]
    writes = [pltpu.make_async_copy(b, c, sems.at[1, i]) for i, (_, b, c) in enumerate(parts)]
    for copy in reads:
        copy.start()
    for read, write in zip(reads, writes):
        read.wait()
        write.start()
    for copy in writes:
        copy.wait()


def kernel(
    gx_size,
    yz_size,
    feat,
    *refs,
):
    small_in, refs = refs[:9], refs[9:]
    mixed, forces, *refs = refs
    small, refs = refs[:9], refs[9:]
    run(gx_size, yz_size, feat, small_in, small, mixed, forces, *refs)


def run(
    gx_size,
    yz_size,
    feat,
    small_in,
    small,
    mixed,
    forces,
    ext0,
    ext1,
    ext2,
    ext3,
    mix0,
    mix1,
    *refs,
):
    n = len(SUMS)
    part_out, part_in, refs = refs[:n], refs[n : 2 * n], refs[2 * n :]
    (
        posx,
        oh,
        coef,
        readout,
        wide,
        w_turned,
        zf,
        ang,
        inverses,
        target,
        edges,
        acc,
        gate,
        gsc,
        raw,
        mix_out,
        side,
        sums,
        grad,
        force_y,
        force_y_in,
        force_x,
        force_x_in,
        small_sem,
        load_sem,
        out_sem,
        pos_send,
        pos_recv,
        x_send,
        x_recv,
        part_send,
        part_recv,
        mix_send,
        mix_recv,
        force_send,
        force_recv,
    ) = refs
    ext, ext2 = (ext0, ext1, ext2, ext3), (mix0, mix1)
    gx = lax.axis_index("gx")
    yz = lax.axis_index("yz")

    def device(dx, dy):
        return (lax.rem(gx + dx + gx_size, gx_size), lax.rem(yz + dy + yz_size, yz_size))

    def remote(src, dst, send, recv, step):
        return pltpu.make_async_remote_copy(
            src_ref=src,
            dst_ref=dst,
            send_sem=send,
            recv_sem=recv,
            device_id=device(*step),
            device_id_type=MESH,
        )

    barrier = pltpu.get_barrier_semaphore()
    for step in NEIGHBOURS:
        pl.semaphore_signal(barrier, inc=1, device_id=device(*step), device_id_type=MESH)

    small_loads = [
        pltpu.make_async_copy(small_in[i], small[i], small_sem.at[i]) for i in range(len(small))
    ]
    feat_load = pltpu.make_async_copy(feat, raw, load_sem)
    feat_load.start()
    for load in small_loads:
        load.start()
    pos, dst, shift, wr, wq, w_scalar, w_gate, w_vector, w_tensor = small

    def turn(g):
        lo, hi = GROUPS[g]
        for i in range(hi - lo):
            for p in range(NP):
                ext[g][p, i] = jnp.transpose(raw[p, 0, :, pl.ds((lo + i) * C, C)])

    feat_load.wait()
    turn(0)
    pl.semaphore_wait(barrier, len(NEIGHBOURS))

    x_copies = []
    for g in range(len(GROUPS)):
        for own, ghost, dx in ((0, 2, -1), (1, 3, 1)):
            x_copies.append(
                remote(ext[g].at[own], ext[g].at[ghost], x_send.at[g, own], x_recv.at[g, own], (dx, 0))
            )
    x_copies[0].start()
    x_copies[1].start()

    for load in small_loads:
        load.wait()
    for p in range(NP):
        posx[0, p] = jnp.zeros((16, S), F32)
        for m in range(3):
            posx[0, p, pl.ds(m, 1), :] = pos[p, m]
        for k in range(NE):
            posx[0, p, pl.ds(3 + k, 1), :] = dst[k, p].astype(F32)
            posx[0, p, pl.ds(6 + k, 1), :] = shift[k, p].astype(F32)
    own = pl.ds(0, NP)
    pos_copies = [
        remote(posx.at[0, 0], posx.at[0, 2], pos_send.at[0], pos_recv.at[0], (-1, 0)),
        remote(posx.at[0, 1], posx.at[0, 3], pos_send.at[1], pos_recv.at[1], (1, 0)),
        remote(posx.at[0, own], posx.at[2, own], pos_send.at[2], pos_recv.at[2], (0, -1)),
        remote(posx.at[0, own], posx.at[1, own], pos_send.at[3], pos_recv.at[3], (0, 1)),
    ]
    for copy in pos_copies:
        copy.start()
    for g in range(1, len(GROUPS)):
        turn(g)
        x_copies[2 * g].start()
        x_copies[2 * g + 1].start()

    def turned(w):
        high, low = split(w)
        rows = jnp.concatenate([high, low, high, jnp.zeros_like(w)], axis=0)
        return jnp.transpose(rows).astype(BF16)

    def widen(f, carry):
        at = pl.ds(pl.multiple_of(f * C, C), C)
        wide[at, :] = turned(wr[:, at])
        return carry

    lax.fori_loop(0, 7, widen, 0)

    for copy in pos_copies:
        copy.wait_recv()
    edges[...] = jnp.zeros_like(edges)
    for q in range(COUNT):
        y, p = q // NP, q % NP
        at = pl.ds(NE * q, NE)
        edges[0, at, :] = posx[y, p, pl.ds(3, NE), :]
        edges[1, at, :] = posx[y, p, pl.ds(6, NE), :]
        edges[2, at, :] = jnp.full((NE, S), p, F32)
        edges[3, at, :] = jnp.full((NE, S), (1, 0, 2)[y], F32)
        for m in range(3):
            edges[4 + m, at, :] = jnp.broadcast_to(posx[y, p, pl.ds(m, 1), :], (NE, S))
    place = edges[0]
    one = jnp.ones_like(place)
    nil = jnp.zeros_like(place)

    def at_least(x, bound):
        return jnp.where(x >= float(bound), one, nil)

    ext_x = at_least(place, 3 * S) + at_least(place, 6 * S) + at_least(place, 9 * S)
    left = place - ext_x * float(3 * S)
    ext_y = at_least(left, S) + at_least(left, 2 * S)
    step_x = ext_x - 1.0 - edges[2]
    step_y = ext_y - 1.0
    far_slot = left - ext_y * S
    target[...] = jnp.where(edges[3] + step_y == 1.0, ext_x * S + far_slot, -1.0)

    atom = lax.broadcasted_iota(jnp.int32, (S, ROWS), 0).astype(F32)

    def pick(y, carry):
        for p in range(NP):
            rows = [target[pl.ds(NE * (NP * y + p) + k, 1), :] for k in range(NE)]
            ends = jnp.concatenate(rows, axis=1) - atom
            for i, x in enumerate((1, 2, 3 * p)):
                hit = jnp.where(ends == float(x * S), 1.0, 0.0).astype(BF16)
                oh[p, pl.ds(i * S, S), pl.ds(pl.multiple_of(y * ROWS, ROWS), ROWS)] = hit
        return carry

    lax.fori_loop(0, 3, pick, 0)

    def in_parts(x):
        first, rest = split(x)
        second, third = split(rest)
        return jnp.concatenate([first, second, third, jnp.zeros_like(first)], 0).astype(BF16)

    def whole(x):
        return (x[0:8] + x[8:16]) + x[16:24]

    lanes = far_slot.astype(jnp.int32)

    def far_place(m):
        found = []
        for slot in (3, 0, 1, 2):
            row = jnp.broadcast_to(posx[0, slot, pl.ds(m, 1), :], (EDGE_ROWS, S))
            found.append(jnp.take_along_axis(row, lanes, axis=1, mode="promise_in_bounds"))
        low = jnp.where(ext_x == 0.0, found[0], found[1])
        high = jnp.where(ext_x == 2.0, found[2], found[3])
        return jnp.where(ext_x < 2.0, low, high)

    disp_x = far_place(0) - edges[4] + step_x
    disp_y = far_place(1) - edges[5] + step_y
    disp_z = far_place(2) - edges[6] + edges[1]
    rho = jnp.sqrt(disp_x * disp_x + disp_y * disp_y + disp_z * disp_z + SOFTENING)
    inverse = 1.0 / rho
    u_x, u_y, u_z = disp_x * inverse, disp_y * inverse, disp_z * inverse
    inverses[...] = inverse
    length_sq = u_x * u_x + u_y * u_y + u_z * u_z
    angular = (
        u_x,
        u_y,
        u_z,
        ROOT_THREE * u_x * u_y,
        ROOT_THREE * u_y * u_z,
        0.5 * (3.0 * u_z * u_z - length_sq),
        ROOT_THREE * u_x * u_z,
        0.5 * ROOT_THREE * (u_x * u_x - u_y * u_y),
    )
    for f in range(8):
        ang[f] = angular[f]
    zf[...] = jnp.zeros_like(zf)
    for b in range(NB):
        off = (rho - (0.5 + SPACING * b)) / SPACING
        basis = jnp.exp(-(off * off))
        slope = basis * off * (-2.0 / SPACING)
        for i, value in enumerate((basis, slope)):
            high, low = split(value)
            zf[32 * i + b] = high
            zf[32 * i + 8 + b] = high
            zf[32 * i + 16 + b] = low

    def columns(k):
        return pl.ds(k * S, S)

    def expanded(q, part, rows):
        edge_rows = [zf[pl.ds(32 * part, 32), NE * q + k, :] for k in range(NP * NE)]
        return dot(rows, jnp.concatenate(edge_rows, axis=1).astype(BF16))

    for q in range(0, COUNT, NP):
        out = expanded(q, 0, wide[pl.ds(0, 7 * C), :])
        for f in range(7):
            for p in range(NP):
                coef[f, q + p] = out[f * C : (f + 1) * C, p * ROWS : (p + 1) * ROWS]

    def columns(k):
        return pl.ds(k * S, S)

    def gather(bufs, g, to, first, last):
        buf = bufs[g]
        n = buf.shape[1]

        for p in range(NP):
            tiles = [buf[slot].reshape(n * C, S) for slot in (0, 1, 3 - p)[first:last]]
            out = dot(jnp.concatenate(tiles, axis=1), oh[p, pl.ds(first * S, (last - first) * S), :])
            for i in range(n):
                for y in range(3):
                    gsc[to + i, NP * y + p] = out[i * C : (i + 1) * C, y * ROWS : (y + 1) * ROWS]

    def each_row(fn, lo, hi):
        def run(y, carry):
            for p in range(NP):
                for start in range(0, C, STEP):
                    fn(NP * y + p, pl.ds(start, STEP))
            return carry

        lax.fori_loop(lo // NP, hi // NP, run, 0)

    def angle(f, q, k):
        return ang[f, pl.ds(NE * q + k, 1), :]

    def message_sv(p, r):
        total = [jnp.zeros((STEP, S), F32) for _ in range(READ_BLOCKS)]
        for k in range(NE):
            e = columns(k)
            s = gsc[0, p, r, e]
            v = [gsc[1 + m, p, r, e] for m in range(3)]
            u = [angle(m, p, k) for m in range(3)]
            along = u[0] * v[0] + u[1] * v[1] + u[2] * v[2]
            total[0] = total[0] + coef[0, p, r, e] * s + coef[1, p, r, e] * along
            r3s = coef[3, p, r, e] * s
            r4 = coef[4, p, r, e]
            for m in range(3):
                total[1 + m] = total[1 + m] + r3s * u[m] + r4 * v[m]
        for b in range(READ_BLOCKS):
            acc[b, p, r, :] = total[b]

    def message_st(p, r):
        total = [jnp.zeros((STEP, S), F32) for _ in range(5)]
        for k in range(NE):
            e = columns(k)
            r5s = coef[5, p, r, e] * gsc[0, p, r, e]
            for n in range(5):
                total[n] = total[n] + r5s * angle(3 + n, p, k)
        for n in range(5):
            acc[READ_BLOCKS + n, p, r, :] = total[n]

    def message_t(lo, hi):
        def fn(p, r):
            total = [acc[b, p, r, :] for b in (0, *range(lo, hi))]
            for k in range(NE):
                e = columns(k)
                along = None
                r6 = coef[6, p, r, e]
                for n in range(lo, hi):
                    t = gsc[n, p, r, e]
                    term = angle(n - 1, p, k) * t
                    along = term if along is None else along + term
                    total[1 + n - lo] = total[1 + n - lo] + r6 * t
                total[0] = total[0] + coef[2, p, r, e] * along
            for i, b in enumerate((0, *range(lo, hi))):
                acc[b, p, r, :] = total[i]

        return fn

    third = 1.0 / NE

    def mix(lo, hi, w):
        def run(p, carry):
            terms = [(acc[b, p] * third).astype(BF16) for b in range(lo, hi)]
            out = dot(w_turned[pl.ds(w * C, C), :], jnp.concatenate(terms, axis=1))
            for b in range(lo, hi):
                acc[b, p] = out[:, (b - lo) * S : (b - lo + 1) * S]
            return carry

        for p in range(NP):
            run(p, 0)

    part_copies = []
    for h in range(len(SUMS)):
        for i, dy in ((0, -1), (1, 1)):
            part_copies.append(
                remote(
                    part_out[h].at[i],
                    part_in[h].at[1 - i],
                    part_send.at[h, i],
                    part_recv.at[h, i],
                    (0, dy),
                )
            )

    def send_sums(h):
        for i in range(2):
            for p in range(NP):
                for j, b in enumerate(SUMS[h]):
                    part_out[h][i, p, j] = acc[b, NP * (1 + i) + p].astype(BF16)
            part_copies[2 * h + i].start()

    def add_sums(h):
        for i in range(2):
            part_copies[2 * h + i].wait_recv()
        for p in range(NP):
            for j, b in enumerate(SUMS[h]):
                acc[b, p] = acc[b, p] + part_in[h][0, p, j].astype(F32) + part_in[h][1, p, j].astype(F32)

    for g, (lo, hi) in enumerate(GROUPS):
        x_copies[2 * g].wait_recv()
        x_copies[2 * g + 1].wait_recv()
        gather(ext, g, lo, 0, 3)
        message = message_sv if g == 0 else message_t(lo, hi)
        each_row(message, NP, COUNT)
        send_sums(g)
        each_row(message, 0, NP)
        if g == 0:
            each_row(message_st, 0, COUNT)

    wide[pl.ds(8 * C, C), :] = turned(wq[:, pl.ds(0, C)])
    last = turned(wq[:, pl.ds(C, C)])
    wide[pl.ds(7 * C, C), :] = last
    wide[pl.ds(9 * C, C), :] = last
    for i, w in enumerate((w_scalar, w_gate, w_vector, w_tensor)):
        w_turned[pl.ds(i * C, C), :] = jnp.transpose(w[...])
    for q in range(0, COUNT, NP):
        outs = [expanded(q, 0, wide[pl.ds(7 * C, C), :]), expanded(q, 1, wide[pl.ds(8 * C, 2 * C), :])]
        for p in range(NP):
            at = slice(p * ROWS, (p + 1) * ROWS)
            readout[q + p, 0] = outs[0][:, at]
            readout[q + p, 1] = outs[1][0:C, at]
            readout[q + p, 2] = outs[1][C : 2 * C, at]
    add_sums(0)
    mix(1, 4, 2)
    add_sums(1)
    add_sums(2)
    add_sums(3)

    def scalars(p, carry):
        out = dot(w_turned[pl.ds(0, 2 * C), :], (acc[0, p] * third).astype(BF16))
        pre = out[0:C]
        acc[0, p] = pre * jax.nn.sigmoid(pre)
        gate[p] = jax.nn.sigmoid(out[C : 2 * C])
        return carry

    for p in range(NP):
        scalars(p, 0)

    def read_block(b, y, slot):
        g = b // 2
        return ext2[g].at[y, slot, b - GROUPS2[g][0]]

    def read_block(b, at):
        return ext2[b // 2].at[at, b % 2]

    def update_sv(p, r):
        g = gate[p, r, :]
        for b in range(READ_BLOCKS):
            old = ext[0][p, b, r, :].astype(F32)
            step = g * acc[b, p, r, :] if b > 0 else acc[0, p, r, :]
            read_block(b, p)[r, :] = (old + step).astype(BF16)

    each_row(update_sv, 0, NP)
    mix_x, mix_y = [], []
    for g, buf in enumerate(ext2):
        spans = (
            (mix_x, buf.at[0], buf.at[2], (-1, 0)),
            (mix_x, buf.at[1], buf.at[3], (1, 0)),
            (mix_y, buf.at[own], buf.at[pl.ds(6, NP)], (0, -1)),
            (mix_y, buf.at[own], buf.at[pl.ds(4, NP)], (0, 1)),
        )
        for n, (into, src, to, step) in enumerate(spans):
            into.append(remote(src, to, mix_send.at[g, n], mix_recv.at[g, n], step))
    for copy in (*mix_x[:2], *mix_y, *mix_x[2:]):
        copy.start()

    def near_side(q, r):
        at = jnp.where(q < NP, q, q + 2)
        row = [read_block(b, at)[r, :].astype(F32) for b in range(READ_BLOCKS)]
        s, v = row[0], row[1:]
        for k in range(NE):
            e = columns(k)
            u = [angle(m, q, k) for m in range(3)]
            along = u[0] * v[0] + u[1] * v[1] + u[2] * v[2]
            q1 = readout[q, 0, r, e]
            side[q, 0, r, e] = readout[q, 1, r, e] * s
            side[q, 1, r, e] = readout[q, 2, r, e] * along
            side[q, 2, r, e] = q1 * along
            for m in range(3):
                side[q, 3 + m, r, e] = q1 * v[m]

    for g, (lo, hi) in enumerate(GROUPS2):
        gather(ext2, g, lo, 0, 2)
    each_row(near_side, 0, NP)

    def fold(x):
        return sum(x[8 * i : 8 * i + 8] for i in range(1, STEP // 8)) + x[0:8]

    sums[...] = jnp.zeros_like(sums)

    def pairs(q, lo, first):
        totals = [None if first else sums[i % 4, NE * q + i // 4] for i in range(4 * NE)]

        def add(i, term):
            totals[i] = fold(term) if totals[i] is None else totals[i] + fold(term)

        for start in range(0, C, STEP):
            r = pl.ds(start, STEP)
            for k in range(NE):
                e = columns(k)
                far = [gsc[lo + b, q, r, e] for b in range(READ_BLOCKS)]
                u = [angle(m, q, k) for m in range(3)]
                along = u[0] * far[1] + u[1] * far[2] + u[2] * far[3]
                add(4 * k, side[q, 0, r, e] * far[0] + side[q, 1, r, e] * along)
                own_q = side[q, 2, r, e]
                for m in range(3):
                    add(4 * k + 1 + m, side[q, 3 + m, r, e] * along + own_q * far[1 + m])
        for i in range(4 * NE):
            sums[i % 4, NE * q + i // 4] = totals[i]

    def each_pairs(lo, first, pillars):
        def run(y, carry):
            for p in range(NP):
                pairs(NP * y + p, lo, first)
            return carry

        lax.fori_loop(pillars[0] // NP, pillars[1] // NP, run, 0)

    each_pairs(0, True, (0, NP))
    for copy in mix_y:
        copy.wait_recv()
    each_row(near_side, NP, COUNT)
    each_pairs(0, True, (NP, COUNT))
    for copy in (*pos_copies, *x_copies, *part_copies):
        copy.wait_send()
    for g, (lo, hi) in enumerate(GROUPS2):
        mix_x[2 * g].wait_recv()
        mix_x[2 * g + 1].wait_recv()
        gather(ext2, g, READ_BLOCKS + lo, 2, 3)
    each_pairs(READ_BLOCKS, False, (0, COUNT))

    t_rho, g_x, g_y, g_z = (jnp.sum(sums[i], axis=1) for i in range(4))
    u_x, u_y, u_z, inverse = ang[0], ang[1], ang[2], inverses[...]
    radial_part = t_rho - (u_x * g_x + u_y * g_y + u_z * g_z) * inverse
    grad[...] = jnp.zeros_like(grad)
    grad[0] = radial_part * u_x + g_x * inverse
    grad[1] = radial_part * u_y + g_y * inverse
    grad[2] = radial_part * u_z + g_z * inverse

    def at_atoms(q):
        return (grad[:, NE * q, :] + grad[:, NE * q + 1, :]) + grad[:, NE * q + 2, :]

    force_copies = []
    for i, dy in ((0, -1), (1, 1)):
        force_copies.append(
            remote(force_y.at[i], force_y_in.at[1 - i], force_send.at[i], force_recv.at[i], (0, dy))
        )
    for i, (p, dx) in enumerate(((0, 1), (1, -1))):
        force_copies.append(
            remote(force_x.at[p], force_x_in.at[p], force_send.at[2 + i], force_recv.at[2 + i], (dx, 0))
        )
    parts = []
    for p in range(NP):
        used = [NE * (NP * y + p) + k for y in range(3) for k in range(NE)]
        parts.append(in_parts(jnp.concatenate([grad[:, row, :] for row in used], axis=1)))
    total = [at_atoms(p) for p in range(NP)]
    def scatter(p, lo, hi):
        return whole(jnp.transpose(dot(oh[p, pl.ds(lo * S, (hi - lo) * S), :], parts[p], (1, 1))))

    for p in range(NP):
        force_x[1 - p] = -scatter(p, 2, 3)
        force_copies[3 - p].start()
    for i in range(2):
        for p in range(NP):
            force_y[i, p] = at_atoms(NP * (1 + i) + p)
        force_copies[i].start()
    for p in range(NP):
        out = scatter(p, 0, 2)
        for i in range(NP):
            total[i] = total[i] - out[:, i * S : (i + 1) * S]
    def results(lo, hi, value):
        for i in range(hi - lo):
            for p in range(NP):
                mix_out[p, 0, :, pl.ds((lo + i) * C, C)] = jnp.transpose(value(p, i).astype(BF16))

    mix(4, 9, 3)
    for g, (lo, hi) in enumerate(GROUPS2):
        results(lo, hi, lambda p, i: ext2[g][p, i])
    for g, (lo, hi) in enumerate(GROUPS):
        if g > 0:
            results(lo, hi, lambda p, i: ext[g][p, i].astype(F32) + gate[p] * acc[lo + i, p])
    write = pltpu.make_async_copy(mix_out, mixed, out_sem)
    write.start()

    for copy in force_copies:
        copy.wait_recv()
    for p in range(NP):
        value = (total[p] + force_x_in[p]) + (force_y_in[0, p] + force_y_in[1, p])
        for m in range(3):
            forces[p, m] = value[m : m + 1]

    for copy in (*mix_x, *mix_y, *force_copies):
        copy.wait_send()
    write.wait()


def solution(mesh):
    gx_size, yz_size = mesh.shape["gx"], mesh.shape["yz"]

    def body(features, positions, *rest):
        args = (features, jnp.transpose(positions, (0, 2, 1, 3)), *rest)
        vmem = pl.BlockSpec(memory_space=pltpu.VMEM)
        anywhere = pl.BlockSpec(memory_space=pl.ANY)
        dma = pltpu.SemaphoreType.DMA

        def run_all(*refs):
            kernel(gx_size, yz_size, *refs)

        small = [pltpu.VMEM(x.shape, x.dtype) for x in args[1:]]
        new_features, force = pl.pallas_call(
            run_all,
            out_shape=(
                jax.ShapeDtypeStruct((NP, 1, S, BLOCKS * C), BF16),
                jax.ShapeDtypeStruct((NP, 3, 1, S), F32),
            ),
            in_specs=[anywhere] * 10,
            out_specs=(anywhere, vmem),
            scratch_shapes=small
            + [
                *[pltpu.VMEM((4, hi - lo, C, S), BF16) for lo, hi in GROUPS],
                *[pltpu.VMEM((8, hi - lo, C, S), BF16) for lo, hi in GROUPS2],
                *[pltpu.VMEM((2, NP, len(blocks), C, S), BF16) for blocks in SUMS],
                *[pltpu.VMEM((2, NP, len(blocks), C, S), BF16) for blocks in SUMS],
                pltpu.VMEM((3, 4, 16, S), F32),
                pltpu.VMEM((NP, 3 * S, 3 * ROWS), BF16),
                pltpu.VMEM((7, COUNT, C, ROWS), F32),
                pltpu.VMEM((COUNT, 3, C, ROWS), F32),
                pltpu.VMEM((10 * C, 32), BF16),
                pltpu.VMEM((4 * C, C), BF16),
                pltpu.VMEM((64, EDGE_ROWS, S), F32),
                pltpu.VMEM((8, EDGE_ROWS, S), F32),
                pltpu.VMEM((EDGE_ROWS, S), F32),
                pltpu.VMEM((EDGE_ROWS, S), F32),
                pltpu.VMEM((7, EDGE_ROWS, S), F32),
                pltpu.VMEM((BLOCKS, COUNT, C, S), F32),
                pltpu.VMEM((NP, C, S), F32),
                pltpu.VMEM((BLOCKS, COUNT, C, ROWS), F32),
                pltpu.VMEM((NP, 1, S, BLOCKS * C), BF16),
                pltpu.VMEM((NP, 1, S, BLOCKS * C), BF16),
                pltpu.VMEM((COUNT, 6, C, ROWS), F32),
                pltpu.VMEM((4, EDGE_ROWS, 8, S), F32),
                pltpu.VMEM((8, EDGE_ROWS, S), F32),
                pltpu.VMEM((2, NP, 8, S), F32),
                pltpu.VMEM((2, NP, 8, S), F32),
                pltpu.VMEM((NP, 8, S), F32),
                pltpu.VMEM((NP, 8, S), F32),
                dma((len(small),)),
                dma,
                dma,
                dma((4,)),
                dma((4,)),
                dma((len(GROUPS), 2)),
                dma((len(GROUPS), 2)),
                dma((len(SUMS), 2)),
                dma((len(SUMS), 2)),
                dma((len(GROUPS2), 4)),
                dma((len(GROUPS2), 4)),
                dma((4,)),
                dma((4,)),
            ],
            compiler_params=pltpu.CompilerParams(
                collective_id=0, has_side_effects=True, vmem_limit_bytes=60 * 1024 * 1024
            ),
            cost_estimate=pl.CostEstimate(
                flops=6 * 10**9, bytes_accessed=2 * 10**6, transcendentals=10**5
            ),
        )(*args)
        new_features, force = pl.pallas_call(
            deliver,
            out_shape=(
                jax.ShapeDtypeStruct((NP, 1, S, BLOCKS * C), BF16),
                jax.ShapeDtypeStruct((NP, 3, 1, S), F32),
            ),
            in_specs=[anywhere] * 2,
            out_specs=(anywhere, anywhere),
            scratch_shapes=[
                pltpu.VMEM((NP, 1, S, BLOCKS * C), BF16),
                pltpu.VMEM((NP, 3, 1, S), F32),
                dma((2, 1 + NP)),
            ],
            compiler_params=pltpu.CompilerParams(vmem_limit_bytes=60 * 1024 * 1024),
            cost_estimate=pl.CostEstimate(flops=0, bytes_accessed=12 * 10**5, transcendentals=0),
        )(new_features, force)
        return new_features, jnp.transpose(force, (0, 2, 1, 3))

    in_specs = (
        P("gx", "yz", None, None),
        P("gx", "yz", None, None),
        P(None, "gx", "yz", None),
        P(None, "gx", "yz", None),
        P(),
        P(),
        P(),
        P(),
        P(),
        P(),
    )
    out_specs = (P("gx", "yz", None, None), P("gx", "yz", None, None))
    return jax.shard_map(body, mesh=mesh, in_specs=in_specs, out_specs=out_specs, check_vma=False)
```
